32 devices in a mesh: dp: 4 (over x, core), seq: 2 (over y), tensor: 4 (over z).
Axes of the slice: x: 2, y: 2, z: 4, core: 2. Of those that a mesh axis runs over, the one named last changes fastest.
Arguments:
- hidden_in: bfloat16 [8192, 2048], P(('dp', 'seq', 'tensor')), may hold values from -6 to 6
- teacher: bfloat16 [8192, 2048], P(('dp', 'seq', 'tensor')), may hold values from -6 to 6
- segment_ids: int32 [8192], P(('dp', 'seq')), may hold values from 0 to 3, as said below
- norm_gain: bfloat16 [2048], P('tensor'), may hold values from 0.5 to 1.5
- input_projection_weight: bfloat16 [2048, 2, 4096], P(('dp', 'seq'), None, 'tensor'), may hold values from -0.125 to 0.125
- conv_weight: bfloat16 [4, 4096], P(None, 'tensor'), may hold values from -3 to 3
- conv_bias: bfloat16 [4096], P('tensor'), may hold values from -3 to 3
- xproj_weight: bfloat16 [4096, 160], P('tensor', ('dp', 'seq')), may hold values from -0.09375 to 0.09375
- dtproj_weight: bfloat16 [128, 4096], P(('dp', 'seq'), 'tensor'), may hold values from -0.5 to 0.5
- dt_bias: float32 [4096], P('tensor'), may hold values from -4.6 to -2.2
- a_log: float32 [16, 4096], P(None, 'tensor'), may hold values from -4 to 2.8
- d_skip: float32 [4096], P('tensor'), may hold values from 0.5 to 1.5
- output_projection_weight: bfloat16 [4096, 2048], P('tensor', ('dp', 'seq')), may hold values from -0.25 to 0.25
Outputs:
- output: bfloat16 [8192, 2048], P(('dp', 'seq', 'tensor'))
- input_grad: float32 [8192, 2048], P(('dp', 'seq', 'tensor'))
- gain_grad: float32 [2048], P('tensor')
- in_weight_grad: float32 [2048, 2, 4096], P(('dp', 'seq'), None, 'tensor')
- conv_weight_grad: float32 [4, 4096], P(None, 'tensor')
- conv_bias_grad: float32 [4096], P('tensor')
- xproj_grad: float32 [4096, 128], P('tensor', ('dp', 'seq'))
- xproj_state_grad: float32 [4096, 32], P('tensor', ('dp', 'seq'))
- dtproj_grad: float32 [128, 4096], P(('dp', 'seq'), 'tensor')
- dt_bias_grad: float32 [4096], P('tensor')
- a_log_grad: float32 [16, 4096], P(None, 'tensor')
- d_skip_grad: float32 [4096], P('tensor')
- out_weight_grad: float32 [4096, 2048], P('tensor', ('dp', 'seq'))
The draws below stay inside these ranges and needn't reach their ends.
Inputs may be any that keep to these rules, and one draw needn't show every extreme that they name: `segment_ids`: in each sequence of 2048 tokens the ids are 1, 2, 3 in runs in that order, then a final run of 0 of 1 to 2048 / 20 tokens; document 1 has 2048 / 10 to 512 tokens, and document 2 covers the tokens from 512 to 1280.
All inputs are finite; a program needn't handle non-finite values.
Results may differ from the reference program's by a relative error of at most 0.0075.
Values may be sent and summed in bfloat16 or wider, within the bound.
A program may use at most 896 MiB of HBM per device.

```python
import math
import jax
import jax.numpy as jnp
from jax import lax

D = 2048
E = 4096
N = 16
R = 128
K = 4
XW = 160
LEN = 2048
SEQS = 4
TOKENS = 8192
LOSS_SCALE = 4096


def draw_segment_ids(key, part):

    def one_sequence(seq_key):
        pad_key, first_key, second_key = jax.random.split(seq_key, 3)
        pad_len = jax.random.randint(pad_key, (), 1, LEN // 20 + 1)
        first_cut = jax.random.randint(first_key, (), LEN // 10, LEN // 4 + 1)
        second_cut = jax.random.randint(second_key, (), LEN // 2 + LEN // 8, 3 * LEN // 4 + 1)
        valid_end = LEN - pad_len
        places = jnp.arange(LEN, dtype=jnp.int32)
        labels = jnp.where(places < first_cut, 1, jnp.where(places < second_cut, 2, jnp.where(places < valid_end, 3, 0)))
        return labels.astype(jnp.int32)
    seq_keys = jax.random.split(jax.random.fold_in(key, 7), SEQS)
    return jax.vmap(one_sequence)(seq_keys).reshape(-1)


def levels(rng, extent, shards, low, high):
    def one(position, shards_of):
        heights = jax.random.uniform(jax.random.fold_in(jax.random.fold_in(rng, 6), position), (shards_of,), jnp.float32, low / len(shards), high / len(shards))
        return jnp.repeat(jnp.exp(heights), extent[position] // shards_of).reshape((-1,) + (1,) * (len(extent) - position - 1))

    loudness = one(*shards[0])
    for cut in shards[1:]:
        loudness = loudness * one(*cut)
    return loudness


def centred(stream_key, extent, spread, reach, pieces=(), kind=jnp.bfloat16):
    gain = levels(stream_key, extent, pieces, -0.22, 0.18) if pieces else 1.0
    drawn = jax.random.normal(stream_key, extent, jnp.float32) * spread * gain
    return jnp.minimum(jnp.maximum(drawn, -reach), reach).astype(kind)


def setup_inputs(seed: int = 0) -> dict:
    key_list = jax.random.split(jax.random.key(seed), 14)
    return {
        "hidden_in": centred(key_list[0], (TOKENS, D), 1.0, 6.0, ((0, 32),)),
        "teacher": centred(key_list[1], (TOKENS, D), 1.0, 6.0, ((0, 32),)),
        "segment_ids": draw_segment_ids(jax.random.fold_in(key_list[13], 71), 0),
        "norm_gain": jnp.clip(1.0 + 0.1 * jax.random.normal(key_list[3], (D,), jnp.float32), 0.5, 1.5).astype(jnp.bfloat16),
        "input_projection_weight": centred(key_list[4], (D, 2, E), D ** -0.5, 0.125, ((0, 8), (2, 4))),
        "conv_weight": centred(key_list[5], (K, E), K ** -0.5, 3.0, ((1, 4),)),
        "conv_bias": centred(key_list[6], (E,), 0.5, 3.0, ((0, 4),)),
        "xproj_weight": centred(key_list[7], (E, XW), E ** -0.5, 0.09375, ((0, 4), (1, 8))),
        "dtproj_weight": centred(key_list[8], (R, E), R ** -0.5, 0.5, ((0, 8), (1, 4))),
        "dt_bias": jnp.clip(-4.6 + 2.3999999 * jax.random.uniform(key_list[9], (E,), jnp.float32) ** levels(key_list[9], (E,), ((0, 4),), -0.2, 0.2), -4.6, -2.2),
        "a_log": jnp.clip(-4.0 + 6.8 * jax.random.uniform(key_list[10], (N, E), jnp.float32) ** levels(key_list[10], (N, E), ((1, 4),), -0.2, 0.2), -4.0, 2.8),
        "d_skip": jnp.clip(0.5 + 1.0 * jax.random.uniform(key_list[11], (E,), jnp.float32) ** levels(key_list[11], (E,), ((0, 4),), -0.2, 0.2), 0.5, 1.5),
        "output_projection_weight": centred(key_list[12], (E, D), (E // 8) ** -0.5, 0.25, ((0, 4), (1, 8))),
    }


EPS = 1e-05

@jax.custom_vjp
def low(v):
    return lax.optimization_barrier(v.astype(jnp.bfloat16)).astype(jnp.float32)

@jax.custom_vjp
def low_back(v):
    return v

def low_keep(v):
    return (low(v), None)

def low_pass(kept, grad):
    return (grad,)

def back_keep(v):
    return (v, None)

def back_low(kept, grad):
    return (low(grad),)
low.defvjp(low_keep, low_pass)
low_back.defvjp(back_keep, back_low)

def selective_scan(step_size, x_low, b_in, c_out, same_doc, decay_rates):
    block_len = math.gcd(LEN, 64)

    def arrange(values):
        shifted = jnp.moveaxis(values, 1, 0)
        return shifted.reshape((LEN // block_len, block_len) + shifted.shape[1:])

    def one_step(carry_state, inputs):
        step_now, x_now, b_now, c_now, keep_now = inputs
        decay_now = jnp.exp(step_now[:, None, :] * decay_rates[None]) * keep_now[:, None, None]
        carry_state = decay_now * carry_state + (step_now * x_now)[:, None, :] * b_now[:, :, None]
        return (carry_state, lax.optimization_barrier(jnp.sum(c_now[:, :, None] * carry_state, axis=1)))

    @jax.checkpoint
    def one_block(carry_state, inputs):
        return lax.scan(one_step, carry_state, inputs)
    zero_state = jnp.zeros((SEQS, decay_rates.shape[0], decay_rates.shape[1]), jnp.float32)
    blocked = (arrange(step_size), arrange(x_low), arrange(b_in), arrange(c_out), arrange(same_doc))
    _, scan_rows = lax.scan(one_block, zero_state, blocked)
    scan_rows = scan_rows.reshape((LEN,) + scan_rows.shape[2:])
    return jnp.moveaxis(scan_rows, 0, 1)

def mixer_layer(hidden, segments, norm_gain, input_projection_weight, conv_weight, conv_bias, xproj_weight, dtproj_weight, dt_bias, a_log, d_skip, output_projection_weight):
    inv_rms = lax.rsqrt(lax.optimization_barrier(jnp.mean(hidden * hidden, axis=-1, keepdims=True)) + EPS)
    normalized_rows = low(hidden * inv_rms * norm_gain)
    projected_input_gate = low_back(jnp.einsum('rvx,xnq->rvnq', normalized_rows, input_projection_weight, precision=lax.Precision.HIGHEST))
    x_inner = projected_input_gate[:, :, 0]
    z_gate = projected_input_gate[:, :, 1]
    conv_taps = conv_weight.shape[0]
    conv_sum = conv_bias + jnp.zeros_like(x_inner)
    for offset in range(conv_taps):
        delay_rows = conv_taps - 1 - offset
        shifted = jnp.pad(x_inner, ((0, 0), (delay_rows, 0), (0, 0)))[:, :LEN]
        shifted_seg = jnp.pad(segments, ((0, 0), (delay_rows, 0)), constant_values=-1)[:, :LEN]
        same_tap = (shifted_seg == segments).astype(jnp.float32)[:, :, None]
        conv_sum = conv_sum + conv_weight[offset] * shifted * same_tap
    x_low = low(jax.nn.silu(conv_sum))
    mixed_rows = low_back(jnp.einsum('sle,ej->slj', x_low, xproj_weight, precision=lax.Precision.HIGHEST))
    rank_width = dtproj_weight.shape[0]
    state_width = (mixed_rows.shape[-1] - rank_width) // 2
    step_low = low(mixed_rows[:, :, :rank_width])
    b_in = mixed_rows[:, :, rank_width:rank_width + state_width]
    c_out = mixed_rows[:, :, rank_width + state_width:]
    pre_act = low_back(jnp.einsum('slr,re->sle', step_low, dtproj_weight, precision=lax.Precision.HIGHEST)) + dt_bias
    step_size = jax.nn.softplus(pre_act)
    decay_rates = -jnp.exp(a_log)
    prev_seg = jnp.pad(segments, ((0, 0), (1, 0)), constant_values=-1)[:, :LEN]
    same_doc = (prev_seg == segments).astype(jnp.float32)
    scan_out = selective_scan(step_size, x_low, b_in, c_out, same_doc, decay_rates) + d_skip * x_low
    gated_output_rows = low(scan_out * jax.nn.silu(z_gate))
    residual_branch = low_back(jnp.einsum('ouv,vf->ouf', gated_output_rows, output_projection_weight, precision=lax.Precision.HIGHEST))
    return hidden + residual_branch

def reference(hidden_in, teacher, segment_ids, norm_gain, input_projection_weight, conv_weight, conv_bias, xproj_weight, dtproj_weight, dt_bias, a_log, d_skip, output_projection_weight):
    segments = segment_ids.reshape(SEQS, LEN)
    target = teacher.astype(jnp.float32).reshape(SEQS, LEN, D)
    valid = (segments != 0).astype(jnp.float32)[:, :, None]
    count = jnp.sum(valid)
    params = (hidden_in.astype(jnp.float32).reshape(SEQS, LEN, D), norm_gain.astype(jnp.float32), input_projection_weight.astype(jnp.float32), conv_weight.astype(jnp.float32), conv_bias.astype(jnp.float32), xproj_weight.astype(jnp.float32), dtproj_weight.astype(jnp.float32), dt_bias.astype(jnp.float32), a_log.astype(jnp.float32), d_skip.astype(jnp.float32), output_projection_weight.astype(jnp.float32))

    def loss_of(*weights):
        result = mixer_layer(weights[0], segments, *weights[1:])
        loss = LOSS_SCALE * jnp.sum(valid * (result - target) ** 2) / count
        return (loss, result)
    _, pullback, result = jax.vjp(loss_of, *params, has_aux=True)
    grads = pullback(jnp.ones((), jnp.float32))
    output = result.reshape(TOKENS, D).astype(jnp.bfloat16)
    input_grad = grads[0].reshape(TOKENS, D)
    xproj_whole = grads[5]
    return (output, input_grad, grads[1], grads[2], grads[3], grads[4], xproj_whole[:, :R], xproj_whole[:, R:], grads[6], grads[7], grads[8], grads[9], grads[10])
```

```python
import functools

import jax
import jax.numpy as jnp
from jax import lax
from jax.experimental import pallas as pl
from jax.experimental.pallas import tpu as pltpu
from jax.sharding import PartitionSpec as P

EPS = 1e-05
LOG2E = 1.4426950408889634
LN2 = 0.6931471805599453
FAR = 1e30


def passed_along(x, axis, by):
    size = lax.axis_size(axis)
    pairs = [(i, i + by) for i in range(size) if 0 <= i + by < size]
    return lax.ppermute(x, axis, pairs)


def silu_slope(values):
    logistic = jax.nn.sigmoid(values)
    return logistic * (1.0 + values * (1.0 - logistic))


F32, BF16 = jnp.float32, jnp.bfloat16
N = 16
CH = 16

def fwd_kernel(stepd_ref, u_ref, bc_ref, cdiag_ref, rate_ref, y_ref, ckpt_ref, last_ref, state_ref, sbf_ref, *, unroll):
    @pl.when(pl.program_id(1) == 0)
    def _():
        state_ref[...] = jnp.zeros_like(state_ref)
    ckpt_ref[0] = state_ref[...]
    rate = rate_ref[...]
    tb = stepd_ref.shape[0]

    def chunk(c, s):
        base = pl.multiple_of(c * CH, CH)
        bc = bc_ref[c]
        for k in range(CH):
            dec = jnp.exp2(rate * stepd_ref[pl.ds(base + k, 1), :])
            s = dec * s + bc[:, k:k + 1] * u_ref[pl.ds(base + k, 1), :]
            sbf_ref[k * N:(k + 1) * N, :] = s.astype(BF16)
        y_ref[pl.ds(base, CH), :] = jnp.dot(cdiag_ref[pl.ds(base, CH), :], sbf_ref[...], preferred_element_type=F32)
        return s

    s = lax.fori_loop(0, tb // CH, chunk, state_ref[...], unroll=unroll)
    state_ref[...] = s
    last_ref[...] = s

def fwd(stepd, u, bc, cdiag, rate, tb=128, w=512, unroll=1):
    t, c = stepd.shape
    w = min(w, c)
    grid = (c // w, t // tb)
    return pl.pallas_call(
        functools.partial(fwd_kernel, unroll=unroll),
        grid=grid,
        in_specs=[
            pl.BlockSpec((tb, w), lambda j, i: (i, j)),
            pl.BlockSpec((tb, w), lambda j, i: (i, j)),
            pl.BlockSpec((tb // CH, N, 2 * CH), lambda j, i: (i, 0, 0)),
            pl.BlockSpec((tb, CH * N), lambda j, i: (i, 0)),
            pl.BlockSpec((N, w), lambda j, i: (0, j)),
        ],
        out_specs=[
            pl.BlockSpec((tb, w), lambda j, i: (i, j)),
            pl.BlockSpec((1, N, w), lambda j, i: (i, 0, j)),
            pl.BlockSpec((N, w), lambda j, i: (0, j)),
        ],
        out_shape=[
            jax.ShapeDtypeStruct((t, c), F32),
            jax.ShapeDtypeStruct((t // tb, N, c), F32),
            jax.ShapeDtypeStruct((N, c), F32),
        ],
        scratch_shapes=[pltpu.VMEM((N, w), F32), pltpu.VMEM((CH * N, w), BF16)],
        compiler_params=pltpu.CompilerParams(vmem_limit_bytes=48 << 20),
        name="scan_forward",
    )(stepd, u, bc, cdiag, rate)

def bwd_kernel(stepd_ref, u_ref, ds_ref, bc_ref, bdiag_ref, ones_ref, rate_ref, ckpt_ref, gin_ref,
               wb_ref, dn_ref, db_ref, dc_ref, acc_ref, g_ref, sbf_ref, abf_ref, rbf_ref, *, unroll):
    @pl.when(pl.program_id(1) == 0)
    def _():
        g_ref[...] = gin_ref[...]
        acc_ref[...] = jnp.zeros_like(acc_ref)
    rate = rate_ref[...]
    tb = stepd_ref.shape[0]
    nc = tb // CH
    row = lax.broadcasted_iota(jnp.int32, (CH, CH * N), 0)
    lane = lax.broadcasted_iota(jnp.int32, (CH, CH * N), 1)
    diag = (row == lane // N).astype(F32)
    sbf_ref[0:N, :] = ckpt_ref[0].astype(BF16)

    def forward(c, s):
        base = pl.multiple_of(c * CH, CH)
        bc = bc_ref[c]
        for k in range(CH):
            dec = jnp.exp2(rate * stepd_ref[pl.ds(base + k, 1), :])
            s = dec * s + bc[:, k:k + 1] * u_ref[pl.ds(base + k, 1), :]
            sbf_ref[pl.ds(pl.multiple_of((base + k + 1) * N, N), N), :] = s.astype(BF16)
        return s

    lax.fori_loop(0, nc, forward, ckpt_ref[0])

    def backward(c, carry):
        g, acc = carry
        c = nc - 1 - c
        base = pl.multiple_of(c * CH, CH)
        bc = bc_ref[c]
        for k in range(CH - 1, -1, -1):
            sd = stepd_ref[pl.ds(base + k, 1), :]
            adj = g + bc[:, CH + k:CH + k + 1] * ds_ref[pl.ds(base + k, 1), :]
            abf_ref[k * N:(k + 1) * N, :] = adj.astype(BF16)
            g = jnp.exp2(rate * sd) * adj
            before = sbf_ref[pl.ds(pl.multiple_of((base + k) * N, N), N), :].astype(F32)
            r = g * before * rate
            rbf_ref[k * N:(k + 1) * N, :] = r.astype(BF16)
            acc = acc + r * sd
        wb_ref[pl.ds(base, CH), :] = jnp.dot(bdiag_ref[pl.ds(base, CH), :], abf_ref[...], preferred_element_type=F32)
        dn_ref[pl.ds(base, CH), :] = jnp.dot(ones_ref[...], rbf_ref[...], preferred_element_type=F32)
        nt = (((1,), (1,)), ((), ()))
        now = sbf_ref[pl.ds(pl.multiple_of((base + 1) * N, N), CH * N), :]
        db = lax.dot_general(u_ref[pl.ds(base, CH), :].astype(BF16), abf_ref[...], nt, preferred_element_type=F32)
        dc = lax.dot_general(ds_ref[pl.ds(base, CH), :].astype(BF16), now, nt, preferred_element_type=F32)
        db_ref[0, pl.ds(c, 1), :] = jnp.sum(db * diag, axis=0, keepdims=True)
        dc_ref[0, pl.ds(c, 1), :] = jnp.sum(dc * diag, axis=0, keepdims=True)
        return g, acc

    g, acc = lax.fori_loop(0, nc, backward, (g_ref[...], acc_ref[...]), unroll=unroll)
    g_ref[...] = g
    acc_ref[...] = acc

def bwd(stepd, u, ds, bc, bdiag, ones, rate, ckpt, gin, tb=128, w=512, unroll=1):
    t, c = stepd.shape
    w = min(w, c)
    nb = t // tb
    grid = (c // w, nb)
    rows = pl.BlockSpec((tb, w), lambda j, i: (nb - 1 - i, j))
    return pl.pallas_call(
        functools.partial(bwd_kernel, unroll=unroll),
        grid=grid,
        in_specs=[
            rows, rows, rows,
            pl.BlockSpec((tb // CH, N, 2 * CH), lambda j, i: (nb - 1 - i, 0, 0)),
            pl.BlockSpec((tb, CH * N), lambda j, i: (nb - 1 - i, 0)),
            pl.BlockSpec((CH, CH * N), lambda j, i: (0, 0)),
            pl.BlockSpec((N, w), lambda j, i: (0, j)),
            pl.BlockSpec((1, N, w), lambda j, i: (nb - 1 - i, 0, j)),
            pl.BlockSpec((N, w), lambda j, i: (0, j)),
        ],
        out_specs=[
            rows, rows,
            pl.BlockSpec((1, tb // CH, CH * N), lambda j, i: (j, nb - 1 - i, 0)),
            pl.BlockSpec((1, tb // CH, CH * N), lambda j, i: (j, nb - 1 - i, 0)),
            pl.BlockSpec((N, w), lambda j, i: (0, j)),
        ],
        out_shape=[
            jax.ShapeDtypeStruct((t, c), F32),
            jax.ShapeDtypeStruct((t, c), F32),
            jax.ShapeDtypeStruct((c // w, t // CH, CH * N), F32),
            jax.ShapeDtypeStruct((c // w, t // CH, CH * N), F32),
            jax.ShapeDtypeStruct((N, c), F32),
        ],
        scratch_shapes=[pltpu.VMEM((N, w), F32), pltpu.VMEM(((tb + 1) * N, w), BF16),
                        pltpu.VMEM((CH * N, w), BF16), pltpu.VMEM((CH * N, w), BF16)],
        compiler_params=pltpu.CompilerParams(vmem_limit_bytes=48 << 20),
        name="scan_backward",
    )(stepd, u, ds, bc, bdiag, ones, rate, ckpt, gin)


def correct_kernel(alive_ref, y_ref, stepd_ref, cdiag_ref, rate_ref, ckpt_ref, sin_ref, yo_ref, ckpto_ref, state_ref, sbf_ref):
    i = pl.program_id(1)

    @pl.when(i == 0)
    def _():
        state_ref[...] = sin_ref[...]

    alive = alive_ref[i] != 0

    @pl.when(alive)
    def _():
        rate = rate_ref[...]
        ckpto_ref[0] = ckpt_ref[0] + state_ref[...]

        def chunk(c, s):
            base = pl.multiple_of(c * CH, CH)
            for k in range(CH):
                s = jnp.exp2(rate * stepd_ref[pl.ds(base + k, 1), :]) * s
                sbf_ref[k * N:(k + 1) * N, :] = s.astype(BF16)
            yo_ref[pl.ds(base, CH), :] = y_ref[pl.ds(base, CH), :] + jnp.dot(
                cdiag_ref[pl.ds(base, CH), :], sbf_ref[...], preferred_element_type=F32
            )
            return s

        state_ref[...] = lax.fori_loop(0, y_ref.shape[0] // CH, chunk, state_ref[...])

    @pl.when(jnp.logical_not(alive))
    def _():
        yo_ref[...] = y_ref[...]
        ckpto_ref[...] = ckpt_ref[...]


def correct(alive, y, stepd, cdiag, rate, ckpt, state_in, tb=128, w=512):
    t, c = stepd.shape
    w = min(w, c)
    rows = pl.BlockSpec((tb, w), lambda j, i, _: (i, j))
    lanes = pl.BlockSpec((N, w), lambda j, i, _: (0, j))
    marks = pl.BlockSpec((1, N, w), lambda j, i, _: (i, 0, j))
    return pl.pallas_call(
        correct_kernel,
        grid_spec=pltpu.PrefetchScalarGridSpec(
            num_scalar_prefetch=1,
            grid=(c // w, t // tb),
            in_specs=[rows, rows, pl.BlockSpec((tb, CH * N), lambda j, i, _: (i, 0)), lanes, marks, lanes],
            out_specs=[rows, marks],
            scratch_shapes=[pltpu.VMEM((N, w), F32), pltpu.VMEM((CH * N, w), BF16)],
        ),
        out_shape=[jax.ShapeDtypeStruct((t, c), F32), jax.ShapeDtypeStruct(ckpt.shape, F32)],
        compiler_params=pltpu.CompilerParams(vmem_limit_bytes=48 << 20),
        name="scan_correct",
    )(alive, y, stepd, cdiag, rate, ckpt, state_in)


def entry_kernel(alive_ref, stepd_ref, ds_ref, bc_ref, rate_ref, g_ref):
    i = pl.program_id(1)

    @pl.when(i == 0)
    def _():
        g_ref[...] = jnp.zeros_like(g_ref)

    @pl.when(alive_ref[pl.num_programs(1) - 1 - i] != 0)
    def _():
        rate = rate_ref[...]
        nc = stepd_ref.shape[0] // CH

        def chunk(c, g):
            c = nc - 1 - c
            base = pl.multiple_of(c * CH, CH)
            bc = bc_ref[c]
            for k in range(CH - 1, -1, -1):
                adj = g + bc[:, CH + k:CH + k + 1] * ds_ref[pl.ds(base + k, 1), :]
                g = jnp.exp2(rate * stepd_ref[pl.ds(base + k, 1), :]) * adj
            return g

        g_ref[...] = lax.fori_loop(0, nc, chunk, g_ref[...])


def entry(alive, stepd, ds, bc, rate, tb=128, w=512):
    t, c = stepd.shape
    w = min(w, c)
    nb = t // tb
    rows = pl.BlockSpec((tb, w), lambda j, i, _: (nb - 1 - i, j))
    lanes = pl.BlockSpec((N, w), lambda j, i, _: (0, j))
    return pl.pallas_call(
        entry_kernel,
        grid_spec=pltpu.PrefetchScalarGridSpec(
            num_scalar_prefetch=1,
            grid=(c // w, nb),
            in_specs=[rows, rows, pl.BlockSpec((tb // CH, N, 2 * CH), lambda j, i, _: (nb - 1 - i, 0, 0)), lanes],
            out_specs=lanes,
        ),
        out_shape=jax.ShapeDtypeStruct((N, c), F32),
        compiler_params=pltpu.CompilerParams(vmem_limit_bytes=48 << 20),
        name="scan_entry",
    )(alive, stepd, ds, bc, rate)


def carried(local, reach, axis, by):
    found = jnp.zeros_like(local)
    for _ in range(lax.axis_size(axis) - 1):
        found = passed_along(local + reach * found, axis, by)
    return found


def columns(values):
    tokens = values.shape[0]
    return values.reshape(tokens // CH, CH, N).transpose(0, 2, 1)


def diagonal(values):
    tokens = values.shape[0]
    mine = jnp.arange(CH * N)[None] // N == jnp.arange(tokens)[:, None] % CH
    return jnp.where(mine, jnp.tile(values.astype(BF16), (1, CH)), 0)


def on_device(
    hidden_in,
    teacher,
    segment_ids,
    norm_gain,
    input_projection_weight,
    conv_weight,
    conv_bias,
    xproj_weight,
    dtproj_weight,
    dt_bias,
    a_log,
    d_skip,
    output_projection_weight,
):
    tok_rows = segment_ids.shape[0]
    row_share = hidden_in.shape[0]
    model_width = hidden_in.shape[1]
    conv_taps = conv_weight.shape[0]
    chan_lanes = conv_weight.shape[1]
    back_rows = conv_taps - 1
    row_start = lax.axis_index("tensor") * row_share
    valid_mask = (segment_ids != 0).astype(jnp.float32)
    count_here = jnp.sum((segment_ids != 0).astype(jnp.int32))
    count_pair = (
        jnp.stack([count_here // 32, count_here % 32]).astype(jnp.float32).astype(jnp.bfloat16)
    )
    w_in, w_x, w_dt, w_out, count_pairs = (
        lax.all_gather(input_projection_weight, ("dp", "seq"), axis=0, tiled=True),
        lax.all_gather(xproj_weight, ("dp", "seq"), axis=1, tiled=True),
        lax.all_gather(dtproj_weight, ("dp", "seq"), axis=0, tiled=True),
        lax.all_gather(output_projection_weight, ("dp", "seq"), axis=1, tiled=True),
        lax.all_gather(count_pair, ("dp", "seq"), axis=0, tiled=True),
    )
    count_pairs = count_pairs.astype(jnp.float32).reshape(-1, 2)
    total_count = 32.0 * jnp.sum(count_pairs[:, 0]) + jnp.sum(count_pairs[:, 1])
    full_rows_b, full_gain_b = (
        lax.all_gather(hidden_in, "tensor", axis=0, tiled=True),
        lax.all_gather(norm_gain, "tensor", axis=0, tiled=True),
    )
    full_rows = full_rows_b.astype(jnp.float32)
    full_gain = full_gain_b.astype(jnp.float32)
    inv_rms = lax.rsqrt(jnp.mean(full_rows * full_rows, axis=1, keepdims=True) + EPS)
    normalized_rows = (full_rows * inv_rms * full_gain[None]).astype(jnp.bfloat16)
    projected_input_gate = jnp.einsum(
        "td,dke->tke", normalized_rows, w_in, preferred_element_type=jnp.float32
    )
    x_inner = projected_input_gate[:, 0]
    z_gate = projected_input_gate[:, 1]
    seg_float = segment_ids.astype(jnp.float32)
    prev_x, prev_seg = passed_along(
        (x_inner[tok_rows - back_rows :], seg_float[tok_rows - back_rows :]), "seq", 1
    )
    ext_x = jnp.concatenate([prev_x, x_inner], 0)
    ext_seg = jnp.concatenate([prev_seg, seg_float], 0)
    tap_keeps = []
    conv_sum = jnp.broadcast_to(conv_bias.astype(jnp.float32)[None], (tok_rows, chan_lanes))
    for offset in range(conv_taps):
        keep_tap = (ext_seg[offset : offset + tok_rows] == seg_float).astype(jnp.float32)[:, None]
        tap_keeps.append(keep_tap)
        conv_sum = (
            conv_sum
            + conv_weight[offset].astype(jnp.float32)[None]
            * ext_x[offset : offset + tok_rows]
            * keep_tap
        )
    x_low = jax.nn.silu(conv_sum).astype(jnp.bfloat16)
    x_float = x_low.astype(jnp.float32)
    mixed_rows = lax.psum(jnp.dot(x_low, w_x, preferred_element_type=jnp.float32), "tensor")
    rank_width = w_dt.shape[0]
    state_width = (mixed_rows.shape[1] - rank_width) // 2
    step_low = mixed_rows[:, :rank_width].astype(jnp.bfloat16)
    b_in = mixed_rows[:, rank_width : rank_width + state_width]
    c_out = mixed_rows[:, rank_width + state_width :]
    pre_act = jnp.dot(step_low, w_dt, preferred_element_type=jnp.float32) + dt_bias[None]
    step_size = jax.nn.softplus(pre_act)
    decay_rates = -jnp.exp(a_log)
    same_doc = (seg_float == ext_seg[back_rows - 1 : back_rows - 1 + tok_rows]).astype(jnp.float32)
    rates = decay_rates * LOG2E
    block = 128
    stepd = jnp.where(same_doc[:, None] != 0, step_size, FAR)
    inject = step_size * x_float
    col_pair = jnp.concatenate([columns(b_in), columns(c_out)], -1)
    b_diag, c_diag = diagonal(b_in), diagonal(c_out)
    resets = jnp.sum((same_doc == 0).astype(jnp.int32).reshape(-1, block), axis=1)
    alive = (jnp.cumsum(resets) - resets == 0).astype(jnp.int32)
    y_local, marks, state_last = fwd(stepd, inject, col_pair, c_diag, rates, tb=block, unroll=2)
    reach = jnp.exp2(rates * jnp.sum(stepd, axis=0)[None])
    state_in = carried(state_last, reach, "seq", 1)
    y_rows, marks = correct(alive, y_local, stepd, c_diag, rates, marks, state_in, tb=block)
    scan_out = y_rows + d_skip[None] * x_float
    gate_act = jax.nn.silu(z_gate)
    gated_output_rows = (scan_out * gate_act).astype(jnp.bfloat16)
    branch_share = lax.psum_scatter(
        jnp.dot(gated_output_rows, w_out, preferred_element_type=jnp.float32),
        "tensor",
        scatter_dimension=0,
        tiled=True,
    )
    share_rows = hidden_in.astype(jnp.float32)
    result = share_rows + branch_share
    output = result.astype(jnp.bfloat16)
    valid_share = lax.dynamic_slice_in_dim(valid_mask, row_start, row_share, 0)
    total_tokens = float(tok_rows * lax.axis_size(("dp", "seq")))
    grad_out = (
        total_tokens / total_count * valid_share[:, None] * (result - teacher.astype(jnp.float32))
    )
    grad_low = grad_out.astype(jnp.bfloat16)
    piece = lax.all_gather(grad_low, "tensor", axis=0, tiled=True)
    block_rows = jnp.einsum("tw,ew->te", piece, w_out, preferred_element_type=jnp.float32)
    d_gated = block_rows
    d_wout = jnp.einsum("te,tw->ew", gated_output_rows, piece, preferred_element_type=jnp.float32)
    d_gated, d_wout = (d_gated, d_wout)
    d_scan = d_gated * gate_act
    d_z = d_gated * scan_out * silu_slope(z_gate)
    d_skip_part = jnp.sum(d_scan * x_float, axis=0)
    adjoint_first = entry(alive, stepd, d_scan, col_pair, rates, tb=block)
    adjoint_in = carried(adjoint_first, reach, "seq", -1)
    ones = diagonal(jnp.ones((CH, N), F32))
    weighted_b, d_rate, d_b_part, d_c_part, a_log_part = bwd(
        stepd, inject, d_scan, col_pair, b_diag, ones, rates, marks, adjoint_in, tb=block, w=1024
    )
    d_step = LN2 * d_rate + x_float * weighted_b
    a_log_part = LN2 * a_log_part
    d_b_part = jnp.sum(d_b_part, axis=0).reshape(tok_rows, N)
    d_c_part = jnp.sum(d_c_part, axis=0).reshape(tok_rows, N)
    d_xlow = d_skip[None] * d_scan + step_size * weighted_b
    d_pre = d_step * jax.nn.sigmoid(pre_act)
    dt_bias_part = jnp.sum(d_pre, axis=0)
    d_pre_low = d_pre.astype(jnp.bfloat16)
    d_wdt = jnp.einsum("tr,te->re", step_low, d_pre_low, preferred_element_type=jnp.float32)
    d_rank = jnp.einsum("te,re->tr", d_pre_low, w_dt, preferred_element_type=jnp.float32)
    d_mixed = lax.psum(jnp.concatenate([d_rank, d_b_part, d_c_part], 1), "tensor")
    d_mixed_low = d_mixed.astype(jnp.bfloat16)
    d_wx = jnp.einsum("te,tj->ej", x_low, d_mixed_low, preferred_element_type=jnp.float32)
    d_wx_rank = d_wx[:, :rank_width]
    d_wx_state = d_wx[:, rank_width:]
    d_xlow = d_xlow + jnp.einsum("tj,ej->te", d_mixed_low, w_x, preferred_element_type=jnp.float32)
    d_conv = d_xlow * silu_slope(conv_sum)
    conv_bias_part = jnp.sum(d_conv, axis=0)
    conv_weight_rows = []
    for offset in range(conv_taps):
        conv_weight_rows.append(
            jnp.sum(d_conv * ext_x[offset : offset + tok_rows] * tap_keeps[offset], axis=0)
        )
    conv_weight_part = jnp.stack(conv_weight_rows, 0)
    conv_padded = jnp.concatenate([d_conv, jnp.zeros((back_rows, chan_lanes), jnp.float32)], 0)
    d_x = jnp.zeros((tok_rows, chan_lanes), jnp.float32)
    for offset in range(conv_taps):
        lead = back_rows - offset
        keep_padded = jnp.concatenate(
            [tap_keeps[offset], jnp.zeros((back_rows, 1), jnp.float32)], 0
        )
        d_x = (
            d_x
            + conv_weight[offset].astype(jnp.float32)[None]
            * conv_padded[lead : lead + tok_rows]
            * keep_padded[lead : lead + tok_rows]
        )
    front_rows = []
    for place in range(back_rows):
        front_total = jnp.zeros((chan_lanes,), jnp.float32)
        for offset in range(place + 1):
            front_total = (
                front_total
                + conv_weight[offset].astype(jnp.float32)
                * d_conv[place - offset]
                * tap_keeps[offset][place - offset, 0]
            )
        front_rows.append(front_total)
    front_grad = jnp.stack(front_rows, 0)
    carried_grad = passed_along(front_grad, "seq", -1)
    d_x = d_x.at[tok_rows - back_rows :].add(carried_grad)
    d_xz = jnp.stack([d_x, d_z], 1).astype(jnp.bfloat16)
    d_win = jnp.einsum("td,tke->dke", normalized_rows, d_xz, preferred_element_type=jnp.float32)
    d_norm_part = jnp.einsum("tke,dke->td", d_xz, w_in, preferred_element_type=jnp.float32)
    scaled_rows = full_rows * inv_rms
    gain_partial = jnp.sum(d_norm_part * scaled_rows, axis=0)
    d_norm_share, gain_part = (
        lax.psum_scatter(d_norm_part, "tensor", scatter_dimension=0, tiled=True),
        lax.psum_scatter(gain_partial, "tensor", scatter_dimension=0, tiled=True),
    )
    inv_share = lax.dynamic_slice_in_dim(inv_rms, row_start, row_share, 0)
    inner_sum = jnp.sum(d_norm_share * full_gain[None] * share_rows, axis=1, keepdims=True)
    inv_cube = inv_share * inv_share * inv_share
    input_grad = (
        grad_out
        + inv_share * full_gain[None] * d_norm_share
        - share_rows * inv_cube * inner_sum / model_width
    )
    g_in, g_x_rank, g_x_state, g_dt, g_out = (
        lax.psum_scatter(d_win, ("dp", "seq"), scatter_dimension=0, tiled=True),
        lax.psum_scatter(d_wx_rank, ("dp", "seq"), scatter_dimension=1, tiled=True),
        lax.psum_scatter(d_wx_state, ("dp", "seq"), scatter_dimension=1, tiled=True),
        lax.psum_scatter(d_wdt, ("dp", "seq"), scatter_dimension=0, tiled=True),
        lax.psum_scatter(d_wout, ("dp", "seq"), scatter_dimension=1, tiled=True),
    )
    g_gain, g_conv_w, g_conv_b, g_bias, g_alog, g_skip = lax.psum(
        (gain_part, conv_weight_part, conv_bias_part, dt_bias_part, a_log_part, d_skip_part),
        ("dp", "seq"),
    )
    return (
        output,
        input_grad,
        g_gain,
        g_in,
        g_conv_w,
        g_conv_b,
        g_x_rank,
        g_x_state,
        g_dt,
        g_bias,
        g_alog,
        g_skip,
        g_out,
    )


def solution(mesh):
    placed = (
        P(("dp", "seq", "tensor"), None),
        P(("dp", "seq", "tensor"), None),
        P(("dp", "seq")),
        P("tensor"),
        P(("dp", "seq"), None, "tensor"),
        P(None, "tensor"),
        P("tensor"),
        P("tensor", ("dp", "seq")),
        P(("dp", "seq"), "tensor"),
        P("tensor"),
        P(None, "tensor"),
        P("tensor"),
        P("tensor", ("dp", "seq")),
    )
    return jax.shard_map(
        on_device,
        mesh=mesh,
        in_specs=placed,
        out_specs=(
            P(("dp", "seq", "tensor"), None),
            P(("dp", "seq", "tensor"), None),
            P("tensor"),
            P(("dp", "seq"), None, "tensor"),
            P(None, "tensor"),
            P("tensor"),
            P("tensor", ("dp", "seq")),
            P("tensor", ("dp", "seq")),
            P(("dp", "seq"), "tensor"),
            P("tensor"),
            P(None, "tensor"),
            P("tensor"),
            P("tensor", ("dp", "seq")),
        ),
        check_vma=False,
    )
```

```python
import functools

import jax
import jax.numpy as jnp
from jax import lax
from jax.experimental import pallas as pl
from jax.experimental.pallas import tpu as pltpu
from jax.sharding import PartitionSpec as P

EPS = 1e-05
LOG2E = 1.4426950408889634
LN2 = 0.6931471805599453
FAR = 1e30


def passed_along(x, axis, by):
    size = lax.axis_size(axis)
    pairs = [(i, i + by) for i in range(size) if 0 <= i + by < size]
    return lax.ppermute(x, axis, pairs)


def silu_slope(values):
    logistic = jax.nn.sigmoid(values)
    return logistic * (1.0 + values * (1.0 - logistic))


F32, BF16 = jnp.float32, jnp.bfloat16
N = 16
CH = 16

def fwd_kernel(stepd_ref, u_ref, bc_ref, cdiag_ref, rate_ref, y_ref, ckpt_ref, last_ref, state_ref, sbf_ref, *, unroll):
    @pl.when(pl.program_id(1) == 0)
    def _():
        state_ref[...] = jnp.zeros_like(state_ref)
    ckpt_ref[0] = state_ref[...]
    rate = rate_ref[...]
    tb = stepd_ref.shape[0]

    def chunk(c, s):
        base = pl.multiple_of(c * CH, CH)
        bc = bc_ref[c]
        for k in range(CH):
            dec = jnp.exp2(rate * stepd_ref[pl.ds(base + k, 1), :])
            s = dec * s + bc[:, k:k + 1] * u_ref[pl.ds(base + k, 1), :]
            sbf_ref[k * N:(k + 1) * N, :] = s.astype(BF16)
        y_ref[pl.ds(base, CH), :] = jnp.dot(cdiag_ref[pl.ds(base, CH), :], sbf_ref[...], preferred_element_type=F32)
        return s

    s = lax.fori_loop(0, tb // CH, chunk, state_ref[...], unroll=unroll)
    state_ref[...] = s
    last_ref[...] = s

def fwd(stepd, u, bc, cdiag, rate, tb=128, w=512, unroll=1):
    t, c = stepd.shape
    w = min(w, c)
    grid = (c // w, t // tb)
    return pl.pallas_call(
        functools.partial(fwd_kernel, unroll=unroll),
        grid=grid,
        in_specs=[
            pl.BlockSpec((tb, w), lambda j, i: (i, j)),
            pl.BlockSpec((tb, w), lambda j, i: (i, j)),
            pl.BlockSpec((tb // CH, N, 2 * CH), lambda j, i: (i, 0, 0)),
            pl.BlockSpec((tb, CH * N), lambda j, i: (i, 0)),
            pl.BlockSpec((N, w), lambda j, i: (0, j)),
        ],
        out_specs=[
            pl.BlockSpec((tb, w), lambda j, i: (i, j)),
            pl.BlockSpec((1, N, w), lambda j, i: (i, 0, j)),
            pl.BlockSpec((N, w), lambda j, i: (0, j)),
        ],
        out_shape=[
            jax.ShapeDtypeStruct((t, c), F32),
            jax.ShapeDtypeStruct((t // tb, N, c), F32),
            jax.ShapeDtypeStruct((N, c), F32),
        ],
        scratch_shapes=[pltpu.VMEM((N, w), F32), pltpu.VMEM((CH * N, w), BF16)],
        compiler_params=pltpu.CompilerParams(vmem_limit_bytes=48 << 20),
        name="scan_forward",
    )(stepd, u, bc, cdiag, rate)

def bwd_kernel(stepd_ref, u_ref, ds_ref, bc_ref, bdiag_ref, ones_ref, rate_ref, ckpt_ref, gin_ref,
               wb_ref, dn_ref, db_ref, dc_ref, acc_ref, g_ref, sbf_ref, abf_ref, rbf_ref, *, unroll):
    @pl.when(pl.program_id(1) == 0)
    def _():
        g_ref[...] = gin_ref[...]
        acc_ref[...] = jnp.zeros_like(acc_ref)
    rate = rate_ref[...]
    tb = stepd_ref.shape[0]
    nc = tb // CH
    row = lax.broadcasted_iota(jnp.int32, (CH, CH * N), 0)
    lane = lax.broadcasted_iota(jnp.int32, (CH, CH * N), 1)
    diag = (row == lane // N).astype(F32)
    sbf_ref[0:N, :] = ckpt_ref[0].astype(BF16)

    def forward(c, s):
        base = pl.multiple_of(c * CH, CH)
        bc = bc_ref[c]
        for k in range(CH):
            dec = jnp.exp2(rate * stepd_ref[pl.ds(base + k, 1), :])
            s = dec * s + bc[:, k:k + 1] * u_ref[pl.ds(base + k, 1), :]
            sbf_ref[pl.ds(pl.multiple_of((base + k + 1) * N, N), N), :] = s.astype(BF16)
        return s

    lax.fori_loop(0, nc, forward, ckpt_ref[0])

    def backward(c, carry):
        g, acc = carry
        c = nc - 1 - c
        base = pl.multiple_of(c * CH, CH)
        bc = bc_ref[c]
        for k in range(CH - 1, -1, -1):
            sd = stepd_ref[pl.ds(base + k, 1), :]
            adj = g + bc[:, CH + k:CH + k + 1] * ds_ref[pl.ds(base + k, 1), :]
            abf_ref[k * N:(k + 1) * N, :] = adj.astype(BF16)
            g = jnp.exp2(rate * sd) * adj
            before = sbf_ref[pl.ds(pl.multiple_of((base + k) * N, N), N), :].astype(F32)
            r = g * before * rate
            rbf_ref[k * N:(k + 1) * N, :] = r.astype(BF16)
            acc = acc + r * sd
        wb_ref[pl.ds(base, CH), :] = jnp.dot(bdiag_ref[pl.ds(base, CH), :], abf_ref[...], preferred_element_type=F32)
        dn_ref[pl.ds(base, CH), :] = jnp.dot(ones_ref[...], rbf_ref[...], preferred_element_type=F32)
        nt = (((1,), (1,)), ((), ()))
        now = sbf_ref[pl.ds(pl.multiple_of((base + 1) * N, N), CH * N), :]
        db = lax.dot_general(u_ref[pl.ds(base, CH), :].astype(BF16), abf_ref[...], nt, preferred_element_type=F32)
        dc = lax.dot_general(ds_ref[pl.ds(base, CH), :].astype(BF16), now, nt, preferred_element_type=F32)
        db_ref[0, pl.ds(c, 1), :] = jnp.sum(db * diag, axis=0, keepdims=True)
        dc_ref[0, pl.ds(c, 1), :] = jnp.sum(dc * diag, axis=0, keepdims=True)
        return g, acc

    g, acc = lax.fori_loop(0, nc, backward, (g_ref[...], acc_ref[...]), unroll=unroll)
    g_ref[...] = g
    acc_ref[...] = acc

def bwd(stepd, u, ds, bc, bdiag, ones, rate, ckpt, gin, tb=128, w=512, unroll=1):
    t, c = stepd.shape
    w = min(w, c)
    nb = t // tb
    grid = (c // w, nb)
    rows = pl.BlockSpec((tb, w), lambda j, i: (nb - 1 - i, j))
    return pl.pallas_call(
        functools.partial(bwd_kernel, unroll=unroll),
        grid=grid,
        in_specs=[
            rows, rows, rows,
            pl.BlockSpec((tb // CH, N, 2 * CH), lambda j, i: (nb - 1 - i, 0, 0)),
            pl.BlockSpec((tb, CH * N), lambda j, i: (nb - 1 - i, 0)),
            pl.BlockSpec((CH, CH * N), lambda j, i: (0, 0)),
            pl.BlockSpec((N, w), lambda j, i: (0, j)),
            pl.BlockSpec((1, N, w), lambda j, i: (nb - 1 - i, 0, j)),
            pl.BlockSpec((N, w), lambda j, i: (0, j)),
        ],
        out_specs=[
            rows, rows,
            pl.BlockSpec((1, tb // CH, CH * N), lambda j, i: (j, nb - 1 - i, 0)),
            pl.BlockSpec((1, tb // CH, CH * N), lambda j, i: (j, nb - 1 - i, 0)),
            pl.BlockSpec((N, w), lambda j, i: (0, j)),
        ],
        out_shape=[
            jax.ShapeDtypeStruct((t, c), F32),
            jax.ShapeDtypeStruct((t, c), F32),
            jax.ShapeDtypeStruct((c // w, t // CH, CH * N), F32),
            jax.ShapeDtypeStruct((c // w, t // CH, CH * N), F32),
            jax.ShapeDtypeStruct((N, c), F32),
        ],
        scratch_shapes=[pltpu.VMEM((N, w), F32), pltpu.VMEM(((tb + 1) * N, w), BF16),
                        pltpu.VMEM((CH * N, w), BF16), pltpu.VMEM((CH * N, w), BF16)],
        compiler_params=pltpu.CompilerParams(vmem_limit_bytes=48 << 20),
        name="scan_backward",
    )(stepd, u, ds, bc, bdiag, ones, rate, ckpt, gin)


def correct_kernel(alive_ref, y_ref, stepd_ref, cdiag_ref, rate_ref, ckpt_ref, sin_ref, yo_ref, ckpto_ref, state_ref, sbf_ref):
    i = pl.program_id(1)

    @pl.when(i == 0)
    def _():
        state_ref[...] = sin_ref[...]

    alive = alive_ref[i] != 0

    @pl.when(alive)
    def _():
        rate = rate_ref[...]
        ckpto_ref[0] = ckpt_ref[0] + state_ref[...]

        def chunk(c, s):
            base = pl.multiple_of(c * CH, CH)
            for k in range(CH):
                s = jnp.exp2(rate * stepd_ref[pl.ds(base + k, 1), :]) * s
                sbf_ref[k * N:(k + 1) * N, :] = s.astype(BF16)
            yo_ref[pl.ds(base, CH), :] = y_ref[pl.ds(base, CH), :] + jnp.dot(
                cdiag_ref[pl.ds(base, CH), :], sbf_ref[...], preferred_element_type=F32
            )
            return s

        state_ref[...] = lax.fori_loop(0, y_ref.shape[0] // CH, chunk, state_ref[...])

    @pl.when(jnp.logical_not(alive))
    def _():
        yo_ref[...] = y_ref[...]
        ckpto_ref[...] = ckpt_ref[...]


def correct(alive, y, stepd, cdiag, rate, ckpt, state_in, tb=128, w=512):
    t, c = stepd.shape
    w = min(w, c)
    rows = pl.BlockSpec((tb, w), lambda j, i, _: (i, j))
    lanes = pl.BlockSpec((N, w), lambda j, i, _: (0, j))
    marks = pl.BlockSpec((1, N, w), lambda j, i, _: (i, 0, j))
    return pl.pallas_call(
        correct_kernel,
        grid_spec=pltpu.PrefetchScalarGridSpec(
            num_scalar_prefetch=1,
            grid=(c // w, t // tb),
            in_specs=[rows, rows, pl.BlockSpec((tb, CH * N), lambda j, i, _: (i, 0)), lanes, marks, lanes],
            out_specs=[rows, marks],
            scratch_shapes=[pltpu.VMEM((N, w), F32), pltpu.VMEM((CH * N, w), BF16)],
        ),
        out_shape=[jax.ShapeDtypeStruct((t, c), F32), jax.ShapeDtypeStruct(ckpt.shape, F32)],
        compiler_params=pltpu.CompilerParams(vmem_limit_bytes=48 << 20),
        name="scan_correct",
    )(alive, y, stepd, cdiag, rate, ckpt, state_in)


def entry_kernel(alive_ref, stepd_ref, ds_ref, bc_ref, rate_ref, g_ref):
    i = pl.program_id(1)

    @pl.when(i == 0)
    def _():
        g_ref[...] = jnp.zeros_like(g_ref)

    @pl.when(alive_ref[pl.num_programs(1) - 1 - i] != 0)
    def _():
        rate = rate_ref[...]
        nc = stepd_ref.shape[0] // CH

        def chunk(c, g):
            c = nc - 1 - c
            base = pl.multiple_of(c * CH, CH)
            bc = bc_ref[c]
            for k in range(CH - 1, -1, -1):
                adj = g + bc[:, CH + k:CH + k + 1] * ds_ref[pl.ds(base + k, 1), :]
                g = jnp.exp2(rate * stepd_ref[pl.ds(base + k, 1), :]) * adj
            return g

        g_ref[...] = lax.fori_loop(0, nc, chunk, g_ref[...])


def entry(alive, stepd, ds, bc, rate, tb=128, w=512):
    t, c = stepd.shape
    w = min(w, c)
    nb = t // tb
    rows = pl.BlockSpec((tb, w), lambda j, i, _: (nb - 1 - i, j))
    lanes = pl.BlockSpec((N, w), lambda j, i, _: (0, j))
    return pl.pallas_call(
        entry_kernel,
        grid_spec=pltpu.PrefetchScalarGridSpec(
            num_scalar_prefetch=1,
            grid=(c // w, nb),
            in_specs=[rows, rows, pl.BlockSpec((tb // CH, N, 2 * CH), lambda j, i, _: (nb - 1 - i, 0, 0)), lanes],
            out_specs=lanes,
        ),
        out_shape=jax.ShapeDtypeStruct((N, c), F32),
        compiler_params=pltpu.CompilerParams(vmem_limit_bytes=48 << 20),
        name="scan_entry",
    )(alive, stepd, ds, bc, rate)


def carried(local, reach, axis, by):
    found = jnp.zeros_like(local)
    for _ in range(lax.axis_size(axis) - 1):
        found = passed_along(local + reach * found, axis, by)
    return found


def columns(values):
    tokens = values.shape[0]
    return values.reshape(tokens // CH, CH, N).transpose(0, 2, 1)


def diagonal(values):
    tokens = values.shape[0]
    mine = jnp.arange(CH * N)[None] // N == jnp.arange(tokens)[:, None] % CH
    return jnp.where(mine, jnp.tile(values.astype(BF16), (1, CH)), 0)


def on_device(
    hidden_in,
    teacher,
    segment_ids,
    norm_gain,
    input_projection_weight,
    conv_weight,
    conv_bias,
    xproj_weight,
    dtproj_weight,
    dt_bias,
    a_log,
    d_skip,
    output_projection_weight,
):
    tok_rows = segment_ids.shape[0]
    row_share = hidden_in.shape[0]
    model_width = hidden_in.shape[1]
    conv_taps = conv_weight.shape[0]
    chan_lanes = conv_weight.shape[1]
    back_rows = conv_taps - 1
    row_start = lax.axis_index("tensor") * row_share
    valid_mask = (segment_ids != 0).astype(jnp.float32)
    count_here = jnp.sum((segment_ids != 0).astype(jnp.int32))
    count_pair = (
        jnp.stack([count_here // 32, count_here % 32]).astype(jnp.float32).astype(jnp.bfloat16)
    )
    w_in, w_x, w_dt, w_out, count_pairs = (
        lax.all_gather(input_projection_weight, ("dp", "seq"), axis=0, tiled=True),
        lax.all_gather(xproj_weight, ("dp", "seq"), axis=1, tiled=True),
        lax.all_gather(dtproj_weight, ("dp", "seq"), axis=0, tiled=True),
        lax.all_gather(output_projection_weight, ("dp", "seq"), axis=1, tiled=True),
        lax.all_gather(count_pair, ("dp", "seq"), axis=0, tiled=True),
    )
    count_pairs = count_pairs.astype(jnp.float32).reshape(-1, 2)
    total_count = 32.0 * jnp.sum(count_pairs[:, 0]) + jnp.sum(count_pairs[:, 1])
    full_rows_b, full_gain_b = (
        lax.all_gather(hidden_in, "tensor", axis=0, tiled=True),
        lax.all_gather(norm_gain, "tensor", axis=0, tiled=True),
    )
    full_rows = full_rows_b.astype(jnp.float32)
    full_gain = full_gain_b.astype(jnp.float32)
    inv_rms = lax.rsqrt(jnp.mean(full_rows * full_rows, axis=1, keepdims=True) + EPS)
    normalized_rows = (full_rows * inv_rms * full_gain[None]).astype(jnp.bfloat16)
    projected_input_gate = jnp.einsum(
        "td,dke->tke", normalized_rows, w_in, preferred_element_type=jnp.float32
    )
    x_inner = projected_input_gate[:, 0]
    z_gate = projected_input_gate[:, 1]
    seg_float = segment_ids.astype(jnp.float32)
    prev_x, prev_seg = passed_along(
        (x_inner[tok_rows - back_rows :], seg_float[tok_rows - back_rows :]), "seq", 1
    )
    ext_x = jnp.concatenate([prev_x, x_inner], 0)
    ext_seg = jnp.concatenate([prev_seg, seg_float], 0)
    tap_keeps = []
    conv_sum = jnp.broadcast_to(conv_bias.astype(jnp.float32)[None], (tok_rows, chan_lanes))
    for offset in range(conv_taps):
        keep_tap = (ext_seg[offset : offset + tok_rows] == seg_float).astype(jnp.float32)[:, None]
        tap_keeps.append(keep_tap)
        conv_sum = (
            conv_sum
            + conv_weight[offset].astype(jnp.float32)[None]
            * ext_x[offset : offset + tok_rows]
            * keep_tap
        )
    x_low = jax.nn.silu(conv_sum).astype(jnp.bfloat16)
    x_float = x_low.astype(jnp.float32)
    mixed_rows = lax.psum(jnp.dot(x_low, w_x, preferred_element_type=jnp.float32), "tensor")
    rank_width = w_dt.shape[0]
    state_width = (mixed_rows.shape[1] - rank_width) // 2
    step_low = mixed_rows[:, :rank_width].astype(jnp.bfloat16)
    b_in = mixed_rows[:, rank_width : rank_width + state_width]
    c_out = mixed_rows[:, rank_width + state_width :]
    pre_act = jnp.dot(step_low, w_dt, preferred_element_type=jnp.float32) + dt_bias[None]
    step_size = jax.nn.softplus(pre_act)
    decay_rates = -jnp.exp(a_log)
    same_doc = (seg_float == ext_seg[back_rows - 1 : back_rows - 1 + tok_rows]).astype(jnp.float32)
    rates = decay_rates * LOG2E
    block = 128
    stepd = jnp.where(same_doc[:, None] != 0, step_size, FAR)
    inject = step_size * x_float
    col_pair = jnp.concatenate([columns(b_in), columns(c_out)], -1)
    b_diag, c_diag = diagonal(b_in), diagonal(c_out)
    resets = jnp.sum((same_doc == 0).astype(jnp.int32).reshape(-1, block), axis=1)
    alive = (jnp.cumsum(resets) - resets == 0).astype(jnp.int32)
    y_local, marks, state_last = fwd(stepd, inject, col_pair, c_diag, rates, tb=block, unroll=2)
    reach = jnp.exp2(rates * jnp.sum(stepd, axis=0)[None])
    state_in = carried(state_last, reach, "seq", 1)
    y_rows, marks = correct(alive, y_local, stepd, c_diag, rates, marks, state_in, tb=block)
    scan_out = y_rows + d_skip[None] * x_float
    gate_act = jax.nn.silu(z_gate)
    gated_output_rows = (scan_out * gate_act).astype(jnp.bfloat16)
    branch_share = lax.psum_scatter(
        jnp.dot(gated_output_rows, w_out, preferred_element_type=F32).astype(BF16),
        "tensor",
        scatter_dimension=0,
        tiled=True,
    ).astype(F32)
    share_rows = hidden_in.astype(jnp.float32)
    result = share_rows + branch_share
    output = result.astype(jnp.bfloat16)
    valid_share = lax.dynamic_slice_in_dim(valid_mask, row_start, row_share, 0)
    total_tokens = float(tok_rows * lax.axis_size(("dp", "seq")))
    grad_out = (
        total_tokens / total_count * valid_share[:, None] * (result - teacher.astype(jnp.float32))
    )
    grad_low = grad_out.astype(jnp.bfloat16)
    piece = lax.all_gather(grad_low, "tensor", axis=0, tiled=True)
    block_rows = jnp.einsum("tw,ew->te", piece, w_out, preferred_element_type=jnp.float32)
    d_gated = block_rows
    d_wout = jnp.einsum("te,tw->we", gated_output_rows, piece, preferred_element_type=jnp.float32)
    d_gated, d_wout = (d_gated, d_wout)
    d_scan = d_gated * gate_act
    d_z = d_gated * scan_out * silu_slope(z_gate)
    d_skip_part = jnp.sum(d_scan * x_float, axis=0)
    adjoint_first = entry(alive, stepd, d_scan, col_pair, rates, tb=block)
    adjoint_in = carried(adjoint_first, reach, "seq", -1)
    ones = diagonal(jnp.ones((CH, N), F32))
    weighted_b, d_rate, d_b_part, d_c_part, a_log_part = bwd(
        stepd, inject, d_scan, col_pair, b_diag, ones, rates, marks, adjoint_in, tb=block, w=1024
    )
    d_step = LN2 * d_rate + x_float * weighted_b
    a_log_part = LN2 * a_log_part
    d_b_part = jnp.sum(d_b_part, axis=0).reshape(tok_rows, N)
    d_c_part = jnp.sum(d_c_part, axis=0).reshape(tok_rows, N)
    d_xlow = d_skip[None] * d_scan + step_size * weighted_b
    d_pre = d_step * jax.nn.sigmoid(pre_act)
    dt_bias_part = jnp.sum(d_pre, axis=0)
    d_pre_low = d_pre.astype(jnp.bfloat16)
    d_wdt = jnp.einsum("tr,te->re", step_low, d_pre_low, preferred_element_type=jnp.float32)
    d_rank = jnp.einsum("te,re->tr", d_pre_low, w_dt, preferred_element_type=jnp.float32)
    d_mixed = lax.psum(jnp.concatenate([d_rank, d_b_part, d_c_part], 1), "tensor")
    d_mixed_low = d_mixed.astype(jnp.bfloat16)
    d_wx = jnp.einsum("te,tj->ej", x_low, d_mixed_low, preferred_element_type=jnp.float32)
    d_wx_rank = d_wx[:, :rank_width]
    d_wx_state = d_wx[:, rank_width:]
    d_xlow = d_xlow + jnp.einsum("tj,ej->te", d_mixed_low, w_x, preferred_element_type=jnp.float32)
    d_conv = d_xlow * silu_slope(conv_sum)
    conv_bias_part = jnp.sum(d_conv, axis=0)
    conv_weight_rows = []
    for offset in range(conv_taps):
        conv_weight_rows.append(
            jnp.sum(d_conv * ext_x[offset : offset + tok_rows] * tap_keeps[offset], axis=0)
        )
    conv_weight_part = jnp.stack(conv_weight_rows, 0)
    conv_padded = jnp.concatenate([d_conv, jnp.zeros((back_rows, chan_lanes), jnp.float32)], 0)
    d_x = jnp.zeros((tok_rows, chan_lanes), jnp.float32)
    for offset in range(conv_taps):
        lead = back_rows - offset
        keep_padded = jnp.concatenate(
            [tap_keeps[offset], jnp.zeros((back_rows, 1), jnp.float32)], 0
        )
        d_x = (
            d_x
            + conv_weight[offset].astype(jnp.float32)[None]
            * conv_padded[lead : lead + tok_rows]
            * keep_padded[lead : lead + tok_rows]
        )
    front_rows = []
    for place in range(back_rows):
        front_total = jnp.zeros((chan_lanes,), jnp.float32)
        for offset in range(place + 1):
            front_total = (
                front_total
                + conv_weight[offset].astype(jnp.float32)
                * d_conv[place - offset]
                * tap_keeps[offset][place - offset, 0]
            )
        front_rows.append(front_total)
    front_grad = jnp.stack(front_rows, 0)
    carried_grad = passed_along(front_grad, "seq", -1)
    d_x = d_x.at[tok_rows - back_rows :].add(carried_grad)
    d_xz = jnp.stack([d_x, d_z], 1).astype(jnp.bfloat16)
    d_win = jnp.einsum("td,tke->dke", normalized_rows, d_xz, preferred_element_type=jnp.float32)
    d_norm_part = jnp.einsum("tke,dke->td", d_xz, w_in, preferred_element_type=jnp.float32)
    inv_share = lax.dynamic_slice_in_dim(inv_rms, row_start, row_share, 0)
    d_norm_share = lax.psum_scatter(d_norm_part.astype(BF16), "tensor", scatter_dimension=0, tiled=True).astype(F32)
    gain_partial = jnp.sum(d_norm_share * share_rows * inv_share, axis=0)
    gain_part = lax.psum_scatter(gain_partial, "tensor", scatter_dimension=0, tiled=True)
    inner_sum = jnp.sum(d_norm_share * full_gain[None] * share_rows, axis=1, keepdims=True)
    inv_cube = inv_share * inv_share * inv_share
    input_grad = (
        grad_out
        + inv_share * full_gain[None] * d_norm_share
        - share_rows * inv_cube * inner_sum / model_width
    )
    parts = lax.axis_size(("dp", "seq"))
    rows_x = jnp.concatenate([d_wx_rank.T.reshape(parts, -1, chan_lanes), d_wx_state.T.reshape(parts, -1, chan_lanes)], 1)
    rows_dt = d_wdt.reshape(parts, -1, chan_lanes)
    g_small = lax.psum_scatter(
        jnp.concatenate([rows_x, rows_dt], 1), ("dp", "seq"), scatter_dimension=0, tiled=True
    )[0]
    rank_here = rank_width // parts
    state_here = 2 * state_width // parts
    g_x_rank = g_small[:rank_here].T
    g_x_state = g_small[rank_here : rank_here + state_here].T
    g_dt = g_small[rank_here + state_here :]
    g_in = lax.psum_scatter(d_win.astype(BF16), ("dp", "seq"), scatter_dimension=0, tiled=True).astype(F32)
    g_out = lax.psum_scatter(d_wout.astype(BF16), ("dp", "seq"), scatter_dimension=0, tiled=True).astype(F32).T
    g_gain, g_conv_w, g_conv_b, g_bias, g_alog, g_skip = lax.psum(
        (gain_part, conv_weight_part, conv_bias_part, dt_bias_part, a_log_part, d_skip_part),
        ("dp", "seq"),
    )
    return (
        output,
        input_grad,
        g_gain,
        g_in,
        g_conv_w,
        g_conv_b,
        g_x_rank,
        g_x_state,
        g_dt,
        g_bias,
        g_alog,
        g_skip,
        g_out,
    )


def solution(mesh):
    placed = (
        P(("dp", "seq", "tensor"), None),
        P(("dp", "seq", "tensor"), None),
        P(("dp", "seq")),
        P("tensor"),
        P(("dp", "seq"), None, "tensor"),
        P(None, "tensor"),
        P("tensor"),
        P("tensor", ("dp", "seq")),
        P(("dp", "seq"), "tensor"),
        P("tensor"),
        P(None, "tensor"),
        P("tensor"),
        P("tensor", ("dp", "seq")),
    )
    return jax.shard_map(
        on_device,
        mesh=mesh,
        in_specs=placed,
        out_specs=(
            P(("dp", "seq", "tensor"), None),
            P(("dp", "seq", "tensor"), None),
            P("tensor"),
            P(("dp", "seq"), None, "tensor"),
            P(None, "tensor"),
            P("tensor"),
            P("tensor", ("dp", "seq")),
            P("tensor", ("dp", "seq")),
            P(("dp", "seq"), "tensor"),
            P("tensor"),
            P(None, "tensor"),
            P("tensor"),
            P("tensor", ("dp", "seq")),
        ),
        check_vma=False,
    )
```

```python
import functools

import jax
import jax.numpy as jnp
from jax import lax
from jax.experimental import pallas as pl
from jax.experimental.pallas import tpu as pltpu
from jax.sharding import PartitionSpec as P

EPS = 1e-05
LOG2E = 1.4426950408889634
LN2 = 0.6931471805599453
FAR = 1e30
MESH = pl.DeviceIdType.MESH


def passed_along(x, axis, by):
    size = lax.axis_size(axis)
    pairs = [(i, i + by) for i in range(size) if 0 <= i + by < size]
    return lax.ppermute(x, axis, pairs)


def silu_slope(values):
    logistic = jax.nn.sigmoid(values)
    return logistic * (1.0 + values * (1.0 - logistic))


F32, BF16 = jnp.float32, jnp.bfloat16
N = 16
CH = 16

def fwd_kernel(stepd_ref, u_ref, bc_ref, cdiag_ref, rate_ref, y_ref, ckpt_ref, last_ref, state_ref, sbf_ref, *, unroll):
    @pl.when(pl.program_id(1) == 0)
    def _():
        state_ref[...] = jnp.zeros_like(state_ref)
    ckpt_ref[0] = state_ref[...]
    rate = rate_ref[...]
    tb = stepd_ref.shape[0]

    def chunk(c, s):
        base = pl.multiple_of(c * CH, CH)
        bc = bc_ref[c]
        for k in range(CH):
            dec = jnp.exp2(rate * stepd_ref[pl.ds(base + k, 1), :])
            s = dec * s + bc[:, k:k + 1] * u_ref[pl.ds(base + k, 1), :]
            sbf_ref[k * N:(k + 1) * N, :] = s.astype(BF16)
        y_ref[pl.ds(base, CH), :] = jnp.dot(cdiag_ref[pl.ds(base, CH), :], sbf_ref[...], preferred_element_type=F32)
        return s

    s = lax.fori_loop(0, tb // CH, chunk, state_ref[...], unroll=unroll)
    state_ref[...] = s
    last_ref[...] = s

def fwd(stepd, u, bc, cdiag, rate, tb=128, w=512, unroll=1):
    t, c = stepd.shape
    w = min(w, c)
    grid = (c // w, t // tb)
    return pl.pallas_call(
        functools.partial(fwd_kernel, unroll=unroll),
        grid=grid,
        in_specs=[
            pl.BlockSpec((tb, w), lambda j, i: (i, j)),
            pl.BlockSpec((tb, w), lambda j, i: (i, j)),
            pl.BlockSpec((tb // CH, N, 2 * CH), lambda j, i: (i, 0, 0)),
            pl.BlockSpec((tb, CH * N), lambda j, i: (i, 0)),
            pl.BlockSpec((N, w), lambda j, i: (0, j)),
        ],
        out_specs=[
            pl.BlockSpec((tb, w), lambda j, i: (i, j)),
            pl.BlockSpec((1, N, w), lambda j, i: (i, 0, j)),
            pl.BlockSpec((N, w), lambda j, i: (0, j)),
        ],
        out_shape=[
            jax.ShapeDtypeStruct((t, c), F32),
            jax.ShapeDtypeStruct((t // tb, N, c), F32),
            jax.ShapeDtypeStruct((N, c), F32),
        ],
        scratch_shapes=[pltpu.VMEM((N, w), F32), pltpu.VMEM((CH * N, w), BF16)],
        compiler_params=pltpu.CompilerParams(vmem_limit_bytes=48 << 20),
        name="scan_forward",
    )(stepd, u, bc, cdiag, rate)

def bwd_kernel(stepd_ref, u_ref, ds_ref, bc_ref, bdiag_ref, ones_ref, rate_ref, ckpt_ref, gin_ref,
               wb_ref, dn_ref, db_ref, dc_ref, acc_ref, g_ref, sbf_ref, abf_ref, rbf_ref, *, unroll):
    @pl.when(pl.program_id(1) == 0)
    def _():
        g_ref[...] = gin_ref[...]
        acc_ref[...] = jnp.zeros_like(acc_ref)
    rate = rate_ref[...]
    tb = stepd_ref.shape[0]
    nc = tb // CH
    row = lax.broadcasted_iota(jnp.int32, (CH, CH * N), 0)
    lane = lax.broadcasted_iota(jnp.int32, (CH, CH * N), 1)
    diag = (row == lane // N).astype(F32)
    sbf_ref[0:N, :] = ckpt_ref[0].astype(BF16)

    def forward(c, s):
        base = pl.multiple_of(c * CH, CH)
        bc = bc_ref[c]
        for k in range(CH):
            dec = jnp.exp2(rate * stepd_ref[pl.ds(base + k, 1), :])
            s = dec * s + bc[:, k:k + 1] * u_ref[pl.ds(base + k, 1), :]
            sbf_ref[pl.ds(pl.multiple_of((base + k + 1) * N, N), N), :] = s.astype(BF16)
        return s

    lax.fori_loop(0, nc, forward, ckpt_ref[0])

    def backward(c, carry):
        g, acc = carry
        c = nc - 1 - c
        base = pl.multiple_of(c * CH, CH)
        bc = bc_ref[c]
        for k in range(CH - 1, -1, -1):
            sd = stepd_ref[pl.ds(base + k, 1), :]
            adj = g + bc[:, CH + k:CH + k + 1] * ds_ref[pl.ds(base + k, 1), :]
            abf_ref[k * N:(k + 1) * N, :] = adj.astype(BF16)
            g = jnp.exp2(rate * sd) * adj
            before = sbf_ref[pl.ds(pl.multiple_of((base + k) * N, N), N), :].astype(F32)
            r = g * before * rate
            rbf_ref[k * N:(k + 1) * N, :] = r.astype(BF16)
            acc = acc + r * sd
        wb_ref[pl.ds(base, CH), :] = jnp.dot(bdiag_ref[pl.ds(base, CH), :], abf_ref[...], preferred_element_type=F32)
        dn_ref[pl.ds(base, CH), :] = jnp.dot(ones_ref[...], rbf_ref[...], preferred_element_type=F32)
        nt = (((1,), (1,)), ((), ()))
        now = sbf_ref[pl.ds(pl.multiple_of((base + 1) * N, N), CH * N), :]
        db = lax.dot_general(u_ref[pl.ds(base, CH), :].astype(BF16), abf_ref[...], nt, preferred_element_type=F32)
        dc = lax.dot_general(ds_ref[pl.ds(base, CH), :].astype(BF16), now, nt, preferred_element_type=F32)
        db_ref[0, pl.ds(c, 1), :] = jnp.sum(db * diag, axis=0, keepdims=True)
        dc_ref[0, pl.ds(c, 1), :] = jnp.sum(dc * diag, axis=0, keepdims=True)
        return g, acc

    g, acc = lax.fori_loop(0, nc, backward, (g_ref[...], acc_ref[...]), unroll=unroll)
    g_ref[...] = g
    acc_ref[...] = acc

def bwd(stepd, u, ds, bc, bdiag, ones, rate, ckpt, gin, tb=128, w=512, unroll=1):
    t, c = stepd.shape
    w = min(w, c)
    nb = t // tb
    grid = (c // w, nb)
    rows = pl.BlockSpec((tb, w), lambda j, i: (nb - 1 - i, j))
    return pl.pallas_call(
        functools.partial(bwd_kernel, unroll=unroll),
        grid=grid,
        in_specs=[
            rows, rows, rows,
            pl.BlockSpec((tb // CH, N, 2 * CH), lambda j, i: (nb - 1 - i, 0, 0)),
            pl.BlockSpec((tb, CH * N), lambda j, i: (nb - 1 - i, 0)),
            pl.BlockSpec((CH, CH * N), lambda j, i: (0, 0)),
            pl.BlockSpec((N, w), lambda j, i: (0, j)),
            pl.BlockSpec((1, N, w), lambda j, i: (nb - 1 - i, 0, j)),
            pl.BlockSpec((N, w), lambda j, i: (0, j)),
        ],
        out_specs=[
            rows, rows,
            pl.BlockSpec((1, tb // CH, CH * N), lambda j, i: (j, nb - 1 - i, 0)),
            pl.BlockSpec((1, tb // CH, CH * N), lambda j, i: (j, nb - 1 - i, 0)),
            pl.BlockSpec((N, w), lambda j, i: (0, j)),
        ],
        out_shape=[
            jax.ShapeDtypeStruct((t, c), F32),
            jax.ShapeDtypeStruct((t, c), F32),
            jax.ShapeDtypeStruct((c // w, t // CH, CH * N), F32),
            jax.ShapeDtypeStruct((c // w, t // CH, CH * N), F32),
            jax.ShapeDtypeStruct((N, c), F32),
        ],
        scratch_shapes=[pltpu.VMEM((N, w), F32), pltpu.VMEM(((tb + 1) * N, w), BF16),
                        pltpu.VMEM((CH * N, w), BF16), pltpu.VMEM((CH * N, w), BF16)],
        compiler_params=pltpu.CompilerParams(vmem_limit_bytes=48 << 20),
        name="scan_backward",
    )(stepd, u, ds, bc, bdiag, ones, rate, ckpt, gin)


def correct_kernel(alive_ref, y_ref, stepd_ref, cdiag_ref, rate_ref, ckpt_ref, sin_ref, yo_ref, ckpto_ref, state_ref, sbf_ref):
    i = pl.program_id(1)

    @pl.when(i == 0)
    def _():
        state_ref[...] = sin_ref[...]

    alive = alive_ref[i] != 0

    @pl.when(alive)
    def _():
        rate = rate_ref[...]
        ckpto_ref[0] = ckpt_ref[0] + state_ref[...]

        def chunk(c, s):
            base = pl.multiple_of(c * CH, CH)
            for k in range(CH):
                s = jnp.exp2(rate * stepd_ref[pl.ds(base + k, 1), :]) * s
                sbf_ref[k * N:(k + 1) * N, :] = s.astype(BF16)
            yo_ref[pl.ds(base, CH), :] = y_ref[pl.ds(base, CH), :] + jnp.dot(
                cdiag_ref[pl.ds(base, CH), :], sbf_ref[...], preferred_element_type=F32
            )
            return s

        state_ref[...] = lax.fori_loop(0, y_ref.shape[0] // CH, chunk, state_ref[...])

    @pl.when(jnp.logical_not(alive))
    def _():
        yo_ref[...] = y_ref[...]
        ckpto_ref[...] = ckpt_ref[...]


def correct(alive, y, stepd, cdiag, rate, ckpt, state_in, tb=128, w=512):
    t, c = stepd.shape
    w = min(w, c)
    rows = pl.BlockSpec((tb, w), lambda j, i, _: (i, j))
    lanes = pl.BlockSpec((N, w), lambda j, i, _: (0, j))
    marks = pl.BlockSpec((1, N, w), lambda j, i, _: (i, 0, j))
    return pl.pallas_call(
        correct_kernel,
        grid_spec=pltpu.PrefetchScalarGridSpec(
            num_scalar_prefetch=1,
            grid=(c // w, t // tb),
            in_specs=[rows, rows, pl.BlockSpec((tb, CH * N), lambda j, i, _: (i, 0)), lanes, marks, lanes],
            out_specs=[rows, marks],
            scratch_shapes=[pltpu.VMEM((N, w), F32), pltpu.VMEM((CH * N, w), BF16)],
        ),
        out_shape=[jax.ShapeDtypeStruct((t, c), F32), jax.ShapeDtypeStruct(ckpt.shape, F32)],
        compiler_params=pltpu.CompilerParams(vmem_limit_bytes=48 << 20),
        name="scan_correct",
    )(alive, y, stepd, cdiag, rate, ckpt, state_in)


def entry_kernel(alive_ref, stepd_ref, ds_ref, bc_ref, rate_ref, g_ref):
    i = pl.program_id(1)

    @pl.when(i == 0)
    def _():
        g_ref[...] = jnp.zeros_like(g_ref)

    @pl.when(alive_ref[pl.num_programs(1) - 1 - i] != 0)
    def _():
        rate = rate_ref[...]
        nc = stepd_ref.shape[0] // CH

        def chunk(c, g):
            c = nc - 1 - c
            base = pl.multiple_of(c * CH, CH)
            bc = bc_ref[c]
            for k in range(CH - 1, -1, -1):
                adj = g + bc[:, CH + k:CH + k + 1] * ds_ref[pl.ds(base + k, 1), :]
                g = jnp.exp2(rate * stepd_ref[pl.ds(base + k, 1), :]) * adj
            return g

        g_ref[...] = lax.fori_loop(0, nc, chunk, g_ref[...])


def entry(alive, stepd, ds, bc, rate, tb=128, w=512):
    t, c = stepd.shape
    w = min(w, c)
    nb = t // tb
    rows = pl.BlockSpec((tb, w), lambda j, i, _: (nb - 1 - i, j))
    lanes = pl.BlockSpec((N, w), lambda j, i, _: (0, j))
    return pl.pallas_call(
        entry_kernel,
        grid_spec=pltpu.PrefetchScalarGridSpec(
            num_scalar_prefetch=1,
            grid=(c // w, nb),
            in_specs=[rows, rows, pl.BlockSpec((tb // CH, N, 2 * CH), lambda j, i, _: (nb - 1 - i, 0, 0)), lanes],
            out_specs=lanes,
        ),
        out_shape=jax.ShapeDtypeStruct((N, c), F32),
        compiler_params=pltpu.CompilerParams(vmem_limit_bytes=48 << 20),
        name="scan_entry",
    )(alive, stepd, ds, bc, rate)


def carried(local, reach, axis, by):
    found = jnp.zeros_like(local)
    for _ in range(lax.axis_size(axis) - 1):
        found = passed_along(local + reach * found, axis, by)
    return found


def columns(values):
    tokens = values.shape[0]
    return values.reshape(tokens // CH, CH, N).transpose(0, 2, 1)


def diagonal(values):
    tokens = values.shape[0]
    mine = jnp.arange(CH * N)[None] // N == jnp.arange(tokens)[:, None] % CH
    return jnp.where(mine, jnp.tile(values.astype(BF16), (1, CH)), 0)


def mesh_copy(src, dst, send, recv, **where):
    return pltpu.make_async_remote_copy(
        src_ref=src, dst_ref=dst, send_sem=send, recv_sem=recv, device_id=where, device_id_type=MESH
    )


def place():
    dp, seq, mine = lax.axis_index("dp"), lax.axis_index("seq"), lax.axis_index("tensor")
    return dp, seq, mine


def tail_kernel(n, dps, seqs, subs, lag, dx_ref, dz_ref, w_ref, nrm_ref, sm_ref, all_ref,
                dn_ref, gin_ref, gs_ref, ga_ref,
                zr, zl, part_r, part_l, one_send, one_recv, two_recv, sm_one, sm_two, all_one, all_two,
                r_send, r_recv, l_send, l_recv, w1s, w1r, w2s, w2r, s1s, s1r, s2s, s2r, a1s, a1r, a2s, a2r):
    dp, seq, t = place()
    core, hi = dp % 2, dp // 2
    chips = dps // 2 * seqs
    chip = hi * seqs + seq
    rows = dn_ref.shape[0]
    part = rows // subs
    wide = dn_ref.shape[1]
    wrows = gin_ref.shape[1]
    tile = 512

    def owner(q, c):
        return (q // seqs * 2 + c) * seqs + q % seqs

    def to_chip(q):
        return dict(dp=q // seqs * 2 + core, seq=q % seqs)

    barrier = pltpu.get_barrier_semaphore()
    pl.semaphore_signal(barrier, inc=1, device_id=dict(dp=hi * 2 + 1 - core), device_id_type=MESH)
    for step in range(1, chips):
        q = lax.rem(chip + step, chips)
        pl.semaphore_signal(barrier, inc=1, device_id=to_chip(q), device_id_type=MESH)

    for peer in (lax.rem(t + 1, n), lax.rem(t + n - 1, n)):
        pl.semaphore_signal(barrier, inc=1, device_id=dict(tensor=peer), device_id_type=MESH)
    pl.semaphore_wait(barrier, chips + 2)

    partner = dict(dp=hi * 2 + 1 - core)
    right, left = dict(tensor=lax.rem(t + 1, n)), dict(tensor=lax.rem(t + n - 1, n))

    def r_copy(i):
        return mesh_copy(zr.at[i], zr.at[i], r_send.at[i], r_recv.at[i], **right)

    def l_copy(i):
        return mesh_copy(zl.at[i], zl.at[i], l_send.at[i], l_recv.at[i], **left)

    def w1_copy(q):
        return mesh_copy(one_send.at[q], one_recv.at[q], w1s.at[q], w1r.at[q], **partner)

    def w2_copy(q, slot):
        return mesh_copy(one_recv.at[q], two_recv.at[slot], w2s.at[q], w2r.at[slot], **to_chip(q))

    def s1_copy(q):
        return mesh_copy(sm_ref.at[owner(q, 1 - core)], sm_one.at[q], s1s.at[q], s1r.at[q], **partner)

    def s2_copy(q, slot):
        return mesh_copy(sm_one.at[q], sm_two.at[slot], s2s.at[q], s2r.at[slot], **to_chip(q))

    def a1_copy():
        return mesh_copy(all_ref, all_one, a1s, a1r, **partner)

    def a2_copy(q, slot):
        return mesh_copy(all_one, all_two.at[slot], a2s.at[q], a2r.at[slot], **to_chip(q))

    def partial_rows(o, dst):
        here = pl.ds(pl.multiple_of(o * rows, rows), rows)

        @pl.loop(0, wide // tile)
        def _(j):
            cols = pl.ds(pl.multiple_of(j * tile, tile), tile)
            nt = (((1,), (1,)), ((), ()))
            dst[:, cols] = lax.dot_general(
                dx_ref[here, :], w_ref[0, cols, :], nt, preferred_element_type=F32
            ) + lax.dot_general(dz_ref[here, :], w_ref[1, cols, :], nt, preferred_element_type=F32)

    def weight_rows(p, k):
        cols = pl.ds(pl.multiple_of(p * wrows, wrows), wrows)
        tn = (((0,), (0,)), ((), ()))
        d_ref = dx_ref if k == 0 else dz_ref
        return lax.dot_general(nrm_ref[:, cols], d_ref[...], tn, preferred_element_type=F32)

    for q in range(chips):
        s1_copy(q).start()
    a1_copy().start()

    def stream(i, limit, start, buf, copy, part_ref, owner_of):
        @pl.when(jnp.logical_and(i >= 0, i < limit))
        def _():
            k, sub = i // subs, i % subs

            @pl.when(sub == 0)
            def _():
                partial_rows(owner_of(k), part_ref)

            here = part_ref[pl.ds(pl.multiple_of(sub * part, part), part), :]

            @pl.when(start)
            def _():
                buf[i] = here.astype(BF16)

            @pl.when(jnp.logical_not(start))
            def _():
                copy(i).wait_recv()
                buf[i] = (here + buf[i].astype(F32)).astype(BF16)

            copy(i).start()

    def step(g, _):
        stream(g - lag * t, (n - 1 - t) * subs, t == 0, zr, r_copy, part_r, lambda k: n - 1 - k)
        stream(g - lag * (n - 1 - t), t * subs, t == n - 1, zl, l_copy, part_l, lambda k: k)

        @pl.when(g < chips)
        def _():
            for k in range(2):
                one_send[g, k] = weight_rows(owner(g, 1 - core), k).astype(BF16)
            w1_copy(g).start()

        @pl.when(jnp.logical_and(g >= chips, g < 2 * chips - 1))
        def _():
            q = lax.rem(chip + 1 + g - chips, chips)
            w1_copy(q).wait_recv()
            for k in range(2):
                one_recv[q, k] = (weight_rows(owner(q, core), k) + one_recv[q, k].astype(F32)).astype(BF16)
            w2_copy(q, chip).start()

        @pl.when(g == 2 * chips - 1)
        def _():
            for q in range(chips):
                s1_copy(q).wait_recv()
                sm_one[q] = sm_one[q] + sm_ref[owner(q, core)]
            a1_copy().wait_recv()
            all_one[...] = all_one[...] + all_ref[...]
            for ahead in range(1, chips):
                q = lax.rem(chip + ahead, chips)
                s2_copy(q, chip).start()
                a2_copy(q, chip).start()
            w1_copy(chip).wait_recv()
            for k in range(2):
                gin_ref[k] = weight_rows(owner(chip, core), k) + one_recv[chip, k].astype(F32)

        @pl.when(g == 2 * chips)
        def _():
            partial_rows(t, dn_ref)

        return 0

    steps = max((n - 1) * max(subs, lag), 2 * chips + 1)
    lax.fori_loop(0, steps, step, 0)

    @pl.loop(0, subs)
    def _(s):
        here = pl.ds(pl.multiple_of(s * part, part), part)

        @pl.when(t > 0)
        def _():
            i = (n - 1 - t) * subs + s
            r_copy(i).wait_recv()
            dn_ref[here, :] = dn_ref[here, :] + zr[i].astype(F32)

        @pl.when(t < n - 1)
        def _():
            i = t * subs + s
            l_copy(i).wait_recv()
            dn_ref[here, :] = dn_ref[here, :] + zl[i].astype(F32)

    gs_ref[...] = sm_one[chip]
    ga_ref[...] = all_one[...]
    for ahead in range(1, chips):
        q = lax.rem(chip + ahead, chips)
        s2_copy(q, q).wait_recv()
        gs_ref[...] = gs_ref[...] + sm_two[q]
        a2_copy(q, q).wait_recv()
        ga_ref[...] = ga_ref[...] + all_two[q]
        w2_copy(q, q).wait_recv()
        gin_ref[...] = gin_ref[...] + two_recv[q].astype(F32)

    for q in range(chips):
        s1_copy(q).wait_send()
        w1_copy(q).wait_send()
    a1_copy().wait_send()
    for ahead in range(1, chips):
        q = lax.rem(chip + ahead, chips)
        s2_copy(q, chip).wait_send()
        a2_copy(q, chip).wait_send()
        w2_copy(q, chip).wait_send()

    @pl.loop(0, (n - 1) * subs)
    def _(i):
        @pl.when(i < (n - 1 - t) * subs)
        def _():
            r_copy(i).wait_send()

        @pl.when(i < t * subs)
        def _():
            l_copy(i).wait_send()


def tail(dx, dz, w_full, normed, small, whole):
    n, dps, seqs = (lax.axis_size(axis) for axis in ("tensor", "dp", "seq"))
    chips = dps // 2 * seqs
    rows = dx.shape[0] // n
    wide, lanes = w_full.shape[1], w_full.shape[2]
    wrows = wide // (dps * seqs)
    subs = max(1, rows // 64)
    hops = (n - 1) * subs
    vmem = pl.BlockSpec(memory_space=pltpu.VMEM)
    dma = pltpu.SemaphoreType.DMA
    few = dma((chips,))
    return pl.pallas_call(
        functools.partial(tail_kernel, n, dps, seqs, subs, 2),
        out_shape=[
            jax.ShapeDtypeStruct((rows, wide), F32),
            jax.ShapeDtypeStruct((2, wrows, lanes), F32),
            jax.ShapeDtypeStruct(small.shape[1:], F32),
            jax.ShapeDtypeStruct(whole.shape, F32),
        ],
        in_specs=[vmem] * 6,
        out_specs=[vmem] * 4,
        scratch_shapes=[
            pltpu.VMEM((hops, rows // subs, wide), BF16),
            pltpu.VMEM((hops, rows // subs, wide), BF16),
            pltpu.VMEM((rows, wide), F32),
            pltpu.VMEM((rows, wide), F32),
            pltpu.VMEM((chips, 2, wrows, lanes), BF16),
            pltpu.VMEM((chips, 2, wrows, lanes), BF16),
            pltpu.VMEM((chips, 2, wrows, lanes), BF16),
            pltpu.VMEM((chips,) + small.shape[1:], F32),
            pltpu.VMEM((chips,) + small.shape[1:], F32),
            pltpu.VMEM(whole.shape, F32),
            pltpu.VMEM((chips,) + whole.shape, F32),
            dma((hops,)), dma((hops,)), dma((hops,)), dma((hops,)),
            few, few, few, few, few, few, few, few, dma, dma, few, few,
        ],
        compiler_params=pltpu.CompilerParams(
            collective_id=2, has_side_effects=True, vmem_limit_bytes=60 << 20
        ),
        name="tail_sums",
    )(dx, dz, w_full, normed, small, whole)


def on_device(
    hidden_in,
    teacher,
    segment_ids,
    norm_gain,
    input_projection_weight,
    conv_weight,
    conv_bias,
    xproj_weight,
    dtproj_weight,
    dt_bias,
    a_log,
    d_skip,
    output_projection_weight,
):
    tok_rows = segment_ids.shape[0]
    row_share = hidden_in.shape[0]
    model_width = hidden_in.shape[1]
    conv_taps = conv_weight.shape[0]
    chan_lanes = conv_weight.shape[1]
    back_rows = conv_taps - 1
    row_start = lax.axis_index("tensor") * row_share
    valid_mask = (segment_ids != 0).astype(jnp.float32)
    count_here = jnp.sum((segment_ids != 0).astype(jnp.int32))
    count_pair = (
        jnp.stack([count_here // 32, count_here % 32]).astype(jnp.float32).astype(jnp.bfloat16)
    )
    w_in, w_x, w_dt, w_out, count_pairs = (
        lax.all_gather(jnp.swapaxes(input_projection_weight, 0, 1), ("dp", "seq"), axis=1, tiled=True),
        lax.all_gather(xproj_weight, ("dp", "seq"), axis=1, tiled=True),
        lax.all_gather(dtproj_weight, ("dp", "seq"), axis=0, tiled=True),
        lax.all_gather(output_projection_weight, ("dp", "seq"), axis=1, tiled=True),
        lax.all_gather(count_pair, ("dp", "seq"), axis=0, tiled=True),
    )
    count_pairs = count_pairs.astype(jnp.float32).reshape(-1, 2)
    total_count = 32.0 * jnp.sum(count_pairs[:, 0]) + jnp.sum(count_pairs[:, 1])
    full_rows_b, full_gain_b = (
        lax.all_gather(hidden_in, "tensor", axis=0, tiled=True),
        lax.all_gather(norm_gain, "tensor", axis=0, tiled=True),
    )
    full_rows = full_rows_b.astype(jnp.float32)
    full_gain = full_gain_b.astype(jnp.float32)
    inv_rms = lax.rsqrt(jnp.mean(full_rows * full_rows, axis=1, keepdims=True) + EPS)
    normalized_rows = (full_rows * inv_rms * full_gain[None]).astype(jnp.bfloat16)
    x_inner = jnp.dot(normalized_rows, w_in[0], preferred_element_type=F32)
    z_gate = jnp.dot(normalized_rows, w_in[1], preferred_element_type=F32)
    seg_float = segment_ids.astype(jnp.float32)
    prev_x, prev_seg = passed_along(
        (x_inner[tok_rows - back_rows :], seg_float[tok_rows - back_rows :]), "seq", 1
    )
    ext_x = jnp.concatenate([prev_x, x_inner], 0)
    ext_seg = jnp.concatenate([prev_seg, seg_float], 0)
    tap_keeps = []
    conv_sum = jnp.broadcast_to(conv_bias.astype(jnp.float32)[None], (tok_rows, chan_lanes))
    for offset in range(conv_taps):
        keep_tap = (ext_seg[offset : offset + tok_rows] == seg_float).astype(jnp.float32)[:, None]
        tap_keeps.append(keep_tap)
        conv_sum = (
            conv_sum
            + conv_weight[offset].astype(jnp.float32)[None]
            * ext_x[offset : offset + tok_rows]
            * keep_tap
        )
    x_low = jax.nn.silu(conv_sum).astype(jnp.bfloat16)
    x_float = x_low.astype(jnp.float32)
    mixed_rows = lax.psum(jnp.dot(x_low, w_x, preferred_element_type=jnp.float32), "tensor")
    rank_width = w_dt.shape[0]
    state_width = (mixed_rows.shape[1] - rank_width) // 2
    step_low = mixed_rows[:, :rank_width].astype(jnp.bfloat16)
    b_in = mixed_rows[:, rank_width : rank_width + state_width]
    c_out = mixed_rows[:, rank_width + state_width :]
    pre_act = jnp.dot(step_low, w_dt, preferred_element_type=jnp.float32) + dt_bias[None]
    step_size = jax.nn.softplus(pre_act)
    decay_rates = -jnp.exp(a_log)
    same_doc = (seg_float == ext_seg[back_rows - 1 : back_rows - 1 + tok_rows]).astype(jnp.float32)
    rates = decay_rates * LOG2E
    block = 128
    stepd = jnp.where(same_doc[:, None] != 0, step_size, FAR)
    inject = step_size * x_float
    col_pair = jnp.concatenate([columns(b_in), columns(c_out)], -1)
    b_diag, c_diag = diagonal(b_in), diagonal(c_out)
    resets = jnp.sum((same_doc == 0).astype(jnp.int32).reshape(-1, block), axis=1)
    alive = (jnp.cumsum(resets) - resets == 0).astype(jnp.int32)
    y_local, marks, state_last = fwd(stepd, inject, col_pair, c_diag, rates, tb=block, unroll=2)
    reach = jnp.exp2(rates * jnp.sum(stepd, axis=0)[None])
    state_in = carried(state_last, reach, "seq", 1)
    y_rows, marks = correct(alive, y_local, stepd, c_diag, rates, marks, state_in, tb=block)
    scan_out = y_rows + d_skip[None] * x_float
    gate_act = jax.nn.silu(z_gate)
    gated_output_rows = (scan_out * gate_act).astype(jnp.bfloat16)
    branch_share = lax.psum_scatter(
        jnp.dot(gated_output_rows, w_out, preferred_element_type=F32).astype(BF16),
        "tensor",
        scatter_dimension=0,
        tiled=True,
    ).astype(F32)
    share_rows = hidden_in.astype(jnp.float32)
    result = share_rows + branch_share
    output = result.astype(jnp.bfloat16)
    valid_share = lax.dynamic_slice_in_dim(valid_mask, row_start, row_share, 0)
    total_tokens = float(tok_rows * lax.axis_size(("dp", "seq")))
    grad_out = (
        total_tokens / total_count * valid_share[:, None] * (result - teacher.astype(jnp.float32))
    )
    grad_low = grad_out.astype(jnp.bfloat16)
    piece = lax.all_gather(grad_low, "tensor", axis=0, tiled=True)
    block_rows = jnp.einsum("tw,ew->te", piece, w_out, preferred_element_type=jnp.float32)
    d_gated = block_rows
    d_wout = jnp.einsum("te,tw->we", gated_output_rows, piece, preferred_element_type=jnp.float32)
    d_gated, d_wout = (d_gated, d_wout)
    d_scan = d_gated * gate_act
    d_z = d_gated * scan_out * silu_slope(z_gate)
    d_skip_part = jnp.sum(d_scan * x_float, axis=0)
    adjoint_first = entry(alive, stepd, d_scan, col_pair, rates, tb=block)
    adjoint_in = carried(adjoint_first, reach, "seq", -1)
    ones = diagonal(jnp.ones((CH, N), F32))
    weighted_b, d_rate, d_b_part, d_c_part, a_log_part = bwd(
        stepd, inject, d_scan, col_pair, b_diag, ones, rates, marks, adjoint_in, tb=block, w=1024
    )
    d_step = LN2 * d_rate + x_float * weighted_b
    a_log_part = LN2 * a_log_part
    d_b_part = jnp.sum(d_b_part, axis=0).reshape(tok_rows, N)
    d_c_part = jnp.sum(d_c_part, axis=0).reshape(tok_rows, N)
    d_xlow = d_skip[None] * d_scan + step_size * weighted_b
    d_pre = d_step * jax.nn.sigmoid(pre_act)
    dt_bias_part = jnp.sum(d_pre, axis=0)
    d_pre_low = d_pre.astype(jnp.bfloat16)
    d_wdt = jnp.einsum("tr,te->re", step_low, d_pre_low, preferred_element_type=jnp.float32)
    d_rank = jnp.einsum("te,re->tr", d_pre_low, w_dt, preferred_element_type=jnp.float32)
    d_mixed = lax.psum(jnp.concatenate([d_rank, d_b_part, d_c_part], 1), "tensor")
    d_mixed_low = d_mixed.astype(jnp.bfloat16)
    d_wx = jnp.einsum("te,tj->ej", x_low, d_mixed_low, preferred_element_type=jnp.float32)
    d_wx_rank = d_wx[:, :rank_width]
    d_wx_state = d_wx[:, rank_width:]
    d_xlow = d_xlow + jnp.einsum("tj,ej->te", d_mixed_low, w_x, preferred_element_type=jnp.float32)
    d_conv = d_xlow * silu_slope(conv_sum)
    conv_bias_part = jnp.sum(d_conv, axis=0)
    conv_weight_rows = []
    for offset in range(conv_taps):
        conv_weight_rows.append(
            jnp.sum(d_conv * ext_x[offset : offset + tok_rows] * tap_keeps[offset], axis=0)
        )
    conv_weight_part = jnp.stack(conv_weight_rows, 0)
    conv_padded = jnp.concatenate([d_conv, jnp.zeros((back_rows, chan_lanes), jnp.float32)], 0)
    d_x = jnp.zeros((tok_rows, chan_lanes), jnp.float32)
    for offset in range(conv_taps):
        lead = back_rows - offset
        keep_padded = jnp.concatenate(
            [tap_keeps[offset], jnp.zeros((back_rows, 1), jnp.float32)], 0
        )
        d_x = (
            d_x
            + conv_weight[offset].astype(jnp.float32)[None]
            * conv_padded[lead : lead + tok_rows]
            * keep_padded[lead : lead + tok_rows]
        )
    front_rows = []
    for place in range(back_rows):
        front_total = jnp.zeros((chan_lanes,), jnp.float32)
        for offset in range(place + 1):
            front_total = (
                front_total
                + conv_weight[offset].astype(jnp.float32)
                * d_conv[place - offset]
                * tap_keeps[offset][place - offset, 0]
            )
        front_rows.append(front_total)
    front_grad = jnp.stack(front_rows, 0)
    carried_grad = passed_along(front_grad, "seq", -1)
    d_x = d_x.at[tok_rows - back_rows :].add(carried_grad)
    parts = lax.axis_size(("dp", "seq"))
    small = jnp.concatenate(
        [
            d_wx_rank.T.reshape(parts, -1, chan_lanes),
            d_wx_state.T.reshape(parts, -1, chan_lanes),
            d_wdt.reshape(parts, -1, chan_lanes),
            jnp.zeros((parts, 4, chan_lanes), F32),
        ],
        1,
    )
    whole = jnp.concatenate(
        [a_log_part, conv_weight_part, jnp.stack([conv_bias_part, dt_bias_part, d_skip_part, d_skip_part], 0)], 0
    )
    d_norm_share, g_in, g_small, g_whole = tail(d_x.astype(BF16), d_z.astype(BF16), w_in, normalized_rows, small, whole)
    g_in = jnp.swapaxes(g_in, 0, 1)
    inv_share = lax.dynamic_slice_in_dim(inv_rms, row_start, row_share, 0)
    gain_partial = jnp.sum(d_norm_share * share_rows * inv_share, axis=0)
    gain_part = lax.psum_scatter(gain_partial, "tensor", scatter_dimension=0, tiled=True)
    inner_sum = jnp.sum(d_norm_share * full_gain[None] * share_rows, axis=1, keepdims=True)
    inv_cube = inv_share * inv_share * inv_share
    input_grad = (
        grad_out
        + inv_share * full_gain[None] * d_norm_share
        - share_rows * inv_cube * inner_sum / model_width
    )
    rank_here = rank_width // parts
    state_here = 2 * state_width // parts
    g_x_rank = g_small[:rank_here].T
    g_x_state = g_small[rank_here : rank_here + state_here].T
    g_dt = g_small[rank_here + state_here : rank_here + state_here + rank_here]
    g_out = lax.psum_scatter(d_wout.astype(BF16), ("dp", "seq"), scatter_dimension=0, tiled=True).astype(F32).T
    g_gain = lax.psum(gain_part, ("dp", "seq"))
    g_alog, g_conv_w = g_whole[:N], g_whole[N : N + conv_taps]
    g_conv_b, g_bias, g_skip = g_whole[N + conv_taps], g_whole[N + conv_taps + 1], g_whole[N + conv_taps + 2]
    return (
        output,
        input_grad,
        g_gain,
        g_in,
        g_conv_w,
        g_conv_b,
        g_x_rank,
        g_x_state,
        g_dt,
        g_bias,
        g_alog,
        g_skip,
        g_out,
    )


def solution(mesh):
    placed = (
        P(("dp", "seq", "tensor"), None),
        P(("dp", "seq", "tensor"), None),
        P(("dp", "seq")),
        P("tensor"),
        P(("dp", "seq"), None, "tensor"),
        P(None, "tensor"),
        P("tensor"),
        P("tensor", ("dp", "seq")),
        P(("dp", "seq"), "tensor"),
        P("tensor"),
        P(None, "tensor"),
        P("tensor"),
        P("tensor", ("dp", "seq")),
    )
    return jax.shard_map(
        on_device,
        mesh=mesh,
        in_specs=placed,
        out_specs=(
            P(("dp", "seq", "tensor"), None),
            P(("dp", "seq", "tensor"), None),
            P("tensor"),
            P(("dp", "seq"), None, "tensor"),
            P(None, "tensor"),
            P("tensor"),
            P("tensor", ("dp", "seq")),
            P("tensor", ("dp", "seq")),
            P(("dp", "seq"), "tensor"),
            P("tensor"),
            P(None, "tensor"),
            P("tensor"),
            P("tensor", ("dp", "seq")),
        ),
        check_vma=False,
    )
```

```python
import functools

import jax
import jax.numpy as jnp
from jax import lax
from jax.experimental import pallas as pl
from jax.experimental.pallas import tpu as pltpu
from jax.sharding import PartitionSpec as P

EPS = 1e-05
LOG2E = 1.4426950408889634
LN2 = 0.6931471805599453
FAR = 1e30
MESH = pl.DeviceIdType.MESH


def passed_along(x, axis, by):
    size = lax.axis_size(axis)
    pairs = [(i, i + by) for i in range(size) if 0 <= i + by < size]
    return lax.ppermute(x, axis, pairs)


def silu_slope(values):
    logistic = jax.nn.sigmoid(values)
    return logistic * (1.0 + values * (1.0 - logistic))


F32, BF16 = jnp.float32, jnp.bfloat16
N = 16
CH = 16

def fwd_kernel(stepd_ref, u_ref, bc_ref, cdiag_ref, rate_ref, y_ref, ckpt_ref, last_ref, state_ref, sbf_ref, *, unroll):
    @pl.when(pl.program_id(1) == 0)
    def _():
        state_ref[...] = jnp.zeros_like(state_ref)
    ckpt_ref[0] = state_ref[...]
    rate = rate_ref[...]
    tb = stepd_ref.shape[0]

    def chunk(c, s):
        base = pl.multiple_of(c * CH, CH)
        bc = bc_ref[c]
        for k in range(CH):
            dec = jnp.exp2(rate * stepd_ref[pl.ds(base + k, 1), :])
            s = dec * s + bc[:, k:k + 1] * u_ref[pl.ds(base + k, 1), :]
            sbf_ref[k * N:(k + 1) * N, :] = s.astype(BF16)
        y_ref[pl.ds(base, CH), :] = jnp.dot(cdiag_ref[pl.ds(base, CH), :], sbf_ref[...], preferred_element_type=F32)
        return s

    s = lax.fori_loop(0, tb // CH, chunk, state_ref[...], unroll=unroll)
    state_ref[...] = s
    last_ref[...] = s

def fwd(stepd, u, bc, cdiag, rate, tb=128, w=512, unroll=1):
    t, c = stepd.shape
    w = min(w, c)
    grid = (c // w, t // tb)
    return pl.pallas_call(
        functools.partial(fwd_kernel, unroll=unroll),
        grid=grid,
        in_specs=[
            pl.BlockSpec((tb, w), lambda j, i: (i, j)),
            pl.BlockSpec((tb, w), lambda j, i: (i, j)),
            pl.BlockSpec((tb // CH, N, 2 * CH), lambda j, i: (i, 0, 0)),
            pl.BlockSpec((tb, CH * N), lambda j, i: (i, 0)),
            pl.BlockSpec((N, w), lambda j, i: (0, j)),
        ],
        out_specs=[
            pl.BlockSpec((tb, w), lambda j, i: (i, j)),
            pl.BlockSpec((1, N, w), lambda j, i: (i, 0, j)),
            pl.BlockSpec((N, w), lambda j, i: (0, j)),
        ],
        out_shape=[
            jax.ShapeDtypeStruct((t, c), F32),
            jax.ShapeDtypeStruct((t // tb, N, c), F32),
            jax.ShapeDtypeStruct((N, c), F32),
        ],
        scratch_shapes=[pltpu.VMEM((N, w), F32), pltpu.VMEM((CH * N, w), BF16)],
        compiler_params=pltpu.CompilerParams(vmem_limit_bytes=48 << 20),
        name="scan_forward",
    )(stepd, u, bc, cdiag, rate)

def bwd_kernel(stepd_ref, u_ref, ds_ref, bc_ref, bdiag_ref, ones_ref, rate_ref, ckpt_ref, gin_ref,
               wb_ref, dn_ref, db_ref, dc_ref, acc_ref, g_ref, sbf_ref, abf_ref, rbf_ref, *, unroll):
    @pl.when(pl.program_id(1) == 0)
    def _():
        g_ref[...] = gin_ref[...]
        acc_ref[...] = jnp.zeros_like(acc_ref)
    rate = rate_ref[...]
    tb = stepd_ref.shape[0]
    nc = tb // CH
    row = lax.broadcasted_iota(jnp.int32, (CH, CH * N), 0)
    lane = lax.broadcasted_iota(jnp.int32, (CH, CH * N), 1)
    diag = (row == lane // N).astype(F32)
    sbf_ref[0:N, :] = ckpt_ref[0].astype(BF16)

    def forward(c, s):
        base = pl.multiple_of(c * CH, CH)
        bc = bc_ref[c]
        for k in range(CH):
            dec = jnp.exp2(rate * stepd_ref[pl.ds(base + k, 1), :])
            s = dec * s + bc[:, k:k + 1] * u_ref[pl.ds(base + k, 1), :]
            sbf_ref[pl.ds(pl.multiple_of((base + k + 1) * N, N), N), :] = s.astype(BF16)
        return s

    lax.fori_loop(0, nc, forward, ckpt_ref[0])

    def backward(c, carry):
        g, acc = carry
        c = nc - 1 - c
        base = pl.multiple_of(c * CH, CH)
        bc = bc_ref[c]
        for k in range(CH - 1, -1, -1):
            sd = stepd_ref[pl.ds(base + k, 1), :]
            adj = g + bc[:, CH + k:CH + k + 1] * ds_ref[pl.ds(base + k, 1), :]
            abf_ref[k * N:(k + 1) * N, :] = adj.astype(BF16)
            g = jnp.exp2(rate * sd) * adj
            before = sbf_ref[pl.ds(pl.multiple_of((base + k) * N, N), N), :].astype(F32)
            r = g * before * rate
            rbf_ref[k * N:(k + 1) * N, :] = r.astype(BF16)
            acc = acc + r * sd
        wb_ref[pl.ds(base, CH), :] = jnp.dot(bdiag_ref[pl.ds(base, CH), :], abf_ref[...], preferred_element_type=F32)
        dn_ref[pl.ds(base, CH), :] = jnp.dot(ones_ref[...], rbf_ref[...], preferred_element_type=F32)
        nt = (((1,), (1,)), ((), ()))
        now = sbf_ref[pl.ds(pl.multiple_of((base + 1) * N, N), CH * N), :]
        db = lax.dot_general(u_ref[pl.ds(base, CH), :].astype(BF16), abf_ref[...], nt, preferred_element_type=F32)
        dc = lax.dot_general(ds_ref[pl.ds(base, CH), :].astype(BF16), now, nt, preferred_element_type=F32)
        db_ref[0, pl.ds(c, 1), :] = jnp.sum(db * diag, axis=0, keepdims=True)
        dc_ref[0, pl.ds(c, 1), :] = jnp.sum(dc * diag, axis=0, keepdims=True)
        return g, acc

    g, acc = lax.fori_loop(0, nc, backward, (g_ref[...], acc_ref[...]), unroll=unroll)
    g_ref[...] = g
    acc_ref[...] = acc

def bwd(stepd, u, ds, bc, bdiag, ones, rate, ckpt, gin, tb=128, w=512, unroll=1):
    t, c = stepd.shape
    w = min(w, c)
    nb = t // tb
    grid = (c // w, nb)
    rows = pl.BlockSpec((tb, w), lambda j, i: (nb - 1 - i, j))
    return pl.pallas_call(
        functools.partial(bwd_kernel, unroll=unroll),
        grid=grid,
        in_specs=[
            rows, rows, rows,
            pl.BlockSpec((tb // CH, N, 2 * CH), lambda j, i: (nb - 1 - i, 0, 0)),
            pl.BlockSpec((tb, CH * N), lambda j, i: (nb - 1 - i, 0)),
            pl.BlockSpec((CH, CH * N), lambda j, i: (0, 0)),
            pl.BlockSpec((N, w), lambda j, i: (0, j)),
            pl.BlockSpec((1, N, w), lambda j, i: (nb - 1 - i, 0, j)),
            pl.BlockSpec((N, w), lambda j, i: (0, j)),
        ],
        out_specs=[
            rows, rows,
            pl.BlockSpec((1, tb // CH, CH * N), lambda j, i: (j, nb - 1 - i, 0)),
            pl.BlockSpec((1, tb // CH, CH * N), lambda j, i: (j, nb - 1 - i, 0)),
            pl.BlockSpec((N, w), lambda j, i: (0, j)),
        ],
        out_shape=[
            jax.ShapeDtypeStruct((t, c), F32),
            jax.ShapeDtypeStruct((t, c), F32),
            jax.ShapeDtypeStruct((c // w, t // CH, CH * N), F32),
            jax.ShapeDtypeStruct((c // w, t // CH, CH * N), F32),
            jax.ShapeDtypeStruct((N, c), F32),
        ],
        scratch_shapes=[pltpu.VMEM((N, w), F32), pltpu.VMEM(((tb + 1) * N, w), BF16),
                        pltpu.VMEM((CH * N, w), BF16), pltpu.VMEM((CH * N, w), BF16)],
        compiler_params=pltpu.CompilerParams(vmem_limit_bytes=48 << 20),
        name="scan_backward",
    )(stepd, u, ds, bc, bdiag, ones, rate, ckpt, gin)


def correct_kernel(alive_ref, y_ref, stepd_ref, cdiag_ref, rate_ref, ckpt_ref, sin_ref, yo_ref, ckpto_ref, state_ref, sbf_ref):
    i = pl.program_id(1)

    @pl.when(i == 0)
    def _():
        state_ref[...] = sin_ref[...]

    alive = alive_ref[i] != 0

    @pl.when(alive)
    def _():
        rate = rate_ref[...]
        ckpto_ref[0] = ckpt_ref[0] + state_ref[...]

        def chunk(c, s):
            base = pl.multiple_of(c * CH, CH)
            for k in range(CH):
                s = jnp.exp2(rate * stepd_ref[pl.ds(base + k, 1), :]) * s
                sbf_ref[k * N:(k + 1) * N, :] = s.astype(BF16)
            yo_ref[pl.ds(base, CH), :] = y_ref[pl.ds(base, CH), :] + jnp.dot(
                cdiag_ref[pl.ds(base, CH), :], sbf_ref[...], preferred_element_type=F32
            )
            return s

        state_ref[...] = lax.fori_loop(0, y_ref.shape[0] // CH, chunk, state_ref[...])

    @pl.when(jnp.logical_not(alive))
    def _():
        yo_ref[...] = y_ref[...]
        ckpto_ref[...] = ckpt_ref[...]


def correct(alive, y, stepd, cdiag, rate, ckpt, state_in, tb=128, w=512):
    t, c = stepd.shape
    w = min(w, c)
    rows = pl.BlockSpec((tb, w), lambda j, i, _: (i, j))
    lanes = pl.BlockSpec((N, w), lambda j, i, _: (0, j))
    marks = pl.BlockSpec((1, N, w), lambda j, i, _: (i, 0, j))
    return pl.pallas_call(
        correct_kernel,
        grid_spec=pltpu.PrefetchScalarGridSpec(
            num_scalar_prefetch=1,
            grid=(c // w, t // tb),
            in_specs=[rows, rows, pl.BlockSpec((tb, CH * N), lambda j, i, _: (i, 0)), lanes, marks, lanes],
            out_specs=[rows, marks],
            scratch_shapes=[pltpu.VMEM((N, w), F32), pltpu.VMEM((CH * N, w), BF16)],
        ),
        out_shape=[jax.ShapeDtypeStruct((t, c), F32), jax.ShapeDtypeStruct(ckpt.shape, F32)],
        compiler_params=pltpu.CompilerParams(vmem_limit_bytes=48 << 20),
        name="scan_correct",
    )(alive, y, stepd, cdiag, rate, ckpt, state_in)


def entry_kernel(alive_ref, stepd_ref, ds_ref, bc_ref, rate_ref, g_ref):
    i = pl.program_id(1)

    @pl.when(i == 0)
    def _():
        g_ref[...] = jnp.zeros_like(g_ref)

    @pl.when(alive_ref[pl.num_programs(1) - 1 - i] != 0)
    def _():
        rate = rate_ref[...]
        nc = stepd_ref.shape[0] // CH

        def chunk(c, g):
            c = nc - 1 - c
            base = pl.multiple_of(c * CH, CH)
            bc = bc_ref[c]
            for k in range(CH - 1, -1, -1):
                adj = g + bc[:, CH + k:CH + k + 1] * ds_ref[pl.ds(base + k, 1), :]
                g = jnp.exp2(rate * stepd_ref[pl.ds(base + k, 1), :]) * adj
            return g

        g_ref[...] = lax.fori_loop(0, nc, chunk, g_ref[...])


def entry(alive, stepd, ds, bc, rate, tb=128, w=512):
    t, c = stepd.shape
    w = min(w, c)
    nb = t // tb
    rows = pl.BlockSpec((tb, w), lambda j, i, _: (nb - 1 - i, j))
    lanes = pl.BlockSpec((N, w), lambda j, i, _: (0, j))
    return pl.pallas_call(
        entry_kernel,
        grid_spec=pltpu.PrefetchScalarGridSpec(
            num_scalar_prefetch=1,
            grid=(c // w, nb),
            in_specs=[rows, rows, pl.BlockSpec((tb // CH, N, 2 * CH), lambda j, i, _: (nb - 1 - i, 0, 0)), lanes],
            out_specs=lanes,
        ),
        out_shape=jax.ShapeDtypeStruct((N, c), F32),
        compiler_params=pltpu.CompilerParams(vmem_limit_bytes=48 << 20),
        name="scan_entry",
    )(alive, stepd, ds, bc, rate)


def carried(local, reach, axis, by):
    found = jnp.zeros_like(local)
    for _ in range(lax.axis_size(axis) - 1):
        found = passed_along(local + reach * found, axis, by)
    return found


def columns(values):
    tokens = values.shape[0]
    return values.reshape(tokens // CH, CH, N).transpose(0, 2, 1)


def diagonal(values):
    tokens = values.shape[0]
    mine = jnp.arange(CH * N)[None] // N == jnp.arange(tokens)[:, None] % CH
    return jnp.where(mine, jnp.tile(values.astype(BF16), (1, CH)), 0)


def mesh_copy(src, dst, send, recv, **where):
    return pltpu.make_async_remote_copy(
        src_ref=src, dst_ref=dst, send_sem=send, recv_sem=recv, device_id=where, device_id_type=MESH
    )


def place():
    dp, seq, mine = lax.axis_index("dp"), lax.axis_index("seq"), lax.axis_index("tensor")
    return dp, seq, mine


def tail_kernel(n, dps, seqs, subs, lag, dx_ref, dz_ref, w_ref, nrm_ref, sm_ref, all_ref,
                dn_ref, gin_ref, gs_ref, ga_ref,
                gacc, gsend, grecv, all_mine,
                zr, zl, part_r, part_l, one_send, one_recv, two_recv, sm_one, sm_two, all_one, all_two,
                r_send, r_recv, l_send, l_recv, w1s, w1r, w2s, w2r, s1s, s1r, s2s, s2r, a1s, a1r, a2s, a2r, gs, gr):
    dp, seq, t = place()
    core, hi = dp % 2, dp // 2
    chips = dps // 2 * seqs
    chip = hi * seqs + seq
    rows = dn_ref.shape[0]
    part = rows // subs
    wide = dn_ref.shape[1]
    wrows = gin_ref.shape[1]
    tile = 512

    def owner(q, c):
        return (q // seqs * 2 + c) * seqs + q % seqs

    def to_chip(q):
        return dict(dp=q // seqs * 2 + core, seq=q % seqs)

    barrier = pltpu.get_barrier_semaphore()
    pl.semaphore_signal(barrier, inc=1, device_id=dict(dp=hi * 2 + 1 - core), device_id_type=MESH)
    for step in range(1, chips):
        q = lax.rem(chip + step, chips)
        pl.semaphore_signal(barrier, inc=1, device_id=to_chip(q), device_id_type=MESH)

    for ahead in range(1, n):
        pl.semaphore_signal(barrier, inc=1, device_id=dict(tensor=lax.rem(t + ahead, n)), device_id_type=MESH)
    pl.semaphore_wait(barrier, chips + n - 1)
    gacc[...] = jnp.zeros_like(gacc)

    partner = dict(dp=hi * 2 + 1 - core)
    right, left = dict(tensor=lax.rem(t + 1, n)), dict(tensor=lax.rem(t + n - 1, n))

    def r_copy(i):
        return mesh_copy(zr.at[i], zr.at[i], r_send.at[i], r_recv.at[i], **right)

    def l_copy(i):
        return mesh_copy(zl.at[i], zl.at[i], l_send.at[i], l_recv.at[i], **left)

    def w1_copy(q):
        return mesh_copy(one_send.at[q], one_recv.at[q], w1s.at[q], w1r.at[q], **partner)

    def w2_copy(q, slot):
        return mesh_copy(one_recv.at[q], two_recv.at[slot], w2s.at[q], w2r.at[slot], **to_chip(q))

    def s1_copy(q):
        return mesh_copy(sm_ref.at[owner(q, 1 - core)], sm_one.at[q], s1s.at[q], s1r.at[q], **partner)

    def s2_copy(q, slot):
        return mesh_copy(sm_one.at[q], sm_two.at[slot], s2s.at[q], s2r.at[slot], **to_chip(q))

    def a1_copy():
        return mesh_copy(all_mine, all_one, a1s, a1r, **partner)

    def a2_copy(q, slot):
        return mesh_copy(all_one, all_two.at[slot], a2s.at[q], a2r.at[slot], **to_chip(q))

    def g_copy(p, slot):
        return mesh_copy(gsend.at[p], grecv.at[slot], gs.at[p], gr.at[slot], tensor=p)

    def partial_rows(o, dst):
        here = pl.ds(pl.multiple_of(o * rows, rows), rows)

        @pl.loop(0, wide // tile)
        def _(j):
            cols = pl.ds(pl.multiple_of(j * tile, tile), tile)
            nt = (((1,), (1,)), ((), ()))
            block = lax.dot_general(
                dx_ref[here, :], w_ref[0, cols, :], nt, preferred_element_type=F32
            ) + lax.dot_general(dz_ref[here, :], w_ref[1, cols, :], nt, preferred_element_type=F32)
            dst[:, cols] = block
            scaled = block * nrm_ref[here, cols].astype(F32)
            gacc[:, cols] = gacc[:, cols] + jnp.sum(scaled.reshape(rows // 8, 8, tile), axis=0)

    def weight_rows(p, k):
        cols = pl.ds(pl.multiple_of(p * wrows, wrows), wrows)
        tn = (((0,), (0,)), ((), ()))
        d_ref = dx_ref if k == 0 else dz_ref
        return lax.dot_general(nrm_ref[:, cols], d_ref[...], tn, preferred_element_type=F32)

    for q in range(chips):
        s1_copy(q).start()

    def stream(i, limit, start, buf, copy, part_ref, owner_of):
        @pl.when(jnp.logical_and(i >= 0, i < limit))
        def _():
            k, sub = i // subs, i % subs

            @pl.when(sub == 0)
            def _():
                partial_rows(owner_of(k), part_ref)

            @pl.when(jnp.logical_and(start, sub == 0))
            def _():
                @pl.loop(0, subs)
                def _(j):
                    here = part_ref[pl.ds(pl.multiple_of(j * part, part), part), :]
                    buf[k * subs + j] = here.astype(BF16)
                    copy(k * subs + j).start()

            @pl.when(jnp.logical_not(start))
            def _():
                here = part_ref[pl.ds(pl.multiple_of(sub * part, part), part), :]
                copy(i).wait_recv()
                buf[i] = (here + buf[i].astype(F32)).astype(BF16)
                copy(i).start()

    def step(g, _):
        stream(g - lag * t, (n - 1 - t) * subs, t == 0, zr, r_copy, part_r, lambda k: n - 1 - k)
        stream(g - lag * (n - 1 - t), t * subs, t == n - 1, zl, l_copy, part_l, lambda k: k)

        @pl.when(g < chips)
        def _():
            for k in range(2):
                one_send[g, k] = weight_rows(owner(g, 1 - core), k).astype(BF16)
            w1_copy(g).start()

        @pl.when(jnp.logical_and(g >= chips, g < 2 * chips - 1))
        def _():
            q = lax.rem(chip + 1 + g - chips, chips)
            w1_copy(q).wait_recv()
            for k in range(2):
                one_recv[q, k] = (weight_rows(owner(q, core), k) + one_recv[q, k].astype(F32)).astype(BF16)
            w2_copy(q, chip).start()

        @pl.when(g == 2 * chips - 1)
        def _():
            for q in range(chips):
                s1_copy(q).wait_recv()
                sm_one[q] = sm_one[q] + sm_ref[owner(q, core)]
            for ahead in range(1, chips):
                q = lax.rem(chip + ahead, chips)
                s2_copy(q, chip).start()
            w1_copy(chip).wait_recv()
            for k in range(2):
                gin_ref[k] = weight_rows(owner(chip, core), k) + one_recv[chip, k].astype(F32)

        @pl.when(g == 2 * chips)
        def _():
            partial_rows(t, dn_ref)

        return 0

    steps = max((n - 1) * max(subs, lag), 2 * chips + 1)
    lax.fori_loop(0, steps, step, 0)

    share = wide // n
    for p in range(n):
        gsend[p] = gacc[:, p * share:(p + 1) * share]
    for ahead in range(1, n):
        g_copy(lax.rem(t + ahead, n), t).start()

    @pl.loop(0, subs)
    def _(s):
        here = pl.ds(pl.multiple_of(s * part, part), part)

        @pl.when(t > 0)
        def _():
            i = (n - 1 - t) * subs + s
            r_copy(i).wait_recv()
            dn_ref[here, :] = dn_ref[here, :] + zr[i].astype(F32)

        @pl.when(t < n - 1)
        def _():
            i = t * subs + s
            l_copy(i).wait_recv()
            dn_ref[here, :] = dn_ref[here, :] + zl[i].astype(F32)

    plain = all_ref.shape[0]
    all_mine[0:plain, :] = all_ref[...]
    all_mine[plain:, :] = jnp.zeros((8, all_mine.shape[1]), F32)
    all_mine[plain:, 0:share] = gsend[t]
    for ahead in range(1, n):
        p = lax.rem(t + ahead, n)
        g_copy(p, p).wait_recv()
        all_mine[plain:, 0:share] = all_mine[plain:, 0:share] + grecv[p]
    a1_copy().start()
    gs_ref[...] = sm_one[chip]
    for ahead in range(1, chips):
        q = lax.rem(chip + ahead, chips)
        s2_copy(q, q).wait_recv()
        gs_ref[...] = gs_ref[...] + sm_two[q]
    a1_copy().wait_recv()
    all_one[...] = all_one[...] + all_mine[...]
    for ahead in range(1, chips):
        a2_copy(lax.rem(chip + ahead, chips), chip).start()
    ga_ref[...] = all_one[...]
    for ahead in range(1, chips):
        q = lax.rem(chip + ahead, chips)
        w2_copy(q, q).wait_recv()
        gin_ref[...] = gin_ref[...] + two_recv[q].astype(F32)
    for ahead in range(1, chips):
        q = lax.rem(chip + ahead, chips)
        a2_copy(q, q).wait_recv()
        ga_ref[...] = ga_ref[...] + all_two[q]

    for q in range(chips):
        s1_copy(q).wait_send()
        w1_copy(q).wait_send()
    a1_copy().wait_send()
    for ahead in range(1, n):
        g_copy(lax.rem(t + ahead, n), t).wait_send()
    for ahead in range(1, chips):
        q = lax.rem(chip + ahead, chips)
        s2_copy(q, chip).wait_send()
        a2_copy(q, chip).wait_send()
        w2_copy(q, chip).wait_send()

    @pl.loop(0, (n - 1) * subs)
    def _(i):
        @pl.when(i < (n - 1 - t) * subs)
        def _():
            r_copy(i).wait_send()

        @pl.when(i < t * subs)
        def _():
            l_copy(i).wait_send()


def tail(dx, dz, w_full, normed, small, whole):
    n, dps, seqs = (lax.axis_size(axis) for axis in ("tensor", "dp", "seq"))
    chips = dps // 2 * seqs
    rows = dx.shape[0] // n
    wide, lanes = w_full.shape[1], w_full.shape[2]
    wrows = wide // (dps * seqs)
    subs = max(1, rows // 32)
    hops = (n - 1) * subs
    vmem = pl.BlockSpec(memory_space=pltpu.VMEM)
    dma = pltpu.SemaphoreType.DMA
    few = dma((chips,))
    return pl.pallas_call(
        functools.partial(tail_kernel, n, dps, seqs, subs, 2),
        out_shape=[
            jax.ShapeDtypeStruct((rows, wide), F32),
            jax.ShapeDtypeStruct((2, wrows, lanes), F32),
            jax.ShapeDtypeStruct(small.shape[1:], F32),
            jax.ShapeDtypeStruct((whole.shape[0] + 8, lanes), F32),
        ],
        in_specs=[vmem] * 6,
        out_specs=[vmem] * 4,
        scratch_shapes=[
            pltpu.VMEM((8, wide), F32),
            pltpu.VMEM((n, 8, wide // n), F32),
            pltpu.VMEM((n, 8, wide // n), F32),
            pltpu.VMEM((whole.shape[0] + 8, lanes), F32),
            pltpu.VMEM((hops, rows // subs, wide), BF16),
            pltpu.VMEM((hops, rows // subs, wide), BF16),
            pltpu.VMEM((rows, wide), F32),
            pltpu.VMEM((rows, wide), F32),
            pltpu.VMEM((chips, 2, wrows, lanes), BF16),
            pltpu.VMEM((chips, 2, wrows, lanes), BF16),
            pltpu.VMEM((chips, 2, wrows, lanes), BF16),
            pltpu.VMEM((chips,) + small.shape[1:], F32),
            pltpu.VMEM((chips,) + small.shape[1:], F32),
            pltpu.VMEM((whole.shape[0] + 8, lanes), F32),
            pltpu.VMEM((chips, whole.shape[0] + 8, lanes), F32),
            dma((hops,)), dma((hops,)), dma((hops,)), dma((hops,)),
            few, few, few, few, few, few, few, few, dma, dma, few, few, dma((n,)), dma((n,)),
        ],
        compiler_params=pltpu.CompilerParams(
            collective_id=2, has_side_effects=True, vmem_limit_bytes=60 << 20
        ),
        name="tail_sums",
    )(dx, dz, w_full, normed, small, whole)


def mid_kernel(n, subs, lag, gated_ref, w_ref, hid_ref, tea_ref, scale_ref, z_ref, scan_ref,
               out_ref, go_ref, piece_ref, dscan_ref, dz_ref,
               zr, zl, part_r, part_l, r_send, r_recv, l_send, l_recv, ar_send, ar_recv, al_send, al_recv):
    t = lax.axis_index("tensor")
    rows, wide = hid_ref.shape
    part = rows // subs
    tile = 512
    right, left = dict(tensor=lax.rem(t + 1, n)), dict(tensor=lax.rem(t + n - 1, n))

    barrier = pltpu.get_barrier_semaphore()
    for peer in (right, left):
        pl.semaphore_signal(barrier, inc=1, device_id=peer, device_id_type=MESH)
    pl.semaphore_wait(barrier, 2)

    def r_copy(i):
        return mesh_copy(zr.at[i], zr.at[i], r_send.at[i], r_recv.at[i], **right)

    def l_copy(i):
        return mesh_copy(zl.at[i], zl.at[i], l_send.at[i], l_recv.at[i], **left)

    def at(o, s):
        return pl.ds(pl.multiple_of(o * rows + s * part, part), part)

    def ar_copy(o, s):
        ref = piece_ref.at[at(o, s), :]
        return mesh_copy(ref, ref, ar_send.at[o * subs + s], ar_recv.at[o * subs + s], **right)

    def al_copy(o, s):
        ref = piece_ref.at[at(o, s), :]
        return mesh_copy(ref, ref, al_send.at[o * subs + s], al_recv.at[o * subs + s], **left)

    def partial_rows(o, dst):
        here = pl.ds(pl.multiple_of(o * rows, rows), rows)

        @pl.loop(0, wide // tile)
        def _(j):
            cols = pl.ds(pl.multiple_of(j * tile, tile), tile)
            nt = (((1,), (1,)), ((), ()))
            dst[:, cols] = lax.dot_general(gated_ref[here, :], w_ref[cols, :], nt, preferred_element_type=F32)

    def backward_rows(o):
        here = pl.ds(pl.multiple_of(o * rows, rows), rows)
        d_gated = jnp.dot(piece_ref[here, :], w_ref[...], preferred_element_type=F32)
        z = z_ref[here, :]
        s = 1.0 / (1.0 + jnp.exp(-z))
        dscan_ref[here, :] = d_gated * (z * s)
        dz_ref[here, :] = (d_gated * scan_ref[here, :] * (s * (1.0 + z * (1.0 - s)))).astype(BF16)

    def stream(i, limit, start, buf, copy, part_ref, owner_of):
        @pl.when(jnp.logical_and(i >= 0, i < limit))
        def _():
            k, sub = i // subs, i % subs

            @pl.when(sub == 0)
            def _():
                partial_rows(owner_of(k), part_ref)

            @pl.when(jnp.logical_and(start, sub == 0))
            def _():
                @pl.loop(0, subs)
                def _(j):
                    here = part_ref[pl.ds(pl.multiple_of(j * part, part), part), :]
                    buf[k * subs + j] = here.astype(BF16)
                    copy(k * subs + j).start()

            @pl.when(jnp.logical_not(start))
            def _():
                here = part_ref[pl.ds(pl.multiple_of(sub * part, part), part), :]
                copy(i).wait_recv()
                buf[i] = (here + buf[i].astype(F32)).astype(BF16)
                copy(i).start()

    def ready(o):
        from_left = jnp.where(o > 0, lag * o + (n - 1 - o) * subs, 0)
        from_right = jnp.where(o < n - 1, lag * (n - 1 - o) + o * subs, 0)
        return jnp.maximum(from_left, from_right)

    gap = max(subs, lag)
    base = lag + (n - 2) * subs if subs >= lag else (n - 1) * lag

    def turn(d, o):
        inner = base + (d - o) * gap
        inner = jnp.where(d == 0, (n - 1) * gap, inner)
        return jnp.where(d == n - 1, base + (n - 2 - o) * gap + lag, inner)

    def finish(s):
        here = pl.ds(pl.multiple_of(s * part, part), part)

        @pl.when(s == 0)
        def _():
            partial_rows(t, go_ref)

        @pl.when(t > 0)
        def _():
            i = (n - 1 - t) * subs + s
            r_copy(i).wait_recv()
            go_ref[here, :] = go_ref[here, :] + zr[i].astype(F32)

        @pl.when(t < n - 1)
        def _():
            i = t * subs + s
            l_copy(i).wait_recv()
            go_ref[here, :] = go_ref[here, :] + zl[i].astype(F32)

        result = hid_ref[here, :].astype(F32) + go_ref[here, :]
        out_ref[here, :] = result.astype(BF16)
        grad = scale_ref[here, :] * (result - tea_ref[here, :].astype(F32))
        go_ref[here, :] = grad
        piece_ref[at(t, s), :] = grad.astype(BF16)

    def step(g, _):
        stream(g - lag * t, (n - 1 - t) * subs, t == 0, zr, r_copy, part_r, lambda k: n - 1 - k)
        stream(g - lag * (n - 1 - t), t * subs, t == n - 1, zl, l_copy, part_l, lambda k: k)

        @pl.loop(0, n)
        def _(o):
            s_own = g - ready(t)
            s_right = g - turn(t, o)
            s_left = g - turn(n - 1 - t, n - 1 - o)

            @pl.when(jnp.logical_and(o == t, jnp.logical_and(s_own >= 0, s_own < subs)))
            def _():
                finish(s_own)

            @pl.when(jnp.logical_and(o <= t, jnp.logical_and(s_right >= 0, s_right < subs)))
            def _():
                @pl.when(o < t)
                def _():
                    ar_copy(o, s_right).wait_recv()

                @pl.when(t < n - 1)
                def _():
                    ar_copy(o, s_right).start()

            @pl.when(jnp.logical_and(o >= t, jnp.logical_and(s_left >= 0, s_left < subs)))
            def _():
                @pl.when(o > t)
                def _():
                    al_copy(o, s_left).wait_recv()

                @pl.when(t > 0)
                def _():
                    al_copy(o, s_left).start()

            s_done = jnp.where(o == t, s_own, jnp.where(o < t, s_right, s_left))

            @pl.when(s_done == subs - 1)
            def _():
                backward_rows(o)

        return 0

    steps = base + (n - 1) * gap + subs + lag
    lax.fori_loop(0, steps, step, 0)

    @pl.loop(0, (n - 1) * subs)
    def _(i):
        @pl.when(i < (n - 1 - t) * subs)
        def _():
            r_copy(i).wait_send()

        @pl.when(i < t * subs)
        def _():
            l_copy(i).wait_send()

    @pl.loop(0, n * subs)
    def _(i):
        o, s = i // subs, i % subs

        @pl.when(jnp.logical_and(o <= t, t < n - 1))
        def _():
            ar_copy(o, s).wait_send()

        @pl.when(jnp.logical_and(o >= t, t > 0))
        def _():
            al_copy(o, s).wait_send()


def middle(gated, w_out, hidden, teacher, scale, z_gate, scan_out):
    n = lax.axis_size("tensor")
    rows, wide = hidden.shape
    tokens, lanes = gated.shape
    subs = max(1, rows // 32)
    hops = (n - 1) * subs
    vmem = pl.BlockSpec(memory_space=pltpu.VMEM)
    dma = pltpu.SemaphoreType.DMA
    return pl.pallas_call(
        functools.partial(mid_kernel, n, subs, 2),
        out_shape=[
            jax.ShapeDtypeStruct((rows, wide), BF16),
            jax.ShapeDtypeStruct((rows, wide), F32),
            jax.ShapeDtypeStruct((tokens, wide), BF16),
            jax.ShapeDtypeStruct((tokens, lanes), F32),
            jax.ShapeDtypeStruct((tokens, lanes), BF16),
        ],
        in_specs=[vmem] * 7,
        out_specs=[vmem] * 5,
        scratch_shapes=[
            pltpu.VMEM((hops, rows // subs, wide), BF16),
            pltpu.VMEM((hops, rows // subs, wide), BF16),
            pltpu.VMEM((rows, wide), F32),
            pltpu.VMEM((rows, wide), F32),
            dma((hops,)), dma((hops,)), dma((hops,)), dma((hops,)),
            dma((n * subs,)), dma((n * subs,)), dma((n * subs,)), dma((n * subs,)),
        ],
        compiler_params=pltpu.CompilerParams(
            collective_id=1, has_side_effects=True, vmem_limit_bytes=60 << 20
        ),
        name="middle",
    )(gated, w_out, hidden, teacher, scale, z_gate, scan_out)


def on_device(
    hidden_in,
    teacher,
    segment_ids,
    norm_gain,
    input_projection_weight,
    conv_weight,
    conv_bias,
    xproj_weight,
    dtproj_weight,
    dt_bias,
    a_log,
    d_skip,
    output_projection_weight,
):
    tok_rows = segment_ids.shape[0]
    row_share = hidden_in.shape[0]
    model_width = hidden_in.shape[1]
    conv_taps = conv_weight.shape[0]
    chan_lanes = conv_weight.shape[1]
    back_rows = conv_taps - 1
    row_start = lax.axis_index("tensor") * row_share
    valid_mask = (segment_ids != 0).astype(jnp.float32)
    count_here = jnp.sum((segment_ids != 0).astype(jnp.int32))
    count_pair = (
        jnp.stack([count_here // 32, count_here % 32]).astype(jnp.float32).astype(jnp.bfloat16)
    )
    w_in, w_x, w_dt, w_out, count_pairs = (
        lax.all_gather(jnp.swapaxes(input_projection_weight, 0, 1), ("dp", "seq"), axis=1, tiled=True),
        lax.all_gather(xproj_weight, ("dp", "seq"), axis=1, tiled=True),
        lax.all_gather(dtproj_weight, ("dp", "seq"), axis=0, tiled=True),
        lax.all_gather(output_projection_weight.T, ("dp", "seq"), axis=0, tiled=True),
        lax.all_gather(count_pair, ("dp", "seq"), axis=0, tiled=True),
    )
    count_pairs = count_pairs.astype(jnp.float32).reshape(-1, 2)
    total_count = 32.0 * jnp.sum(count_pairs[:, 0]) + jnp.sum(count_pairs[:, 1])
    full_rows_b, full_gain_b = (
        lax.all_gather(hidden_in, "tensor", axis=0, tiled=True),
        lax.all_gather(norm_gain, "tensor", axis=0, tiled=True),
    )
    full_rows = full_rows_b.astype(jnp.float32)
    full_gain = full_gain_b.astype(jnp.float32)
    inv_rms = lax.rsqrt(jnp.mean(full_rows * full_rows, axis=1, keepdims=True) + EPS)
    normalized_rows = (full_rows * inv_rms * full_gain[None]).astype(jnp.bfloat16)
    x_inner = jnp.dot(normalized_rows, w_in[0], preferred_element_type=F32)
    z_gate = jnp.dot(normalized_rows, w_in[1], preferred_element_type=F32)
    seg_float = segment_ids.astype(jnp.float32)
    prev_x, prev_seg = passed_along(
        (x_inner[tok_rows - back_rows :], seg_float[tok_rows - back_rows :]), "seq", 1
    )
    ext_x = jnp.concatenate([prev_x, x_inner], 0)
    ext_seg = jnp.concatenate([prev_seg, seg_float], 0)
    tap_keeps = []
    conv_sum = jnp.broadcast_to(conv_bias.astype(jnp.float32)[None], (tok_rows, chan_lanes))
    for offset in range(conv_taps):
        keep_tap = (ext_seg[offset : offset + tok_rows] == seg_float).astype(jnp.float32)[:, None]
        tap_keeps.append(keep_tap)
        conv_sum = (
            conv_sum
            + conv_weight[offset].astype(jnp.float32)[None]
            * ext_x[offset : offset + tok_rows]
            * keep_tap
        )
    x_low = jax.nn.silu(conv_sum).astype(jnp.bfloat16)
    x_float = x_low.astype(jnp.float32)
    mixed_rows = lax.psum(jnp.dot(x_low, w_x, preferred_element_type=jnp.float32), "tensor")
    rank_width = w_dt.shape[0]
    state_width = (mixed_rows.shape[1] - rank_width) // 2
    step_low = mixed_rows[:, :rank_width].astype(jnp.bfloat16)
    b_in = mixed_rows[:, rank_width : rank_width + state_width]
    c_out = mixed_rows[:, rank_width + state_width :]
    pre_act = jnp.dot(step_low, w_dt, preferred_element_type=jnp.float32) + dt_bias[None]
    step_size = jax.nn.softplus(pre_act)
    decay_rates = -jnp.exp(a_log)
    same_doc = (seg_float == ext_seg[back_rows - 1 : back_rows - 1 + tok_rows]).astype(jnp.float32)
    rates = decay_rates * LOG2E
    block = 128
    stepd = jnp.where(same_doc[:, None] != 0, step_size, FAR)
    inject = step_size * x_float
    col_pair = jnp.concatenate([columns(b_in), columns(c_out)], -1)
    b_diag, c_diag = diagonal(b_in), diagonal(c_out)
    resets = jnp.sum((same_doc == 0).astype(jnp.int32).reshape(-1, block), axis=1)
    alive = (jnp.cumsum(resets) - resets == 0).astype(jnp.int32)
    y_local, marks, state_last = fwd(stepd, inject, col_pair, c_diag, rates, tb=block, unroll=2)
    reach = jnp.exp2(rates * jnp.sum(stepd, axis=0)[None])
    state_in = carried(state_last, reach, "seq", 1)
    y_rows, marks = correct(alive, y_local, stepd, c_diag, rates, marks, state_in, tb=block)
    scan_out = y_rows + d_skip[None] * x_float
    gate_act = jax.nn.silu(z_gate)
    gated_output_rows = (scan_out * gate_act).astype(jnp.bfloat16)
    share_rows = hidden_in.astype(F32)
    valid_share = lax.dynamic_slice_in_dim(valid_mask, row_start, row_share, 0)
    total_tokens = float(tok_rows * lax.axis_size(("dp", "seq")))
    scale = (total_tokens / total_count * valid_share)[:, None]
    output, grad_out, piece, d_scan, d_z = middle(
        gated_output_rows, w_out, hidden_in, teacher, scale, z_gate, scan_out
    )
    d_wout = jnp.einsum("te,tw->we", gated_output_rows, piece, preferred_element_type=jnp.float32)
    d_skip_part = jnp.sum(d_scan * x_float, axis=0)
    adjoint_first = entry(alive, stepd, d_scan, col_pair, rates, tb=block)
    adjoint_in = carried(adjoint_first, reach, "seq", -1)
    ones = diagonal(jnp.ones((CH, N), F32))
    weighted_b, d_rate, d_b_part, d_c_part, a_log_part = bwd(
        stepd, inject, d_scan, col_pair, b_diag, ones, rates, marks, adjoint_in, tb=block, w=1024
    )
    d_step = LN2 * d_rate + x_float * weighted_b
    a_log_part = LN2 * a_log_part
    d_b_part = jnp.sum(d_b_part, axis=0).reshape(tok_rows, N)
    d_c_part = jnp.sum(d_c_part, axis=0).reshape(tok_rows, N)
    d_xlow = d_skip[None] * d_scan + step_size * weighted_b
    d_pre = d_step * jax.nn.sigmoid(pre_act)
    dt_bias_part = jnp.sum(d_pre, axis=0)
    d_pre_low = d_pre.astype(jnp.bfloat16)
    d_wdt = jnp.einsum("tr,te->re", step_low, d_pre_low, preferred_element_type=jnp.float32)
    d_rank = jnp.einsum("te,re->tr", d_pre_low, w_dt, preferred_element_type=jnp.float32)
    d_mixed = lax.psum(jnp.concatenate([d_rank, d_b_part, d_c_part], 1), "tensor")
    d_mixed_low = d_mixed.astype(jnp.bfloat16)
    d_wx = jnp.einsum("te,tj->ej", x_low, d_mixed_low, preferred_element_type=jnp.float32)
    d_wx_rank = d_wx[:, :rank_width]
    d_wx_state = d_wx[:, rank_width:]
    d_xlow = d_xlow + jnp.einsum("tj,ej->te", d_mixed_low, w_x, preferred_element_type=jnp.float32)
    d_conv = d_xlow * silu_slope(conv_sum)
    conv_bias_part = jnp.sum(d_conv, axis=0)
    conv_weight_rows = []
    for offset in range(conv_taps):
        conv_weight_rows.append(
            jnp.sum(d_conv * ext_x[offset : offset + tok_rows] * tap_keeps[offset], axis=0)
        )
    conv_weight_part = jnp.stack(conv_weight_rows, 0)
    conv_padded = jnp.concatenate([d_conv, jnp.zeros((back_rows, chan_lanes), jnp.float32)], 0)
    d_x = jnp.zeros((tok_rows, chan_lanes), jnp.float32)
    for offset in range(conv_taps):
        lead = back_rows - offset
        keep_padded = jnp.concatenate(
            [tap_keeps[offset], jnp.zeros((back_rows, 1), jnp.float32)], 0
        )
        d_x = (
            d_x
            + conv_weight[offset].astype(jnp.float32)[None]
            * conv_padded[lead : lead + tok_rows]
            * keep_padded[lead : lead + tok_rows]
        )
    front_rows = []
    for place in range(back_rows):
        front_total = jnp.zeros((chan_lanes,), jnp.float32)
        for offset in range(place + 1):
            front_total = (
                front_total
                + conv_weight[offset].astype(jnp.float32)
                * d_conv[place - offset]
                * tap_keeps[offset][place - offset, 0]
            )
        front_rows.append(front_total)
    front_grad = jnp.stack(front_rows, 0)
    carried_grad = passed_along(front_grad, "seq", -1)
    d_x = d_x.at[tok_rows - back_rows :].add(carried_grad)
    parts = lax.axis_size(("dp", "seq"))
    small = jnp.concatenate(
        [
            d_wx_rank.T.reshape(parts, -1, chan_lanes),
            d_wx_state.T.reshape(parts, -1, chan_lanes),
            d_wdt.reshape(parts, -1, chan_lanes),
            jnp.zeros((parts, 4, chan_lanes), F32),
        ],
        1,
    )
    whole = jnp.concatenate(
        [a_log_part, conv_weight_part, jnp.stack([conv_bias_part, dt_bias_part, d_skip_part, d_skip_part], 0)], 0
    )
    d_norm_share, g_in, g_small, g_whole = tail(d_x.astype(BF16), d_z, w_in, normalized_rows, small, whole)
    g_in = jnp.swapaxes(g_in, 0, 1)
    inv_share = lax.dynamic_slice_in_dim(inv_rms, row_start, row_share, 0)
    inner_sum = jnp.sum(d_norm_share * full_gain[None] * share_rows, axis=1, keepdims=True)
    inv_cube = inv_share * inv_share * inv_share
    input_grad = (
        grad_out
        + inv_share * full_gain[None] * d_norm_share
        - share_rows * inv_cube * inner_sum / model_width
    )
    rank_here = rank_width // parts
    state_here = 2 * state_width // parts
    g_x_rank = g_small[:rank_here].T
    g_x_state = g_small[rank_here : rank_here + state_here].T
    g_dt = g_small[rank_here + state_here : rank_here + state_here + rank_here]
    g_out = lax.psum_scatter(d_wout.astype(BF16), ("dp", "seq"), scatter_dimension=0, tiled=True).astype(F32).T
    g_gain = jnp.sum(g_whole[N + conv_taps + 4 :, : norm_gain.shape[0]], axis=0) / norm_gain.astype(F32)
    g_alog, g_conv_w = g_whole[:N], g_whole[N : N + conv_taps]
    g_conv_b, g_bias, g_skip = g_whole[N + conv_taps], g_whole[N + conv_taps + 1], g_whole[N + conv_taps + 2]
    return (
        output,
        input_grad,
        g_gain,
        g_in,
        g_conv_w,
        g_conv_b,
        g_x_rank,
        g_x_state,
        g_dt,
        g_bias,
        g_alog,
        g_skip,
        g_out,
    )


def solution(mesh):
    placed = (
        P(("dp", "seq", "tensor"), None),
        P(("dp", "seq", "tensor"), None),
        P(("dp", "seq")),
        P("tensor"),
        P(("dp", "seq"), None, "tensor"),
        P(None, "tensor"),
        P("tensor"),
        P("tensor", ("dp", "seq")),
        P(("dp", "seq"), "tensor"),
        P("tensor"),
        P(None, "tensor"),
        P("tensor"),
        P("tensor", ("dp", "seq")),
    )
    return jax.shard_map(
        on_device,
        mesh=mesh,
        in_specs=placed,
        out_specs=(
            P(("dp", "seq", "tensor"), None),
            P(("dp", "seq", "tensor"), None),
            P("tensor"),
            P(("dp", "seq"), None, "tensor"),
            P(None, "tensor"),
            P("tensor"),
            P("tensor", ("dp", "seq")),
            P("tensor", ("dp", "seq")),
            P(("dp", "seq"), "tensor"),
            P("tensor"),
            P(None, "tensor"),
            P("tensor"),
            P("tensor", ("dp", "seq")),
        ),
        check_vma=False,
    )
```

```python
import functools

import jax
import jax.numpy as jnp
from jax import lax
from jax.experimental import pallas as pl
from jax.experimental.pallas import tpu as pltpu
from jax.sharding import PartitionSpec as P

EPS = 1e-05
LOG2E = 1.4426950408889634
LN2 = 0.6931471805599453
FAR = 1e30
MESH = pl.DeviceIdType.MESH


def passed_along(x, axis, by):
    size = lax.axis_size(axis)
    pairs = [(i, i + by) for i in range(size) if 0 <= i + by < size]
    return lax.ppermute(x, axis, pairs)


def silu_slope(values):
    logistic = jax.nn.sigmoid(values)
    return logistic * (1.0 + values * (1.0 - logistic))


F32, BF16 = jnp.float32, jnp.bfloat16
N = 16
CH = 16

def fwd_kernel(stepd_ref, u_ref, bc_ref, cdiag_ref, rate_ref, y_ref, ckpt_ref, last_ref, state_ref, sbf_ref, *, unroll):
    @pl.when(pl.program_id(1) == 0)
    def _():
        state_ref[...] = jnp.zeros_like(state_ref)
    ckpt_ref[0] = state_ref[...]
    rate = rate_ref[...]
    tb = stepd_ref.shape[0]

    def chunk(c, s):
        base = pl.multiple_of(c * CH, CH)
        bc = bc_ref[c]
        for k in range(CH):
            dec = jnp.exp2(rate * stepd_ref[pl.ds(base + k, 1), :])
            s = dec * s + bc[:, k:k + 1] * u_ref[pl.ds(base + k, 1), :]
            sbf_ref[k * N:(k + 1) * N, :] = s.astype(BF16)
        y_ref[pl.ds(base, CH), :] = jnp.dot(cdiag_ref[pl.ds(base, CH), :], sbf_ref[...], preferred_element_type=F32)
        return s

    s = lax.fori_loop(0, tb // CH, chunk, state_ref[...], unroll=unroll)
    state_ref[...] = s
    last_ref[...] = s

def fwd(stepd, u, bc, cdiag, rate, tb=128, w=512, unroll=1):
    t, c = stepd.shape
    w = min(w, c)
    grid = (c // w, t // tb)
    return pl.pallas_call(
        functools.partial(fwd_kernel, unroll=unroll),
        grid=grid,
        in_specs=[
            pl.BlockSpec((tb, w), lambda j, i: (i, j)),
            pl.BlockSpec((tb, w), lambda j, i: (i, j)),
            pl.BlockSpec((tb // CH, N, 2 * CH), lambda j, i: (i, 0, 0)),
            pl.BlockSpec((tb, CH * N), lambda j, i: (i, 0)),
            pl.BlockSpec((N, w), lambda j, i: (0, j)),
        ],
        out_specs=[
            pl.BlockSpec((tb, w), lambda j, i: (i, j)),
            pl.BlockSpec((1, N, w), lambda j, i: (i, 0, j)),
            pl.BlockSpec((N, w), lambda j, i: (0, j)),
        ],
        out_shape=[
            jax.ShapeDtypeStruct((t, c), F32),
            jax.ShapeDtypeStruct((t // tb, N, c), F32),
            jax.ShapeDtypeStruct((N, c), F32),
        ],
        scratch_shapes=[pltpu.VMEM((N, w), F32), pltpu.VMEM((CH * N, w), BF16)],
        compiler_params=pltpu.CompilerParams(vmem_limit_bytes=48 << 20),
        name="scan_forward",
    )(stepd, u, bc, cdiag, rate)

def bwd_kernel(stepd_ref, u_ref, ds_ref, bc_ref, bdiag_ref, ones_ref, rate_ref, ckpt_ref, gin_ref,
               wb_ref, dn_ref, db_ref, dc_ref, acc_ref, g_ref, sbf_ref, abf_ref, rbf_ref, *, unroll):
    @pl.when(pl.program_id(1) == 0)
    def _():
        g_ref[...] = gin_ref[...]
        acc_ref[...] = jnp.zeros_like(acc_ref)
    rate = rate_ref[...]
    tb = stepd_ref.shape[0]
    nc = tb // CH
    row = lax.broadcasted_iota(jnp.int32, (CH, CH * N), 0)
    lane = lax.broadcasted_iota(jnp.int32, (CH, CH * N), 1)
    diag = (row == lane // N).astype(F32)
    sbf_ref[0:N, :] = ckpt_ref[0].astype(BF16)

    def forward(c, s):
        base = pl.multiple_of(c * CH, CH)
        bc = bc_ref[c]
        for k in range(CH):
            dec = jnp.exp2(rate * stepd_ref[pl.ds(base + k, 1), :])
            s = dec * s + bc[:, k:k + 1] * u_ref[pl.ds(base + k, 1), :]
            sbf_ref[pl.ds(pl.multiple_of((base + k + 1) * N, N), N), :] = s.astype(BF16)
        return s

    lax.fori_loop(0, nc, forward, ckpt_ref[0])

    def backward(c, carry):
        g, acc = carry
        c = nc - 1 - c
        base = pl.multiple_of(c * CH, CH)
        bc = bc_ref[c]
        for k in range(CH - 1, -1, -1):
            sd = stepd_ref[pl.ds(base + k, 1), :]
            adj = g + bc[:, CH + k:CH + k + 1] * ds_ref[pl.ds(base + k, 1), :]
            abf_ref[k * N:(k + 1) * N, :] = adj.astype(BF16)
            g = jnp.exp2(rate * sd) * adj
            before = sbf_ref[pl.ds(pl.multiple_of((base + k) * N, N), N), :].astype(F32)
            r = g * before * rate
            rbf_ref[k * N:(k + 1) * N, :] = r.astype(BF16)
            acc = acc + r * sd
        wb_ref[pl.ds(base, CH), :] = jnp.dot(bdiag_ref[pl.ds(base, CH), :], abf_ref[...], preferred_element_type=F32)
        dn_ref[pl.ds(base, CH), :] = jnp.dot(ones_ref[...], rbf_ref[...], preferred_element_type=F32)
        nt = (((1,), (1,)), ((), ()))
        now = sbf_ref[pl.ds(pl.multiple_of((base + 1) * N, N), CH * N), :]
        db = lax.dot_general(u_ref[pl.ds(base, CH), :].astype(BF16), abf_ref[...], nt, preferred_element_type=F32)
        dc = lax.dot_general(ds_ref[pl.ds(base, CH), :].astype(BF16), now, nt, preferred_element_type=F32)
        db_ref[0, pl.ds(c, 1), :] = jnp.sum(db * diag, axis=0, keepdims=True)
        dc_ref[0, pl.ds(c, 1), :] = jnp.sum(dc * diag, axis=0, keepdims=True)
        return g, acc

    g, acc = lax.fori_loop(0, nc, backward, (g_ref[...], acc_ref[...]), unroll=unroll)
    g_ref[...] = g
    acc_ref[...] = acc

def bwd(stepd, u, ds, bc, bdiag, ones, rate, ckpt, gin, tb=128, w=512, unroll=1):
    t, c = stepd.shape
    w = min(w, c)
    nb = t // tb
    grid = (c // w, nb)
    rows = pl.BlockSpec((tb, w), lambda j, i: (nb - 1 - i, j))
    return pl.pallas_call(
        functools.partial(bwd_kernel, unroll=unroll),
        grid=grid,
        in_specs=[
            rows, rows, rows,
            pl.BlockSpec((tb // CH, N, 2 * CH), lambda j, i: (nb - 1 - i, 0, 0)),
            pl.BlockSpec((tb, CH * N), lambda j, i: (nb - 1 - i, 0)),
            pl.BlockSpec((CH, CH * N), lambda j, i: (0, 0)),
            pl.BlockSpec((N, w), lambda j, i: (0, j)),
            pl.BlockSpec((1, N, w), lambda j, i: (nb - 1 - i, 0, j)),
            pl.BlockSpec((N, w), lambda j, i: (0, j)),
        ],
        out_specs=[
            rows, rows,
            pl.BlockSpec((1, tb // CH, CH * N), lambda j, i: (j, nb - 1 - i, 0)),
            pl.BlockSpec((1, tb // CH, CH * N), lambda j, i: (j, nb - 1 - i, 0)),
            pl.BlockSpec((N, w), lambda j, i: (0, j)),
        ],
        out_shape=[
            jax.ShapeDtypeStruct((t, c), F32),
            jax.ShapeDtypeStruct((t, c), F32),
            jax.ShapeDtypeStruct((c // w, t // CH, CH * N), F32),
            jax.ShapeDtypeStruct((c // w, t // CH, CH * N), F32),
            jax.ShapeDtypeStruct((N, c), F32),
        ],
        scratch_shapes=[pltpu.VMEM((N, w), F32), pltpu.VMEM(((tb + 1) * N, w), BF16),
                        pltpu.VMEM((CH * N, w), BF16), pltpu.VMEM((CH * N, w), BF16)],
        compiler_params=pltpu.CompilerParams(vmem_limit_bytes=48 << 20),
        name="scan_backward",
    )(stepd, u, ds, bc, bdiag, ones, rate, ckpt, gin)


def correct_kernel(alive_ref, y_ref, stepd_ref, cdiag_ref, rate_ref, ckpt_ref, sin_ref, yo_ref, ckpto_ref, state_ref, sbf_ref):
    i = pl.program_id(1)

    @pl.when(i == 0)
    def _():
        state_ref[...] = sin_ref[...]

    alive = alive_ref[i] != 0

    @pl.when(alive)
    def _():
        rate = rate_ref[...]
        ckpto_ref[0] = ckpt_ref[0] + state_ref[...]

        def chunk(c, s):
            base = pl.multiple_of(c * CH, CH)
            for k in range(CH):
                s = jnp.exp2(rate * stepd_ref[pl.ds(base + k, 1), :]) * s
                sbf_ref[k * N:(k + 1) * N, :] = s.astype(BF16)
            yo_ref[pl.ds(base, CH), :] = y_ref[pl.ds(base, CH), :] + jnp.dot(
                cdiag_ref[pl.ds(base, CH), :], sbf_ref[...], preferred_element_type=F32
            )
            return s

        state_ref[...] = lax.fori_loop(0, y_ref.shape[0] // CH, chunk, state_ref[...])

    @pl.when(jnp.logical_not(alive))
    def _():
        yo_ref[...] = y_ref[...]
        ckpto_ref[...] = ckpt_ref[...]


def correct(alive, y, stepd, cdiag, rate, ckpt, state_in, tb=128, w=512):
    t, c = stepd.shape
    w = min(w, c)
    rows = pl.BlockSpec((tb, w), lambda j, i, _: (i, j))
    lanes = pl.BlockSpec((N, w), lambda j, i, _: (0, j))
    marks = pl.BlockSpec((1, N, w), lambda j, i, _: (i, 0, j))
    return pl.pallas_call(
        correct_kernel,
        grid_spec=pltpu.PrefetchScalarGridSpec(
            num_scalar_prefetch=1,
            grid=(c // w, t // tb),
            in_specs=[rows, rows, pl.BlockSpec((tb, CH * N), lambda j, i, _: (i, 0)), lanes, marks, lanes],
            out_specs=[rows, marks],
            scratch_shapes=[pltpu.VMEM((N, w), F32), pltpu.VMEM((CH * N, w), BF16)],
        ),
        out_shape=[jax.ShapeDtypeStruct((t, c), F32), jax.ShapeDtypeStruct(ckpt.shape, F32)],
        compiler_params=pltpu.CompilerParams(vmem_limit_bytes=48 << 20),
        name="scan_correct",
    )(alive, y, stepd, cdiag, rate, ckpt, state_in)


def entry_kernel(alive_ref, stepd_ref, ds_ref, bc_ref, rate_ref, g_ref):
    i = pl.program_id(1)

    @pl.when(i == 0)
    def _():
        g_ref[...] = jnp.zeros_like(g_ref)

    @pl.when(alive_ref[pl.num_programs(1) - 1 - i] != 0)
    def _():
        rate = rate_ref[...]
        nc = stepd_ref.shape[0] // CH

        def chunk(c, g):
            c = nc - 1 - c
            base = pl.multiple_of(c * CH, CH)
            bc = bc_ref[c]
            for k in range(CH - 1, -1, -1):
                adj = g + bc[:, CH + k:CH + k + 1] * ds_ref[pl.ds(base + k, 1), :]
                g = jnp.exp2(rate * stepd_ref[pl.ds(base + k, 1), :]) * adj
            return g

        g_ref[...] = lax.fori_loop(0, nc, chunk, g_ref[...])


def entry(alive, stepd, ds, bc, rate, tb=128, w=512):
    t, c = stepd.shape
    w = min(w, c)
    nb = t // tb
    rows = pl.BlockSpec((tb, w), lambda j, i, _: (nb - 1 - i, j))
    lanes = pl.BlockSpec((N, w), lambda j, i, _: (0, j))
    return pl.pallas_call(
        entry_kernel,
        grid_spec=pltpu.PrefetchScalarGridSpec(
            num_scalar_prefetch=1,
            grid=(c // w, nb),
            in_specs=[rows, rows, pl.BlockSpec((tb // CH, N, 2 * CH), lambda j, i, _: (nb - 1 - i, 0, 0)), lanes],
            out_specs=lanes,
        ),
        out_shape=jax.ShapeDtypeStruct((N, c), F32),
        compiler_params=pltpu.CompilerParams(vmem_limit_bytes=48 << 20),
        name="scan_entry",
    )(alive, stepd, ds, bc, rate)


def carried(local, reach, axis, by):
    found = jnp.zeros_like(local)
    for _ in range(lax.axis_size(axis) - 1):
        found = passed_along(local + reach * found, axis, by)
    return found


def columns(values):
    tokens = values.shape[0]
    return values.reshape(tokens // CH, CH, N).transpose(0, 2, 1)


def diagonal(values):
    tokens = values.shape[0]
    mine = jnp.arange(CH * N)[None] // N == jnp.arange(tokens)[:, None] % CH
    return jnp.where(mine, jnp.tile(values.astype(BF16), (1, CH)), 0)


def mesh_copy(src, dst, send, recv, **where):
    return pltpu.make_async_remote_copy(
        src_ref=src, dst_ref=dst, send_sem=send, recv_sem=recv, device_id=where, device_id_type=MESH
    )


def place():
    dp, seq, mine = lax.axis_index("dp"), lax.axis_index("seq"), lax.axis_index("tensor")
    return dp, seq, mine


def tail_kernel(n, dps, seqs, subs, lag, dx_ref, dz_ref, w_ref, nrm_ref, sm_ref, all_ref,
                dn_ref, gin_ref, gs_ref, ga_ref,
                gacc, gsend, grecv, all_mine,
                zr, zl, part_r, part_l, one_send, one_recv, two_recv, sm_one, sm_two, all_one, all_two,
                r_send, r_recv, l_send, l_recv, w1s, w1r, w2s, w2r, s1s, s1r, s2s, s2r, a1s, a1r, a2s, a2r, gs, gr):
    dp, seq, t = place()
    core, hi = dp % 2, dp // 2
    chips = dps // 2 * seqs
    chip = hi * seqs + seq
    rows = dn_ref.shape[0]
    part = rows // subs
    wide = dn_ref.shape[1]
    wrows = gin_ref.shape[1]
    tile = 512

    def owner(q, c):
        return (q // seqs * 2 + c) * seqs + q % seqs

    def to_chip(q):
        return dict(dp=q // seqs * 2 + core, seq=q % seqs)

    barrier = pltpu.get_barrier_semaphore()
    pl.semaphore_signal(barrier, inc=1, device_id=dict(dp=hi * 2 + 1 - core), device_id_type=MESH)
    for step in range(1, chips):
        q = lax.rem(chip + step, chips)
        pl.semaphore_signal(barrier, inc=1, device_id=to_chip(q), device_id_type=MESH)

    for ahead in range(1, n):
        pl.semaphore_signal(barrier, inc=1, device_id=dict(tensor=lax.rem(t + ahead, n)), device_id_type=MESH)
    pl.semaphore_wait(barrier, chips + n - 1)
    gacc[...] = jnp.zeros_like(gacc)

    partner = dict(dp=hi * 2 + 1 - core)
    right, left = dict(tensor=lax.rem(t + 1, n)), dict(tensor=lax.rem(t + n - 1, n))

    def r_copy(i):
        return mesh_copy(zr.at[i], zr.at[i], r_send.at[i], r_recv.at[i], **right)

    def l_copy(i):
        return mesh_copy(zl.at[i], zl.at[i], l_send.at[i], l_recv.at[i], **left)

    def w1_copy(q):
        return mesh_copy(one_send.at[q], one_recv.at[q], w1s.at[q], w1r.at[q], **partner)

    def w2_copy(q, slot):
        return mesh_copy(one_recv.at[q], two_recv.at[slot], w2s.at[q], w2r.at[slot], **to_chip(q))

    def s1_copy(q):
        return mesh_copy(sm_ref.at[owner(q, 1 - core)], sm_one.at[q], s1s.at[q], s1r.at[q], **partner)

    def s2_copy(q, slot):
        return mesh_copy(sm_one.at[q], sm_two.at[slot], s2s.at[q], s2r.at[slot], **to_chip(q))

    def a1_copy():
        return mesh_copy(all_mine, all_one, a1s, a1r, **partner)

    def a2_copy(q, slot):
        return mesh_copy(all_one, all_two.at[slot], a2s.at[q], a2r.at[slot], **to_chip(q))

    def g_copy(p, slot):
        return mesh_copy(gsend.at[p], grecv.at[slot], gs.at[p], gr.at[slot], tensor=p)

    def partial_rows(o, dst):
        here = pl.ds(pl.multiple_of(o * rows, rows), rows)

        @pl.loop(0, wide // tile)
        def _(j):
            cols = pl.ds(pl.multiple_of(j * tile, tile), tile)
            nt = (((1,), (1,)), ((), ()))
            block = lax.dot_general(
                dx_ref[here, :], w_ref[0, cols, :], nt, preferred_element_type=F32
            ) + lax.dot_general(dz_ref[here, :], w_ref[1, cols, :], nt, preferred_element_type=F32)
            dst[:, cols] = block
            scaled = block * nrm_ref[here, cols].astype(F32)
            gacc[:, cols] = gacc[:, cols] + jnp.sum(scaled.reshape(rows // 8, 8, tile), axis=0)

    def weight_rows(p, k):
        cols = pl.ds(pl.multiple_of(p * wrows, wrows), wrows)
        tn = (((0,), (0,)), ((), ()))
        d_ref = dx_ref if k == 0 else dz_ref
        return lax.dot_general(nrm_ref[:, cols], d_ref[...], tn, preferred_element_type=F32)

    for q in range(chips):
        s1_copy(q).start()

    def stream(i, limit, start, buf, copy, part_ref, owner_of):
        @pl.when(jnp.logical_and(i >= 0, i < limit))
        def _():
            k, sub = i // subs, i % subs

            @pl.when(sub == 0)
            def _():
                partial_rows(owner_of(k), part_ref)

            @pl.when(jnp.logical_and(start, sub == 0))
            def _():
                @pl.loop(0, subs)
                def _(j):
                    here = part_ref[pl.ds(pl.multiple_of(j * part, part), part), :]
                    buf[k * subs + j] = here.astype(BF16)
                    copy(k * subs + j).start()

            @pl.when(jnp.logical_not(start))
            def _():
                here = part_ref[pl.ds(pl.multiple_of(sub * part, part), part), :]
                copy(i).wait_recv()
                buf[i] = (here + buf[i].astype(F32)).astype(BF16)
                copy(i).start()

    def step(g, _):
        stream(g - lag * t, (n - 1 - t) * subs, t == 0, zr, r_copy, part_r, lambda k: n - 1 - k)
        stream(g - lag * (n - 1 - t), t * subs, t == n - 1, zl, l_copy, part_l, lambda k: k)

        @pl.when(g < chips)
        def _():
            for k in range(2):
                one_send[g, k] = weight_rows(owner(g, 1 - core), k).astype(BF16)
            w1_copy(g).start()

        @pl.when(jnp.logical_and(g >= chips, g < 2 * chips - 1))
        def _():
            q = lax.rem(chip + 1 + g - chips, chips)
            w1_copy(q).wait_recv()
            for k in range(2):
                one_recv[q, k] = (weight_rows(owner(q, core), k) + one_recv[q, k].astype(F32)).astype(BF16)
            w2_copy(q, chip).start()

        @pl.when(g == 2 * chips - 1)
        def _():
            for q in range(chips):
                s1_copy(q).wait_recv()
                sm_one[q] = sm_one[q] + sm_ref[owner(q, core)]
            for ahead in range(1, chips):
                q = lax.rem(chip + ahead, chips)
                s2_copy(q, chip).start()
            w1_copy(chip).wait_recv()
            for k in range(2):
                gin_ref[k] = weight_rows(owner(chip, core), k) + one_recv[chip, k].astype(F32)

        @pl.when(g == 2 * chips)
        def _():
            partial_rows(t, dn_ref)

        return 0

    steps = max((n - 1) * max(subs, lag), 2 * chips + 1)
    lax.fori_loop(0, steps, step, 0)

    share = wide // n
    for p in range(n):
        gsend[p] = gacc[:, p * share:(p + 1) * share]
    for ahead in range(1, n):
        g_copy(lax.rem(t + ahead, n), t).start()

    @pl.loop(0, subs)
    def _(s):
        here = pl.ds(pl.multiple_of(s * part, part), part)

        @pl.when(t > 0)
        def _():
            i = (n - 1 - t) * subs + s
            r_copy(i).wait_recv()
            dn_ref[here, :] = dn_ref[here, :] + zr[i].astype(F32)

        @pl.when(t < n - 1)
        def _():
            i = t * subs + s
            l_copy(i).wait_recv()
            dn_ref[here, :] = dn_ref[here, :] + zl[i].astype(F32)

    plain = all_ref.shape[0]
    all_mine[0:plain, :] = all_ref[...]
    all_mine[plain:, :] = jnp.zeros((8, all_mine.shape[1]), F32)
    all_mine[plain:, 0:share] = gsend[t]
    for ahead in range(1, n):
        p = lax.rem(t + ahead, n)
        g_copy(p, p).wait_recv()
        all_mine[plain:, 0:share] = all_mine[plain:, 0:share] + grecv[p]
    a1_copy().start()
    gs_ref[...] = sm_one[chip]
    for ahead in range(1, chips):
        q = lax.rem(chip + ahead, chips)
        s2_copy(q, q).wait_recv()
        gs_ref[...] = gs_ref[...] + sm_two[q]
    a1_copy().wait_recv()
    all_one[...] = all_one[...] + all_mine[...]
    for ahead in range(1, chips):
        a2_copy(lax.rem(chip + ahead, chips), chip).start()
    ga_ref[...] = all_one[...]
    for ahead in range(1, chips):
        q = lax.rem(chip + ahead, chips)
        w2_copy(q, q).wait_recv()
        gin_ref[...] = gin_ref[...] + two_recv[q].astype(F32)
    for ahead in range(1, chips):
        q = lax.rem(chip + ahead, chips)
        a2_copy(q, q).wait_recv()
        ga_ref[...] = ga_ref[...] + all_two[q]

    for q in range(chips):
        s1_copy(q).wait_send()
        w1_copy(q).wait_send()
    a1_copy().wait_send()
    for ahead in range(1, n):
        g_copy(lax.rem(t + ahead, n), t).wait_send()
    for ahead in range(1, chips):
        q = lax.rem(chip + ahead, chips)
        s2_copy(q, chip).wait_send()
        a2_copy(q, chip).wait_send()
        w2_copy(q, chip).wait_send()

    @pl.loop(0, (n - 1) * subs)
    def _(i):
        @pl.when(i < (n - 1 - t) * subs)
        def _():
            r_copy(i).wait_send()

        @pl.when(i < t * subs)
        def _():
            l_copy(i).wait_send()


def tail(dx, dz, w_full, normed, small, whole):
    n, dps, seqs = (lax.axis_size(axis) for axis in ("tensor", "dp", "seq"))
    chips = dps // 2 * seqs
    rows = dx.shape[0] // n
    wide, lanes = w_full.shape[1], w_full.shape[2]
    wrows = wide // (dps * seqs)
    subs = max(1, rows // 32)
    hops = (n - 1) * subs
    vmem = pl.BlockSpec(memory_space=pltpu.VMEM)
    dma = pltpu.SemaphoreType.DMA
    few = dma((chips,))
    return pl.pallas_call(
        functools.partial(tail_kernel, n, dps, seqs, subs, 2),
        out_shape=[
            jax.ShapeDtypeStruct((rows, wide), F32),
            jax.ShapeDtypeStruct((2, wrows, lanes), F32),
            jax.ShapeDtypeStruct(small.shape[1:], F32),
            jax.ShapeDtypeStruct((whole.shape[0] + 8, lanes), F32),
        ],
        in_specs=[vmem] * 6,
        out_specs=[vmem] * 4,
        scratch_shapes=[
            pltpu.VMEM((8, wide), F32),
            pltpu.VMEM((n, 8, wide // n), F32),
            pltpu.VMEM((n, 8, wide // n), F32),
            pltpu.VMEM((whole.shape[0] + 8, lanes), F32),
            pltpu.VMEM((hops, rows // subs, wide), BF16),
            pltpu.VMEM((hops, rows // subs, wide), BF16),
            pltpu.VMEM((rows, wide), F32),
            pltpu.VMEM((rows, wide), F32),
            pltpu.VMEM((chips, 2, wrows, lanes), BF16),
            pltpu.VMEM((chips, 2, wrows, lanes), BF16),
            pltpu.VMEM((chips, 2, wrows, lanes), BF16),
            pltpu.VMEM((chips,) + small.shape[1:], F32),
            pltpu.VMEM((chips,) + small.shape[1:], F32),
            pltpu.VMEM((whole.shape[0] + 8, lanes), F32),
            pltpu.VMEM((chips, whole.shape[0] + 8, lanes), F32),
            dma((hops,)), dma((hops,)), dma((hops,)), dma((hops,)),
            few, few, few, few, few, few, few, few, dma, dma, few, few, dma((n,)), dma((n,)),
        ],
        compiler_params=pltpu.CompilerParams(
            collective_id=2, has_side_effects=True, vmem_limit_bytes=60 << 20
        ),
        name="tail_sums",
    )(dx, dz, w_full, normed, small, whole)


def mid_kernel(n, subs, lag, gated_ref, w_ref, hid_ref, tea_ref, scale_ref, z_ref, scan_ref,
               out_ref, go_ref, piece_ref, dscan_ref, dz_ref,
               zr, zl, part_r, part_l, r_send, r_recv, l_send, l_recv, ar_send, ar_recv, al_send, al_recv):
    t = lax.axis_index("tensor")
    rows, wide = hid_ref.shape
    part = rows // subs
    tile = 512
    right, left = dict(tensor=lax.rem(t + 1, n)), dict(tensor=lax.rem(t + n - 1, n))

    barrier = pltpu.get_barrier_semaphore()
    for peer in (right, left):
        pl.semaphore_signal(barrier, inc=1, device_id=peer, device_id_type=MESH)
    pl.semaphore_wait(barrier, 2)

    def r_copy(i):
        return mesh_copy(zr.at[i], zr.at[i], r_send.at[i], r_recv.at[i], **right)

    def l_copy(i):
        return mesh_copy(zl.at[i], zl.at[i], l_send.at[i], l_recv.at[i], **left)

    def at(o, s):
        return pl.ds(pl.multiple_of(o * rows + s * part, part), part)

    def ar_copy(o, s):
        ref = piece_ref.at[at(o, s), :]
        return mesh_copy(ref, ref, ar_send.at[o * subs + s], ar_recv.at[o * subs + s], **right)

    def al_copy(o, s):
        ref = piece_ref.at[at(o, s), :]
        return mesh_copy(ref, ref, al_send.at[o * subs + s], al_recv.at[o * subs + s], **left)

    def partial_rows(o, dst):
        here = pl.ds(pl.multiple_of(o * rows, rows), rows)

        @pl.loop(0, wide // tile)
        def _(j):
            cols = pl.ds(pl.multiple_of(j * tile, tile), tile)
            nt = (((1,), (1,)), ((), ()))
            dst[:, cols] = lax.dot_general(gated_ref[here, :], w_ref[cols, :], nt, preferred_element_type=F32)

    def backward_rows(o):
        here = pl.ds(pl.multiple_of(o * rows, rows), rows)
        d_gated = jnp.dot(piece_ref[here, :], w_ref[...], preferred_element_type=F32)
        z = z_ref[here, :]
        s = 1.0 / (1.0 + jnp.exp(-z))
        dscan_ref[here, :] = d_gated * (z * s)
        dz_ref[here, :] = (d_gated * scan_ref[here, :] * (s * (1.0 + z * (1.0 - s)))).astype(BF16)

    def stream(i, limit, start, buf, copy, part_ref, owner_of):
        @pl.when(jnp.logical_and(i >= 0, i < limit))
        def _():
            k, sub = i // subs, i % subs

            @pl.when(sub == 0)
            def _():
                partial_rows(owner_of(k), part_ref)

            @pl.when(jnp.logical_and(start, sub == 0))
            def _():
                @pl.loop(0, subs)
                def _(j):
                    here = part_ref[pl.ds(pl.multiple_of(j * part, part), part), :]
                    buf[k * subs + j] = here.astype(BF16)
                    copy(k * subs + j).start()

            @pl.when(jnp.logical_not(start))
            def _():
                here = part_ref[pl.ds(pl.multiple_of(sub * part, part), part), :]
                copy(i).wait_recv()
                buf[i] = (here + buf[i].astype(F32)).astype(BF16)
                copy(i).start()

    def ready(o):
        from_left = jnp.where(o > 0, lag * o + (n - 1 - o) * subs, 0)
        from_right = jnp.where(o < n - 1, lag * (n - 1 - o) + o * subs, 0)
        return jnp.maximum(from_left, from_right)

    gap = max(subs, lag)
    base = lag + (n - 2) * subs if subs >= lag else (n - 1) * lag

    def turn(d, o):
        inner = base + (d - o) * gap
        inner = jnp.where(d == 0, (n - 1) * gap, inner)
        return jnp.where(d == n - 1, base + (n - 2 - o) * gap + lag, inner)

    def finish(s):
        here = pl.ds(pl.multiple_of(s * part, part), part)

        @pl.when(s == 0)
        def _():
            partial_rows(t, go_ref)

        @pl.when(t > 0)
        def _():
            i = (n - 1 - t) * subs + s
            r_copy(i).wait_recv()
            go_ref[here, :] = go_ref[here, :] + zr[i].astype(F32)

        @pl.when(t < n - 1)
        def _():
            i = t * subs + s
            l_copy(i).wait_recv()
            go_ref[here, :] = go_ref[here, :] + zl[i].astype(F32)

        result = hid_ref[here, :].astype(F32) + go_ref[here, :]
        out_ref[here, :] = result.astype(BF16)
        grad = scale_ref[here, :] * (result - tea_ref[here, :].astype(F32))
        go_ref[here, :] = grad
        piece_ref[at(t, s), :] = grad.astype(BF16)

    def step(g, _):
        stream(g - lag * t, (n - 1 - t) * subs, t == 0, zr, r_copy, part_r, lambda k: n - 1 - k)
        stream(g - lag * (n - 1 - t), t * subs, t == n - 1, zl, l_copy, part_l, lambda k: k)

        @pl.loop(0, n)
        def _(o):
            s_own = g - ready(t)
            s_right = g - turn(t, o)
            s_left = g - turn(n - 1 - t, n - 1 - o)

            @pl.when(jnp.logical_and(o == t, jnp.logical_and(s_own >= 0, s_own < subs)))
            def _():
                finish(s_own)

            @pl.when(jnp.logical_and(o <= t, jnp.logical_and(s_right >= 0, s_right < subs)))
            def _():
                @pl.when(o < t)
                def _():
                    ar_copy(o, s_right).wait_recv()

                @pl.when(t < n - 1)
                def _():
                    ar_copy(o, s_right).start()

            @pl.when(jnp.logical_and(o >= t, jnp.logical_and(s_left >= 0, s_left < subs)))
            def _():
                @pl.when(o > t)
                def _():
                    al_copy(o, s_left).wait_recv()

                @pl.when(t > 0)
                def _():
                    al_copy(o, s_left).start()

            s_done = jnp.where(o == t, s_own, jnp.where(o < t, s_right, s_left))

            @pl.when(s_done == subs - 1)
            def _():
                backward_rows(o)

        return 0

    steps = base + (n - 1) * gap + subs + lag
    lax.fori_loop(0, steps, step, 0)

    @pl.loop(0, (n - 1) * subs)
    def _(i):
        @pl.when(i < (n - 1 - t) * subs)
        def _():
            r_copy(i).wait_send()

        @pl.when(i < t * subs)
        def _():
            l_copy(i).wait_send()

    @pl.loop(0, n * subs)
    def _(i):
        o, s = i // subs, i % subs

        @pl.when(jnp.logical_and(o <= t, t < n - 1))
        def _():
            ar_copy(o, s).wait_send()

        @pl.when(jnp.logical_and(o >= t, t > 0))
        def _():
            al_copy(o, s).wait_send()


def middle(gated, w_out, hidden, teacher, scale, z_gate, scan_out):
    n = lax.axis_size("tensor")
    rows, wide = hidden.shape
    tokens, lanes = gated.shape
    subs = max(1, rows // 32)
    hops = (n - 1) * subs
    vmem = pl.BlockSpec(memory_space=pltpu.VMEM)
    dma = pltpu.SemaphoreType.DMA
    return pl.pallas_call(
        functools.partial(mid_kernel, n, subs, 2),
        out_shape=[
            jax.ShapeDtypeStruct((rows, wide), BF16),
            jax.ShapeDtypeStruct((rows, wide), F32),
            jax.ShapeDtypeStruct((tokens, wide), BF16),
            jax.ShapeDtypeStruct((tokens, lanes), F32),
            jax.ShapeDtypeStruct((tokens, lanes), BF16),
        ],
        in_specs=[vmem] * 7,
        out_specs=[vmem] * 5,
        scratch_shapes=[
            pltpu.VMEM((hops, rows // subs, wide), BF16),
            pltpu.VMEM((hops, rows // subs, wide), BF16),
            pltpu.VMEM((rows, wide), F32),
            pltpu.VMEM((rows, wide), F32),
            dma((hops,)), dma((hops,)), dma((hops,)), dma((hops,)),
            dma((n * subs,)), dma((n * subs,)), dma((n * subs,)), dma((n * subs,)),
        ],
        compiler_params=pltpu.CompilerParams(
            collective_id=1, has_side_effects=True, vmem_limit_bytes=60 << 20
        ),
        name="middle",
    )(gated, w_out, hidden, teacher, scale, z_gate, scan_out)


def front_kernel(n, dps, seqs, subs, lag, hid_ref, gain_ref, cnt_ref, win_ref, wsm_ref,
                 x_ref, z_ref, nrm_ref, w_ref, prev_ref, total_ref, gfull, ws_ref,
                 rows_ref, grecv, cnt_one, cnt_two,
                 ar_send, ar_recv, al_send, al_recv, gs, gr, c1s, c1r, c2s, c2r, hs, hr, ls,
                 chip_send, chip_recv, core_send, core_recv):
    dp, seq, t = place()
    core, hi = dp % 2, dp // 2
    chips = dps // 2 * seqs
    chip = hi * seqs + seq
    rows, wide = hid_ref.shape
    part = rows // subs
    share = wide // n
    wrows = win_ref.shape[1]
    tile = 512
    gap = max(subs, lag)
    partner = dict(dp=hi * 2 + 1 - core)
    right, left = dict(tensor=lax.rem(t + 1, n)), dict(tensor=lax.rem(t + n - 1, n))

    def owner(q, c):
        return (q // seqs * 2 + c) * seqs + q % seqs

    def to_chip(q):
        return dict(dp=q // seqs * 2 + core, seq=q % seqs)

    barrier = pltpu.get_barrier_semaphore()
    pl.semaphore_signal(barrier, inc=1, device_id=partner, device_id_type=MESH)
    for ahead in range(1, chips):
        pl.semaphore_signal(barrier, inc=1, device_id=to_chip(lax.rem(chip + ahead, chips)), device_id_type=MESH)
    for ahead in range(1, n):
        pl.semaphore_signal(barrier, inc=1, device_id=dict(tensor=lax.rem(t + ahead, n)), device_id_type=MESH)
    pl.semaphore_wait(barrier, chips + n - 1)

    def at(o, s):
        return pl.ds(pl.multiple_of(o * rows + s * part, part), part)

    def ar_copy(o, s):
        ref = rows_ref.at[at(o, s), :]
        return mesh_copy(ref, ref, ar_send.at[o * subs + s], ar_recv.at[o * subs + s], **right)

    def al_copy(o, s):
        ref = rows_ref.at[at(o, s), :]
        return mesh_copy(ref, ref, al_send.at[o * subs + s], al_recv.at[o * subs + s], **left)

    def g_copy(p, slot):
        return mesh_copy(gain_ref, grecv.at[slot], gs.at[p], gr.at[slot], tensor=p)

    def block(kind, p):
        if kind == 0:
            return w_ref.at[:, pl.ds(pl.multiple_of(p * wrows, wrows), wrows), :]
        return ws_ref.at[p]

    stored = (win_ref, wsm_ref)

    def chip_copy(kind, q, p):
        return mesh_copy(stored[kind], block(kind, p), chip_send.at[kind, q], chip_recv.at[kind, p], **to_chip(q))

    def core_copy(kind, p, own):
        src = stored[kind] if own else block(kind, p)
        return mesh_copy(src, block(kind, p), core_send.at[kind, p], core_recv.at[kind, p], **partner)

    mine = owner(chip, core)

    def count_one():
        return mesh_copy(cnt_ref, cnt_one, c1s, c1r, **partner)

    def count_two(q, slot):
        return mesh_copy(cnt_one, cnt_two.at[slot], c2s.at[q], c2r.at[slot], **to_chip(q))

    def edge_copy():
        last = x_ref.at[pl.ds(x_ref.shape[0] - 8, 8), :]
        return mesh_copy(last, prev_ref, hs, hr, seq=lax.rem(seq + 1, seqs))

    def local_copy():
        return pltpu.make_async_copy(wsm_ref, block(1, mine), ls)

    for ahead in range(1, n):
        g_copy(lax.rem(t + ahead, n), t).start()
    count_one().start()
    rows_ref[pl.ds(pl.multiple_of(t * rows, rows), rows), :] = hid_ref[...]

    @pl.loop(0, subs)
    def _(s):
        @pl.when(t < n - 1)
        def _():
            ar_copy(t, s).start()

        @pl.when(t > 0)
        def _():
            al_copy(t, s).start()

    def share_out(kind):
        for ahead in range(1, chips):
            chip_copy(kind, lax.rem(chip + ahead, chips), mine).start()
        core_copy(kind, mine, True).start()

    share_out(1)
    share_out(0)
    local_copy().start()
    w_ref[:, pl.ds(pl.multiple_of(mine * wrows, wrows), wrows), :] = win_ref[...]

    gfull[...] = jnp.zeros_like(gfull)
    for ahead in range(1, n):
        p = lax.rem(t + ahead, n)
        g_copy(p, p).wait_recv()
    grecv[t] = gain_ref[...]
    for p in range(n):
        gfull[:, p * share:(p + 1) * share] = grecv[p]
    count_one().wait_recv()
    count_one().wait_send()
    cnt_one[...] = cnt_one[...] + cnt_ref[...]
    for ahead in range(1, chips):
        count_two(lax.rem(chip + ahead, chips), chip).start()

    def normalize(o):
        @pl.loop(0, subs)
        def _(s):
            here = at(o, s)
            values = rows_ref[here, :].astype(F32)
            inv = lax.rsqrt(jnp.mean(values * values, axis=1, keepdims=True) + EPS)
            nrm_ref[here, :] = (values * inv * gfull[0:1, :]).astype(BF16)

    def project(o):
        here = pl.ds(pl.multiple_of(o * rows, rows), rows)
        for k, dst in enumerate((x_ref, z_ref)):
            lanes = dst.shape[1]
            width = min(tile, lanes)

            @pl.loop(0, lanes // width)
            def _(j):
                cols = pl.ds(pl.multiple_of(j * width, width), width)
                dst[here, cols] = jnp.dot(nrm_ref[here, :], w_ref[k, :, cols], preferred_element_type=F32)

    def turn(d, o):
        final = jnp.where(o == 0, (n - 1) * gap + 1, (n - 2 - o) * gap + lag)
        return jnp.where(d == n - 1, final, (d - o) * gap)

    weights_at = (n - 1) * gap

    def step(g, _):
        @pl.when(g == 0)
        def _():
            normalize(t)

        @pl.when(g == weights_at)
        def _():
            for kind in (1, 0):
                for ahead in range(1, chips):
                    q = lax.rem(chip + ahead, chips)
                    chip_copy(kind, q, owner(q, core)).wait_recv()
                    core_copy(kind, owner(q, core), False).start()
            for kind in (1, 0):
                for q in range(chips):
                    core_copy(kind, owner(q, 1 - core), True).wait_recv()
            project(t)

        @pl.loop(0, n)
        def _(o):
            s_right = g - turn(t, o)
            s_left = g - turn(n - 1 - t, n - 1 - o)

            @pl.when(jnp.logical_and(o < t, jnp.logical_and(s_right >= 0, s_right < subs)))
            def _():
                ar_copy(o, s_right).wait_recv()

                @pl.when(t < n - 1)
                def _():
                    ar_copy(o, s_right).start()

            @pl.when(jnp.logical_and(o > t, jnp.logical_and(s_left >= 0, s_left < subs)))
            def _():
                al_copy(o, s_left).wait_recv()

                @pl.when(t > 0)
                def _():
                    al_copy(o, s_left).start()

            landed = jnp.where(o < t, s_right, s_left) - subs + 1

            @pl.when(jnp.logical_and(o != t, landed == 0))
            def _():
                normalize(o)

            ripe = jnp.where(g == weights_at, landed >= 0, jnp.logical_and(g > weights_at, landed == 0))

            @pl.when(jnp.logical_and(o != t, ripe))
            def _():
                project(o)

        return 0

    steps = weights_at + 1 + subs
    lax.fori_loop(0, steps, step, 0)

    @pl.when(seq < seqs - 1)
    def _():
        edge_copy().start()

    total_ref[...] = cnt_one[...]
    for ahead in range(1, chips):
        q = lax.rem(chip + ahead, chips)
        count_two(q, q).wait_recv()
        total_ref[...] = total_ref[...] + cnt_two[q]

    @pl.when(seq == 0)
    def _():
        prev_ref[...] = jnp.zeros_like(prev_ref)

    @pl.when(seq > 0)
    def _():
        edge_copy().wait_recv()

    @pl.when(seq < seqs - 1)
    def _():
        edge_copy().wait_send()

    local_copy().wait()
    for kind in range(2):
        for ahead in range(1, chips):
            chip_copy(kind, lax.rem(chip + ahead, chips), mine).wait_send()
        for q in range(chips):
            core_copy(kind, owner(q, core), False).wait_send()
    for ahead in range(1, chips):
        count_two(lax.rem(chip + ahead, chips), chip).wait_send()
    for ahead in range(1, n):
        g_copy(lax.rem(t + ahead, n), t).wait_send()

    @pl.loop(0, n * subs)
    def _(i):
        o, s = i // subs, i % subs

        @pl.when(jnp.logical_and(o <= t, t < n - 1))
        def _():
            ar_copy(o, s).wait_send()

        @pl.when(jnp.logical_and(o >= t, t > 0))
        def _():
            al_copy(o, s).wait_send()


def front(hidden, gain, count, w_in, w_small):
    n, dps, seqs = (lax.axis_size(axis) for axis in ("tensor", "dp", "seq"))
    parts = dps * seqs
    chips = parts // 2
    rows, wide = hidden.shape
    lanes = w_in.shape[2]
    tokens = rows * n
    subs = max(1, rows // 32)
    vmem, hbm = pl.BlockSpec(memory_space=pltpu.VMEM), pl.BlockSpec(memory_space=pl.ANY)
    dma = pltpu.SemaphoreType.DMA
    many, few, peers = dma((n * subs,)), dma((chips,)), dma((n,))
    return pl.pallas_call(
        functools.partial(front_kernel, n, dps, seqs, subs, 2),
        out_shape=[
            jax.ShapeDtypeStruct((tokens, lanes), F32),
            jax.ShapeDtypeStruct((tokens, lanes), F32),
            jax.ShapeDtypeStruct((tokens, wide), BF16),
            jax.ShapeDtypeStruct((2, wide, lanes), BF16),
            jax.ShapeDtypeStruct((8, lanes), F32),
            jax.ShapeDtypeStruct(count.shape, F32),
            jax.ShapeDtypeStruct((gain.shape[0], wide), F32),
            jax.ShapeDtypeStruct((parts,) + w_small.shape, BF16),
        ],
        in_specs=[vmem] * 5,
        out_specs=[vmem] * 7 + [hbm],
        scratch_shapes=[
            pltpu.VMEM((tokens, wide), BF16),
            pltpu.VMEM((n,) + gain.shape, F32),
            pltpu.VMEM(count.shape, F32),
            pltpu.VMEM((chips,) + count.shape, F32),
            many, many, many, many, peers, peers, dma, dma, few, few, dma, dma, dma,
            dma((2, chips)), dma((2, parts)), dma((2, parts)), dma((2, parts)),
        ],
        compiler_params=pltpu.CompilerParams(
            collective_id=3, has_side_effects=True, vmem_limit_bytes=60 << 20
        ),
        name="front",
    )(hidden, gain, count, w_in, w_small)


def on_device(
    hidden_in,
    teacher,
    segment_ids,
    norm_gain,
    input_projection_weight,
    conv_weight,
    conv_bias,
    xproj_weight,
    dtproj_weight,
    dt_bias,
    a_log,
    d_skip,
    output_projection_weight,
):
    tok_rows = segment_ids.shape[0]
    row_share = hidden_in.shape[0]
    model_width = hidden_in.shape[1]
    conv_taps = conv_weight.shape[0]
    chan_lanes = conv_weight.shape[1]
    back_rows = conv_taps - 1
    row_start = lax.axis_index("tensor") * row_share
    valid_mask = (segment_ids != 0).astype(jnp.float32)
    count_here = jnp.full((8, 128), jnp.sum(valid_mask))
    parts = lax.axis_size(("dp", "seq"))
    gain_tile = jnp.broadcast_to(norm_gain.astype(F32)[None], (8, norm_gain.shape[0]))
    x_cols, dt_rows = xproj_weight.shape[1], dtproj_weight.shape[0]
    pad = -(x_cols + dt_rows) % 16
    w_small = jnp.concatenate([xproj_weight.T, dtproj_weight, jnp.zeros((pad, chan_lanes), BF16)], 0)
    x_inner, z_gate, normalized_rows, w_in, prev_rows, total, gain_rows, w_small = front(
        hidden_in,
        gain_tile,
        count_here,
        jnp.swapaxes(input_projection_weight, 0, 1),
        w_small,
    )
    w_out_rows, z_gate = lax.optimization_barrier((output_projection_weight.T, z_gate))
    w_out = lax.all_gather(w_out_rows, ("dp", "seq"), axis=0, tiled=True)
    total_count = total[0, 0]
    w_x = w_small[:, :x_cols].reshape(parts * x_cols, chan_lanes)
    w_dt = w_small[:, x_cols : x_cols + dt_rows].reshape(parts * dt_rows, chan_lanes)
    share_rows = hidden_in.astype(F32)
    full_gain = gain_rows[0]
    inv_share = lax.rsqrt(jnp.mean(share_rows * share_rows, axis=1, keepdims=True) + EPS)
    seg_float = segment_ids.astype(F32)
    prev_x = prev_rows[8 - back_rows :]
    prev_seg = jnp.where(lax.axis_index("seq") > 0, seg_float[:1], jnp.zeros((back_rows,), F32))
    ext_x = jnp.concatenate([prev_x, x_inner], 0)
    ext_seg = jnp.concatenate([prev_seg, seg_float], 0)
    tap_keeps = []
    conv_sum = jnp.broadcast_to(conv_bias.astype(jnp.float32)[None], (tok_rows, chan_lanes))
    for offset in range(conv_taps):
        keep_tap = (ext_seg[offset : offset + tok_rows] == seg_float).astype(jnp.float32)[:, None]
        tap_keeps.append(keep_tap)
        conv_sum = (
            conv_sum
            + conv_weight[offset].astype(jnp.float32)[None]
            * ext_x[offset : offset + tok_rows]
            * keep_tap
        )
    x_low = jax.nn.silu(conv_sum).astype(jnp.bfloat16)
    x_float = x_low.astype(jnp.float32)
    mixed_rows = lax.psum(jnp.einsum("te,je->tj", x_low, w_x, preferred_element_type=F32), "tensor")
    rank_width = w_dt.shape[0]
    state_width = (mixed_rows.shape[1] - rank_width) // 2
    step_low = mixed_rows[:, :rank_width].astype(jnp.bfloat16)
    b_in = mixed_rows[:, rank_width : rank_width + state_width]
    c_out = mixed_rows[:, rank_width + state_width :]
    pre_act = jnp.dot(step_low, w_dt, preferred_element_type=jnp.float32) + dt_bias[None]
    step_size = jax.nn.softplus(pre_act)
    decay_rates = -jnp.exp(a_log)
    same_doc = (seg_float == ext_seg[back_rows - 1 : back_rows - 1 + tok_rows]).astype(jnp.float32)
    rates = decay_rates * LOG2E
    block = 128
    stepd = jnp.where(same_doc[:, None] != 0, step_size, FAR)
    inject = step_size * x_float
    col_pair = jnp.concatenate([columns(b_in), columns(c_out)], -1)
    b_diag, c_diag = diagonal(b_in), diagonal(c_out)
    resets = jnp.sum((same_doc == 0).astype(jnp.int32).reshape(-1, block), axis=1)
    alive = (jnp.cumsum(resets) - resets == 0).astype(jnp.int32)
    y_local, marks, state_last = fwd(stepd, inject, col_pair, c_diag, rates, tb=block, unroll=2)
    reach = jnp.exp2(rates * jnp.sum(stepd, axis=0)[None])
    state_in = carried(state_last, reach, "seq", 1)
    y_rows, marks = correct(alive, y_local, stepd, c_diag, rates, marks, state_in, tb=block)
    scan_out = y_rows + d_skip[None] * x_float
    gate_act = jax.nn.silu(z_gate)
    gated_output_rows = (scan_out * gate_act).astype(jnp.bfloat16)
    valid_share = lax.dynamic_slice_in_dim(valid_mask, row_start, row_share, 0)
    total_tokens = float(tok_rows * lax.axis_size(("dp", "seq")))
    scale = (total_tokens / total_count * valid_share)[:, None]
    output, grad_out, piece, d_scan, d_z = middle(
        gated_output_rows, w_out, hidden_in, teacher, scale, z_gate, scan_out
    )
    d_wout = jnp.einsum("te,tw->we", gated_output_rows, piece, preferred_element_type=jnp.float32)
    d_skip_part = jnp.sum(d_scan * x_float, axis=0)
    adjoint_first = entry(alive, stepd, d_scan, col_pair, rates, tb=block)
    adjoint_in = carried(adjoint_first, reach, "seq", -1)
    ones = diagonal(jnp.ones((CH, N), F32))
    weighted_b, d_rate, d_b_part, d_c_part, a_log_part = bwd(
        stepd, inject, d_scan, col_pair, b_diag, ones, rates, marks, adjoint_in, tb=block, w=1024
    )
    d_step = LN2 * d_rate + x_float * weighted_b
    a_log_part = LN2 * a_log_part
    d_b_part = jnp.sum(d_b_part, axis=0).reshape(tok_rows, N)
    d_c_part = jnp.sum(d_c_part, axis=0).reshape(tok_rows, N)
    d_xlow = d_skip[None] * d_scan + step_size * weighted_b
    d_pre = d_step * jax.nn.sigmoid(pre_act)
    dt_bias_part = jnp.sum(d_pre, axis=0)
    d_pre_low = d_pre.astype(jnp.bfloat16)
    d_wdt = jnp.einsum("tr,te->re", step_low, d_pre_low, preferred_element_type=jnp.float32)
    d_rank = jnp.einsum("te,re->tr", d_pre_low, w_dt, preferred_element_type=jnp.float32)
    d_mixed = lax.psum(jnp.concatenate([d_rank, d_b_part, d_c_part], 1), "tensor")
    d_mixed_low = d_mixed.astype(jnp.bfloat16)
    d_wx = jnp.einsum("te,tj->ej", x_low, d_mixed_low, preferred_element_type=jnp.float32)
    d_wx_rank = d_wx[:, :rank_width]
    d_wx_state = d_wx[:, rank_width:]
    d_xlow = d_xlow + jnp.dot(d_mixed_low, w_x, preferred_element_type=F32)
    d_conv = d_xlow * silu_slope(conv_sum)
    conv_bias_part = jnp.sum(d_conv, axis=0)
    conv_weight_rows = []
    for offset in range(conv_taps):
        conv_weight_rows.append(
            jnp.sum(d_conv * ext_x[offset : offset + tok_rows] * tap_keeps[offset], axis=0)
        )
    conv_weight_part = jnp.stack(conv_weight_rows, 0)
    conv_padded = jnp.concatenate([d_conv, jnp.zeros((back_rows, chan_lanes), jnp.float32)], 0)
    d_x = jnp.zeros((tok_rows, chan_lanes), jnp.float32)
    for offset in range(conv_taps):
        lead = back_rows - offset
        keep_padded = jnp.concatenate(
            [tap_keeps[offset], jnp.zeros((back_rows, 1), jnp.float32)], 0
        )
        d_x = (
            d_x
            + conv_weight[offset].astype(jnp.float32)[None]
            * conv_padded[lead : lead + tok_rows]
            * keep_padded[lead : lead + tok_rows]
        )
    front_rows = []
    for place in range(back_rows):
        front_total = jnp.zeros((chan_lanes,), jnp.float32)
        for offset in range(place + 1):
            front_total = (
                front_total
                + conv_weight[offset].astype(jnp.float32)
                * d_conv[place - offset]
                * tap_keeps[offset][place - offset, 0]
            )
        front_rows.append(front_total)
    front_grad = jnp.stack(front_rows, 0)
    carried_grad = passed_along(front_grad, "seq", -1)
    d_x = d_x.at[tok_rows - back_rows :].add(carried_grad)
    small = jnp.concatenate(
        [
            d_wx_rank.T.reshape(parts, -1, chan_lanes),
            d_wx_state.T.reshape(parts, -1, chan_lanes),
            d_wdt.reshape(parts, -1, chan_lanes),
            jnp.zeros((parts, 4, chan_lanes), F32),
        ],
        1,
    )
    whole = jnp.concatenate(
        [a_log_part, conv_weight_part, jnp.stack([conv_bias_part, dt_bias_part, d_skip_part, d_skip_part], 0)], 0
    )
    d_norm_share, g_in, g_small, g_whole = tail(d_x.astype(BF16), d_z, w_in, normalized_rows, small, whole)
    g_in = jnp.swapaxes(g_in, 0, 1)
    inner_sum = jnp.sum(d_norm_share * full_gain[None] * share_rows, axis=1, keepdims=True)
    inv_cube = inv_share * inv_share * inv_share
    input_grad = (
        grad_out
        + inv_share * full_gain[None] * d_norm_share
        - share_rows * inv_cube * inner_sum / model_width
    )
    rank_here = rank_width // parts
    state_here = 2 * state_width // parts
    g_x_rank = g_small[:rank_here].T
    g_x_state = g_small[rank_here : rank_here + state_here].T
    g_dt = g_small[rank_here + state_here : rank_here + state_here + rank_here]
    g_out = lax.psum_scatter(d_wout.astype(BF16), ("dp", "seq"), scatter_dimension=0, tiled=True).astype(F32).T
    g_gain = jnp.sum(g_whole[N + conv_taps + 4 :, : norm_gain.shape[0]], axis=0) / norm_gain.astype(F32)
    g_alog, g_conv_w = g_whole[:N], g_whole[N : N + conv_taps]
    g_conv_b, g_bias, g_skip = g_whole[N + conv_taps], g_whole[N + conv_taps + 1], g_whole[N + conv_taps + 2]
    return (
        output,
        input_grad,
        g_gain,
        g_in,
        g_conv_w,
        g_conv_b,
        g_x_rank,
        g_x_state,
        g_dt,
        g_bias,
        g_alog,
        g_skip,
        g_out,
    )


def solution(mesh):
    placed = (
        P(("dp", "seq", "tensor"), None),
        P(("dp", "seq", "tensor"), None),
        P(("dp", "seq")),
        P("tensor"),
        P(("dp", "seq"), None, "tensor"),
        P(None, "tensor"),
        P("tensor"),
        P("tensor", ("dp", "seq")),
        P(("dp", "seq"), "tensor"),
        P("tensor"),
        P(None, "tensor"),
        P("tensor"),
        P("tensor", ("dp", "seq")),
    )
    return jax.shard_map(
        on_device,
        mesh=mesh,
        in_specs=placed,
        out_specs=(
            P(("dp", "seq", "tensor"), None),
            P(("dp", "seq", "tensor"), None),
            P("tensor"),
            P(("dp", "seq"), None, "tensor"),
            P(None, "tensor"),
            P("tensor"),
            P("tensor", ("dp", "seq")),
            P("tensor", ("dp", "seq")),
            P(("dp", "seq"), "tensor"),
            P("tensor"),
            P(None, "tensor"),
            P("tensor"),
            P("tensor", ("dp", "seq")),
        ),
        check_vma=False,
    )
```

```python
import functools

import jax
import jax.numpy as jnp
from jax import lax
from jax.experimental import pallas as pl
from jax.experimental.pallas import tpu as pltpu
from jax.sharding import PartitionSpec as P

EPS = 1e-05
LOG2E = 1.4426950408889634
LN2 = 0.6931471805599453
FAR = 1e30
SMALL_ROWS = 24
MESH = pl.DeviceIdType.MESH


def passed_along(x, axis, by):
    size = lax.axis_size(axis)
    pairs = [(i, i + by) for i in range(size) if 0 <= i + by < size]
    return lax.ppermute(x, axis, pairs)


def silu_slope(values):
    logistic = jax.nn.sigmoid(values)
    return logistic * (1.0 + values * (1.0 - logistic))


F32, BF16 = jnp.float32, jnp.bfloat16
N = 16
CH = 16

def fwd_kernel(stepd_ref, u_ref, bc_ref, cdiag_ref, rate_ref, y_ref, ckpt_ref, last_ref, state_ref, sbf_ref, *, unroll):
    @pl.when(pl.program_id(1) == 0)
    def _():
        state_ref[...] = jnp.zeros_like(state_ref)
    ckpt_ref[0] = state_ref[...]
    rate = rate_ref[...]
    tb = stepd_ref.shape[0]

    def chunk(c, s):
        base = pl.multiple_of(c * CH, CH)
        bc = bc_ref[c]
        for k in range(CH):
            dec = jnp.exp2(rate * stepd_ref[pl.ds(base + k, 1), :])
            s = dec * s + bc[:, k:k + 1] * u_ref[pl.ds(base + k, 1), :]
            sbf_ref[k * N:(k + 1) * N, :] = s.astype(BF16)
        y_ref[pl.ds(base, CH), :] = jnp.dot(cdiag_ref[pl.ds(base, CH), :], sbf_ref[...], preferred_element_type=F32)
        return s

    s = lax.fori_loop(0, tb // CH, chunk, state_ref[...], unroll=unroll)
    state_ref[...] = s
    last_ref[...] = s

def fwd(stepd, u, bc, cdiag, rate, tb=128, w=512, unroll=1):
    t, c = stepd.shape
    w = min(w, c)
    grid = (c // w, t // tb)
    return pl.pallas_call(
        functools.partial(fwd_kernel, unroll=unroll),
        grid=grid,
        in_specs=[
            pl.BlockSpec((tb, w), lambda j, i: (i, j)),
            pl.BlockSpec((tb, w), lambda j, i: (i, j)),
            pl.BlockSpec((tb // CH, N, 2 * CH), lambda j, i: (i, 0, 0)),
            pl.BlockSpec((tb, CH * N), lambda j, i: (i, 0)),
            pl.BlockSpec((N, w), lambda j, i: (0, j)),
        ],
        out_specs=[
            pl.BlockSpec((tb, w), lambda j, i: (i, j)),
            pl.BlockSpec((1, N, w), lambda j, i: (i, 0, j)),
            pl.BlockSpec((N, w), lambda j, i: (0, j)),
        ],
        out_shape=[
            jax.ShapeDtypeStruct((t, c), F32),
            jax.ShapeDtypeStruct((t // tb, N, c), F32),
            jax.ShapeDtypeStruct((N, c), F32),
        ],
        scratch_shapes=[pltpu.VMEM((N, w), F32), pltpu.VMEM((CH * N, w), BF16)],
        compiler_params=pltpu.CompilerParams(vmem_limit_bytes=48 << 20),
        name="scan_forward",
    )(stepd, u, bc, cdiag, rate)

def bwd_kernel(stepd_ref, u_ref, ds_ref, bc_ref, bdiag_ref, ones_ref, rate_ref, ckpt_ref, gin_ref,
               wb_ref, dn_ref, db_ref, dc_ref, acc_ref, g_ref, sbf_ref, abf_ref, rbf_ref, pb_ref, pc_ref, *, unroll):
    @pl.when(pl.program_id(1) == 0)
    def _():
        g_ref[...] = gin_ref[...]
        acc_ref[...] = jnp.zeros_like(acc_ref)
    rate = rate_ref[...]
    tb = stepd_ref.shape[0]
    nc = tb // CH
    def fold(v):
        p = v[:, 0:128]
        for q in range(1, v.shape[1] // 128):
            p = p + v[:, q * 128:(q + 1) * 128]
        return p
    row = lax.broadcasted_iota(jnp.int32, (CH, CH * N), 0)
    lane = lax.broadcasted_iota(jnp.int32, (CH, CH * N), 1)
    diag = (row == lane // N).astype(F32)
    sbf_ref[0:N, :] = ckpt_ref[0].astype(BF16)
    nt = (((1,), (1,)), ((), ()))
    lanes = jnp.ones((8, 128), BF16)

    def forward(c, s):
        base = pl.multiple_of(c * CH, CH)
        bc = bc_ref[c]
        for k in range(CH):
            dec = jnp.exp2(rate * stepd_ref[pl.ds(base + k, 1), :])
            s = dec * s + bc[:, k:k + 1] * u_ref[pl.ds(base + k, 1), :]
            sbf_ref[pl.ds(pl.multiple_of((base + k + 1) * N, N), N), :] = s.astype(BF16)
            pc_ref[k * N:(k + 1) * N, :] = fold(s * ds_ref[pl.ds(base + k, 1), :])
        dc = lax.dot_general(lanes, pc_ref[...].astype(BF16), nt, preferred_element_type=F32)
        dc_ref[0, pl.ds(c, 1), :] = dc[0:1]
        return s

    lax.fori_loop(0, nc, forward, ckpt_ref[0], unroll=unroll)

    def backward(c, carry):
        g, acc = carry
        c = nc - 1 - c
        base = pl.multiple_of(c * CH, CH)
        bc = bc_ref[c]
        for k in range(CH - 1, -1, -1):
            sd = stepd_ref[pl.ds(base + k, 1), :]
            adj = g + bc[:, CH + k:CH + k + 1] * ds_ref[pl.ds(base + k, 1), :]
            abf_ref[k * N:(k + 1) * N, :] = adj.astype(BF16)
            pb_ref[k * N:(k + 1) * N, :] = fold(adj * u_ref[pl.ds(base + k, 1), :])
            g = jnp.exp2(rate * sd) * adj
            before = sbf_ref[pl.ds(pl.multiple_of((base + k) * N, N), N), :].astype(F32)
            r = g * before * rate
            rbf_ref[k * N:(k + 1) * N, :] = r.astype(BF16)
            acc = acc + r * sd
        wb_ref[pl.ds(base, CH), :] = jnp.dot(bdiag_ref[pl.ds(base, CH), :], abf_ref[...], preferred_element_type=F32)
        dn_ref[pl.ds(base, CH), :] = jnp.dot(ones_ref[...], rbf_ref[...], preferred_element_type=F32)
        db = lax.dot_general(lanes, pb_ref[...].astype(BF16), nt, preferred_element_type=F32)
        db_ref[0, pl.ds(c, 1), :] = db[0:1]
        return g, acc

    g, acc = lax.fori_loop(0, nc, backward, (g_ref[...], acc_ref[...]), unroll=unroll)
    g_ref[...] = g
    acc_ref[...] = acc

def bwd(stepd, u, ds, bc, bdiag, ones, rate, ckpt, gin, tb=128, w=512, unroll=1):
    t, c = stepd.shape
    w = min(w, c)
    nb = t // tb
    grid = (c // w, nb)
    rows = pl.BlockSpec((tb, w), lambda j, i: (nb - 1 - i, j))
    return pl.pallas_call(
        functools.partial(bwd_kernel, unroll=unroll),
        grid=grid,
        in_specs=[
            rows, rows, rows,
            pl.BlockSpec((tb // CH, N, 2 * CH), lambda j, i: (nb - 1 - i, 0, 0)),
            pl.BlockSpec((tb, CH * N), lambda j, i: (nb - 1 - i, 0)),
            pl.BlockSpec((CH, CH * N), lambda j, i: (0, 0)),
            pl.BlockSpec((N, w), lambda j, i: (0, j)),
            pl.BlockSpec((1, N, w), lambda j, i: (nb - 1 - i, 0, j)),
            pl.BlockSpec((N, w), lambda j, i: (0, j)),
        ],
        out_specs=[
            rows, rows,
            pl.BlockSpec((1, tb // CH, CH * N), lambda j, i: (j, nb - 1 - i, 0)),
            pl.BlockSpec((1, tb // CH, CH * N), lambda j, i: (j, nb - 1 - i, 0)),
            pl.BlockSpec((N, w), lambda j, i: (0, j)),
        ],
        out_shape=[
            jax.ShapeDtypeStruct((t, c), F32),
            jax.ShapeDtypeStruct((t, c), F32),
            jax.ShapeDtypeStruct((c // w, t // CH, CH * N), F32),
            jax.ShapeDtypeStruct((c // w, t // CH, CH * N), F32),
            jax.ShapeDtypeStruct((N, c), F32),
        ],
        scratch_shapes=[pltpu.VMEM((N, w), F32), pltpu.VMEM(((tb + 1) * N, w), BF16),
                        pltpu.VMEM((CH * N, w), BF16), pltpu.VMEM((CH * N, w), BF16), pltpu.VMEM((CH * N, 128), F32), pltpu.VMEM((CH * N, 128), F32)],
        compiler_params=pltpu.CompilerParams(vmem_limit_bytes=48 << 20),
        name="scan_backward",
    )(stepd, u, ds, bc, bdiag, ones, rate, ckpt, gin)


def correct_kernel(alive_ref, y_ref, stepd_ref, cdiag_ref, rate_ref, ckpt_ref, sin_ref, yo_ref, ckpto_ref, state_ref, sbf_ref):
    i = pl.program_id(1)

    @pl.when(i == 0)
    def _():
        state_ref[...] = sin_ref[...]

    alive = alive_ref[i] != 0

    @pl.when(alive)
    def _():
        rate = rate_ref[...]
        ckpto_ref[0] = ckpt_ref[0] + state_ref[...]

        def chunk(c, s):
            base = pl.multiple_of(c * CH, CH)
            for k in range(CH):
                s = jnp.exp2(rate * stepd_ref[pl.ds(base + k, 1), :]) * s
                sbf_ref[k * N:(k + 1) * N, :] = s.astype(BF16)
            yo_ref[pl.ds(base, CH), :] = y_ref[pl.ds(base, CH), :] + jnp.dot(
                cdiag_ref[pl.ds(base, CH), :], sbf_ref[...], preferred_element_type=F32
            )
            return s

        state_ref[...] = lax.fori_loop(0, y_ref.shape[0] // CH, chunk, state_ref[...], unroll=8)

    @pl.when(jnp.logical_not(alive))
    def _():
        yo_ref[...] = y_ref[...]
        ckpto_ref[...] = ckpt_ref[...]


def correct(alive, y, stepd, cdiag, rate, ckpt, state_in, tb=128, w=512):
    t, c = stepd.shape
    w = min(w, c)
    rows = pl.BlockSpec((tb, w), lambda j, i, _: (i, j))
    lanes = pl.BlockSpec((N, w), lambda j, i, _: (0, j))
    marks = pl.BlockSpec((1, N, w), lambda j, i, _: (i, 0, j))
    return pl.pallas_call(
        correct_kernel,
        grid_spec=pltpu.PrefetchScalarGridSpec(
            num_scalar_prefetch=1,
            grid=(c // w, t // tb),
            in_specs=[rows, rows, pl.BlockSpec((tb, CH * N), lambda j, i, _: (i, 0)), lanes, marks, lanes],
            out_specs=[rows, marks],
            scratch_shapes=[pltpu.VMEM((N, w), F32), pltpu.VMEM((CH * N, w), BF16)],
        ),
        out_shape=[jax.ShapeDtypeStruct((t, c), F32), jax.ShapeDtypeStruct(ckpt.shape, F32)],
        compiler_params=pltpu.CompilerParams(vmem_limit_bytes=48 << 20),
        name="scan_correct",
    )(alive, y, stepd, cdiag, rate, ckpt, state_in)


def entry_kernel(alive_ref, stepd_ref, ds_ref, bc_ref, rate_ref, g_ref):
    i = pl.program_id(1)

    @pl.when(i == 0)
    def _():
        g_ref[...] = jnp.zeros_like(g_ref)

    @pl.when(alive_ref[pl.num_programs(1) - 1 - i] != 0)
    def _():
        rate = rate_ref[...]
        nc = stepd_ref.shape[0] // CH

        def chunk(c, g):
            c = nc - 1 - c
            base = pl.multiple_of(c * CH, CH)
            bc = bc_ref[c]
            for k in range(CH - 1, -1, -1):
                adj = g + bc[:, CH + k:CH + k + 1] * ds_ref[pl.ds(base + k, 1), :]
                g = jnp.exp2(rate * stepd_ref[pl.ds(base + k, 1), :]) * adj
            return g

        g_ref[...] = lax.fori_loop(0, nc, chunk, g_ref[...], unroll=8)


def entry(alive, stepd, ds, bc, rate, tb=128, w=512):
    t, c = stepd.shape
    w = min(w, c)
    nb = t // tb
    rows = pl.BlockSpec((tb, w), lambda j, i, _: (nb - 1 - i, j))
    lanes = pl.BlockSpec((N, w), lambda j, i, _: (0, j))
    return pl.pallas_call(
        entry_kernel,
        grid_spec=pltpu.PrefetchScalarGridSpec(
            num_scalar_prefetch=1,
            grid=(c // w, nb),
            in_specs=[rows, rows, pl.BlockSpec((tb // CH, N, 2 * CH), lambda j, i, _: (nb - 1 - i, 0, 0)), lanes],
            out_specs=lanes,
        ),
        out_shape=jax.ShapeDtypeStruct((N, c), F32),
        compiler_params=pltpu.CompilerParams(vmem_limit_bytes=48 << 20),
        name="scan_entry",
    )(alive, stepd, ds, bc, rate)


def carried(local, reach, axis, by):
    found = jnp.zeros_like(local)
    for _ in range(lax.axis_size(axis) - 1):
        found = passed_along(local + reach * found, axis, by)
    return found


def columns(values):
    tokens = values.shape[0]
    return values.reshape(tokens // CH, CH, N).transpose(0, 2, 1)


def diagonal(values):
    tokens = values.shape[0]
    mine = jnp.arange(CH * N)[None] // N == jnp.arange(tokens)[:, None] % CH
    return jnp.where(mine, jnp.tile(values.astype(BF16), (1, CH)), 0)


def mesh_copy(src, dst, send, recv, **where):
    return pltpu.make_async_remote_copy(
        src_ref=src, dst_ref=dst, send_sem=send, recv_sem=recv, device_id=where, device_id_type=MESH
    )


def place():
    dp, seq, mine = lax.axis_index("dp"), lax.axis_index("seq"), lax.axis_index("tensor")
    return dp, seq, mine


def tail_kernel(n, dps, seqs, subs, lag, dx_ref, dz_ref, w_ref, nrm_ref, sm_ref, all_ref,
                dn_ref, gin_ref, gs_ref, ga_ref,
                gacc, gsend, grecv, all_mine,
                zr, zl, part_r, part_l, one_send, one_recv, two_recv, sm_one, sm_two, all_one, all_two,
                r_send, r_recv, l_send, l_recv, w1s, w1r, w2s, w2r, s1s, s1r, s2s, s2r, a1s, a1r, a2s, a2r, gs, gr):
    dp, seq, t = place()
    core, hi = dp % 2, dp // 2
    chips = dps // 2 * seqs
    chip = hi * seqs + seq
    rows = dn_ref.shape[0]
    part = rows // subs
    wide = dn_ref.shape[1]
    wrows = gin_ref.shape[1]
    tile = 512

    def owner(q, c):
        return (q // seqs * 2 + c) * seqs + q % seqs

    def to_chip(q):
        return dict(dp=q // seqs * 2 + core, seq=q % seqs)

    barrier = pltpu.get_barrier_semaphore()
    pl.semaphore_signal(barrier, inc=1, device_id=dict(dp=hi * 2 + 1 - core), device_id_type=MESH)
    for step in range(1, chips):
        q = lax.rem(chip + step, chips)
        pl.semaphore_signal(barrier, inc=1, device_id=to_chip(q), device_id_type=MESH)

    for ahead in range(1, n):
        pl.semaphore_signal(barrier, inc=1, device_id=dict(tensor=lax.rem(t + ahead, n)), device_id_type=MESH)
    pl.semaphore_wait(barrier, chips + n - 1)
    gacc[...] = jnp.zeros_like(gacc)

    partner = dict(dp=hi * 2 + 1 - core)
    right, left = dict(tensor=lax.rem(t + 1, n)), dict(tensor=lax.rem(t + n - 1, n))

    def r_copy(i):
        return mesh_copy(zr.at[i], zr.at[i], r_send.at[i], r_recv.at[i], **right)

    def l_copy(i):
        return mesh_copy(zl.at[i], zl.at[i], l_send.at[i], l_recv.at[i], **left)

    def w1_copy(q):
        return mesh_copy(one_send.at[q], one_recv.at[q], w1s.at[q], w1r.at[q], **partner)

    def w2_copy(q, slot):
        return mesh_copy(one_recv.at[q], two_recv.at[slot], w2s.at[q], w2r.at[slot], **to_chip(q))

    def s1_copy(q):
        return mesh_copy(sm_ref.at[owner(q, 1 - core)], sm_one.at[q], s1s.at[q], s1r.at[q], **partner)

    def s2_copy(q, slot):
        return mesh_copy(sm_one.at[q], sm_two.at[slot], s2s.at[q], s2r.at[slot], **to_chip(q))

    def a1_copy():
        return mesh_copy(all_mine, all_one, a1s, a1r, **partner)

    def a2_copy(q, slot):
        return mesh_copy(all_one, all_two.at[slot], a2s.at[q], a2r.at[slot], **to_chip(q))

    def g_copy(p, slot):
        return mesh_copy(gsend.at[p], grecv.at[slot], gs.at[p], gr.at[slot], tensor=p)

    def partial_rows(o, dst):
        here = pl.ds(pl.multiple_of(o * rows, rows), rows)

        @pl.loop(0, wide // tile)
        def _(j):
            cols = pl.ds(pl.multiple_of(j * tile, tile), tile)
            nt = (((1,), (1,)), ((), ()))
            block = lax.dot_general(
                dx_ref[here, :], w_ref[0, cols, :], nt, preferred_element_type=F32
            ) + lax.dot_general(dz_ref[here, :], w_ref[1, cols, :], nt, preferred_element_type=F32)
            dst[:, cols] = block
            scaled = block * nrm_ref[here, cols].astype(F32)
            gacc[:, cols] = gacc[:, cols] + jnp.sum(scaled.reshape(rows // 8, 8, tile), axis=0)

    def weight_rows(p, k):
        cols = pl.ds(pl.multiple_of(p * wrows, wrows), wrows)
        tn = (((0,), (0,)), ((), ()))
        d_ref = dx_ref if k == 0 else dz_ref
        return lax.dot_general(nrm_ref[:, cols], d_ref[...], tn, preferred_element_type=F32)

    for q in range(chips):
        s1_copy(q).start()

    def stream(i, limit, start, buf, copy, part_ref, owner_of):
        @pl.when(jnp.logical_and(i >= 0, i < limit))
        def _():
            k, sub = i // subs, i % subs

            @pl.when(sub == 0)
            def _():
                partial_rows(owner_of(k), part_ref)

            @pl.when(jnp.logical_and(start, sub == 0))
            def _():
                @pl.loop(0, subs)
                def _(j):
                    here = part_ref[pl.ds(pl.multiple_of(j * part, part), part), :]
                    buf[k * subs + j] = here.astype(BF16)
                    copy(k * subs + j).start()

            @pl.when(jnp.logical_not(start))
            def _():
                here = part_ref[pl.ds(pl.multiple_of(sub * part, part), part), :]
                copy(i).wait_recv()
                buf[i] = (here + buf[i].astype(F32)).astype(BF16)
                copy(i).start()

    def step(g, _):
        stream(g - lag * t, (n - 1 - t) * subs, t == 0, zr, r_copy, part_r, lambda k: n - 1 - k)
        stream(g - lag * (n - 1 - t), t * subs, t == n - 1, zl, l_copy, part_l, lambda k: k)

        @pl.when(g < chips)
        def _():
            for k in range(2):
                one_send[g, k] = weight_rows(owner(g, 1 - core), k).astype(BF16)
            w1_copy(g).start()

        @pl.when(jnp.logical_and(g >= chips, g < 2 * chips - 1))
        def _():
            q = lax.rem(chip + 1 + g - chips, chips)
            w1_copy(q).wait_recv()
            for k in range(2):
                one_recv[q, k] = (weight_rows(owner(q, core), k) + one_recv[q, k].astype(F32)).astype(BF16)
            w2_copy(q, chip).start()

        @pl.when(g == 2 * chips - 1)
        def _():
            for q in range(chips):
                s1_copy(q).wait_recv()
                sm_one[q] = sm_one[q] + sm_ref[owner(q, core)]
            for ahead in range(1, chips):
                q = lax.rem(chip + ahead, chips)
                s2_copy(q, chip).start()
            w1_copy(chip).wait_recv()
            for k in range(2):
                gin_ref[k] = weight_rows(owner(chip, core), k) + one_recv[chip, k].astype(F32)

        @pl.when(g == 2 * chips)
        def _():
            partial_rows(t, dn_ref)

        return 0

    steps = max((n - 1) * max(subs, lag), 2 * chips + 1)
    lax.fori_loop(0, steps, step, 0)

    share = wide // n
    for p in range(n):
        gsend[p] = gacc[:, p * share:(p + 1) * share]
    for ahead in range(1, n):
        g_copy(lax.rem(t + ahead, n), t).start()

    @pl.loop(0, subs)
    def _(s):
        here = pl.ds(pl.multiple_of(s * part, part), part)

        @pl.when(t > 0)
        def _():
            i = (n - 1 - t) * subs + s
            r_copy(i).wait_recv()
            dn_ref[here, :] = dn_ref[here, :] + zr[i].astype(F32)

        @pl.when(t < n - 1)
        def _():
            i = t * subs + s
            l_copy(i).wait_recv()
            dn_ref[here, :] = dn_ref[here, :] + zl[i].astype(F32)

    plain = all_ref.shape[0]
    all_mine[0:plain, :] = all_ref[...]
    all_mine[plain:, :] = jnp.zeros((8, all_mine.shape[1]), F32)
    all_mine[plain:, 0:share] = gsend[t]
    for ahead in range(1, n):
        p = lax.rem(t + ahead, n)
        g_copy(p, p).wait_recv()
        all_mine[plain:, 0:share] = all_mine[plain:, 0:share] + grecv[p]
    a1_copy().start()
    gs_ref[...] = sm_one[chip]
    for ahead in range(1, chips):
        q = lax.rem(chip + ahead, chips)
        s2_copy(q, q).wait_recv()
        gs_ref[...] = gs_ref[...] + sm_two[q]
    a1_copy().wait_recv()
    all_one[...] = all_one[...] + all_mine[...]
    for ahead in range(1, chips):
        a2_copy(lax.rem(chip + ahead, chips), chip).start()
    ga_ref[...] = all_one[...]
    for ahead in range(1, chips):
        q = lax.rem(chip + ahead, chips)
        w2_copy(q, q).wait_recv()
        gin_ref[...] = gin_ref[...] + two_recv[q].astype(F32)
    for ahead in range(1, chips):
        q = lax.rem(chip + ahead, chips)
        a2_copy(q, q).wait_recv()
        ga_ref[...] = ga_ref[...] + all_two[q]

    for q in range(chips):
        s1_copy(q).wait_send()
        w1_copy(q).wait_send()
    a1_copy().wait_send()
    for ahead in range(1, n):
        g_copy(lax.rem(t + ahead, n), t).wait_send()
    for ahead in range(1, chips):
        q = lax.rem(chip + ahead, chips)
        s2_copy(q, chip).wait_send()
        a2_copy(q, chip).wait_send()
        w2_copy(q, chip).wait_send()

    @pl.loop(0, (n - 1) * subs)
    def _(i):
        @pl.when(i < (n - 1 - t) * subs)
        def _():
            r_copy(i).wait_send()

        @pl.when(i < t * subs)
        def _():
            l_copy(i).wait_send()


def tail(dx, dz, w_full, normed, small, whole):
    n, dps, seqs = (lax.axis_size(axis) for axis in ("tensor", "dp", "seq"))
    chips = dps // 2 * seqs
    rows = dx.shape[0] // n
    wide, lanes = w_full.shape[1], w_full.shape[2]
    wrows = wide // (dps * seqs)
    subs = max(1, rows // 32)
    hops = (n - 1) * subs
    vmem = pl.BlockSpec(memory_space=pltpu.VMEM)
    dma = pltpu.SemaphoreType.DMA
    few = dma((chips,))
    return pl.pallas_call(
        functools.partial(tail_kernel, n, dps, seqs, subs, 2),
        out_shape=[
            jax.ShapeDtypeStruct((rows, wide), F32),
            jax.ShapeDtypeStruct((2, wrows, lanes), F32),
            jax.ShapeDtypeStruct(small.shape[1:], F32),
            jax.ShapeDtypeStruct((whole.shape[0] + 8, lanes), F32),
        ],
        in_specs=[vmem] * 6,
        out_specs=[vmem] * 4,
        scratch_shapes=[
            pltpu.VMEM((8, wide), F32),
            pltpu.VMEM((n, 8, wide // n), F32),
            pltpu.VMEM((n, 8, wide // n), F32),
            pltpu.VMEM((whole.shape[0] + 8, lanes), F32),
            pltpu.VMEM((hops, rows // subs, wide), BF16),
            pltpu.VMEM((hops, rows // subs, wide), BF16),
            pltpu.VMEM((rows, wide), F32),
            pltpu.VMEM((rows, wide), F32),
            pltpu.VMEM((chips, 2, wrows, lanes), BF16),
            pltpu.VMEM((chips, 2, wrows, lanes), BF16),
            pltpu.VMEM((chips, 2, wrows, lanes), BF16),
            pltpu.VMEM((chips,) + small.shape[1:], F32),
            pltpu.VMEM((chips,) + small.shape[1:], F32),
            pltpu.VMEM((whole.shape[0] + 8, lanes), F32),
            pltpu.VMEM((chips, whole.shape[0] + 8, lanes), F32),
            dma((hops,)), dma((hops,)), dma((hops,)), dma((hops,)),
            few, few, few, few, few, few, few, few, dma, dma, few, few, dma((n,)), dma((n,)),
        ],
        compiler_params=pltpu.CompilerParams(
            collective_id=2, has_side_effects=True, vmem_limit_bytes=60 << 20
        ),
        name="tail_sums",
    )(dx, dz, w_full, normed, small, whole)


def mid_kernel(n, subs, lag, gated_ref, w_ref, hid_ref, tea_ref, scale_ref, z_ref, scan_ref,
               out_ref, go_ref, piece_ref, dscan_ref, dz_ref,
               zr, zl, part_r, part_l, r_send, r_recv, l_send, l_recv, ar_send, ar_recv, al_send, al_recv):
    t = lax.axis_index("tensor")
    rows, wide = hid_ref.shape
    part = rows // subs
    tile = 512
    right, left = dict(tensor=lax.rem(t + 1, n)), dict(tensor=lax.rem(t + n - 1, n))

    barrier = pltpu.get_barrier_semaphore()
    for peer in (right, left):
        pl.semaphore_signal(barrier, inc=1, device_id=peer, device_id_type=MESH)
    pl.semaphore_wait(barrier, 2)

    def r_copy(i):
        return mesh_copy(zr.at[i], zr.at[i], r_send.at[i], r_recv.at[i], **right)

    def l_copy(i):
        return mesh_copy(zl.at[i], zl.at[i], l_send.at[i], l_recv.at[i], **left)

    def at(o, s):
        return pl.ds(pl.multiple_of(o * rows + s * part, part), part)

    def ar_copy(o, s):
        ref = piece_ref.at[at(o, s), :]
        return mesh_copy(ref, ref, ar_send.at[o * subs + s], ar_recv.at[o * subs + s], **right)

    def al_copy(o, s):
        ref = piece_ref.at[at(o, s), :]
        return mesh_copy(ref, ref, al_send.at[o * subs + s], al_recv.at[o * subs + s], **left)

    def partial_rows(o, dst):
        here = pl.ds(pl.multiple_of(o * rows, rows), rows)

        @pl.loop(0, wide // tile)
        def _(j):
            cols = pl.ds(pl.multiple_of(j * tile, tile), tile)
            nt = (((1,), (1,)), ((), ()))
            dst[:, cols] = lax.dot_general(gated_ref[here, :], w_ref[cols, :], nt, preferred_element_type=F32)

    def backward_rows(o):
        here = pl.ds(pl.multiple_of(o * rows, rows), rows)
        d_gated = jnp.dot(piece_ref[here, :], w_ref[...], preferred_element_type=F32)
        z = z_ref[here, :]
        s = 1.0 / (1.0 + jnp.exp(-z))
        dscan_ref[here, :] = d_gated * (z * s)
        dz_ref[here, :] = (d_gated * scan_ref[here, :] * (s * (1.0 + z * (1.0 - s)))).astype(BF16)

    def stream(i, limit, start, buf, copy, part_ref, owner_of):
        @pl.when(jnp.logical_and(i >= 0, i < limit))
        def _():
            k, sub = i // subs, i % subs

            @pl.when(sub == 0)
            def _():
                partial_rows(owner_of(k), part_ref)

            @pl.when(jnp.logical_and(start, sub == 0))
            def _():
                @pl.loop(0, subs)
                def _(j):
                    here = part_ref[pl.ds(pl.multiple_of(j * part, part), part), :]
                    buf[k * subs + j] = here.astype(BF16)
                    copy(k * subs + j).start()

            @pl.when(jnp.logical_not(start))
            def _():
                here = part_ref[pl.ds(pl.multiple_of(sub * part, part), part), :]
                copy(i).wait_recv()
                buf[i] = (here + buf[i].astype(F32)).astype(BF16)
                copy(i).start()

    def ready(o):
        from_left = jnp.where(o > 0, lag * o + (n - 1 - o) * subs, 0)
        from_right = jnp.where(o < n - 1, lag * (n - 1 - o) + o * subs, 0)
        return jnp.maximum(from_left, from_right)

    gap = max(subs, lag)
    base = lag + (n - 2) * subs if subs >= lag else (n - 1) * lag

    def turn(d, o):
        inner = base + (d - o) * gap
        inner = jnp.where(d == 0, (n - 1) * gap, inner)
        return jnp.where(d == n - 1, base + (n - 2 - o) * gap + lag, inner)

    def finish(s):
        here = pl.ds(pl.multiple_of(s * part, part), part)

        @pl.when(s == 0)
        def _():
            partial_rows(t, go_ref)

        @pl.when(t > 0)
        def _():
            i = (n - 1 - t) * subs + s
            r_copy(i).wait_recv()
            go_ref[here, :] = go_ref[here, :] + zr[i].astype(F32)

        @pl.when(t < n - 1)
        def _():
            i = t * subs + s
            l_copy(i).wait_recv()
            go_ref[here, :] = go_ref[here, :] + zl[i].astype(F32)

        result = hid_ref[here, :].astype(F32) + go_ref[here, :]
        out_ref[here, :] = result.astype(BF16)
        grad = scale_ref[here, :] * (result - tea_ref[here, :].astype(F32))
        go_ref[here, :] = grad
        piece_ref[at(t, s), :] = grad.astype(BF16)

    def step(g, _):
        stream(g - lag * t, (n - 1 - t) * subs, t == 0, zr, r_copy, part_r, lambda k: n - 1 - k)
        stream(g - lag * (n - 1 - t), t * subs, t == n - 1, zl, l_copy, part_l, lambda k: k)

        @pl.loop(0, n)
        def _(o):
            s_own = g - ready(t)
            s_right = g - turn(t, o)
            s_left = g - turn(n - 1 - t, n - 1 - o)

            @pl.when(jnp.logical_and(o == t, jnp.logical_and(s_own >= 0, s_own < subs)))
            def _():
                finish(s_own)

            @pl.when(jnp.logical_and(o <= t, jnp.logical_and(s_right >= 0, s_right < subs)))
            def _():
                @pl.when(o < t)
                def _():
                    ar_copy(o, s_right).wait_recv()

                @pl.when(t < n - 1)
                def _():
                    ar_copy(o, s_right).start()

            @pl.when(jnp.logical_and(o >= t, jnp.logical_and(s_left >= 0, s_left < subs)))
            def _():
                @pl.when(o > t)
                def _():
                    al_copy(o, s_left).wait_recv()

                @pl.when(t > 0)
                def _():
                    al_copy(o, s_left).start()

            s_done = jnp.where(o == t, s_own, jnp.where(o < t, s_right, s_left))

            @pl.when(s_done == subs - 1)
            def _():
                backward_rows(o)

        return 0

    steps = base + (n - 1) * gap + subs + lag
    lax.fori_loop(0, steps, step, 0)

    @pl.loop(0, (n - 1) * subs)
    def _(i):
        @pl.when(i < (n - 1 - t) * subs)
        def _():
            r_copy(i).wait_send()

        @pl.when(i < t * subs)
        def _():
            l_copy(i).wait_send()

    @pl.loop(0, n * subs)
    def _(i):
        o, s = i // subs, i % subs

        @pl.when(jnp.logical_and(o <= t, t < n - 1))
        def _():
            ar_copy(o, s).wait_send()

        @pl.when(jnp.logical_and(o >= t, t > 0))
        def _():
            al_copy(o, s).wait_send()


def middle(gated, w_out, hidden, teacher, scale, z_gate, scan_out):
    n = lax.axis_size("tensor")
    rows, wide = hidden.shape
    tokens, lanes = gated.shape
    subs = max(1, rows // 32)
    hops = (n - 1) * subs
    vmem = pl.BlockSpec(memory_space=pltpu.VMEM)
    dma = pltpu.SemaphoreType.DMA
    return pl.pallas_call(
        functools.partial(mid_kernel, n, subs, 2),
        out_shape=[
            jax.ShapeDtypeStruct((rows, wide), BF16),
            jax.ShapeDtypeStruct((rows, wide), F32),
            jax.ShapeDtypeStruct((tokens, wide), BF16),
            jax.ShapeDtypeStruct((tokens, lanes), F32),
            jax.ShapeDtypeStruct((tokens, lanes), BF16),
        ],
        in_specs=[vmem] * 7,
        out_specs=[vmem] * 5,
        scratch_shapes=[
            pltpu.VMEM((hops, rows // subs, wide), BF16),
            pltpu.VMEM((hops, rows // subs, wide), BF16),
            pltpu.VMEM((rows, wide), F32),
            pltpu.VMEM((rows, wide), F32),
            dma((hops,)), dma((hops,)), dma((hops,)), dma((hops,)),
            dma((n * subs,)), dma((n * subs,)), dma((n * subs,)), dma((n * subs,)),
        ],
        compiler_params=pltpu.CompilerParams(
            collective_id=1, has_side_effects=True, vmem_limit_bytes=60 << 20
        ),
        name="middle",
    )(gated, w_out, hidden, teacher, scale, z_gate, scan_out)


def front_kernel(n, dps, seqs, subs, lag, hid_ref, gain_ref, cnt_ref, win_ref, wsm_ref, taps_ref, keep_ref,
                 x_out, z_out, nrm_out, w_out, conv_out, low_out, total_ref, gfull, ws_ref, mixed_ref,
                 rows_ref, grecv, cnt_one, cnt_two, x_ref, z_ref, nrm_ref, w_ref, conv_ref, low_ref,
                 mix_send, mix_recv, mix_own, outs, ms, mr, ns, nr,
                 ar_send, ar_recv, al_send, al_recv, gs, gr, c1s, c1r, c2s, c2r, hs, hr, ls,
                 chip_send, chip_recv, core_send, core_recv):
    dp, seq, t = place()
    core, hi = dp % 2, dp // 2
    chips = dps // 2 * seqs
    chip = hi * seqs + seq
    rows, wide = hid_ref.shape
    part = rows // subs
    share = wide // n
    wrows = win_ref.shape[1]
    tile = 512
    gap = max(subs, lag)
    partner = dict(dp=hi * 2 + 1 - core)
    right, left = dict(tensor=lax.rem(t + 1, n)), dict(tensor=lax.rem(t + n - 1, n))

    def owner(q, c):
        return (q // seqs * 2 + c) * seqs + q % seqs

    def to_chip(q):
        return dict(dp=q // seqs * 2 + core, seq=q % seqs)

    barrier = pltpu.get_barrier_semaphore()
    pl.semaphore_signal(barrier, inc=1, device_id=partner, device_id_type=MESH)
    for ahead in range(1, chips):
        pl.semaphore_signal(barrier, inc=1, device_id=to_chip(lax.rem(chip + ahead, chips)), device_id_type=MESH)
    for ahead in range(1, n):
        pl.semaphore_signal(barrier, inc=1, device_id=dict(tensor=lax.rem(t + ahead, n)), device_id_type=MESH)
    pl.semaphore_wait(barrier, chips + n - 1)

    def at(o, s):
        return pl.ds(pl.multiple_of(o * rows + s * part, part), part)

    def ar_copy(o, s):
        ref = rows_ref.at[at(o, s), :]
        return mesh_copy(ref, ref, ar_send.at[o * subs + s], ar_recv.at[o * subs + s], **right)

    def al_copy(o, s):
        ref = rows_ref.at[at(o, s), :]
        return mesh_copy(ref, ref, al_send.at[o * subs + s], al_recv.at[o * subs + s], **left)

    def g_copy(p, slot):
        return mesh_copy(gain_ref, grecv.at[slot], gs.at[p], gr.at[slot], tensor=p)

    def block(kind, p):
        if kind == 0:
            return w_ref.at[:, pl.ds(pl.multiple_of(p * wrows, wrows), wrows), :]
        return ws_ref.at[p]

    stored = (win_ref, wsm_ref)

    def chip_copy(kind, q, p):
        return mesh_copy(stored[kind], block(kind, p), chip_send.at[kind, q], chip_recv.at[kind, p], **to_chip(q))

    def core_copy(kind, p, own):
        src = stored[kind] if own else block(kind, p)
        return mesh_copy(src, block(kind, p), core_send.at[kind, p], core_recv.at[kind, p], **partner)

    mine = owner(chip, core)

    def count_one():
        return mesh_copy(cnt_ref, cnt_one, c1s, c1r, **partner)

    def count_two(q, slot):
        return mesh_copy(cnt_one, cnt_two.at[slot], c2s.at[q], c2r.at[slot], **to_chip(q))

    def edge_copy():
        last = x_ref.at[pl.ds(x_ref.shape[0] - 8, 8), :]
        return mesh_copy(last, x_ref.at[pl.ds(0, 8), :], hs, hr, seq=lax.rem(seq + 1, seqs))

    def mix_copy(p, slot):
        return mesh_copy(mix_send.at[p], mix_recv.at[slot], ms.at[p], mr.at[slot], tensor=p)

    def sum_copy(p, slot):
        return mesh_copy(mixed_ref.at[slot], mixed_ref.at[slot], ns.at[p], nr.at[slot], tensor=p)

    def written(i):
        src = (w_ref, nrm_ref, z_ref, x_ref, conv_ref, low_ref)[i]
        return pltpu.make_async_copy(src, (w_out, nrm_out, z_out, x_out, conv_out, low_out)[i], outs.at[i])

    def local_copy():
        return pltpu.make_async_copy(wsm_ref, block(1, mine), ls)

    for ahead in range(1, n):
        g_copy(lax.rem(t + ahead, n), t).start()
    count_one().start()
    rows_ref[pl.ds(pl.multiple_of(t * rows, rows), rows), :] = hid_ref[...]

    @pl.loop(0, subs)
    def _(s):
        @pl.when(t < n - 1)
        def _():
            ar_copy(t, s).start()

        @pl.when(t > 0)
        def _():
            al_copy(t, s).start()

    def share_out(kind):
        for ahead in range(1, chips):
            chip_copy(kind, lax.rem(chip + ahead, chips), mine).start()
        core_copy(kind, mine, True).start()

    share_out(1)
    share_out(0)
    local_copy().start()
    w_ref[:, pl.ds(pl.multiple_of(mine * wrows, wrows), wrows), :] = win_ref[...]

    gfull[...] = jnp.zeros_like(gfull)
    for ahead in range(1, n):
        p = lax.rem(t + ahead, n)
        g_copy(p, p).wait_recv()
    grecv[t] = gain_ref[...]
    for p in range(n):
        gfull[:, p * share:(p + 1) * share] = grecv[p]
    count_one().wait_recv()
    count_one().wait_send()
    cnt_one[...] = cnt_one[...] + cnt_ref[...]
    for ahead in range(1, chips):
        count_two(lax.rem(chip + ahead, chips), chip).start()

    def normalize(o):
        @pl.loop(0, subs)
        def _(s):
            here = at(o, s)
            values = rows_ref[here, :].astype(F32)
            inv = lax.rsqrt(jnp.mean(values * values, axis=1, keepdims=True) + EPS)
            nrm_ref[here, :] = (values * inv * gfull[0:1, :]).astype(BF16)

    def project(o):
        here = pl.ds(pl.multiple_of(o * rows, rows), rows)
        for k, dst in enumerate((x_ref, z_ref)):
            lanes = dst.shape[1]
            width = min(tile, lanes)
            there = pl.ds(pl.multiple_of(o * rows + 8 - 8 * k, 8), rows)

            @pl.loop(0, lanes // width)
            def _(j):
                cols = pl.ds(pl.multiple_of(j * width, width), width)
                dst[there, cols] = jnp.dot(nrm_ref[here, :], w_ref[k, :, cols], preferred_element_type=F32)

    def turn(d, o):
        final = jnp.where(o == 0, (n - 1) * gap + 1, (n - 2 - o) * gap + lag)
        return jnp.where(d == n - 1, final, (d - o) * gap)

    weights_at = (n - 1) * gap

    def step(g, _):
        @pl.when(g == 0)
        def _():
            normalize(t)

        @pl.when(g == weights_at)
        def _():
            for kind in (1, 0):
                for ahead in range(1, chips):
                    q = lax.rem(chip + ahead, chips)
                    chip_copy(kind, q, owner(q, core)).wait_recv()
                    core_copy(kind, owner(q, core), False).start()
            for kind in (1, 0):
                for q in range(chips):
                    core_copy(kind, owner(q, 1 - core), True).wait_recv()
            project(t)

        @pl.loop(0, n)
        def _(o):
            s_right = g - turn(t, o)
            s_left = g - turn(n - 1 - t, n - 1 - o)

            @pl.when(jnp.logical_and(o < t, jnp.logical_and(s_right >= 0, s_right < subs)))
            def _():
                ar_copy(o, s_right).wait_recv()

                @pl.when(t < n - 1)
                def _():
                    ar_copy(o, s_right).start()

            @pl.when(jnp.logical_and(o > t, jnp.logical_and(s_left >= 0, s_left < subs)))
            def _():
                al_copy(o, s_left).wait_recv()

                @pl.when(t > 0)
                def _():
                    al_copy(o, s_left).start()

            landed = jnp.where(o < t, s_right, s_left) - subs + 1

            @pl.when(jnp.logical_and(o != t, landed == 0))
            def _():
                normalize(o)

            ripe = jnp.where(g == weights_at, landed >= 0, jnp.logical_and(g > weights_at, landed == 0))

            @pl.when(jnp.logical_and(o != t, ripe))
            def _():
                project(o)

        return 0

    steps = weights_at + 1 + subs
    lax.fori_loop(0, steps, step, 0)

    @pl.when(seq < seqs - 1)
    def _():
        edge_copy().start()

    @pl.when(seq == 0)
    def _():
        x_ref[0:8, :] = jnp.zeros((8, x_ref.shape[1]), F32)

    for i in range(3):
        written(i).start()

    @pl.when(seq > 0)
    def _():
        edge_copy().wait_recv()

    @pl.when(seq < seqs - 1)
    def _():
        edge_copy().wait_send()

    written(3).start()
    local_copy().wait()
    lanes = low_ref.shape[1]
    width = min(tile, lanes)
    piece = min(64, rows)
    taps = keep_ref.shape[1]

    def convolve(o):
        @pl.loop(0, rows // piece * (lanes // width))
        def _(i):
            base = o * rows + i // (lanes // width) * piece
            here = pl.ds(pl.multiple_of(base, piece), piece)
            cols = pl.ds(pl.multiple_of(i % (lanes // width) * width, width), width)
            span = x_ref[pl.ds(pl.multiple_of(base, piece), piece + 8), cols]
            keep = keep_ref[here, :]
            total = jnp.broadcast_to(taps_ref[taps:taps + 1, cols], (piece, width))
            for j in range(taps):
                first = 8 - (taps - 1) + j
                total = total + taps_ref[j:j + 1, cols] * span[first:first + piece] * keep[:, j:j + 1]
            conv_ref[here, cols] = total
            low_ref[here, cols] = (total / (1.0 + jnp.exp(-total))).astype(BF16)

    groups, depth = ws_ref.shape[0], ws_ref.shape[1]
    used = mix_own.shape[0] // groups

    @pl.loop(0, n)
    def _(i):
        o = lax.rem(t + 1 + i, n)
        convolve(o)
        nt = (((1,), (1,)), ((), ()))
        low = low_ref[pl.ds(pl.multiple_of(o * rows, rows), rows), :]
        weights = ws_ref[...].reshape(groups * depth, lanes)
        mix = lax.dot_general(weights, low, nt, preferred_element_type=F32)
        mix = jnp.concatenate([mix[p * depth:p * depth + used] for p in range(groups)], 0)

        @pl.when(o != t)
        def _():
            mix_send[o] = mix.astype(BF16)
            mix_copy(o, t).start()

        @pl.when(o == t)
        def _():
            mix_own[...] = mix

    for i in range(4, 6):
        written(i).start()
    for ahead in range(1, n):
        p = lax.rem(t + ahead, n)
        mix_copy(p, p).wait_recv()
        mix_own[...] = mix_own[...] + mix_recv[p].astype(F32)
    mixed_ref[t] = mix_own[...].astype(BF16)
    for ahead in range(1, n):
        sum_copy(lax.rem(t + ahead, n), t).start()
    total_ref[...] = cnt_one[...]
    for ahead in range(1, chips):
        q = lax.rem(chip + ahead, chips)
        count_two(q, q).wait_recv()
        total_ref[...] = total_ref[...] + cnt_two[q]
    for ahead in range(1, n):
        p = lax.rem(t + ahead, n)
        sum_copy(p, p).wait_recv()
    for ahead in range(1, n):
        p = lax.rem(t + ahead, n)
        mix_copy(p, t).wait_send()
        sum_copy(p, t).wait_send()
    for i in range(6):
        written(i).wait()
    for kind in range(2):
        for ahead in range(1, chips):
            chip_copy(kind, lax.rem(chip + ahead, chips), mine).wait_send()
        for q in range(chips):
            core_copy(kind, owner(q, core), False).wait_send()
    for ahead in range(1, chips):
        count_two(lax.rem(chip + ahead, chips), chip).wait_send()
    for ahead in range(1, n):
        g_copy(lax.rem(t + ahead, n), t).wait_send()

    @pl.loop(0, n * subs)
    def _(i):
        o, s = i // subs, i % subs

        @pl.when(jnp.logical_and(o <= t, t < n - 1))
        def _():
            ar_copy(o, s).wait_send()

        @pl.when(jnp.logical_and(o >= t, t > 0))
        def _():
            al_copy(o, s).wait_send()


def front(hidden, gain, count, w_in, w_small, taps, keeps):
    n, dps, seqs = (lax.axis_size(axis) for axis in ("tensor", "dp", "seq"))
    parts = dps * seqs
    chips = parts // 2
    rows, wide = hidden.shape
    lanes = w_in.shape[2]
    tokens = rows * n
    mixed = parts * SMALL_ROWS
    subs = max(1, rows // 32)
    vmem, hbm = pl.BlockSpec(memory_space=pltpu.VMEM), pl.BlockSpec(memory_space=pl.ANY)
    dma = pltpu.SemaphoreType.DMA
    many, few, peers = dma((n * subs,)), dma((chips,)), dma((n,))
    return pl.pallas_call(
        functools.partial(front_kernel, n, dps, seqs, subs, 2),
        out_shape=[
            jax.ShapeDtypeStruct((tokens + 8, lanes), F32),
            jax.ShapeDtypeStruct((tokens, lanes), F32),
            jax.ShapeDtypeStruct((tokens, wide), BF16),
            jax.ShapeDtypeStruct((2, wide, lanes), BF16),
            jax.ShapeDtypeStruct((tokens, lanes), F32),
            jax.ShapeDtypeStruct((tokens, lanes), BF16),
            jax.ShapeDtypeStruct(count.shape, F32),
            jax.ShapeDtypeStruct((gain.shape[0], wide), F32),
            jax.ShapeDtypeStruct((parts,) + w_small.shape, BF16),
            jax.ShapeDtypeStruct((n, mixed, rows), BF16),
        ],
        in_specs=[vmem] * 7,
        out_specs=[hbm] * 6 + [vmem] * 4,
        scratch_shapes=[
            pltpu.VMEM((tokens, wide), BF16),
            pltpu.VMEM((n,) + gain.shape, F32),
            pltpu.VMEM(count.shape, F32),
            pltpu.VMEM((chips,) + count.shape, F32),
            pltpu.VMEM((tokens + 8, lanes), F32),
            pltpu.VMEM((tokens, lanes), F32),
            pltpu.VMEM((tokens, wide), BF16),
            pltpu.VMEM((2, wide, lanes), BF16),
            pltpu.VMEM((tokens, lanes), F32),
            pltpu.VMEM((tokens, lanes), BF16),
            pltpu.VMEM((n, mixed, rows), BF16),
            pltpu.VMEM((n, mixed, rows), BF16),
            pltpu.VMEM((mixed, rows), F32),
            dma((6,)), peers, peers, peers, peers,
            many, many, many, many, peers, peers, dma, dma, few, few, dma, dma, dma,
            dma((2, chips)), dma((2, parts)), dma((2, parts)), dma((2, parts)),
        ],
        compiler_params=pltpu.CompilerParams(
            collective_id=3, has_side_effects=True, vmem_limit_bytes=60 << 20
        ),
        name="front",
    )(hidden, gain, count, w_in, w_small, taps, keeps)


def on_device(
    hidden_in,
    teacher,
    segment_ids,
    norm_gain,
    input_projection_weight,
    conv_weight,
    conv_bias,
    xproj_weight,
    dtproj_weight,
    dt_bias,
    a_log,
    d_skip,
    output_projection_weight,
):
    tok_rows = segment_ids.shape[0]
    row_share = hidden_in.shape[0]
    model_width = hidden_in.shape[1]
    conv_taps = conv_weight.shape[0]
    chan_lanes = conv_weight.shape[1]
    back_rows = conv_taps - 1
    row_start = lax.axis_index("tensor") * row_share
    valid_mask = (segment_ids != 0).astype(jnp.float32)
    count_here = jnp.full((8, 128), jnp.sum(valid_mask))
    parts = lax.axis_size(("dp", "seq"))
    gain_tile = jnp.broadcast_to(norm_gain.astype(F32)[None], (8, norm_gain.shape[0]))
    x_cols, dt_rows = xproj_weight.shape[1], dtproj_weight.shape[0]
    w_small = jnp.concatenate(
        [
            xproj_weight.T,
            jnp.zeros((SMALL_ROWS - x_cols, chan_lanes), BF16),
            dtproj_weight,
            jnp.zeros((-(SMALL_ROWS + dt_rows) % 16, chan_lanes), BF16),
        ],
        0,
    )
    seg_float = segment_ids.astype(F32)
    prev_seg = jnp.where(lax.axis_index("seq") > 0, seg_float[:1], jnp.zeros((back_rows,), F32))
    ext_seg = jnp.concatenate([prev_seg, seg_float], 0)
    tap_keeps = []
    for offset in range(conv_taps):
        tap_keeps.append((ext_seg[offset : offset + tok_rows] == seg_float).astype(F32)[:, None])
    taps = jnp.concatenate(
        [conv_weight.astype(F32), conv_bias.astype(F32)[None], jnp.zeros((7 - conv_taps, chan_lanes), F32)], 0
    )
    x_rows, z_gate, normalized_rows, w_in, conv_sum, x_low, total, gain_rows, w_small, mixed = front(
        hidden_in,
        gain_tile,
        count_here,
        jnp.swapaxes(input_projection_weight, 0, 1),
        w_small,
        taps,
        jnp.concatenate(tap_keeps, 1),
    )
    w_out_rows, z_gate = lax.optimization_barrier((output_projection_weight.T, z_gate))
    w_out = lax.all_gather(w_out_rows, ("dp", "seq"), axis=0, tiled=True)
    total_count = total[0, 0]
    w_x = w_small[:, :x_cols].reshape(parts * x_cols, chan_lanes)
    w_dt = w_small[:, SMALL_ROWS : SMALL_ROWS + dt_rows].reshape(parts * dt_rows, chan_lanes)
    share_rows = hidden_in.astype(F32)
    full_gain = gain_rows[0]
    inv_share = lax.rsqrt(jnp.mean(share_rows * share_rows, axis=1, keepdims=True) + EPS)
    ext_x = x_rows[8 - back_rows :]
    x_float = x_low.astype(F32)
    mixed = mixed.reshape(-1, parts, SMALL_ROWS, row_share)[:, :, :x_cols]
    mixed_rows = mixed.transpose(0, 3, 1, 2).reshape(tok_rows, parts * x_cols).astype(F32)
    rank_width = w_dt.shape[0]
    state_width = (mixed_rows.shape[1] - rank_width) // 2
    step_low = mixed_rows[:, :rank_width].astype(jnp.bfloat16)
    b_in = mixed_rows[:, rank_width : rank_width + state_width]
    c_out = mixed_rows[:, rank_width + state_width :]
    pre_act = jnp.dot(step_low, w_dt, preferred_element_type=jnp.float32) + dt_bias[None]
    step_size = jax.nn.softplus(pre_act)
    decay_rates = -jnp.exp(a_log)
    same_doc = (seg_float == ext_seg[back_rows - 1 : back_rows - 1 + tok_rows]).astype(jnp.float32)
    rates = decay_rates * LOG2E
    block = 128
    stepd = jnp.where(same_doc[:, None] != 0, step_size, FAR)
    inject = step_size * x_float
    col_pair = jnp.concatenate([columns(b_in), columns(c_out)], -1)
    b_diag, c_diag = diagonal(b_in), diagonal(c_out)
    resets = jnp.sum((same_doc == 0).astype(jnp.int32).reshape(-1, block), axis=1)
    alive = (jnp.cumsum(resets) - resets == 0).astype(jnp.int32)
    y_local, marks, state_last = fwd(stepd, inject, col_pair, c_diag, rates, tb=block, unroll=8)
    reach = jnp.exp2(rates * jnp.sum(stepd, axis=0)[None])
    state_in = carried(state_last, reach, "seq", 1)
    y_rows, marks = correct(alive, y_local, stepd, c_diag, rates, marks, state_in, tb=block)
    scan_out = y_rows + d_skip[None] * x_float
    gate_act = jax.nn.silu(z_gate)
    gated_output_rows = (scan_out * gate_act).astype(jnp.bfloat16)
    valid_share = lax.dynamic_slice_in_dim(valid_mask, row_start, row_share, 0)
    total_tokens = float(tok_rows * lax.axis_size(("dp", "seq")))
    scale = (total_tokens / total_count * valid_share)[:, None]
    output, grad_out, piece, d_scan, d_z = middle(
        gated_output_rows, w_out, hidden_in, teacher, scale, z_gate, scan_out
    )
    d_wout = jnp.einsum("te,tw->we", gated_output_rows, piece, preferred_element_type=jnp.float32)
    d_skip_part = jnp.sum(d_scan * x_float, axis=0)
    adjoint_first = entry(alive, stepd, d_scan, col_pair, rates, tb=block)
    adjoint_in = carried(adjoint_first, reach, "seq", -1)
    ones = diagonal(jnp.ones((CH, N), F32))
    weighted_b, d_rate, d_b_part, d_c_part, a_log_part = bwd(
        stepd, inject, d_scan, col_pair, b_diag, ones, rates, marks, adjoint_in, tb=block, unroll=8
    )
    d_step = LN2 * d_rate + x_float * weighted_b
    a_log_part = LN2 * a_log_part
    d_b_part = jnp.sum(d_b_part, axis=0).reshape(tok_rows, N)
    d_c_part = jnp.sum(d_c_part, axis=0).reshape(tok_rows, N)
    d_xlow = d_skip[None] * d_scan + step_size * weighted_b
    d_pre = d_step * jax.nn.sigmoid(pre_act)
    dt_bias_part = jnp.sum(d_pre, axis=0)
    d_pre_low = d_pre.astype(jnp.bfloat16)
    d_wdt = jnp.einsum("tr,te->re", step_low, d_pre_low, preferred_element_type=jnp.float32)
    d_rank = jnp.einsum("te,re->tr", d_pre_low, w_dt, preferred_element_type=jnp.float32)
    d_mixed = lax.psum(jnp.concatenate([d_rank, d_b_part, d_c_part], 1), "tensor")
    d_mixed_low = d_mixed.astype(jnp.bfloat16)
    d_wx = jnp.einsum("te,tj->ej", x_low, d_mixed_low, preferred_element_type=jnp.float32)
    d_wx_rank = d_wx[:, :rank_width]
    d_wx_state = d_wx[:, rank_width:]
    d_xlow = d_xlow + jnp.dot(d_mixed_low, w_x, preferred_element_type=F32)
    d_conv = d_xlow * silu_slope(conv_sum)
    conv_bias_part = jnp.sum(d_conv, axis=0)
    conv_weight_rows = []
    for offset in range(conv_taps):
        conv_weight_rows.append(
            jnp.sum(d_conv * ext_x[offset : offset + tok_rows] * tap_keeps[offset], axis=0)
        )
    conv_weight_part = jnp.stack(conv_weight_rows, 0)
    conv_padded = jnp.concatenate([d_conv, jnp.zeros((back_rows, chan_lanes), jnp.float32)], 0)
    d_x = jnp.zeros((tok_rows, chan_lanes), jnp.float32)
    for offset in range(conv_taps):
        lead = back_rows - offset
        keep_padded = jnp.concatenate(
            [tap_keeps[offset], jnp.zeros((back_rows, 1), jnp.float32)], 0
        )
        d_x = (
            d_x
            + conv_weight[offset].astype(jnp.float32)[None]
            * conv_padded[lead : lead + tok_rows]
            * keep_padded[lead : lead + tok_rows]
        )
    front_rows = []
    for place in range(back_rows):
        front_total = jnp.zeros((chan_lanes,), jnp.float32)
        for offset in range(place + 1):
            front_total = (
                front_total
                + conv_weight[offset].astype(jnp.float32)
                * d_conv[place - offset]
                * tap_keeps[offset][place - offset, 0]
            )
        front_rows.append(front_total)
    front_grad = jnp.stack(front_rows, 0)
    carried_grad = passed_along(front_grad, "seq", -1)
    d_x = d_x.at[tok_rows - back_rows :].add(carried_grad)
    small = jnp.concatenate(
        [
            d_wx_rank.T.reshape(parts, -1, chan_lanes),
            d_wx_state.T.reshape(parts, -1, chan_lanes),
            d_wdt.reshape(parts, -1, chan_lanes),
            jnp.zeros((parts, 4, chan_lanes), F32),
        ],
        1,
    )
    whole = jnp.concatenate(
        [a_log_part, conv_weight_part, jnp.stack([conv_bias_part, dt_bias_part, d_skip_part, d_skip_part], 0)], 0
    )
    d_norm_share, g_in, g_small, g_whole = tail(d_x.astype(BF16), d_z, w_in, normalized_rows, small, whole)
    g_in = jnp.swapaxes(g_in, 0, 1)
    inner_sum = jnp.sum(d_norm_share * full_gain[None] * share_rows, axis=1, keepdims=True)
    inv_cube = inv_share * inv_share * inv_share
    input_grad = (
        grad_out
        + inv_share * full_gain[None] * d_norm_share
        - share_rows * inv_cube * inner_sum / model_width
    )
    rank_here = rank_width // parts
    state_here = 2 * state_width // parts
    g_x_rank = g_small[:rank_here].T
    g_x_state = g_small[rank_here : rank_here + state_here].T
    g_dt = g_small[rank_here + state_here : rank_here + state_here + rank_here]
    g_out = lax.psum_scatter(d_wout.astype(BF16), ("dp", "seq"), scatter_dimension=0, tiled=True).astype(F32).T
    g_gain = jnp.sum(g_whole[N + conv_taps + 4 :, : norm_gain.shape[0]], axis=0) / norm_gain.astype(F32)
    g_alog, g_conv_w = g_whole[:N], g_whole[N : N + conv_taps]
    g_conv_b, g_bias, g_skip = g_whole[N + conv_taps], g_whole[N + conv_taps + 1], g_whole[N + conv_taps + 2]
    return (
        output,
        input_grad,
        g_gain,
        g_in,
        g_conv_w,
        g_conv_b,
        g_x_rank,
        g_x_state,
        g_dt,
        g_bias,
        g_alog,
        g_skip,
        g_out,
    )


def solution(mesh):
    placed = (
        P(("dp", "seq", "tensor"), None),
        P(("dp", "seq", "tensor"), None),
        P(("dp", "seq")),
        P("tensor"),
        P(("dp", "seq"), None, "tensor"),
        P(None, "tensor"),
        P("tensor"),
        P("tensor", ("dp", "seq")),
        P(("dp", "seq"), "tensor"),
        P("tensor"),
        P(None, "tensor"),
        P("tensor"),
        P("tensor", ("dp", "seq")),
    )
    return jax.shard_map(
        on_device,
        mesh=mesh,
        in_specs=placed,
        out_specs=(
            P(("dp", "seq", "tensor"), None),
            P(("dp", "seq", "tensor"), None),
            P("tensor"),
            P(("dp", "seq"), None, "tensor"),
            P(None, "tensor"),
            P("tensor"),
            P("tensor", ("dp", "seq")),
            P("tensor", ("dp", "seq")),
            P(("dp", "seq"), "tensor"),
            P("tensor"),
            P(None, "tensor"),
            P("tensor"),
            P("tensor", ("dp", "seq")),
        ),
        check_vma=False,
    )
```

```python
import functools

import jax
import jax.numpy as jnp
from jax import lax
from jax.experimental import pallas as pl
from jax.experimental.pallas import tpu as pltpu
from jax.sharding import PartitionSpec as P

EPS = 1e-05
LOG2E = 1.4426950408889634
LN2 = 0.6931471805599453
FAR = 1e30
SMALL_ROWS = 24
MESH = pl.DeviceIdType.MESH


def passed_along(x, axis, by):
    size = lax.axis_size(axis)
    pairs = [(i, i + by) for i in range(size) if 0 <= i + by < size]
    return lax.ppermute(x, axis, pairs)


def silu_slope(values):
    logistic = jax.nn.sigmoid(values)
    return logistic * (1.0 + values * (1.0 - logistic))


F32, BF16 = jnp.float32, jnp.bfloat16
N = 16
CH = 16

def fwd_kernel(stepd_ref, u_ref, bc_ref, cdiag_ref, rate_ref, y_ref, ckpt_ref, last_ref, state_ref, sbf_ref, *, unroll):
    @pl.when(pl.program_id(1) == 0)
    def _():
        state_ref[...] = jnp.zeros_like(state_ref)
    ckpt_ref[0] = state_ref[...]
    rate = rate_ref[...]
    tb = stepd_ref.shape[0]

    def chunk(c, s):
        base = pl.multiple_of(c * CH, CH)
        bc = bc_ref[c]
        for k in range(CH):
            dec = jnp.exp2(rate * stepd_ref[pl.ds(base + k, 1), :])
            s = dec * s + bc[:, k:k + 1] * u_ref[pl.ds(base + k, 1), :]
            sbf_ref[k * N:(k + 1) * N, :] = s.astype(BF16)
        y_ref[pl.ds(base, CH), :] = jnp.dot(cdiag_ref[pl.ds(base, CH), :], sbf_ref[...], preferred_element_type=F32)
        return s

    s = lax.fori_loop(0, tb // CH, chunk, state_ref[...], unroll=unroll)
    state_ref[...] = s
    last_ref[...] = s

def fwd(stepd, u, bc, cdiag, rate, tb=128, w=512, unroll=1):
    t, c = stepd.shape
    w = min(w, c)
    grid = (c // w, t // tb)
    return pl.pallas_call(
        functools.partial(fwd_kernel, unroll=unroll),
        grid=grid,
        in_specs=[
            pl.BlockSpec((tb, w), lambda j, i: (i, j)),
            pl.BlockSpec((tb, w), lambda j, i: (i, j)),
            pl.BlockSpec((tb // CH, N, 2 * CH), lambda j, i: (i, 0, 0)),
            pl.BlockSpec((tb, CH * N), lambda j, i: (i, 0)),
            pl.BlockSpec((N, w), lambda j, i: (0, j)),
        ],
        out_specs=[
            pl.BlockSpec((tb, w), lambda j, i: (i, j)),
            pl.BlockSpec((1, N, w), lambda j, i: (i, 0, j)),
            pl.BlockSpec((N, w), lambda j, i: (0, j)),
        ],
        out_shape=[
            jax.ShapeDtypeStruct((t, c), F32),
            jax.ShapeDtypeStruct((t // tb, N, c), F32),
            jax.ShapeDtypeStruct((N, c), F32),
        ],
        scratch_shapes=[pltpu.VMEM((N, w), F32), pltpu.VMEM((CH * N, w), BF16)],
        compiler_params=pltpu.CompilerParams(vmem_limit_bytes=48 << 20),
        name="scan_forward",
    )(stepd, u, bc, cdiag, rate)

def bwd_kernel(stepd_ref, u_ref, ds_ref, bc_ref, bdiag_ref, ones_ref, rate_ref, ckpt_ref, gin_ref,
               step_ref, sig_ref, low_ref, skip_ref, wdt_ref,
               dpl_ref, e_ref, rank_ref, db_ref, dc_ref, acc_ref, bias_ref, dskip_ref,
               g_ref, sbf_ref, abf_ref, rbf_ref, pb_ref, pc_ref, wb_ref, dn_ref, *, unroll):
    @pl.when(pl.program_id(1) == 0)
    def _():
        g_ref[...] = gin_ref[...]
        acc_ref[...] = jnp.zeros_like(acc_ref)
        bias_ref[...] = jnp.zeros_like(bias_ref)
        dskip_ref[...] = jnp.zeros_like(dskip_ref)

    rate = rate_ref[...]
    tb = stepd_ref.shape[0]
    nc = tb // CH

    def fold(v):
        p = v[:, 0:128]
        for q in range(1, v.shape[1] // 128):
            p = p + v[:, q * 128:(q + 1) * 128]
        return p

    sbf_ref[0:N, :] = ckpt_ref[0].astype(BF16)
    nt = (((1,), (1,)), ((), ()))
    lanes = jnp.ones((8, 128), BF16)

    def forward(c, s):
        base = pl.multiple_of(c * CH, CH)
        bc = bc_ref[c]
        for k in range(CH):
            dec = jnp.exp2(rate * stepd_ref[pl.ds(base + k, 1), :])
            s = dec * s + bc[:, k:k + 1] * u_ref[pl.ds(base + k, 1), :]
            sbf_ref[pl.ds(pl.multiple_of((base + k + 1) * N, N), N), :] = s.astype(BF16)
            pc_ref[k * N:(k + 1) * N, :] = fold(s * ds_ref[pl.ds(base + k, 1), :])
        dc = lax.dot_general(lanes, pc_ref[...].astype(BF16), nt, preferred_element_type=F32)
        dc_ref[0, pl.ds(c, 1), :] = dc[0:1]
        return s

    lax.fori_loop(0, nc, forward, ckpt_ref[0], unroll=unroll)

    def backward(c, carry):
        g, acc = carry
        c = nc - 1 - c
        base = pl.multiple_of(c * CH, CH)
        bc = bc_ref[c]
        for k in range(CH - 1, -1, -1):
            sd = stepd_ref[pl.ds(base + k, 1), :]
            adj = g + bc[:, CH + k:CH + k + 1] * ds_ref[pl.ds(base + k, 1), :]
            abf_ref[k * N:(k + 1) * N, :] = adj.astype(BF16)
            pb_ref[k * N:(k + 1) * N, :] = fold(adj * u_ref[pl.ds(base + k, 1), :])
            g = jnp.exp2(rate * sd) * adj
            before = sbf_ref[pl.ds(pl.multiple_of((base + k) * N, N), N), :].astype(F32)
            r = g * before * rate
            rbf_ref[k * N:(k + 1) * N, :] = r.astype(BF16)
            acc = acc + r * sd
        wb_ref[pl.ds(base, CH), :] = jnp.dot(bdiag_ref[pl.ds(base, CH), :], abf_ref[...], preferred_element_type=F32)
        dn_ref[pl.ds(base, CH), :] = jnp.dot(ones_ref[...], rbf_ref[...], preferred_element_type=F32)
        db = lax.dot_general(lanes, pb_ref[...].astype(BF16), nt, preferred_element_type=F32)
        db_ref[0, pl.ds(c, 1), :] = db[0:1]
        return g, acc

    g, acc = lax.fori_loop(0, nc, backward, (g_ref[...], acc_ref[...]), unroll=unroll)
    g_ref[...] = g
    acc_ref[...] = acc

    low, ds, weighted = low_ref[...].astype(F32), ds_ref[...], wb_ref[...]
    d_pre = (LN2 * dn_ref[...] + low * weighted) * sig_ref[...]
    d_pre_low = d_pre.astype(BF16)
    dpl_ref[...] = d_pre_low
    e_ref[...] = skip_ref[...] * ds + step_ref[...] * weighted
    bias_ref[...] = bias_ref[...] + jnp.sum(d_pre, axis=0, keepdims=True)
    dskip_ref[...] = dskip_ref[...] + jnp.sum(ds * low, axis=0, keepdims=True)
    rank_ref[0] = lax.dot_general(wdt_ref[...], d_pre_low, nt, preferred_element_type=F32)


def bwd(stepd, u, ds, bc, bdiag, ones, rate, ckpt, gin, step, sig, low, skip, w_dt, tb=128, w=512, unroll=1):
    t, c = stepd.shape
    w = min(w, c)
    nb = t // tb
    grid = (c // w, nb)
    rank = w_dt.shape[0]
    rows = pl.BlockSpec((tb, w), lambda j, i: (nb - 1 - i, j))
    return pl.pallas_call(
        functools.partial(bwd_kernel, unroll=unroll),
        grid=grid,
        in_specs=[
            rows, rows, rows,
            pl.BlockSpec((tb // CH, N, 2 * CH), lambda j, i: (nb - 1 - i, 0, 0)),
            pl.BlockSpec((tb, CH * N), lambda j, i: (nb - 1 - i, 0)),
            pl.BlockSpec((CH, CH * N), lambda j, i: (0, 0)),
            pl.BlockSpec((N, w), lambda j, i: (0, j)),
            pl.BlockSpec((1, N, w), lambda j, i: (nb - 1 - i, 0, j)),
            pl.BlockSpec((N, w), lambda j, i: (0, j)),
            rows, rows, rows,
            pl.BlockSpec((1, w), lambda j, i: (0, j)),
            pl.BlockSpec((rank, w), lambda j, i: (0, j)),
        ],
        out_specs=[
            rows, rows,
            pl.BlockSpec((1, rank, tb), lambda j, i: (j, 0, nb - 1 - i)),
            pl.BlockSpec((1, tb // CH, CH * N), lambda j, i: (j, nb - 1 - i, 0)),
            pl.BlockSpec((1, tb // CH, CH * N), lambda j, i: (j, nb - 1 - i, 0)),
            pl.BlockSpec((N, w), lambda j, i: (0, j)),
            pl.BlockSpec((1, w), lambda j, i: (0, j)),
            pl.BlockSpec((1, w), lambda j, i: (0, j)),
        ],
        out_shape=[
            jax.ShapeDtypeStruct((t, c), BF16),
            jax.ShapeDtypeStruct((t, c), F32),
            jax.ShapeDtypeStruct((c // w, rank, t), F32),
            jax.ShapeDtypeStruct((c // w, t // CH, CH * N), F32),
            jax.ShapeDtypeStruct((c // w, t // CH, CH * N), F32),
            jax.ShapeDtypeStruct((N, c), F32),
            jax.ShapeDtypeStruct((1, c), F32),
            jax.ShapeDtypeStruct((1, c), F32),
        ],
        scratch_shapes=[pltpu.VMEM((N, w), F32), pltpu.VMEM(((tb + 1) * N, w), BF16),
                        pltpu.VMEM((CH * N, w), BF16), pltpu.VMEM((CH * N, w), BF16), pltpu.VMEM((CH * N, 128), F32), pltpu.VMEM((CH * N, 128), F32),
                        pltpu.VMEM((tb, w), F32), pltpu.VMEM((tb, w), F32)],
        compiler_params=pltpu.CompilerParams(vmem_limit_bytes=48 << 20),
        name="scan_backward",
    )(stepd, u, ds, bc, bdiag, ones, rate, ckpt, gin, step, sig, low, skip, w_dt)


def correct_kernel(alive_ref, y_ref, stepd_ref, cdiag_ref, rate_ref, ckpt_ref, sin_ref, yo_ref, ckpto_ref, state_ref, sbf_ref):
    i = pl.program_id(1)

    @pl.when(i == 0)
    def _():
        state_ref[...] = sin_ref[...]

    alive = alive_ref[i] != 0

    @pl.when(alive)
    def _():
        rate = rate_ref[...]
        ckpto_ref[0] = ckpt_ref[0] + state_ref[...]

        def chunk(c, s):
            base = pl.multiple_of(c * CH, CH)
            for k in range(CH):
                s = jnp.exp2(rate * stepd_ref[pl.ds(base + k, 1), :]) * s
                sbf_ref[k * N:(k + 1) * N, :] = s.astype(BF16)
            yo_ref[pl.ds(base, CH), :] = y_ref[pl.ds(base, CH), :] + jnp.dot(
                cdiag_ref[pl.ds(base, CH), :], sbf_ref[...], preferred_element_type=F32
            )
            return s

        state_ref[...] = lax.fori_loop(0, y_ref.shape[0] // CH, chunk, state_ref[...], unroll=8)

    @pl.when(jnp.logical_not(alive))
    def _():
        yo_ref[...] = y_ref[...]
        ckpto_ref[...] = ckpt_ref[...]


def correct(alive, y, stepd, cdiag, rate, ckpt, state_in, tb=128, w=512):
    t, c = stepd.shape
    w = min(w, c)
    rows = pl.BlockSpec((tb, w), lambda j, i, _: (i, j))
    lanes = pl.BlockSpec((N, w), lambda j, i, _: (0, j))
    marks = pl.BlockSpec((1, N, w), lambda j, i, _: (i, 0, j))
    return pl.pallas_call(
        correct_kernel,
        grid_spec=pltpu.PrefetchScalarGridSpec(
            num_scalar_prefetch=1,
            grid=(c // w, t // tb),
            in_specs=[rows, rows, pl.BlockSpec((tb, CH * N), lambda j, i, _: (i, 0)), lanes, marks, lanes],
            out_specs=[rows, marks],
            scratch_shapes=[pltpu.VMEM((N, w), F32), pltpu.VMEM((CH * N, w), BF16)],
        ),
        out_shape=[jax.ShapeDtypeStruct((t, c), F32), jax.ShapeDtypeStruct(ckpt.shape, F32)],
        compiler_params=pltpu.CompilerParams(vmem_limit_bytes=48 << 20),
        name="scan_correct",
    )(alive, y, stepd, cdiag, rate, ckpt, state_in)


def entry_kernel(alive_ref, stepd_ref, ds_ref, bc_ref, rate_ref, g_ref):
    i = pl.program_id(1)

    @pl.when(i == 0)
    def _():
        g_ref[...] = jnp.zeros_like(g_ref)

    @pl.when(alive_ref[pl.num_programs(1) - 1 - i] != 0)
    def _():
        rate = rate_ref[...]
        nc = stepd_ref.shape[0] // CH

        def chunk(c, g):
            c = nc - 1 - c
            base = pl.multiple_of(c * CH, CH)
            bc = bc_ref[c]
            for k in range(CH - 1, -1, -1):
                adj = g + bc[:, CH + k:CH + k + 1] * ds_ref[pl.ds(base + k, 1), :]
                g = jnp.exp2(rate * stepd_ref[pl.ds(base + k, 1), :]) * adj
            return g

        g_ref[...] = lax.fori_loop(0, nc, chunk, g_ref[...], unroll=8)


def entry(alive, stepd, ds, bc, rate, tb=128, w=512):
    t, c = stepd.shape
    w = min(w, c)
    nb = t // tb
    rows = pl.BlockSpec((tb, w), lambda j, i, _: (nb - 1 - i, j))
    lanes = pl.BlockSpec((N, w), lambda j, i, _: (0, j))
    return pl.pallas_call(
        entry_kernel,
        grid_spec=pltpu.PrefetchScalarGridSpec(
            num_scalar_prefetch=1,
            grid=(c // w, nb),
            in_specs=[rows, rows, pl.BlockSpec((tb // CH, N, 2 * CH), lambda j, i, _: (nb - 1 - i, 0, 0)), lanes],
            out_specs=lanes,
        ),
        out_shape=jax.ShapeDtypeStruct((N, c), F32),
        compiler_params=pltpu.CompilerParams(vmem_limit_bytes=48 << 20),
        name="scan_entry",
    )(alive, stepd, ds, bc, rate)


def carried(local, reach, axis, by):
    found = jnp.zeros_like(local)
    for _ in range(lax.axis_size(axis) - 1):
        found = passed_along(local + reach * found, axis, by)
    return found


def columns(values):
    tokens = values.shape[0]
    return values.reshape(tokens // CH, CH, N).transpose(0, 2, 1)


def diagonal(values):
    tokens = values.shape[0]
    mine = jnp.arange(CH * N)[None] // N == jnp.arange(tokens)[:, None] % CH
    return jnp.where(mine, jnp.tile(values.astype(BF16), (1, CH)), 0)


def mesh_copy(src, dst, send, recv, **where):
    return pltpu.make_async_remote_copy(
        src_ref=src, dst_ref=dst, send_sem=send, recv_sem=recv, device_id=where, device_id_type=MESH
    )


def place():
    dp, seq, mine = lax.axis_index("dp"), lax.axis_index("seq"), lax.axis_index("tensor")
    return dp, seq, mine


def tail_kernel(n, dps, seqs, subs, lag, dx_ref, dz_ref, w_ref, nrm_ref, sm_ref, all_ref,
                dn_ref, gin_ref, gs_ref, ga_ref,
                gacc, gsend, grecv, all_mine,
                zr, zl, part_r, part_l, one_send, one_recv, two_recv, sm_one, sm_two, all_one, all_two,
                r_send, r_recv, l_send, l_recv, w1s, w1r, w2s, w2r, s1s, s1r, s2s, s2r, a1s, a1r, a2s, a2r, gs, gr):
    dp, seq, t = place()
    core, hi = dp % 2, dp // 2
    chips = dps // 2 * seqs
    chip = hi * seqs + seq
    rows = dn_ref.shape[0]
    part = rows // subs
    wide = dn_ref.shape[1]
    wrows = gin_ref.shape[1]
    tile = 512

    def owner(q, c):
        return (q // seqs * 2 + c) * seqs + q % seqs

    def to_chip(q):
        return dict(dp=q // seqs * 2 + core, seq=q % seqs)

    barrier = pltpu.get_barrier_semaphore()
    pl.semaphore_signal(barrier, inc=1, device_id=dict(dp=hi * 2 + 1 - core), device_id_type=MESH)
    for step in range(1, chips):
        q = lax.rem(chip + step, chips)
        pl.semaphore_signal(barrier, inc=1, device_id=to_chip(q), device_id_type=MESH)

    for ahead in range(1, n):
        pl.semaphore_signal(barrier, inc=1, device_id=dict(tensor=lax.rem(t + ahead, n)), device_id_type=MESH)
    pl.semaphore_wait(barrier, chips + n - 1)
    gacc[...] = jnp.zeros_like(gacc)

    partner = dict(dp=hi * 2 + 1 - core)
    right, left = dict(tensor=lax.rem(t + 1, n)), dict(tensor=lax.rem(t + n - 1, n))

    def r_copy(i):
        return mesh_copy(zr.at[i], zr.at[i], r_send.at[i], r_recv.at[i], **right)

    def l_copy(i):
        return mesh_copy(zl.at[i], zl.at[i], l_send.at[i], l_recv.at[i], **left)

    def w1_copy(q):
        return mesh_copy(one_send.at[q], one_recv.at[q], w1s.at[q], w1r.at[q], **partner)

    def w2_copy(q, slot):
        return mesh_copy(one_recv.at[q], two_recv.at[slot], w2s.at[q], w2r.at[slot], **to_chip(q))

    def s1_copy(q):
        return mesh_copy(sm_ref.at[owner(q, 1 - core)], sm_one.at[q], s1s.at[q], s1r.at[q], **partner)

    def s2_copy(q, slot):
        return mesh_copy(sm_one.at[q], sm_two.at[slot], s2s.at[q], s2r.at[slot], **to_chip(q))

    def a1_copy():
        return mesh_copy(all_mine, all_one, a1s, a1r, **partner)

    def a2_copy(q, slot):
        return mesh_copy(all_one, all_two.at[slot], a2s.at[q], a2r.at[slot], **to_chip(q))

    def g_copy(p, slot):
        return mesh_copy(gsend.at[p], grecv.at[slot], gs.at[p], gr.at[slot], tensor=p)

    def partial_rows(o, dst):
        here = pl.ds(pl.multiple_of(o * rows, rows), rows)

        @pl.loop(0, wide // tile)
        def _(j):
            cols = pl.ds(pl.multiple_of(j * tile, tile), tile)
            nt = (((1,), (1,)), ((), ()))
            block = lax.dot_general(
                dx_ref[here, :], w_ref[0, cols, :], nt, preferred_element_type=F32
            ) + lax.dot_general(dz_ref[here, :], w_ref[1, cols, :], nt, preferred_element_type=F32)
            dst[:, cols] = block
            scaled = block * nrm_ref[here, cols].astype(F32)
            gacc[:, cols] = gacc[:, cols] + jnp.sum(scaled.reshape(rows // 8, 8, tile), axis=0)

    def weight_rows(p, k):
        cols = pl.ds(pl.multiple_of(p * wrows, wrows), wrows)
        tn = (((0,), (0,)), ((), ()))
        d_ref = dx_ref if k == 0 else dz_ref
        return lax.dot_general(nrm_ref[:, cols], d_ref[...], tn, preferred_element_type=F32)

    for q in range(chips):
        s1_copy(q).start()

    def stream(i, limit, start, buf, copy, part_ref, owner_of):
        @pl.when(jnp.logical_and(i >= 0, i < limit))
        def _():
            k, sub = i // subs, i % subs

            @pl.when(sub == 0)
            def _():
                partial_rows(owner_of(k), part_ref)

            @pl.when(jnp.logical_and(start, sub == 0))
            def _():
                @pl.loop(0, subs)
                def _(j):
                    here = part_ref[pl.ds(pl.multiple_of(j * part, part), part), :]
                    buf[k * subs + j] = here.astype(BF16)
                    copy(k * subs + j).start()

            @pl.when(jnp.logical_not(start))
            def _():
                here = part_ref[pl.ds(pl.multiple_of(sub * part, part), part), :]
                copy(i).wait_recv()
                buf[i] = (here + buf[i].astype(F32)).astype(BF16)
                copy(i).start()

    def step(g, _):
        stream(g - lag * t, (n - 1 - t) * subs, t == 0, zr, r_copy, part_r, lambda k: n - 1 - k)
        stream(g - lag * (n - 1 - t), t * subs, t == n - 1, zl, l_copy, part_l, lambda k: k)

        @pl.when(g < chips)
        def _():
            for k in range(2):
                one_send[g, k] = weight_rows(owner(g, 1 - core), k).astype(BF16)
            w1_copy(g).start()

        @pl.when(jnp.logical_and(g >= chips, g < 2 * chips - 1))
        def _():
            q = lax.rem(chip + 1 + g - chips, chips)
            w1_copy(q).wait_recv()
            for k in range(2):
                one_recv[q, k] = (weight_rows(owner(q, core), k) + one_recv[q, k].astype(F32)).astype(BF16)
            w2_copy(q, chip).start()

        @pl.when(g == 2 * chips - 1)
        def _():
            for q in range(chips):
                s1_copy(q).wait_recv()
                sm_one[q] = sm_one[q] + sm_ref[owner(q, core)]
            for ahead in range(1, chips):
                q = lax.rem(chip + ahead, chips)
                s2_copy(q, chip).start()
            w1_copy(chip).wait_recv()
            for k in range(2):
                gin_ref[k] = weight_rows(owner(chip, core), k) + one_recv[chip, k].astype(F32)

        @pl.when(g == 2 * chips)
        def _():
            partial_rows(t, dn_ref)

        return 0

    steps = max((n - 1) * max(subs, lag), 2 * chips + 1)
    lax.fori_loop(0, steps, step, 0)

    share = wide // n
    for p in range(n):
        gsend[p] = gacc[:, p * share:(p + 1) * share]
    for ahead in range(1, n):
        g_copy(lax.rem(t + ahead, n), t).start()

    @pl.loop(0, subs)
    def _(s):
        here = pl.ds(pl.multiple_of(s * part, part), part)

        @pl.when(t > 0)
        def _():
            i = (n - 1 - t) * subs + s
            r_copy(i).wait_recv()
            dn_ref[here, :] = dn_ref[here, :] + zr[i].astype(F32)

        @pl.when(t < n - 1)
        def _():
            i = t * subs + s
            l_copy(i).wait_recv()
            dn_ref[here, :] = dn_ref[here, :] + zl[i].astype(F32)

    plain = all_ref.shape[0]
    all_mine[0:plain, :] = all_ref[...]
    all_mine[plain:, :] = jnp.zeros((8, all_mine.shape[1]), F32)
    all_mine[plain:, 0:share] = gsend[t]
    for ahead in range(1, n):
        p = lax.rem(t + ahead, n)
        g_copy(p, p).wait_recv()
        all_mine[plain:, 0:share] = all_mine[plain:, 0:share] + grecv[p]
    a1_copy().start()
    gs_ref[...] = sm_one[chip]
    for ahead in range(1, chips):
        q = lax.rem(chip + ahead, chips)
        s2_copy(q, q).wait_recv()
        gs_ref[...] = gs_ref[...] + sm_two[q]
    a1_copy().wait_recv()
    all_one[...] = all_one[...] + all_mine[...]
    for ahead in range(1, chips):
        a2_copy(lax.rem(chip + ahead, chips), chip).start()
    ga_ref[...] = all_one[...]
    for ahead in range(1, chips):
        q = lax.rem(chip + ahead, chips)
        w2_copy(q, q).wait_recv()
        gin_ref[...] = gin_ref[...] + two_recv[q].astype(F32)
    for ahead in range(1, chips):
        q = lax.rem(chip + ahead, chips)
        a2_copy(q, q).wait_recv()
        ga_ref[...] = ga_ref[...] + all_two[q]

    for q in range(chips):
        s1_copy(q).wait_send()
        w1_copy(q).wait_send()
    a1_copy().wait_send()
    for ahead in range(1, n):
        g_copy(lax.rem(t + ahead, n), t).wait_send()
    for ahead in range(1, chips):
        q = lax.rem(chip + ahead, chips)
        s2_copy(q, chip).wait_send()
        a2_copy(q, chip).wait_send()
        w2_copy(q, chip).wait_send()

    @pl.loop(0, (n - 1) * subs)
    def _(i):
        @pl.when(i < (n - 1 - t) * subs)
        def _():
            r_copy(i).wait_send()

        @pl.when(i < t * subs)
        def _():
            l_copy(i).wait_send()


def tail(dx, dz, w_full, normed, small, whole):
    n, dps, seqs = (lax.axis_size(axis) for axis in ("tensor", "dp", "seq"))
    chips = dps // 2 * seqs
    rows = dx.shape[0] // n
    wide, lanes = w_full.shape[1], w_full.shape[2]
    wrows = wide // (dps * seqs)
    subs = max(1, rows // 32)
    hops = (n - 1) * subs
    vmem = pl.BlockSpec(memory_space=pltpu.VMEM)
    dma = pltpu.SemaphoreType.DMA
    few = dma((chips,))
    return pl.pallas_call(
        functools.partial(tail_kernel, n, dps, seqs, subs, 2),
        out_shape=[
            jax.ShapeDtypeStruct((rows, wide), F32),
            jax.ShapeDtypeStruct((2, wrows, lanes), F32),
            jax.ShapeDtypeStruct(small.shape[1:], F32),
            jax.ShapeDtypeStruct((whole.shape[0] + 8, lanes), F32),
        ],
        in_specs=[vmem] * 6,
        out_specs=[vmem] * 4,
        scratch_shapes=[
            pltpu.VMEM((8, wide), F32),
            pltpu.VMEM((n, 8, wide // n), F32),
            pltpu.VMEM((n, 8, wide // n), F32),
            pltpu.VMEM((whole.shape[0] + 8, lanes), F32),
            pltpu.VMEM((hops, rows // subs, wide), BF16),
            pltpu.VMEM((hops, rows // subs, wide), BF16),
            pltpu.VMEM((rows, wide), F32),
            pltpu.VMEM((rows, wide), F32),
            pltpu.VMEM((chips, 2, wrows, lanes), BF16),
            pltpu.VMEM((chips, 2, wrows, lanes), BF16),
            pltpu.VMEM((chips, 2, wrows, lanes), BF16),
            pltpu.VMEM((chips,) + small.shape[1:], F32),
            pltpu.VMEM((chips,) + small.shape[1:], F32),
            pltpu.VMEM((whole.shape[0] + 8, lanes), F32),
            pltpu.VMEM((chips, whole.shape[0] + 8, lanes), F32),
            dma((hops,)), dma((hops,)), dma((hops,)), dma((hops,)),
            few, few, few, few, few, few, few, few, dma, dma, few, few, dma((n,)), dma((n,)),
        ],
        compiler_params=pltpu.CompilerParams(
            collective_id=2, has_side_effects=True, vmem_limit_bytes=60 << 20
        ),
        name="tail_sums",
    )(dx, dz, w_full, normed, small, whole)


def mid_kernel(n, subs, lag, gated_ref, w_ref, hid_ref, tea_ref, scale_ref, z_ref, scan_ref,
               out_ref, go_ref, piece_ref, dscan_ref, dz_ref,
               zr, zl, part_r, part_l, r_send, r_recv, l_send, l_recv, ar_send, ar_recv, al_send, al_recv):
    t = lax.axis_index("tensor")
    rows, wide = hid_ref.shape
    part = rows // subs
    tile = 512
    right, left = dict(tensor=lax.rem(t + 1, n)), dict(tensor=lax.rem(t + n - 1, n))

    barrier = pltpu.get_barrier_semaphore()
    for peer in (right, left):
        pl.semaphore_signal(barrier, inc=1, device_id=peer, device_id_type=MESH)
    pl.semaphore_wait(barrier, 2)

    def r_copy(i):
        return mesh_copy(zr.at[i], zr.at[i], r_send.at[i], r_recv.at[i], **right)

    def l_copy(i):
        return mesh_copy(zl.at[i], zl.at[i], l_send.at[i], l_recv.at[i], **left)

    def at(o, s):
        return pl.ds(pl.multiple_of(o * rows + s * part, part), part)

    def ar_copy(o, s):
        ref = piece_ref.at[at(o, s), :]
        return mesh_copy(ref, ref, ar_send.at[o * subs + s], ar_recv.at[o * subs + s], **right)

    def al_copy(o, s):
        ref = piece_ref.at[at(o, s), :]
        return mesh_copy(ref, ref, al_send.at[o * subs + s], al_recv.at[o * subs + s], **left)

    def partial_rows(o, dst):
        here = pl.ds(pl.multiple_of(o * rows, rows), rows)

        @pl.loop(0, wide // tile)
        def _(j):
            cols = pl.ds(pl.multiple_of(j * tile, tile), tile)
            nt = (((1,), (1,)), ((), ()))
            dst[:, cols] = lax.dot_general(gated_ref[here, :], w_ref[cols, :], nt, preferred_element_type=F32)

    def backward_rows(o):
        here = pl.ds(pl.multiple_of(o * rows, rows), rows)
        d_gated = jnp.dot(piece_ref[here, :], w_ref[...], preferred_element_type=F32)
        z = z_ref[here, :]
        s = 1.0 / (1.0 + jnp.exp(-z))
        dscan_ref[here, :] = d_gated * (z * s)
        dz_ref[here, :] = (d_gated * scan_ref[here, :] * (s * (1.0 + z * (1.0 - s)))).astype(BF16)

    def stream(i, limit, start, buf, copy, part_ref, owner_of):
        @pl.when(jnp.logical_and(i >= 0, i < limit))
        def _():
            k, sub = i // subs, i % subs

            @pl.when(sub == 0)
            def _():
                partial_rows(owner_of(k), part_ref)

            @pl.when(jnp.logical_and(start, sub == 0))
            def _():
                @pl.loop(0, subs)
                def _(j):
                    here = part_ref[pl.ds(pl.multiple_of(j * part, part), part), :]
                    buf[k * subs + j] = here.astype(BF16)
                    copy(k * subs + j).start()

            @pl.when(jnp.logical_not(start))
            def _():
                here = part_ref[pl.ds(pl.multiple_of(sub * part, part), part), :]
                copy(i).wait_recv()
                buf[i] = (here + buf[i].astype(F32)).astype(BF16)
                copy(i).start()

    def ready(o):
        from_left = jnp.where(o > 0, lag * o + (n - 1 - o) * subs, 0)
        from_right = jnp.where(o < n - 1, lag * (n - 1 - o) + o * subs, 0)
        return jnp.maximum(from_left, from_right)

    gap = max(subs, lag)
    base = lag + (n - 2) * subs if subs >= lag else (n - 1) * lag

    def turn(d, o):
        inner = base + (d - o) * gap
        inner = jnp.where(d == 0, (n - 1) * gap, inner)
        return jnp.where(d == n - 1, base + (n - 2 - o) * gap + lag, inner)

    def finish(s):
        here = pl.ds(pl.multiple_of(s * part, part), part)

        @pl.when(s == 0)
        def _():
            partial_rows(t, go_ref)

        @pl.when(t > 0)
        def _():
            i = (n - 1 - t) * subs + s
            r_copy(i).wait_recv()
            go_ref[here, :] = go_ref[here, :] + zr[i].astype(F32)

        @pl.when(t < n - 1)
        def _():
            i = t * subs + s
            l_copy(i).wait_recv()
            go_ref[here, :] = go_ref[here, :] + zl[i].astype(F32)

        result = hid_ref[here, :].astype(F32) + go_ref[here, :]
        out_ref[here, :] = result.astype(BF16)
        grad = scale_ref[here, :] * (result - tea_ref[here, :].astype(F32))
        go_ref[here, :] = grad
        piece_ref[at(t, s), :] = grad.astype(BF16)

    def step(g, _):
        stream(g - lag * t, (n - 1 - t) * subs, t == 0, zr, r_copy, part_r, lambda k: n - 1 - k)
        stream(g - lag * (n - 1 - t), t * subs, t == n - 1, zl, l_copy, part_l, lambda k: k)

        @pl.loop(0, n)
        def _(o):
            s_own = g - ready(t)
            s_right = g - turn(t, o)
            s_left = g - turn(n - 1 - t, n - 1 - o)

            @pl.when(jnp.logical_and(o == t, jnp.logical_and(s_own >= 0, s_own < subs)))
            def _():
                finish(s_own)

            @pl.when(jnp.logical_and(o <= t, jnp.logical_and(s_right >= 0, s_right < subs)))
            def _():
                @pl.when(o < t)
                def _():
                    ar_copy(o, s_right).wait_recv()

                @pl.when(t < n - 1)
                def _():
                    ar_copy(o, s_right).start()

            @pl.when(jnp.logical_and(o >= t, jnp.logical_and(s_left >= 0, s_left < subs)))
            def _():
                @pl.when(o > t)
                def _():
                    al_copy(o, s_left).wait_recv()

                @pl.when(t > 0)
                def _():
                    al_copy(o, s_left).start()

            s_done = jnp.where(o == t, s_own, jnp.where(o < t, s_right, s_left))

            @pl.when(s_done == subs - 1)
            def _():
                backward_rows(o)

        return 0

    steps = base + (n - 1) * gap + subs + lag
    lax.fori_loop(0, steps, step, 0)

    @pl.loop(0, (n - 1) * subs)
    def _(i):
        @pl.when(i < (n - 1 - t) * subs)
        def _():
            r_copy(i).wait_send()

        @pl.when(i < t * subs)
        def _():
            l_copy(i).wait_send()

    @pl.loop(0, n * subs)
    def _(i):
        o, s = i // subs, i % subs

        @pl.when(jnp.logical_and(o <= t, t < n - 1))
        def _():
            ar_copy(o, s).wait_send()

        @pl.when(jnp.logical_and(o >= t, t > 0))
        def _():
            al_copy(o, s).wait_send()


def middle(gated, w_out, hidden, teacher, scale, z_gate, scan_out):
    n = lax.axis_size("tensor")
    rows, wide = hidden.shape
    tokens, lanes = gated.shape
    subs = max(1, rows // 32)
    hops = (n - 1) * subs
    vmem = pl.BlockSpec(memory_space=pltpu.VMEM)
    dma = pltpu.SemaphoreType.DMA
    return pl.pallas_call(
        functools.partial(mid_kernel, n, subs, 2),
        out_shape=[
            jax.ShapeDtypeStruct((rows, wide), BF16),
            jax.ShapeDtypeStruct((rows, wide), F32),
            jax.ShapeDtypeStruct((tokens, wide), BF16),
            jax.ShapeDtypeStruct((tokens, lanes), F32),
            jax.ShapeDtypeStruct((tokens, lanes), BF16),
        ],
        in_specs=[vmem] * 7,
        out_specs=[vmem] * 5,
        scratch_shapes=[
            pltpu.VMEM((hops, rows // subs, wide), BF16),
            pltpu.VMEM((hops, rows // subs, wide), BF16),
            pltpu.VMEM((rows, wide), F32),
            pltpu.VMEM((rows, wide), F32),
            dma((hops,)), dma((hops,)), dma((hops,)), dma((hops,)),
            dma((n * subs,)), dma((n * subs,)), dma((n * subs,)), dma((n * subs,)),
        ],
        compiler_params=pltpu.CompilerParams(
            collective_id=1, has_side_effects=True, vmem_limit_bytes=60 << 20
        ),
        name="middle",
    )(gated, w_out, hidden, teacher, scale, z_gate, scan_out)


def front_kernel(n, dps, seqs, subs, lag, hid_ref, gain_ref, cnt_ref, win_ref, wsm_ref, taps_ref, keep_ref,
                 x_out, z_out, nrm_out, w_out, conv_out, low_out, total_ref, gfull, ws_ref, mixed_ref,
                 rows_ref, grecv, cnt_one, cnt_two, x_ref, z_ref, nrm_ref, w_ref, conv_ref, low_ref,
                 mix_send, mix_recv, mix_own, outs, ms, mr, ns, nr,
                 ar_send, ar_recv, al_send, al_recv, gs, gr, c1s, c1r, c2s, c2r, hs, hr, ls,
                 chip_send, chip_recv, core_send, core_recv):
    dp, seq, t = place()
    core, hi = dp % 2, dp // 2
    chips = dps // 2 * seqs
    chip = hi * seqs + seq
    rows, wide = hid_ref.shape
    part = rows // subs
    share = wide // n
    wrows = win_ref.shape[1]
    tile = 512
    gap = max(subs, lag)
    partner = dict(dp=hi * 2 + 1 - core)
    right, left = dict(tensor=lax.rem(t + 1, n)), dict(tensor=lax.rem(t + n - 1, n))

    def owner(q, c):
        return (q // seqs * 2 + c) * seqs + q % seqs

    def to_chip(q):
        return dict(dp=q // seqs * 2 + core, seq=q % seqs)

    barrier = pltpu.get_barrier_semaphore()
    pl.semaphore_signal(barrier, inc=1, device_id=partner, device_id_type=MESH)
    for ahead in range(1, chips):
        pl.semaphore_signal(barrier, inc=1, device_id=to_chip(lax.rem(chip + ahead, chips)), device_id_type=MESH)
    for ahead in range(1, n):
        pl.semaphore_signal(barrier, inc=1, device_id=dict(tensor=lax.rem(t + ahead, n)), device_id_type=MESH)
    pl.semaphore_wait(barrier, chips + n - 1)

    def at(o, s):
        return pl.ds(pl.multiple_of(o * rows + s * part, part), part)

    def ar_copy(o, s):
        ref = rows_ref.at[at(o, s), :]
        return mesh_copy(ref, ref, ar_send.at[o * subs + s], ar_recv.at[o * subs + s], **right)

    def al_copy(o, s):
        ref = rows_ref.at[at(o, s), :]
        return mesh_copy(ref, ref, al_send.at[o * subs + s], al_recv.at[o * subs + s], **left)

    def g_copy(p, slot):
        return mesh_copy(gain_ref, grecv.at[slot], gs.at[p], gr.at[slot], tensor=p)

    def block(kind, p):
        if kind == 0:
            return w_ref.at[:, pl.ds(pl.multiple_of(p * wrows, wrows), wrows), :]
        return ws_ref.at[p]

    stored = (win_ref, wsm_ref)

    def chip_copy(kind, q, p):
        return mesh_copy(stored[kind], block(kind, p), chip_send.at[kind, q], chip_recv.at[kind, p], **to_chip(q))

    def core_copy(kind, p, own):
        src = stored[kind] if own else block(kind, p)
        return mesh_copy(src, block(kind, p), core_send.at[kind, p], core_recv.at[kind, p], **partner)

    mine = owner(chip, core)

    def count_one():
        return mesh_copy(cnt_ref, cnt_one, c1s, c1r, **partner)

    def count_two(q, slot):
        return mesh_copy(cnt_one, cnt_two.at[slot], c2s.at[q], c2r.at[slot], **to_chip(q))

    def edge_copy():
        last = x_ref.at[pl.ds(x_ref.shape[0] - 8, 8), :]
        return mesh_copy(last, x_ref.at[pl.ds(0, 8), :], hs, hr, seq=lax.rem(seq + 1, seqs))

    def mix_copy(p, slot):
        return mesh_copy(mix_send.at[p], mix_recv.at[slot], ms.at[p], mr.at[slot], tensor=p)

    def sum_copy(p, slot):
        return mesh_copy(mixed_ref.at[slot], mixed_ref.at[slot], ns.at[p], nr.at[slot], tensor=p)

    def written(i):
        src = (w_ref, nrm_ref, z_ref, x_ref, conv_ref, low_ref)[i]
        return pltpu.make_async_copy(src, (w_out, nrm_out, z_out, x_out, conv_out, low_out)[i], outs.at[i])

    def local_copy():
        return pltpu.make_async_copy(wsm_ref, block(1, mine), ls)

    for ahead in range(1, n):
        g_copy(lax.rem(t + ahead, n), t).start()
    count_one().start()
    rows_ref[pl.ds(pl.multiple_of(t * rows, rows), rows), :] = hid_ref[...]

    @pl.loop(0, subs)
    def _(s):
        @pl.when(t < n - 1)
        def _():
            ar_copy(t, s).start()

        @pl.when(t > 0)
        def _():
            al_copy(t, s).start()

    def share_out(kind):
        for ahead in range(1, chips):
            chip_copy(kind, lax.rem(chip + ahead, chips), mine).start()
        core_copy(kind, mine, True).start()

    share_out(1)
    share_out(0)
    local_copy().start()
    w_ref[:, pl.ds(pl.multiple_of(mine * wrows, wrows), wrows), :] = win_ref[...]

    gfull[...] = jnp.zeros_like(gfull)
    for ahead in range(1, n):
        p = lax.rem(t + ahead, n)
        g_copy(p, p).wait_recv()
    grecv[t] = gain_ref[...]
    for p in range(n):
        gfull[:, p * share:(p + 1) * share] = grecv[p]
    count_one().wait_recv()
    count_one().wait_send()
    cnt_one[...] = cnt_one[...] + cnt_ref[...]
    for ahead in range(1, chips):
        count_two(lax.rem(chip + ahead, chips), chip).start()

    def normalize(o):
        @pl.loop(0, subs)
        def _(s):
            here = at(o, s)
            values = rows_ref[here, :].astype(F32)
            inv = lax.rsqrt(jnp.mean(values * values, axis=1, keepdims=True) + EPS)
            nrm_ref[here, :] = (values * inv * gfull[0:1, :]).astype(BF16)

    def project(o):
        here = pl.ds(pl.multiple_of(o * rows, rows), rows)
        for k, dst in enumerate((x_ref, z_ref)):
            lanes = dst.shape[1]
            width = min(tile, lanes)
            there = pl.ds(pl.multiple_of(o * rows + 8 - 8 * k, 8), rows)

            @pl.loop(0, lanes // width)
            def _(j):
                cols = pl.ds(pl.multiple_of(j * width, width), width)
                dst[there, cols] = jnp.dot(nrm_ref[here, :], w_ref[k, :, cols], preferred_element_type=F32)

    def turn(d, o):
        final = jnp.where(o == 0, (n - 1) * gap + 1, (n - 2 - o) * gap + lag)
        return jnp.where(d == n - 1, final, (d - o) * gap)

    weights_at = (n - 1) * gap

    def step(g, _):
        @pl.when(g == 0)
        def _():
            normalize(t)

        @pl.when(g == weights_at)
        def _():
            for kind in (1, 0):
                for ahead in range(1, chips):
                    q = lax.rem(chip + ahead, chips)
                    chip_copy(kind, q, owner(q, core)).wait_recv()
                    core_copy(kind, owner(q, core), False).start()
            for kind in (1, 0):
                for q in range(chips):
                    core_copy(kind, owner(q, 1 - core), True).wait_recv()
            project(t)

        @pl.loop(0, n)
        def _(o):
            s_right = g - turn(t, o)
            s_left = g - turn(n - 1 - t, n - 1 - o)

            @pl.when(jnp.logical_and(o < t, jnp.logical_and(s_right >= 0, s_right < subs)))
            def _():
                ar_copy(o, s_right).wait_recv()

                @pl.when(t < n - 1)
                def _():
                    ar_copy(o, s_right).start()

            @pl.when(jnp.logical_and(o > t, jnp.logical_and(s_left >= 0, s_left < subs)))
            def _():
                al_copy(o, s_left).wait_recv()

                @pl.when(t > 0)
                def _():
                    al_copy(o, s_left).start()

            landed = jnp.where(o < t, s_right, s_left) - subs + 1

            @pl.when(jnp.logical_and(o != t, landed == 0))
            def _():
                normalize(o)

            ripe = jnp.where(g == weights_at, landed >= 0, jnp.logical_and(g > weights_at, landed == 0))

            @pl.when(jnp.logical_and(o != t, ripe))
            def _():
                project(o)

        return 0

    steps = weights_at + 1 + subs
    lax.fori_loop(0, steps, step, 0)

    @pl.when(seq < seqs - 1)
    def _():
        edge_copy().start()

    @pl.when(seq == 0)
    def _():
        x_ref[0:8, :] = jnp.zeros((8, x_ref.shape[1]), F32)

    for i in range(3):
        written(i).start()

    @pl.when(seq > 0)
    def _():
        edge_copy().wait_recv()

    @pl.when(seq < seqs - 1)
    def _():
        edge_copy().wait_send()

    written(3).start()
    local_copy().wait()
    lanes = low_ref.shape[1]
    width = min(tile, lanes)
    piece = min(64, rows)
    taps = keep_ref.shape[1]

    def convolve(o):
        @pl.loop(0, rows // piece * (lanes // width))
        def _(i):
            base = o * rows + i // (lanes // width) * piece
            here = pl.ds(pl.multiple_of(base, piece), piece)
            cols = pl.ds(pl.multiple_of(i % (lanes // width) * width, width), width)
            span = x_ref[pl.ds(pl.multiple_of(base, piece), piece + 8), cols]
            keep = keep_ref[here, :]
            total = jnp.broadcast_to(taps_ref[taps:taps + 1, cols], (piece, width))
            for j in range(taps):
                first = 8 - (taps - 1) + j
                total = total + taps_ref[j:j + 1, cols] * span[first:first + piece] * keep[:, j:j + 1]
            conv_ref[here, cols] = total
            low_ref[here, cols] = (total / (1.0 + jnp.exp(-total))).astype(BF16)

    groups, depth = ws_ref.shape[0], ws_ref.shape[1]
    used = mix_own.shape[0] // groups

    @pl.loop(0, n)
    def _(i):
        o = lax.rem(t + 1 + i, n)
        convolve(o)
        nt = (((1,), (1,)), ((), ()))
        low = low_ref[pl.ds(pl.multiple_of(o * rows, rows), rows), :]
        weights = ws_ref[...].reshape(groups * depth, lanes)
        mix = lax.dot_general(weights, low, nt, preferred_element_type=F32)
        mix = jnp.concatenate([mix[p * depth:p * depth + used] for p in range(groups)], 0)

        @pl.when(o != t)
        def _():
            mix_send[o] = mix.astype(BF16)
            mix_copy(o, t).start()

        @pl.when(o == t)
        def _():
            mix_own[...] = mix

    for i in range(4, 6):
        written(i).start()
    for ahead in range(1, n):
        p = lax.rem(t + ahead, n)
        mix_copy(p, p).wait_recv()
        mix_own[...] = mix_own[...] + mix_recv[p].astype(F32)
    mixed_ref[t] = mix_own[...].astype(BF16)
    for ahead in range(1, n):
        sum_copy(lax.rem(t + ahead, n), t).start()
    total_ref[...] = cnt_one[...]
    for ahead in range(1, chips):
        q = lax.rem(chip + ahead, chips)
        count_two(q, q).wait_recv()
        total_ref[...] = total_ref[...] + cnt_two[q]
    for ahead in range(1, n):
        p = lax.rem(t + ahead, n)
        sum_copy(p, p).wait_recv()
    for ahead in range(1, n):
        p = lax.rem(t + ahead, n)
        mix_copy(p, t).wait_send()
        sum_copy(p, t).wait_send()
    for i in range(6):
        written(i).wait()
    for kind in range(2):
        for ahead in range(1, chips):
            chip_copy(kind, lax.rem(chip + ahead, chips), mine).wait_send()
        for q in range(chips):
            core_copy(kind, owner(q, core), False).wait_send()
    for ahead in range(1, chips):
        count_two(lax.rem(chip + ahead, chips), chip).wait_send()
    for ahead in range(1, n):
        g_copy(lax.rem(t + ahead, n), t).wait_send()

    @pl.loop(0, n * subs)
    def _(i):
        o, s = i // subs, i % subs

        @pl.when(jnp.logical_and(o <= t, t < n - 1))
        def _():
            ar_copy(o, s).wait_send()

        @pl.when(jnp.logical_and(o >= t, t > 0))
        def _():
            al_copy(o, s).wait_send()


def front(hidden, gain, count, w_in, w_small, taps, keeps):
    n, dps, seqs = (lax.axis_size(axis) for axis in ("tensor", "dp", "seq"))
    parts = dps * seqs
    chips = parts // 2
    rows, wide = hidden.shape
    lanes = w_in.shape[2]
    tokens = rows * n
    mixed = parts * SMALL_ROWS
    subs = max(1, rows // 32)
    vmem, hbm = pl.BlockSpec(memory_space=pltpu.VMEM), pl.BlockSpec(memory_space=pl.ANY)
    dma = pltpu.SemaphoreType.DMA
    many, few, peers = dma((n * subs,)), dma((chips,)), dma((n,))
    return pl.pallas_call(
        functools.partial(front_kernel, n, dps, seqs, subs, 2),
        out_shape=[
            jax.ShapeDtypeStruct((tokens + 8, lanes), F32),
            jax.ShapeDtypeStruct((tokens, lanes), F32),
            jax.ShapeDtypeStruct((tokens, wide), BF16),
            jax.ShapeDtypeStruct((2, wide, lanes), BF16),
            jax.ShapeDtypeStruct((tokens, lanes), F32),
            jax.ShapeDtypeStruct((tokens, lanes), BF16),
            jax.ShapeDtypeStruct(count.shape, F32),
            jax.ShapeDtypeStruct((gain.shape[0], wide), F32),
            jax.ShapeDtypeStruct((parts,) + w_small.shape, BF16),
            jax.ShapeDtypeStruct((n, mixed, rows), BF16),
        ],
        in_specs=[vmem] * 7,
        out_specs=[hbm] * 6 + [vmem] * 4,
        scratch_shapes=[
            pltpu.VMEM((tokens, wide), BF16),
            pltpu.VMEM((n,) + gain.shape, F32),
            pltpu.VMEM(count.shape, F32),
            pltpu.VMEM((chips,) + count.shape, F32),
            pltpu.VMEM((tokens + 8, lanes), F32),
            pltpu.VMEM((tokens, lanes), F32),
            pltpu.VMEM((tokens, wide), BF16),
            pltpu.VMEM((2, wide, lanes), BF16),
            pltpu.VMEM((tokens, lanes), F32),
            pltpu.VMEM((tokens, lanes), BF16),
            pltpu.VMEM((n, mixed, rows), BF16),
            pltpu.VMEM((n, mixed, rows), BF16),
            pltpu.VMEM((mixed, rows), F32),
            dma((6,)), peers, peers, peers, peers,
            many, many, many, many, peers, peers, dma, dma, few, few, dma, dma, dma,
            dma((2, chips)), dma((2, parts)), dma((2, parts)), dma((2, parts)),
        ],
        compiler_params=pltpu.CompilerParams(
            collective_id=3, has_side_effects=True, vmem_limit_bytes=60 << 20
        ),
        name="front",
    )(hidden, gain, count, w_in, w_small, taps, keeps)


def mixback_kernel(n, seqs, part_ref, e_hbm, conv_hbm, x_hbm, low_hbm, dpl_hbm, step_ref, wx_ref, taps_ref, keep_ref,
                   dx_hbm, dwx_ref, dwdt_ref, dconvw_ref,
                   e_ref, conv_ref, x_ref, low_ref, dpl_ref, dx_ref, dcv_ref, got, own, done, edge_out, edge_in,
                   loads, store, ms, mr, ns, nr, es, er):
    seq, t = lax.axis_index("seq"), lax.axis_index("tensor")
    rows = part_ref.shape[2]
    tokens, lanes = low_ref.shape
    taps = keep_ref.shape[1]
    width = min(512, lanes)
    piece = min(64, rows)
    across = lanes // width
    pieces = tokens // piece * across
    ahead_seq, behind_seq = lax.rem(seq + 1, seqs), lax.rem(seq + seqs - 1, seqs)

    barrier = pltpu.get_barrier_semaphore()
    for ahead in range(1, n):
        pl.semaphore_signal(barrier, inc=1, device_id=dict(tensor=lax.rem(t + ahead, n)), device_id_type=MESH)
    if seqs > 1:
        for peer in (ahead_seq, behind_seq):
            pl.semaphore_signal(barrier, inc=1, device_id=dict(seq=peer), device_id_type=MESH)
    pl.semaphore_wait(barrier, n - 1 + (2 if seqs > 1 else 0))

    def load(i):
        src = (conv_hbm, dpl_hbm, e_hbm, low_hbm, x_hbm)[i]
        return pltpu.make_async_copy(src, (conv_ref, dpl_ref, e_ref, low_ref, x_ref)[i], loads.at[i])

    def mix_copy(p, slot):
        return mesh_copy(part_ref.at[p], got.at[slot], ms.at[p], mr.at[slot], tensor=p)

    def sum_copy(p, slot):
        return mesh_copy(done.at[slot], done.at[slot], ns.at[p], nr.at[slot], tensor=p)

    def edge_copy():
        return mesh_copy(edge_out, edge_in, es, er, seq=behind_seq)

    for ahead in range(1, n):
        mix_copy(lax.rem(t + ahead, n), t).start()
    for i in range(5):
        load(i).start()

    dcv_ref[0:8, :] = jnp.zeros((8, lanes), F32)
    dcv_ref[tokens + 8:, :] = jnp.zeros((8, lanes), F32)
    load(1).wait()
    tn = (((0,), (0,)), ((), ()))

    @pl.loop(0, across)
    def _(j):
        cols = pl.ds(pl.multiple_of(j * width, width), width)
        dwdt_ref[:, cols] = jnp.dot(step_ref[...], dpl_ref[:, cols], preferred_element_type=F32)

    own[...] = part_ref[t].astype(F32)
    for ahead in range(1, n):
        p = lax.rem(t + ahead, n)
        mix_copy(p, p).wait_recv()
        own[...] = own[...] + got[p].astype(F32)
    done[t] = own[...].astype(BF16)
    for ahead in range(1, n):
        sum_copy(lax.rem(t + ahead, n), t).start()

    load(0).wait()

    @pl.loop(0, pieces)
    def _(i):
        here = pl.ds(pl.multiple_of(i // across * piece, piece), piece)
        cols = pl.ds(pl.multiple_of(i % across * width, width), width)
        v = conv_ref[here, cols]
        s = 1.0 / (1.0 + jnp.exp(-v))
        conv_ref[here, cols] = s * (1.0 + v * (1.0 - s))

    for i in range(2, 5):
        load(i).wait()
    for ahead in range(1, n):
        p = lax.rem(t + ahead, n)
        sum_copy(p, p).wait_recv()

    dwx_ref[...] = jnp.zeros_like(dwx_ref)
    dconvw_ref[...] = jnp.zeros_like(dconvw_ref)

    @pl.loop(0, n)
    def _(o):
        @pl.loop(0, across)
        def _(j):
            cols = pl.ds(pl.multiple_of(j * width, width), width)
            here = pl.ds(pl.multiple_of(o * rows, rows), rows)
            mixed = lax.dot_general(done[o], wx_ref[:, cols], tn, preferred_element_type=F32)
            dcv = (e_ref[here, cols] + mixed) * conv_ref[here, cols]
            dcv_ref[pl.ds(pl.multiple_of(o * rows + 8, 8), rows), cols] = dcv
            dwx_ref[:, cols] = dwx_ref[:, cols] + jnp.dot(done[o], low_ref[here, cols], preferred_element_type=F32)

    def shifted(base, size, cols):
        span = dcv_ref[pl.ds(base, size + 8), cols]
        keep = keep_ref[pl.ds(base, size + 8), :]
        total = jnp.zeros((size, span.shape[1]), F32)
        for j in range(taps):
            late = taps - 1 - j
            total = total + taps_ref[j:j + 1, cols] * (span * keep[:, j:j + 1])[late:late + size]
        return total

    if seqs > 1:
        edge_out[...] = shifted(0, 8, slice(None))

        @pl.when(seq > 0)
        def _():
            edge_copy().start()

    @pl.loop(0, pieces)
    def _(i):
        base = pl.multiple_of(i // across * piece, piece)
        cols = pl.ds(pl.multiple_of(i % across * width, width), width)
        dx_ref[pl.ds(base, piece), cols] = shifted(pl.multiple_of(base + 8, 8), piece, cols).astype(BF16)
        here = dcv_ref[pl.ds(pl.multiple_of(base + 8, 8), piece), cols]
        keep = keep_ref[pl.ds(pl.multiple_of(base + 8, 8), piece), :]
        span = x_ref[pl.ds(base, piece + 8), cols]
        for j in range(taps):
            first = 8 - (taps - 1) + j
            tap = jnp.sum(here * keep[:, j:j + 1] * span[first:first + piece], axis=0, keepdims=True)
            dconvw_ref[j:j + 1, cols] = dconvw_ref[j:j + 1, cols] + tap
        dconvw_ref[taps:taps + 1, cols] = dconvw_ref[taps:taps + 1, cols] + jnp.sum(here, axis=0, keepdims=True)

    if seqs > 1:
        @pl.when(seq < seqs - 1)
        def _():
            edge_copy().wait_recv()
            last = shifted(tokens - 16 + 8, 16, slice(None))
            dx_ref[tokens - 16:, :] = (last + jnp.concatenate([jnp.zeros_like(edge_in), edge_in[...]], 0)).astype(BF16)

        @pl.when(seq > 0)
        def _():
            edge_copy().wait_send()

    out = pltpu.make_async_copy(dx_ref, dx_hbm, store)
    out.start()
    for ahead in range(1, n):
        p = lax.rem(t + ahead, n)
        mix_copy(p, t).wait_send()
        sum_copy(p, t).wait_send()
    out.wait()


def mixback(part, e, conv_sum, x_rows, x_low, d_pre_low, step_t, w_x, taps, keeps):
    n, seqs = lax.axis_size("tensor"), lax.axis_size("seq")
    tokens, lanes = x_low.shape
    mixed, rows = part.shape[1:]
    rank = step_t.shape[0]
    vmem, hbm = pl.BlockSpec(memory_space=pltpu.VMEM), pl.BlockSpec(memory_space=pl.ANY)
    dma = pltpu.SemaphoreType.DMA
    peers = dma((n,))
    return pl.pallas_call(
        functools.partial(mixback_kernel, n, seqs),
        out_shape=[
            jax.ShapeDtypeStruct((tokens, lanes), BF16),
            jax.ShapeDtypeStruct((mixed, lanes), F32),
            jax.ShapeDtypeStruct((rank, lanes), F32),
            jax.ShapeDtypeStruct((8, lanes), F32),
        ],
        in_specs=[vmem] + [hbm] * 5 + [vmem] * 4,
        out_specs=[hbm] + [vmem] * 3,
        scratch_shapes=[
            pltpu.VMEM((tokens, lanes), F32),
            pltpu.VMEM((tokens, lanes), F32),
            pltpu.VMEM((tokens + 8, lanes), F32),
            pltpu.VMEM((tokens, lanes), BF16),
            pltpu.VMEM((tokens, lanes), BF16),
            pltpu.VMEM((tokens, lanes), BF16),
            pltpu.VMEM((tokens + 16, lanes), F32),
            pltpu.VMEM((n, mixed, rows), BF16),
            pltpu.VMEM((mixed, rows), F32),
            pltpu.VMEM((n, mixed, rows), BF16),
            pltpu.VMEM((8, lanes), F32),
            pltpu.VMEM((8, lanes), F32),
            dma((5,)), dma, peers, peers, peers, peers, dma, dma,
        ],
        compiler_params=pltpu.CompilerParams(
            collective_id=4, has_side_effects=True, vmem_limit_bytes=60 << 20
        ),
        name="mix_backward",
    )(part, e, conv_sum, x_rows, x_low, d_pre_low, step_t, w_x, taps, keeps)


def on_device(
    hidden_in,
    teacher,
    segment_ids,
    norm_gain,
    input_projection_weight,
    conv_weight,
    conv_bias,
    xproj_weight,
    dtproj_weight,
    dt_bias,
    a_log,
    d_skip,
    output_projection_weight,
):
    tok_rows = segment_ids.shape[0]
    row_share = hidden_in.shape[0]
    model_width = hidden_in.shape[1]
    conv_taps = conv_weight.shape[0]
    chan_lanes = conv_weight.shape[1]
    back_rows = conv_taps - 1
    row_start = lax.axis_index("tensor") * row_share
    valid_mask = (segment_ids != 0).astype(jnp.float32)
    count_here = jnp.full((8, 128), jnp.sum(valid_mask))
    parts = lax.axis_size(("dp", "seq"))
    gain_tile = jnp.broadcast_to(norm_gain.astype(F32)[None], (8, norm_gain.shape[0]))
    x_cols, dt_rows = xproj_weight.shape[1], dtproj_weight.shape[0]
    w_small = jnp.concatenate(
        [
            xproj_weight.T,
            jnp.zeros((SMALL_ROWS - x_cols, chan_lanes), BF16),
            dtproj_weight,
            jnp.zeros((-(SMALL_ROWS + dt_rows) % 16, chan_lanes), BF16),
        ],
        0,
    )
    seg_float = segment_ids.astype(F32)
    prev_seg = jnp.where(lax.axis_index("seq") > 0, seg_float[:1], jnp.zeros((back_rows,), F32))
    ext_seg = jnp.concatenate([prev_seg, seg_float], 0)
    tap_keeps = []
    for offset in range(conv_taps):
        tap_keeps.append((ext_seg[offset : offset + tok_rows] == seg_float).astype(F32)[:, None])
    taps = jnp.concatenate(
        [conv_weight.astype(F32), conv_bias.astype(F32)[None], jnp.zeros((7 - conv_taps, chan_lanes), F32)], 0
    )
    x_rows, z_gate, normalized_rows, w_in, conv_sum, x_low, total, gain_rows, w_small, mixed = front(
        hidden_in,
        gain_tile,
        count_here,
        jnp.swapaxes(input_projection_weight, 0, 1),
        w_small,
        taps,
        jnp.concatenate(tap_keeps, 1),
    )
    w_out_rows, z_gate = lax.optimization_barrier((output_projection_weight.T, z_gate))
    w_out = lax.all_gather(w_out_rows, ("dp", "seq"), axis=0, tiled=True)
    total_count = total[0, 0]
    w_x = w_small[:, :x_cols].reshape(parts * x_cols, chan_lanes)
    w_dt = w_small[:, SMALL_ROWS : SMALL_ROWS + dt_rows].reshape(parts * dt_rows, chan_lanes)
    share_rows = hidden_in.astype(F32)
    full_gain = gain_rows[0]
    inv_share = lax.rsqrt(jnp.mean(share_rows * share_rows, axis=1, keepdims=True) + EPS)
    ext_x = x_rows[8 - back_rows :]
    x_float = x_low.astype(F32)
    mixed = mixed.reshape(-1, parts, SMALL_ROWS, row_share)[:, :, :x_cols]
    mixed_rows = mixed.transpose(0, 3, 1, 2).reshape(tok_rows, parts * x_cols).astype(F32)
    rank_width = w_dt.shape[0]
    state_width = (mixed_rows.shape[1] - rank_width) // 2
    step_low = mixed_rows[:, :rank_width].astype(jnp.bfloat16)
    b_in = mixed_rows[:, rank_width : rank_width + state_width]
    c_out = mixed_rows[:, rank_width + state_width :]
    pre_act = jnp.dot(step_low, w_dt, preferred_element_type=jnp.float32) + dt_bias[None]
    step_size = jax.nn.softplus(pre_act)
    decay_rates = -jnp.exp(a_log)
    same_doc = (seg_float == ext_seg[back_rows - 1 : back_rows - 1 + tok_rows]).astype(jnp.float32)
    rates = decay_rates * LOG2E
    block = 128
    stepd = jnp.where(same_doc[:, None] != 0, step_size, FAR)
    inject = step_size * x_float
    col_pair = jnp.concatenate([columns(b_in), columns(c_out)], -1)
    b_diag, c_diag = diagonal(b_in), diagonal(c_out)
    resets = jnp.sum((same_doc == 0).astype(jnp.int32).reshape(-1, block), axis=1)
    alive = (jnp.cumsum(resets) - resets == 0).astype(jnp.int32)
    y_local, marks, state_last = fwd(stepd, inject, col_pair, c_diag, rates, tb=block, unroll=8)
    reach = jnp.exp2(rates * jnp.sum(stepd, axis=0)[None])
    state_in = carried(state_last, reach, "seq", 1)
    y_rows, marks = correct(alive, y_local, stepd, c_diag, rates, marks, state_in, tb=block)
    scan_out = y_rows + d_skip[None] * x_float
    gate_act = jax.nn.silu(z_gate)
    gated_output_rows = (scan_out * gate_act).astype(jnp.bfloat16)
    valid_share = lax.dynamic_slice_in_dim(valid_mask, row_start, row_share, 0)
    total_tokens = float(tok_rows * lax.axis_size(("dp", "seq")))
    scale = (total_tokens / total_count * valid_share)[:, None]
    output, grad_out, piece, d_scan, d_z = middle(
        gated_output_rows, w_out, hidden_in, teacher, scale, z_gate, scan_out
    )
    d_wout = jnp.einsum("te,tw->we", gated_output_rows, piece, preferred_element_type=jnp.float32)
    adjoint_first = entry(alive, stepd, d_scan, col_pair, rates, tb=block)
    adjoint_in = carried(adjoint_first, reach, "seq", -1)
    ones = diagonal(jnp.ones((CH, N), F32))
    d_pre_low, d_direct, d_rank_t, d_b_part, d_c_part, a_log_part, dt_bias_part, d_skip_part = bwd(
        stepd, inject, d_scan, col_pair, b_diag, ones, rates, marks, adjoint_in,
        step_size, jax.nn.sigmoid(pre_act), x_low, d_skip[None], w_dt, tb=block, unroll=8
    )
    a_log_part = LN2 * a_log_part
    part = jnp.concatenate(
        [
            jnp.sum(d_rank_t, axis=0),
            jnp.sum(d_b_part, axis=0).reshape(tok_rows, N).T,
            jnp.sum(d_c_part, axis=0).reshape(tok_rows, N).T,
        ],
        0,
    )
    part = part.astype(BF16).reshape(part.shape[0], -1, row_share).transpose(1, 0, 2)
    edge = jnp.zeros((8, conv_taps), F32)
    d_x, d_wx, d_wdt, conv_parts = mixback(
        part, d_direct, conv_sum, x_rows, x_low, d_pre_low, step_low.T, w_x, taps,
        jnp.concatenate([edge] + [jnp.concatenate(tap_keeps, 1)] + [edge], 0),
    )
    d_wx_rank, d_wx_state = d_wx[:rank_width], d_wx[rank_width:]
    conv_weight_part, conv_bias_part = conv_parts[:conv_taps], conv_parts[conv_taps]
    small = jnp.concatenate(
        [
            d_wx_rank.reshape(parts, -1, chan_lanes),
            d_wx_state.reshape(parts, -1, chan_lanes),
            d_wdt.reshape(parts, -1, chan_lanes),
            jnp.zeros((parts, 4, chan_lanes), F32),
        ],
        1,
    )
    whole = jnp.concatenate(
        [a_log_part, conv_weight_part, conv_bias_part[None], dt_bias_part, d_skip_part, d_skip_part], 0
    )
    d_norm_share, g_in, g_small, g_whole = tail(d_x, d_z, w_in, normalized_rows, small, whole)
    g_in = jnp.swapaxes(g_in, 0, 1)
    inner_sum = jnp.sum(d_norm_share * full_gain[None] * share_rows, axis=1, keepdims=True)
    inv_cube = inv_share * inv_share * inv_share
    input_grad = (
        grad_out
        + inv_share * full_gain[None] * d_norm_share
        - share_rows * inv_cube * inner_sum / model_width
    )
    rank_here = rank_width // parts
    state_here = 2 * state_width // parts
    g_x_rank = g_small[:rank_here].T
    g_x_state = g_small[rank_here : rank_here + state_here].T
    g_dt = g_small[rank_here + state_here : rank_here + state_here + rank_here]
    g_out = lax.psum_scatter(d_wout.astype(BF16), ("dp", "seq"), scatter_dimension=0, tiled=True).astype(F32).T
    g_gain = jnp.sum(g_whole[N + conv_taps + 4 :, : norm_gain.shape[0]], axis=0) / norm_gain.astype(F32)
    g_alog, g_conv_w = g_whole[:N], g_whole[N : N + conv_taps]
    g_conv_b, g_bias, g_skip = g_whole[N + conv_taps], g_whole[N + conv_taps + 1], g_whole[N + conv_taps + 2]
    return (
        output,
        input_grad,
        g_gain,
        g_in,
        g_conv_w,
        g_conv_b,
        g_x_rank,
        g_x_state,
        g_dt,
        g_bias,
        g_alog,
        g_skip,
        g_out,
    )


def solution(mesh):
    placed = (
        P(("dp", "seq", "tensor"), None),
        P(("dp", "seq", "tensor"), None),
        P(("dp", "seq")),
        P("tensor"),
        P(("dp", "seq"), None, "tensor"),
        P(None, "tensor"),
        P("tensor"),
        P("tensor", ("dp", "seq")),
        P(("dp", "seq"), "tensor"),
        P("tensor"),
        P(None, "tensor"),
        P("tensor"),
        P("tensor", ("dp", "seq")),
    )
    return jax.shard_map(
        on_device,
        mesh=mesh,
        in_specs=placed,
        out_specs=(
            P(("dp", "seq", "tensor"), None),
            P(("dp", "seq", "tensor"), None),
            P("tensor"),
            P(("dp", "seq"), None, "tensor"),
            P(None, "tensor"),
            P("tensor"),
            P("tensor", ("dp", "seq")),
            P("tensor", ("dp", "seq")),
            P(("dp", "seq"), "tensor"),
            P("tensor"),
            P(None, "tensor"),
            P("tensor"),
            P("tensor", ("dp", "seq")),
        ),
        check_vma=False,
    )
```

```python
import functools

import jax
import jax.numpy as jnp
from jax import lax
from jax.experimental import pallas as pl
from jax.experimental.pallas import tpu as pltpu
from jax.sharding import PartitionSpec as P

EPS = 1e-05
LOG2E = 1.4426950408889634
LN2 = 0.6931471805599453
FAR = 1e30
SMALL_ROWS = 24
MESH = pl.DeviceIdType.MESH


def passed_along(x, axis, by):
    size = lax.axis_size(axis)
    pairs = [(i, i + by) for i in range(size) if 0 <= i + by < size]
    return lax.ppermute(x, axis, pairs)


def silu_slope(values):
    logistic = jax.nn.sigmoid(values)
    return logistic * (1.0 + values * (1.0 - logistic))


F32, BF16 = jnp.float32, jnp.bfloat16
N = 16
CH = 16

def fwd_kernel(rank_ref, wdt_ref, bias_ref, low_ref, keep_ref, bc_ref, cdiag_ref, rate_ref,
               y_ref, ckpt_ref, last_ref, stepd_ref, u_ref, step_ref, sig_ref, state_ref, sbf_ref, *, unroll):
    @pl.when(pl.program_id(1) == 0)
    def _():
        state_ref[...] = jnp.zeros_like(state_ref)
    ckpt_ref[0] = state_ref[...]
    pre = jnp.dot(rank_ref[...], wdt_ref[...], preferred_element_type=F32) + bias_ref[...]
    small = jnp.exp(-jnp.abs(pre))
    step = jnp.maximum(pre, 0.0) + jnp.log1p(small)
    step_ref[...] = step
    sig_ref[...] = jnp.where(pre >= 0, 1.0, small) / (1.0 + small)
    stepd_ref[...] = jnp.where(keep_ref[...] > 0, step, FAR)
    u_ref[...] = step * low_ref[...].astype(F32)
    rate = rate_ref[...]
    tb = stepd_ref.shape[0]

    def chunk(c, s):
        base = pl.multiple_of(c * CH, CH)
        bc = bc_ref[c]
        for k in range(CH):
            dec = jnp.exp2(rate * stepd_ref[pl.ds(base + k, 1), :])
            s = dec * s + bc[:, k:k + 1] * u_ref[pl.ds(base + k, 1), :]
            sbf_ref[k * N:(k + 1) * N, :] = s.astype(BF16)
        y_ref[pl.ds(base, CH), :] = jnp.dot(cdiag_ref[pl.ds(base, CH), :], sbf_ref[...], preferred_element_type=F32)
        return s

    s = lax.fori_loop(0, tb // CH, chunk, state_ref[...], unroll=unroll)
    state_ref[...] = s
    last_ref[...] = s

def fwd(rank, w_dt, bias, low, keep, bc, cdiag, rate, tb=128, w=512, unroll=1):
    t, c = low.shape
    w = min(w, c)
    grid = (c // w, t // tb)
    width = rank.shape[1]
    rows = pl.BlockSpec((tb, w), lambda j, i: (i, j))
    whole = jax.ShapeDtypeStruct((t, c), F32)
    return pl.pallas_call(
        functools.partial(fwd_kernel, unroll=unroll),
        grid=grid,
        in_specs=[
            pl.BlockSpec((tb, width), lambda j, i: (i, 0)),
            pl.BlockSpec((width, w), lambda j, i: (0, j)),
            pl.BlockSpec((1, w), lambda j, i: (0, j)),
            rows,
            pl.BlockSpec((tb, 1), lambda j, i: (i, 0)),
            pl.BlockSpec((tb // CH, N, 2 * CH), lambda j, i: (i, 0, 0)),
            pl.BlockSpec((tb, CH * N), lambda j, i: (i, 0)),
            pl.BlockSpec((N, w), lambda j, i: (0, j)),
        ],
        out_specs=[
            rows,
            pl.BlockSpec((1, N, w), lambda j, i: (i, 0, j)),
            pl.BlockSpec((N, w), lambda j, i: (0, j)),
            rows, rows, rows, rows,
        ],
        out_shape=[
            whole,
            jax.ShapeDtypeStruct((t // tb, N, c), F32),
            jax.ShapeDtypeStruct((N, c), F32),
            whole, whole, whole, whole,
        ],
        scratch_shapes=[pltpu.VMEM((N, w), F32), pltpu.VMEM((CH * N, w), BF16)],
        compiler_params=pltpu.CompilerParams(vmem_limit_bytes=48 << 20),
        name="scan_forward",
    )(rank, w_dt, bias, low, keep, bc, cdiag, rate)


def bwd_kernel(stepd_ref, u_ref, ds_ref, bc_ref, bdiag_ref, ones_ref, rate_ref, ckpt_ref, gin_ref,
               step_ref, sig_ref, low_ref, skip_ref, wdt_ref,
               dpl_ref, e_ref, rank_ref, db_ref, dc_ref, acc_ref, bias_ref, dskip_ref,
               g_ref, sbf_ref, abf_ref, rbf_ref, pb_ref, pc_ref, wb_ref, dn_ref, *, unroll):
    @pl.when(pl.program_id(1) == 0)
    def _():
        g_ref[...] = gin_ref[...]
        acc_ref[...] = jnp.zeros_like(acc_ref)
        bias_ref[...] = jnp.zeros_like(bias_ref)
        dskip_ref[...] = jnp.zeros_like(dskip_ref)

    rate = rate_ref[...]
    tb = stepd_ref.shape[0]
    nc = tb // CH

    def fold(v):
        p = v[:, 0:128]
        for q in range(1, v.shape[1] // 128):
            p = p + v[:, q * 128:(q + 1) * 128]
        return p

    sbf_ref[0:N, :] = ckpt_ref[0].astype(BF16)
    nt = (((1,), (1,)), ((), ()))
    lanes = jnp.ones((8, 128), BF16)

    def forward(c, s):
        base = pl.multiple_of(c * CH, CH)
        bc = bc_ref[c]
        for k in range(CH):
            dec = jnp.exp2(rate * stepd_ref[pl.ds(base + k, 1), :])
            s = dec * s + bc[:, k:k + 1] * u_ref[pl.ds(base + k, 1), :]
            sbf_ref[pl.ds(pl.multiple_of((base + k + 1) * N, N), N), :] = s.astype(BF16)
            pc_ref[k * N:(k + 1) * N, :] = fold(s * ds_ref[pl.ds(base + k, 1), :])
        dc = lax.dot_general(lanes, pc_ref[...].astype(BF16), nt, preferred_element_type=F32)
        dc_ref[0, pl.ds(c, 1), :] = dc[0:1]
        return s

    lax.fori_loop(0, nc, forward, ckpt_ref[0], unroll=unroll)

    def backward(c, carry):
        g, acc = carry
        c = nc - 1 - c
        base = pl.multiple_of(c * CH, CH)
        bc = bc_ref[c]
        for k in range(CH - 1, -1, -1):
            sd = stepd_ref[pl.ds(base + k, 1), :]
            adj = g + bc[:, CH + k:CH + k + 1] * ds_ref[pl.ds(base + k, 1), :]
            abf_ref[k * N:(k + 1) * N, :] = adj.astype(BF16)
            pb_ref[k * N:(k + 1) * N, :] = fold(adj * u_ref[pl.ds(base + k, 1), :])
            g = jnp.exp2(rate * sd) * adj
            before = sbf_ref[pl.ds(pl.multiple_of((base + k) * N, N), N), :].astype(F32)
            r = g * before * rate
            rbf_ref[k * N:(k + 1) * N, :] = r.astype(BF16)
            acc = acc + r * sd
        wb_ref[pl.ds(base, CH), :] = jnp.dot(bdiag_ref[pl.ds(base, CH), :], abf_ref[...], preferred_element_type=F32)
        dn_ref[pl.ds(base, CH), :] = jnp.dot(ones_ref[...], rbf_ref[...], preferred_element_type=F32)
        db = lax.dot_general(lanes, pb_ref[...].astype(BF16), nt, preferred_element_type=F32)
        db_ref[0, pl.ds(c, 1), :] = db[0:1]
        return g, acc

    g, acc = lax.fori_loop(0, nc, backward, (g_ref[...], acc_ref[...]), unroll=unroll)
    g_ref[...] = g
    acc_ref[...] = acc

    low, ds, weighted = low_ref[...].astype(F32), ds_ref[...], wb_ref[...]
    d_pre = (LN2 * dn_ref[...] + low * weighted) * sig_ref[...]
    d_pre_low = d_pre.astype(BF16)
    dpl_ref[...] = d_pre_low
    e_ref[...] = skip_ref[...] * ds + step_ref[...] * weighted
    bias_ref[...] = bias_ref[...] + jnp.sum(d_pre, axis=0, keepdims=True)
    dskip_ref[...] = dskip_ref[...] + jnp.sum(ds * low, axis=0, keepdims=True)
    rank_ref[0] = lax.dot_general(wdt_ref[...], d_pre_low, nt, preferred_element_type=F32)


def bwd(stepd, u, ds, bc, bdiag, ones, rate, ckpt, gin, step, sig, low, skip, w_dt, tb=128, w=512, unroll=1):
    t, c = stepd.shape
    w = min(w, c)
    nb = t // tb
    grid = (c // w, nb)
    rank = w_dt.shape[0]
    rows = pl.BlockSpec((tb, w), lambda j, i: (nb - 1 - i, j))
    return pl.pallas_call(
        functools.partial(bwd_kernel, unroll=unroll),
        grid=grid,
        in_specs=[
            rows, rows, rows,
            pl.BlockSpec((tb // CH, N, 2 * CH), lambda j, i: (nb - 1 - i, 0, 0)),
            pl.BlockSpec((tb, CH * N), lambda j, i: (nb - 1 - i, 0)),
            pl.BlockSpec((CH, CH * N), lambda j, i: (0, 0)),
            pl.BlockSpec((N, w), lambda j, i: (0, j)),
            pl.BlockSpec((1, N, w), lambda j, i: (nb - 1 - i, 0, j)),
            pl.BlockSpec((N, w), lambda j, i: (0, j)),
            rows, rows, rows,
            pl.BlockSpec((1, w), lambda j, i: (0, j)),
            pl.BlockSpec((rank, w), lambda j, i: (0, j)),
        ],
        out_specs=[
            rows, rows,
            pl.BlockSpec((1, rank, tb), lambda j, i: (j, 0, nb - 1 - i)),
            pl.BlockSpec((1, tb // CH, CH * N), lambda j, i: (j, nb - 1 - i, 0)),
            pl.BlockSpec((1, tb // CH, CH * N), lambda j, i: (j, nb - 1 - i, 0)),
            pl.BlockSpec((N, w), lambda j, i: (0, j)),
            pl.BlockSpec((1, w), lambda j, i: (0, j)),
            pl.BlockSpec((1, w), lambda j, i: (0, j)),
        ],
        out_shape=[
            jax.ShapeDtypeStruct((t, c), BF16),
            jax.ShapeDtypeStruct((t, c), F32),
            jax.ShapeDtypeStruct((c // w, rank, t), F32),
            jax.ShapeDtypeStruct((c // w, t // CH, CH * N), F32),
            jax.ShapeDtypeStruct((c // w, t // CH, CH * N), F32),
            jax.ShapeDtypeStruct((N, c), F32),
            jax.ShapeDtypeStruct((1, c), F32),
            jax.ShapeDtypeStruct((1, c), F32),
        ],
        scratch_shapes=[pltpu.VMEM((N, w), F32), pltpu.VMEM(((tb + 1) * N, w), BF16),
                        pltpu.VMEM((CH * N, w), BF16), pltpu.VMEM((CH * N, w), BF16), pltpu.VMEM((CH * N, 128), F32), pltpu.VMEM((CH * N, 128), F32),
                        pltpu.VMEM((tb, w), F32), pltpu.VMEM((tb, w), F32)],
        compiler_params=pltpu.CompilerParams(vmem_limit_bytes=48 << 20),
        name="scan_backward",
    )(stepd, u, ds, bc, bdiag, ones, rate, ckpt, gin, step, sig, low, skip, w_dt)


def correct_kernel(alive_ref, y_ref, stepd_ref, cdiag_ref, rate_ref, ckpt_ref, sin_ref, low_ref, skip_ref, z_ref,
                   yo_ref, ckpto_ref, gated_ref, state_ref, sbf_ref):
    i = pl.program_id(1)

    @pl.when(i == 0)
    def _():
        state_ref[...] = sin_ref[...]

    alive = alive_ref[i] != 0

    @pl.when(alive)
    def _():
        rate = rate_ref[...]
        ckpto_ref[0] = ckpt_ref[0] + state_ref[...]

        def chunk(c, s):
            base = pl.multiple_of(c * CH, CH)
            for k in range(CH):
                s = jnp.exp2(rate * stepd_ref[pl.ds(base + k, 1), :]) * s
                sbf_ref[k * N:(k + 1) * N, :] = s.astype(BF16)
            yo_ref[pl.ds(base, CH), :] = y_ref[pl.ds(base, CH), :] + jnp.dot(
                cdiag_ref[pl.ds(base, CH), :], sbf_ref[...], preferred_element_type=F32
            )
            return s

        state_ref[...] = lax.fori_loop(0, y_ref.shape[0] // CH, chunk, state_ref[...], unroll=8)

    @pl.when(jnp.logical_not(alive))
    def _():
        yo_ref[...] = y_ref[...]
        ckpto_ref[...] = ckpt_ref[...]

    total = yo_ref[...] + skip_ref[...] * low_ref[...].astype(F32)
    z = z_ref[...]
    yo_ref[...] = total
    gated_ref[...] = (total * (z / (1.0 + jnp.exp(-z)))).astype(BF16)


def correct(alive, y, stepd, cdiag, rate, ckpt, state_in, low, skip, z, tb=128, w=512):
    t, c = stepd.shape
    w = min(w, c)
    rows = pl.BlockSpec((tb, w), lambda j, i, _: (i, j))
    lanes = pl.BlockSpec((N, w), lambda j, i, _: (0, j))
    marks = pl.BlockSpec((1, N, w), lambda j, i, _: (i, 0, j))
    return pl.pallas_call(
        correct_kernel,
        grid_spec=pltpu.PrefetchScalarGridSpec(
            num_scalar_prefetch=1,
            grid=(c // w, t // tb),
            in_specs=[rows, rows, pl.BlockSpec((tb, CH * N), lambda j, i, _: (i, 0)), lanes, marks, lanes,
                      rows, pl.BlockSpec((1, w), lambda j, i, _: (0, j)), rows],
            out_specs=[rows, marks, rows],
            scratch_shapes=[pltpu.VMEM((N, w), F32), pltpu.VMEM((CH * N, w), BF16)],
        ),
        out_shape=[jax.ShapeDtypeStruct((t, c), F32), jax.ShapeDtypeStruct(ckpt.shape, F32),
                   jax.ShapeDtypeStruct((t, c), BF16)],
        compiler_params=pltpu.CompilerParams(vmem_limit_bytes=48 << 20),
        name="scan_correct",
    )(alive, y, stepd, cdiag, rate, ckpt, state_in, low, skip, z)


def entry_kernel(alive_ref, stepd_ref, ds_ref, bc_ref, rate_ref, g_ref):
    i = pl.program_id(1)

    @pl.when(i == 0)
    def _():
        g_ref[...] = jnp.zeros_like(g_ref)

    @pl.when(alive_ref[pl.num_programs(1) - 1 - i] != 0)
    def _():
        rate = rate_ref[...]
        nc = stepd_ref.shape[0] // CH

        def chunk(c, g):
            c = nc - 1 - c
            base = pl.multiple_of(c * CH, CH)
            bc = bc_ref[c]
            for k in range(CH - 1, -1, -1):
                adj = g + bc[:, CH + k:CH + k + 1] * ds_ref[pl.ds(base + k, 1), :]
                g = jnp.exp2(rate * stepd_ref[pl.ds(base + k, 1), :]) * adj
            return g

        g_ref[...] = lax.fori_loop(0, nc, chunk, g_ref[...], unroll=8)


def entry(alive, stepd, ds, bc, rate, tb=128, w=512):
    t, c = stepd.shape
    w = min(w, c)
    nb = t // tb
    rows = pl.BlockSpec((tb, w), lambda j, i, _: (nb - 1 - i, j))
    lanes = pl.BlockSpec((N, w), lambda j, i, _: (0, j))
    return pl.pallas_call(
        entry_kernel,
        grid_spec=pltpu.PrefetchScalarGridSpec(
            num_scalar_prefetch=1,
            grid=(c // w, nb),
            in_specs=[rows, rows, pl.BlockSpec((tb // CH, N, 2 * CH), lambda j, i, _: (nb - 1 - i, 0, 0)), lanes],
            out_specs=lanes,
        ),
        out_shape=jax.ShapeDtypeStruct((N, c), F32),
        compiler_params=pltpu.CompilerParams(vmem_limit_bytes=48 << 20),
        name="scan_entry",
    )(alive, stepd, ds, bc, rate)


def carried(local, reach, axis, by):
    found = jnp.zeros_like(local)
    for turn in range(lax.axis_size(axis) - 1):
        found = passed_along(local if turn == 0 else local + reach() * found, axis, by)
    return found


def columns(values):
    tokens = values.shape[0]
    return values.reshape(tokens // CH, CH, N).transpose(0, 2, 1)


def diagonal(values):
    tokens = values.shape[0]
    mine = jnp.arange(CH * N)[None] // N == jnp.arange(tokens)[:, None] % CH
    return jnp.where(mine, jnp.tile(values.astype(BF16), (1, CH)), 0)


def mesh_copy(src, dst, send, recv, **where):
    return pltpu.make_async_remote_copy(
        src_ref=src, dst_ref=dst, send_sem=send, recv_sem=recv, device_id=where, device_id_type=MESH
    )


def place():
    dp, seq, mine = lax.axis_index("dp"), lax.axis_index("seq"), lax.axis_index("tensor")
    return dp, seq, mine


def tail_kernel(n, dps, seqs, tile, lag, dx_ref, dz_ref, w_hbm, nrm_ref, sm_ref, all_ref,
                dn_ref, gin_ref, gs_ref, ga_ref,
                gacc, gsend, grecv, all_mine,
                zr, zl, w_ref, loads, one_send, one_recv, two_recv, sm_one, sm_two, all_one, all_two,
                r_send, r_recv, l_send, l_recv, w1s, w1r, w2s, w2r, s1s, s1r, s2s, s2r, a1s, a1r, a2s, a2r, gs, gr):
    dp, seq, t = place()
    core, hi = dp % 2, dp // 2
    chips = dps // 2 * seqs
    chip = hi * seqs + seq
    rows = dn_ref.shape[0]
    wide = dn_ref.shape[1]
    wrows = gin_ref.shape[1]
    subs = wide // tile

    def owner(q, c):
        return (q // seqs * 2 + c) * seqs + q % seqs

    def to_chip(q):
        return dict(dp=q // seqs * 2 + core, seq=q % seqs)

    barrier = pltpu.get_barrier_semaphore()
    pl.semaphore_signal(barrier, inc=1, device_id=dict(dp=hi * 2 + 1 - core), device_id_type=MESH)
    for step in range(1, chips):
        q = lax.rem(chip + step, chips)
        pl.semaphore_signal(barrier, inc=1, device_id=to_chip(q), device_id_type=MESH)

    for ahead in range(1, n):
        pl.semaphore_signal(barrier, inc=1, device_id=dict(tensor=lax.rem(t + ahead, n)), device_id_type=MESH)
    pl.semaphore_wait(barrier, chips + n - 1)
    gacc[...] = jnp.zeros_like(gacc)

    partner = dict(dp=hi * 2 + 1 - core)
    right, left = dict(tensor=lax.rem(t + 1, n)), dict(tensor=lax.rem(t + n - 1, n))

    def r_copy(i):
        return mesh_copy(zr.at[i], zr.at[i], r_send.at[i], r_recv.at[i], **right)

    def l_copy(i):
        return mesh_copy(zl.at[i], zl.at[i], l_send.at[i], l_recv.at[i], **left)

    def w1_copy(q):
        return mesh_copy(one_send.at[q], one_recv.at[q], w1s.at[q], w1r.at[q], **partner)

    def w2_copy(q, slot):
        return mesh_copy(one_recv.at[q], two_recv.at[slot], w2s.at[q], w2r.at[slot], **to_chip(q))

    def s1_copy(q):
        return mesh_copy(sm_ref.at[owner(q, 1 - core)], sm_one.at[q], s1s.at[q], s1r.at[q], **partner)

    def s2_copy(q, slot):
        return mesh_copy(sm_one.at[q], sm_two.at[slot], s2s.at[q], s2r.at[slot], **to_chip(q))

    def a1_copy():
        return mesh_copy(all_mine, all_one, a1s, a1r, **partner)

    def a2_copy(q, slot):
        return mesh_copy(all_one, all_two.at[slot], a2s.at[q], a2r.at[slot], **to_chip(q))

    def g_copy(p, slot):
        return mesh_copy(gsend.at[p], grecv.at[slot], gs.at[p], gr.at[slot], tensor=p)

    def cols_of(sub):
        return pl.ds(pl.multiple_of(sub * tile, tile), tile)

    def load(sub):
        ref = w_ref.at[:, cols_of(sub), :]
        return pltpu.make_async_copy(w_hbm.at[:, cols_of(sub), :], ref, loads.at[sub])

    def partial_tile(o, sub):
        here = pl.ds(pl.multiple_of(o * rows, rows), rows)
        cols = cols_of(sub)
        nt = (((1,), (1,)), ((), ()))
        block = lax.dot_general(
            dx_ref[here, :], w_ref[0, cols, :], nt, preferred_element_type=F32
        ) + lax.dot_general(dz_ref[here, :], w_ref[1, cols, :], nt, preferred_element_type=F32)
        scaled = block * nrm_ref[here, cols].astype(F32)
        gacc[:, cols] = gacc[:, cols] + jnp.sum(scaled.reshape(rows // 8, 8, tile), axis=0)
        return block

    def weight_rows(p, k):
        cols = pl.ds(pl.multiple_of(p * wrows, wrows), wrows)
        tn = (((0,), (0,)), ((), ()))
        d_ref = dx_ref if k == 0 else dz_ref
        return lax.dot_general(nrm_ref[:, cols], d_ref[...], tn, preferred_element_type=F32)

    @pl.loop(0, subs)
    def _(sub):
        load(sub).start()

    for q in range(chips):
        s1_copy(q).start()

    def stream(i, limit, start, buf, copy, owner_of):
        @pl.when(jnp.logical_and(i >= 0, i < limit))
        def _():
            block = partial_tile(owner_of(i // subs), i % subs)

            @pl.when(start)
            def _():
                buf[i] = block.astype(BF16)

            @pl.when(jnp.logical_not(start))
            def _():
                copy(i).wait_recv()
                buf[i] = (block + buf[i].astype(F32)).astype(BF16)

            copy(i).start()

    def step(g, _):
        @pl.when(g < subs)
        def _():
            load(g).wait()

        stream(g - lag * t, (n - 1 - t) * subs, t == 0, zr, r_copy, lambda k: n - 1 - k)
        stream(g - lag * (n - 1 - t), t * subs, t == n - 1, zl, l_copy, lambda k: k)

        @pl.when(g < chips)
        def _():
            for k in range(2):
                one_send[g, k] = weight_rows(owner(g, 1 - core), k).astype(BF16)
            w1_copy(g).start()

        @pl.when(jnp.logical_and(g >= chips, g < 2 * chips - 1))
        def _():
            q = lax.rem(chip + 1 + g - chips, chips)
            w1_copy(q).wait_recv()
            for k in range(2):
                one_recv[q, k] = (weight_rows(owner(q, core), k) + one_recv[q, k].astype(F32)).astype(BF16)
            w2_copy(q, chip).start()

        @pl.when(g == 2 * chips - 1)
        def _():
            for q in range(chips):
                s1_copy(q).wait_recv()
                sm_one[q] = sm_one[q] + sm_ref[owner(q, core)]
            for ahead in range(1, chips):
                q = lax.rem(chip + ahead, chips)
                s2_copy(q, chip).start()
            w1_copy(chip).wait_recv()
            for k in range(2):
                gin_ref[k] = weight_rows(owner(chip, core), k) + one_recv[chip, k].astype(F32)

        @pl.when(jnp.logical_and(g >= 2 * chips, g < 2 * chips + subs))
        def _():
            dn_ref[:, cols_of(g - 2 * chips)] = partial_tile(t, g - 2 * chips)

        return 0

    steps = max((n - 1) * max(subs, lag), 2 * chips + subs)
    lax.fori_loop(0, steps, step, 0)

    share = wide // n
    for p in range(n):
        gsend[p] = gacc[:, p * share:(p + 1) * share]
    for ahead in range(1, n):
        g_copy(lax.rem(t + ahead, n), t).start()

    @pl.loop(0, subs)
    def _(s):
        cols = cols_of(s)

        @pl.when(t > 0)
        def _():
            i = (n - 1 - t) * subs + s
            r_copy(i).wait_recv()
            dn_ref[:, cols] = dn_ref[:, cols] + zr[i].astype(F32)

        @pl.when(t < n - 1)
        def _():
            i = t * subs + s
            l_copy(i).wait_recv()
            dn_ref[:, cols] = dn_ref[:, cols] + zl[i].astype(F32)

    plain = all_ref.shape[0]
    all_mine[0:plain, :] = all_ref[...]
    all_mine[plain:, :] = jnp.zeros((8, all_mine.shape[1]), F32)
    all_mine[plain:, 0:share] = gsend[t]
    for ahead in range(1, n):
        p = lax.rem(t + ahead, n)
        g_copy(p, p).wait_recv()
        all_mine[plain:, 0:share] = all_mine[plain:, 0:share] + grecv[p]
    a1_copy().start()
    gs_ref[...] = sm_one[chip]
    for ahead in range(1, chips):
        q = lax.rem(chip + ahead, chips)
        s2_copy(q, q).wait_recv()
        gs_ref[...] = gs_ref[...] + sm_two[q]
    a1_copy().wait_recv()
    all_one[...] = all_one[...] + all_mine[...]
    for ahead in range(1, chips):
        a2_copy(lax.rem(chip + ahead, chips), chip).start()
    ga_ref[...] = all_one[...]
    for ahead in range(1, chips):
        q = lax.rem(chip + ahead, chips)
        w2_copy(q, q).wait_recv()
        gin_ref[...] = gin_ref[...] + two_recv[q].astype(F32)
    for ahead in range(1, chips):
        q = lax.rem(chip + ahead, chips)
        a2_copy(q, q).wait_recv()
        ga_ref[...] = ga_ref[...] + all_two[q]

    for q in range(chips):
        s1_copy(q).wait_send()
        w1_copy(q).wait_send()
    a1_copy().wait_send()
    for ahead in range(1, n):
        g_copy(lax.rem(t + ahead, n), t).wait_send()
    for ahead in range(1, chips):
        q = lax.rem(chip + ahead, chips)
        s2_copy(q, chip).wait_send()
        a2_copy(q, chip).wait_send()
        w2_copy(q, chip).wait_send()

    @pl.loop(0, (n - 1) * subs)
    def _(i):
        @pl.when(i < (n - 1 - t) * subs)
        def _():
            r_copy(i).wait_send()

        @pl.when(i < t * subs)
        def _():
            l_copy(i).wait_send()


def tail(dx, dz, w_full, normed, small, whole):
    n, dps, seqs = (lax.axis_size(axis) for axis in ("tensor", "dp", "seq"))
    chips = dps // 2 * seqs
    rows = dx.shape[0] // n
    wide, lanes = w_full.shape[1], w_full.shape[2]
    wrows = wide // (dps * seqs)
    tile = 256
    subs = wide // tile
    hops = (n - 1) * subs
    vmem, hbm = pl.BlockSpec(memory_space=pltpu.VMEM), pl.BlockSpec(memory_space=pl.ANY)
    dma = pltpu.SemaphoreType.DMA
    few = dma((chips,))
    return pl.pallas_call(
        functools.partial(tail_kernel, n, dps, seqs, tile, 2),
        out_shape=[
            jax.ShapeDtypeStruct((rows, wide), F32),
            jax.ShapeDtypeStruct((2, wrows, lanes), F32),
            jax.ShapeDtypeStruct(small.shape[1:], F32),
            jax.ShapeDtypeStruct((whole.shape[0] + 8, lanes), F32),
        ],
        in_specs=[vmem] * 2 + [hbm] + [vmem] * 3,
        out_specs=[vmem] * 4,
        scratch_shapes=[
            pltpu.VMEM((8, wide), F32),
            pltpu.VMEM((n, 8, wide // n), F32),
            pltpu.VMEM((n, 8, wide // n), F32),
            pltpu.VMEM((whole.shape[0] + 8, lanes), F32),
            pltpu.VMEM((hops, rows, tile), BF16),
            pltpu.VMEM((hops, rows, tile), BF16),
            pltpu.VMEM((2, wide, lanes), BF16),
            dma((subs,)),
            pltpu.VMEM((chips, 2, wrows, lanes), BF16),
            pltpu.VMEM((chips, 2, wrows, lanes), BF16),
            pltpu.VMEM((chips, 2, wrows, lanes), BF16),
            pltpu.VMEM((chips,) + small.shape[1:], F32),
            pltpu.VMEM((chips,) + small.shape[1:], F32),
            pltpu.VMEM((whole.shape[0] + 8, lanes), F32),
            pltpu.VMEM((chips, whole.shape[0] + 8, lanes), F32),
            dma((hops,)), dma((hops,)), dma((hops,)), dma((hops,)),
            few, few, few, few, few, few, few, few, dma, dma, few, few, dma((n,)), dma((n,)),
        ],
        compiler_params=pltpu.CompilerParams(
            collective_id=2, has_side_effects=True, vmem_limit_bytes=60 << 20
        ),
        name="tail_sums",
    )(dx, dz, w_full, normed, small, whole)


def mid_kernel(n, tile, lag, gated_ref, w_ref, hid_ref, tea_ref, scale_ref, z_hbm, scan_hbm,
               out_ref, go_ref, dwo_hbm, dscan_hbm, dz_hbm,
               zr, zl, dwo_ref, part_ref, piece_ref, z_ref, scan_ref, acc_ref, dz_ref, loads, stores, wstores,
               r_send, r_recv, l_send, l_recv, ar_send, ar_recv, al_send, al_recv):
    t = lax.axis_index("tensor")
    rows, wide = hid_ref.shape
    tokens, lanes = acc_ref.shape
    waves = wide // tile
    right, left = dict(tensor=lax.rem(t + 1, n)), dict(tensor=lax.rem(t + n - 1, n))

    barrier = pltpu.get_barrier_semaphore()
    for peer in (right, left):
        pl.semaphore_signal(barrier, inc=1, device_id=peer, device_id_type=MESH)
    pl.semaphore_wait(barrier, 2)

    def load(i):
        return pltpu.make_async_copy((z_hbm, scan_hbm)[i], (z_ref, scan_ref)[i], loads.at[i])

    for i in range(2):
        load(i).start()

    def r_copy(i):
        return mesh_copy(zr.at[i], zr.at[i], r_send.at[i], r_recv.at[i], **right)

    def l_copy(i):
        return mesh_copy(zl.at[i], zl.at[i], l_send.at[i], l_recv.at[i], **left)

    def rows_of(o):
        return pl.ds(pl.multiple_of(o * rows, rows), rows)

    def cols_of(w):
        return pl.ds(pl.multiple_of(w * tile, tile), tile)

    def ar_copy(o, w):
        ref = piece_ref.at[rows_of(o), cols_of(w)]
        return mesh_copy(ref, ref, ar_send.at[o * waves + w], ar_recv.at[o * waves + w], **right)

    def al_copy(o, w):
        ref = piece_ref.at[rows_of(o), cols_of(w)]
        return mesh_copy(ref, ref, al_send.at[o * waves + w], al_recv.at[o * waves + w], **left)

    def stream(i, hops, start, buf, copy, owner_of):
        w, k = i // n, i % n

        @pl.when(jnp.logical_and(jnp.logical_and(i >= 0, w < waves), k < hops))
        def _():
            slot = w * (n - 1) + k
            here = part_ref[rows_of(owner_of(k)), cols_of(w)]

            @pl.when(start)
            def _():
                buf[slot] = here.astype(BF16)

            @pl.when(jnp.logical_not(start))
            def _():
                copy(slot).wait_recv()
                buf[slot] = (here + buf[slot].astype(F32)).astype(BF16)

            copy(slot).start()

    def ready(o):
        from_left = jnp.where(o > 0, n - 1 - o + lag * o, 0)
        from_right = jnp.where(o < n - 1, o + lag * (n - 1 - o), 0)
        return jnp.maximum(from_left, from_right)

    def host_ready(o):
        return max((n - 1 - o + lag * o) * (o > 0), (o + lag * (n - 1 - o)) * (o < n - 1))

    def finish(w):
        cols = cols_of(w)
        go_ref[:, cols] = part_ref[rows_of(t), cols]

        @pl.when(t > 0)
        def _():
            slot = w * (n - 1) + n - 1 - t
            r_copy(slot).wait_recv()
            go_ref[:, cols] = go_ref[:, cols] + zr[slot].astype(F32)

        @pl.when(t < n - 1)
        def _():
            slot = w * (n - 1) + t
            l_copy(slot).wait_recv()
            go_ref[:, cols] = go_ref[:, cols] + zl[slot].astype(F32)

        result = hid_ref[:, cols].astype(F32) + go_ref[:, cols]
        out_ref[:, cols] = result.astype(BF16)
        grad = scale_ref[...] * (result - tea_ref[:, cols].astype(F32))
        go_ref[:, cols] = grad
        piece_ref[rows_of(t), cols] = grad.astype(BF16)

        @pl.when(t < n - 1)
        def _():
            ar_copy(t, w).start()

        @pl.when(t > 0)
        def _():
            al_copy(t, w).start()

    def stored(i, o):
        src = (acc_ref, dz_ref)[i].at[rows_of(o), :]
        return pltpu.make_async_copy(src, (dscan_hbm, dz_hbm)[i].at[rows_of(o), :], stores.at[i, o])

    def stored_weight(w):
        here = pl.ds(pl.multiple_of(w * tile, tile), tile)
        return pltpu.make_async_copy(dwo_ref.at[w], dwo_hbm.at[here, :], wstores.at[w])

    def gate(o):
        z = z_ref[rows_of(o), :]
        s = 1.0 / (1.0 + jnp.exp(-z))
        z_ref[rows_of(o), :] = z * s
        scan_ref[rows_of(o), :] = scan_ref[rows_of(o), :] * (s * (1.0 + z * (1.0 - s)))

    def backward(w):
        tn = (((0,), (0,)), ((), ()))
        dwo_ref[w] = lax.dot_general(
            piece_ref[:, cols_of(w)], gated_ref[...], tn, preferred_element_type=F32
        ).astype(BF16)
        stored_weight(w).start()

        @pl.loop(0, n)
        def _(o):
            here = rows_of(o)
            d_gated = jnp.dot(piece_ref[here, cols_of(w)], w_ref[cols_of(w), :], preferred_element_type=F32)

            @pl.when(w == 0)
            def _():
                acc_ref[here, :] = d_gated

            @pl.when(jnp.logical_and(w > 0, w < waves - 1))
            def _():
                acc_ref[here, :] = acc_ref[here, :] + d_gated

            @pl.when(w == waves - 1)
            def _():
                total = acc_ref[here, :] + d_gated
                acc_ref[here, :] = total * z_ref[here, :]
                dz_ref[here, :] = (total * scan_ref[here, :]).astype(BF16)
                stored(0, o).start()
                stored(1, o).start()

    arrived = jnp.int32(0)
    for o in range(n):
        arrived = jnp.maximum(arrived, host_ready(o) + lag * jnp.abs(t - o))

    def step(g, _):
        @pl.when(jnp.logical_and(g % n == 0, g < n * waves))
        def _():
            cols = cols_of(g // n)
            nt = (((1,), (1,)), ((), ()))

            @pl.loop(0, n)
            def _(o):
                part_ref[rows_of(o), cols] = lax.dot_general(
                    gated_ref[rows_of(o), :], w_ref[cols, :], nt, preferred_element_type=F32
                )

        stream(g - lag * t, n - 1 - t, t == 0, zr, r_copy, lambda k: n - 1 - k)
        stream(g - lag * (n - 1 - t), t, t == n - 1, zl, l_copy, lambda k: k)

        own = g - ready(t)

        @pl.when(jnp.logical_and(own >= 0, jnp.logical_and(own % n == 0, own // n < waves)))
        def _():
            finish(own // n)

        @pl.loop(0, n)
        def _(o):
            i = g - ready(o) - lag * jnp.abs(t - o)
            w = i // n

            @pl.when(jnp.logical_and(o != t, jnp.logical_and(i >= 0, jnp.logical_and(i % n == 0, w < waves))))
            def _():
                @pl.when(o < t)
                def _():
                    ar_copy(o, w).wait_recv()

                    @pl.when(t < n - 1)
                    def _():
                        ar_copy(o, w).start()

                @pl.when(o > t)
                def _():
                    al_copy(o, w).wait_recv()

                    @pl.when(t > 0)
                    def _():
                        al_copy(o, w).start()

        @pl.when(g == 1)
        def _():
            for i in range(2):
                load(i).wait()

        @pl.when(jnp.logical_and(g >= 1, g <= n))
        def _():
            gate(g - 1)

        done = g - arrived

        @pl.when(jnp.logical_and(done >= 0, jnp.logical_and(done % n == 0, done // n < waves)))
        def _():
            backward(done // n)

        return 0

    steps = max(host_ready(o) + lag * abs(o - d) for o in range(n) for d in range(n)) + n * (waves - 1) + 1
    lax.fori_loop(0, max(steps, n + 1), step, 0)

    @pl.loop(0, (n - 1) * waves)
    def _(i):
        @pl.when(i % (n - 1) < n - 1 - t)
        def _():
            r_copy(i).wait_send()

        @pl.when(i % (n - 1) < t)
        def _():
            l_copy(i).wait_send()

    @pl.loop(0, n * waves)
    def _(i):
        o, w = i // waves, i % waves

        @pl.when(jnp.logical_and(o <= t, t < n - 1))
        def _():
            ar_copy(o, w).wait_send()

        @pl.when(jnp.logical_and(o >= t, t > 0))
        def _():
            al_copy(o, w).wait_send()

    @pl.loop(0, waves)
    def _(w):
        stored_weight(w).wait()

    @pl.loop(0, n)
    def _(o):
        stored(0, o).wait()
        stored(1, o).wait()


def middle(gated, w_out, hidden, teacher, scale, z_gate, scan_out):
    n = lax.axis_size("tensor")
    rows, wide = hidden.shape
    tokens, lanes = gated.shape
    tile = 256
    waves = wide // tile
    hops = (n - 1) * waves
    vmem, hbm = pl.BlockSpec(memory_space=pltpu.VMEM), pl.BlockSpec(memory_space=pl.ANY)
    dma = pltpu.SemaphoreType.DMA
    return pl.pallas_call(
        functools.partial(mid_kernel, n, tile, 2),
        out_shape=[
            jax.ShapeDtypeStruct((rows, wide), BF16),
            jax.ShapeDtypeStruct((rows, wide), F32),
            jax.ShapeDtypeStruct((wide, lanes), BF16),
            jax.ShapeDtypeStruct((tokens, lanes), F32),
            jax.ShapeDtypeStruct((tokens, lanes), BF16),
        ],
        in_specs=[vmem] * 5 + [hbm] * 2,
        out_specs=[vmem] * 2 + [hbm] * 3,
        scratch_shapes=[
            pltpu.VMEM((hops, rows, tile), BF16),
            pltpu.VMEM((hops, rows, tile), BF16),
            pltpu.VMEM((waves, tile, lanes), BF16),
            pltpu.VMEM((tokens, wide), F32),
            pltpu.VMEM((tokens, wide), BF16),
            pltpu.VMEM((tokens, lanes), F32),
            pltpu.VMEM((tokens, lanes), F32),
            pltpu.VMEM((tokens, lanes), F32),
            pltpu.VMEM((tokens, lanes), BF16),
            dma((2,)), dma((2, n)), dma((waves,)),
            dma((hops,)), dma((hops,)), dma((hops,)), dma((hops,)),
            dma((n * waves,)), dma((n * waves,)), dma((n * waves,)), dma((n * waves,)),
        ],
        compiler_params=pltpu.CompilerParams(
            collective_id=1, has_side_effects=True, vmem_limit_bytes=60 << 20
        ),
        name="middle",
    )(gated, w_out, hidden, teacher, scale, z_gate, scan_out)


def front_kernel(n, dps, seqs, subs, lag, hid_ref, gain_ref, seg_ref, win_ref, wsm_ref, taps_ref, keep_ref,
                 x_out, z_out, nrm_out, w_out, conv_out, low_out, total_ref, gfull, ws_ref, mixed_ref,
                 rows_ref, gain_tile, cnt_tile, grecv, cnt_one, cnt_two, x_ref, z_ref, nrm_ref, w_ref, conv_ref, low_ref,
                 mix_send, mix_recv, mix_own, outs, ms, mr, ns, nr,
                 ar_send, ar_recv, al_send, al_recv, gs, gr, c1s, c1r, c2s, c2r, hs, hr, ls,
                 chip_send, chip_recv, core_send, core_recv):
    dp, seq, t = place()
    core, hi = dp % 2, dp // 2
    chips = dps // 2 * seqs
    chip = hi * seqs + seq
    rows, wide = hid_ref.shape
    part = rows // subs
    share = wide // n
    wrows = win_ref.shape[1]
    tile = 512
    gap = max(subs, lag)
    partner = dict(dp=hi * 2 + 1 - core)
    right, left = dict(tensor=lax.rem(t + 1, n)), dict(tensor=lax.rem(t + n - 1, n))

    def owner(q, c):
        return (q // seqs * 2 + c) * seqs + q % seqs

    def to_chip(q):
        return dict(dp=q // seqs * 2 + core, seq=q % seqs)

    barrier = pltpu.get_barrier_semaphore()
    pl.semaphore_signal(barrier, inc=1, device_id=partner, device_id_type=MESH)
    for ahead in range(1, chips):
        pl.semaphore_signal(barrier, inc=1, device_id=to_chip(lax.rem(chip + ahead, chips)), device_id_type=MESH)
    for ahead in range(1, n):
        pl.semaphore_signal(barrier, inc=1, device_id=dict(tensor=lax.rem(t + ahead, n)), device_id_type=MESH)
    pl.semaphore_wait(barrier, chips + n - 1)

    def at(o, s):
        return pl.ds(pl.multiple_of(o * rows + s * part, part), part)

    def ar_copy(o, s):
        ref = rows_ref.at[at(o, s), :]
        return mesh_copy(ref, ref, ar_send.at[o * subs + s], ar_recv.at[o * subs + s], **right)

    def al_copy(o, s):
        ref = rows_ref.at[at(o, s), :]
        return mesh_copy(ref, ref, al_send.at[o * subs + s], al_recv.at[o * subs + s], **left)

    def g_copy(p, slot):
        return mesh_copy(gain_tile, grecv.at[slot], gs.at[p], gr.at[slot], tensor=p)

    def block(kind, p):
        if kind == 0:
            return w_ref.at[:, pl.ds(pl.multiple_of(p * wrows, wrows), wrows), :]
        return ws_ref.at[p]

    stored = (win_ref, wsm_ref)

    def chip_copy(kind, q, p):
        return mesh_copy(stored[kind], block(kind, p), chip_send.at[kind, q], chip_recv.at[kind, p], **to_chip(q))

    def core_copy(kind, p, own):
        src = stored[kind] if own else block(kind, p)
        return mesh_copy(src, block(kind, p), core_send.at[kind, p], core_recv.at[kind, p], **partner)

    mine = owner(chip, core)

    def count_one():
        return mesh_copy(cnt_tile, cnt_one, c1s, c1r, **partner)

    def count_two(q, slot):
        return mesh_copy(cnt_one, cnt_two.at[slot], c2s.at[q], c2r.at[slot], **to_chip(q))

    def edge_copy():
        last = x_ref.at[pl.ds(x_ref.shape[0] - 8, 8), :]
        return mesh_copy(last, x_ref.at[pl.ds(0, 8), :], hs, hr, seq=lax.rem(seq + 1, seqs))

    def mix_copy(p, slot):
        return mesh_copy(mix_send.at[p], mix_recv.at[slot], ms.at[p], mr.at[slot], tensor=p)

    def sum_copy(p, slot):
        return mesh_copy(mixed_ref.at[slot], mixed_ref.at[slot], ns.at[p], nr.at[slot], tensor=p)

    def written(i):
        src = (w_ref, nrm_ref, z_ref, x_ref, conv_ref, low_ref)[i]
        return pltpu.make_async_copy(src, (w_out, nrm_out, z_out, x_out, conv_out, low_out)[i], outs.at[i])

    def local_copy():
        return pltpu.make_async_copy(wsm_ref, block(1, mine), ls)

    gain_tile[...] = jnp.broadcast_to(gain_ref[...].astype(F32), gain_tile.shape)
    cnt_tile[...] = jnp.full(cnt_tile.shape, jnp.sum((seg_ref[...] != 0).astype(F32)))
    for ahead in range(1, n):
        g_copy(lax.rem(t + ahead, n), t).start()
    count_one().start()
    rows_ref[pl.ds(pl.multiple_of(t * rows, rows), rows), :] = hid_ref[...]

    @pl.loop(0, subs)
    def _(s):
        @pl.when(t < n - 1)
        def _():
            ar_copy(t, s).start()

        @pl.when(t > 0)
        def _():
            al_copy(t, s).start()

    def share_out(kind):
        for ahead in range(1, chips):
            chip_copy(kind, lax.rem(chip + ahead, chips), mine).start()
        core_copy(kind, mine, True).start()

    share_out(1)
    share_out(0)
    local_copy().start()
    w_ref[:, pl.ds(pl.multiple_of(mine * wrows, wrows), wrows), :] = win_ref[...]

    gfull[...] = jnp.zeros_like(gfull)
    for ahead in range(1, n):
        p = lax.rem(t + ahead, n)
        g_copy(p, p).wait_recv()
    grecv[t] = gain_tile[...]
    for p in range(n):
        gfull[:, p * share:(p + 1) * share] = grecv[p]
    count_one().wait_recv()
    count_one().wait_send()
    cnt_one[...] = cnt_one[...] + cnt_tile[...]
    for ahead in range(1, chips):
        count_two(lax.rem(chip + ahead, chips), chip).start()

    def normalize(o):
        @pl.loop(0, subs)
        def _(s):
            here = at(o, s)
            values = rows_ref[here, :].astype(F32)
            inv = lax.rsqrt(jnp.mean(values * values, axis=1, keepdims=True) + EPS)
            nrm_ref[here, :] = (values * inv * gfull[0:1, :]).astype(BF16)

    def project(o):
        here = pl.ds(pl.multiple_of(o * rows, rows), rows)
        for k, dst in enumerate((x_ref, z_ref)):
            lanes = dst.shape[1]
            width = min(tile, lanes)
            there = pl.ds(pl.multiple_of(o * rows + 8 - 8 * k, 8), rows)

            @pl.loop(0, lanes // width)
            def _(j):
                cols = pl.ds(pl.multiple_of(j * width, width), width)
                dst[there, cols] = jnp.dot(nrm_ref[here, :], w_ref[k, :, cols], preferred_element_type=F32)

    def turn(d, o):
        final = jnp.where(o == 0, (n - 1) * gap + 1, (n - 2 - o) * gap + lag)
        return jnp.where(d == n - 1, final, (d - o) * gap)

    weights_at = (n - 1) * gap

    def step(g, _):
        @pl.when(g == 0)
        def _():
            normalize(t)

        @pl.when(g == weights_at)
        def _():
            for kind in (1, 0):
                for ahead in range(1, chips):
                    q = lax.rem(chip + ahead, chips)
                    chip_copy(kind, q, owner(q, core)).wait_recv()
                    core_copy(kind, owner(q, core), False).start()
            for kind in (1, 0):
                for q in range(chips):
                    core_copy(kind, owner(q, 1 - core), True).wait_recv()
            project(t)

        @pl.loop(0, n)
        def _(o):
            s_right = g - turn(t, o)
            s_left = g - turn(n - 1 - t, n - 1 - o)

            @pl.when(jnp.logical_and(o < t, jnp.logical_and(s_right >= 0, s_right < subs)))
            def _():
                ar_copy(o, s_right).wait_recv()

                @pl.when(t < n - 1)
                def _():
                    ar_copy(o, s_right).start()

            @pl.when(jnp.logical_and(o > t, jnp.logical_and(s_left >= 0, s_left < subs)))
            def _():
                al_copy(o, s_left).wait_recv()

                @pl.when(t > 0)
                def _():
                    al_copy(o, s_left).start()

            landed = jnp.where(o < t, s_right, s_left) - subs + 1

            @pl.when(jnp.logical_and(o != t, landed == 0))
            def _():
                normalize(o)

            ripe = jnp.where(g == weights_at, landed >= 0, jnp.logical_and(g > weights_at, landed == 0))

            @pl.when(jnp.logical_and(o != t, ripe))
            def _():
                project(o)

        return 0

    steps = weights_at + 1 + subs
    lax.fori_loop(0, steps, step, 0)

    @pl.when(seq < seqs - 1)
    def _():
        edge_copy().start()

    @pl.when(seq == 0)
    def _():
        x_ref[0:8, :] = jnp.zeros((8, x_ref.shape[1]), F32)

    for i in range(3):
        written(i).start()

    @pl.when(seq > 0)
    def _():
        edge_copy().wait_recv()

    @pl.when(seq < seqs - 1)
    def _():
        edge_copy().wait_send()

    written(3).start()
    local_copy().wait()
    lanes = low_ref.shape[1]
    width = min(tile, lanes)
    piece = min(64, rows)
    taps = keep_ref.shape[1]

    def convolve(o):
        @pl.loop(0, rows // piece * (lanes // width))
        def _(i):
            base = o * rows + i // (lanes // width) * piece
            here = pl.ds(pl.multiple_of(base, piece), piece)
            cols = pl.ds(pl.multiple_of(i % (lanes // width) * width, width), width)
            span = x_ref[pl.ds(pl.multiple_of(base, piece), piece + 8), cols]
            keep = keep_ref[here, :]
            total = jnp.broadcast_to(taps_ref[taps:taps + 1, cols], (piece, width))
            for j in range(taps):
                first = 8 - (taps - 1) + j
                total = total + taps_ref[j:j + 1, cols] * span[first:first + piece] * keep[:, j:j + 1]
            conv_ref[here, cols] = total
            low_ref[here, cols] = (total / (1.0 + jnp.exp(-total))).astype(BF16)

    groups, depth = ws_ref.shape[0], ws_ref.shape[1]
    used = mix_own.shape[0] // groups

    @pl.loop(0, n)
    def _(i):
        o = lax.rem(t + 1 + i, n)
        convolve(o)
        nt = (((1,), (1,)), ((), ()))
        low = low_ref[pl.ds(pl.multiple_of(o * rows, rows), rows), :]
        weights = ws_ref[...].reshape(groups * depth, lanes)
        mix = lax.dot_general(weights, low, nt, preferred_element_type=F32)
        mix = jnp.concatenate([mix[p * depth:p * depth + used] for p in range(groups)], 0)

        @pl.when(o != t)
        def _():
            mix_send[o] = mix.astype(BF16)
            mix_copy(o, t).start()

        @pl.when(o == t)
        def _():
            mix_own[...] = mix

    for i in range(4, 6):
        written(i).start()
    for ahead in range(1, n):
        p = lax.rem(t + ahead, n)
        mix_copy(p, p).wait_recv()
        mix_own[...] = mix_own[...] + mix_recv[p].astype(F32)
    mixed_ref[t] = mix_own[...].astype(BF16)
    for ahead in range(1, n):
        sum_copy(lax.rem(t + ahead, n), t).start()
    total_ref[...] = cnt_one[...]
    for ahead in range(1, chips):
        q = lax.rem(chip + ahead, chips)
        count_two(q, q).wait_recv()
        total_ref[...] = total_ref[...] + cnt_two[q]
    for ahead in range(1, n):
        p = lax.rem(t + ahead, n)
        sum_copy(p, p).wait_recv()
    for ahead in range(1, n):
        p = lax.rem(t + ahead, n)
        mix_copy(p, t).wait_send()
        sum_copy(p, t).wait_send()
    for i in range(6):
        written(i).wait()
    for kind in range(2):
        for ahead in range(1, chips):
            chip_copy(kind, lax.rem(chip + ahead, chips), mine).wait_send()
        for q in range(chips):
            core_copy(kind, owner(q, core), False).wait_send()
    for ahead in range(1, chips):
        count_two(lax.rem(chip + ahead, chips), chip).wait_send()
    for ahead in range(1, n):
        g_copy(lax.rem(t + ahead, n), t).wait_send()

    @pl.loop(0, n * subs)
    def _(i):
        o, s = i // subs, i % subs

        @pl.when(jnp.logical_and(o <= t, t < n - 1))
        def _():
            ar_copy(o, s).wait_send()

        @pl.when(jnp.logical_and(o >= t, t > 0))
        def _():
            al_copy(o, s).wait_send()


def front(hidden, gain, segments, w_in, w_small, taps, keeps):
    n, dps, seqs = (lax.axis_size(axis) for axis in ("tensor", "dp", "seq"))
    parts = dps * seqs
    chips = parts // 2
    rows, wide = hidden.shape
    lanes = w_in.shape[2]
    tokens = rows * n
    mixed = parts * SMALL_ROWS
    subs = max(1, rows // 32)
    vmem, hbm = pl.BlockSpec(memory_space=pltpu.VMEM), pl.BlockSpec(memory_space=pl.ANY)
    dma = pltpu.SemaphoreType.DMA
    many, few, peers = dma((n * subs,)), dma((chips,)), dma((n,))
    return pl.pallas_call(
        functools.partial(front_kernel, n, dps, seqs, subs, 2),
        out_shape=[
            jax.ShapeDtypeStruct((tokens + 8, lanes), F32),
            jax.ShapeDtypeStruct((tokens, lanes), F32),
            jax.ShapeDtypeStruct((tokens, wide), BF16),
            jax.ShapeDtypeStruct((2, wide, lanes), BF16),
            jax.ShapeDtypeStruct((tokens, lanes), F32),
            jax.ShapeDtypeStruct((tokens, lanes), BF16),
            jax.ShapeDtypeStruct((8, 128), F32),
            jax.ShapeDtypeStruct((8, wide), F32),
            jax.ShapeDtypeStruct((parts,) + w_small.shape, BF16),
            jax.ShapeDtypeStruct((n, mixed, rows), BF16),
        ],
        in_specs=[vmem] * 7,
        out_specs=[hbm] * 6 + [vmem] * 4,
        scratch_shapes=[
            pltpu.VMEM((tokens, wide), BF16),
            pltpu.VMEM((8, gain.shape[1]), F32),
            pltpu.VMEM((8, 128), F32),
            pltpu.VMEM((n, 8, gain.shape[1]), F32),
            pltpu.VMEM((8, 128), F32),
            pltpu.VMEM((chips, 8, 128), F32),
            pltpu.VMEM((tokens + 8, lanes), F32),
            pltpu.VMEM((tokens, lanes), F32),
            pltpu.VMEM((tokens, wide), BF16),
            pltpu.VMEM((2, wide, lanes), BF16),
            pltpu.VMEM((tokens, lanes), F32),
            pltpu.VMEM((tokens, lanes), BF16),
            pltpu.VMEM((n, mixed, rows), BF16),
            pltpu.VMEM((n, mixed, rows), BF16),
            pltpu.VMEM((mixed, rows), F32),
            dma((6,)), peers, peers, peers, peers,
            many, many, many, many, peers, peers, dma, dma, few, few, dma, dma, dma,
            dma((2, chips)), dma((2, parts)), dma((2, parts)), dma((2, parts)),
        ],
        compiler_params=pltpu.CompilerParams(
            collective_id=3, has_side_effects=True, vmem_limit_bytes=60 << 20
        ),
        name="front",
    )(hidden, gain, segments, w_in, w_small, taps, keeps)


def mixback_kernel(n, seqs, part_ref, e_hbm, conv_hbm, x_hbm, low_hbm, dpl_hbm, step_ref, wx_ref, taps_ref, keep_ref,
                   dx_hbm, dwx_ref, dwdt_ref, dconvw_ref,
                   e_ref, conv_ref, x_ref, low_ref, dpl_ref, dx_ref, dcv_ref, got, own, done, edge_out, edge_in,
                   loads, store, ms, mr, ns, nr, es, er):
    seq, t = lax.axis_index("seq"), lax.axis_index("tensor")
    rows = part_ref.shape[2]
    tokens, lanes = low_ref.shape
    taps = keep_ref.shape[1]
    width = min(512, lanes)
    piece = min(64, rows)
    across = lanes // width
    pieces = tokens // piece * across
    ahead_seq, behind_seq = lax.rem(seq + 1, seqs), lax.rem(seq + seqs - 1, seqs)

    barrier = pltpu.get_barrier_semaphore()
    for ahead in range(1, n):
        pl.semaphore_signal(barrier, inc=1, device_id=dict(tensor=lax.rem(t + ahead, n)), device_id_type=MESH)
    if seqs > 1:
        for peer in (ahead_seq, behind_seq):
            pl.semaphore_signal(barrier, inc=1, device_id=dict(seq=peer), device_id_type=MESH)
    pl.semaphore_wait(barrier, n - 1 + (2 if seqs > 1 else 0))

    def load(i):
        src = (conv_hbm, dpl_hbm, e_hbm, low_hbm, x_hbm)[i]
        return pltpu.make_async_copy(src, (conv_ref, dpl_ref, e_ref, low_ref, x_ref)[i], loads.at[i])

    def mix_copy(p, slot):
        return mesh_copy(part_ref.at[p], got.at[slot], ms.at[p], mr.at[slot], tensor=p)

    def sum_copy(p, slot):
        return mesh_copy(done.at[slot], done.at[slot], ns.at[p], nr.at[slot], tensor=p)

    def edge_copy():
        return mesh_copy(edge_out, edge_in, es, er, seq=behind_seq)

    for ahead in range(1, n):
        mix_copy(lax.rem(t + ahead, n), t).start()
    for i in range(5):
        load(i).start()

    dcv_ref[0:8, :] = jnp.zeros((8, lanes), F32)
    dcv_ref[tokens + 8:, :] = jnp.zeros((8, lanes), F32)
    load(1).wait()
    tn = (((0,), (0,)), ((), ()))

    @pl.loop(0, across)
    def _(j):
        cols = pl.ds(pl.multiple_of(j * width, width), width)
        dwdt_ref[:, cols] = jnp.dot(step_ref[...], dpl_ref[:, cols], preferred_element_type=F32)

    own[...] = part_ref[t].astype(F32)
    for ahead in range(1, n):
        p = lax.rem(t + ahead, n)
        mix_copy(p, p).wait_recv()
        own[...] = own[...] + got[p].astype(F32)
    done[t] = own[...].astype(BF16)
    for ahead in range(1, n):
        sum_copy(lax.rem(t + ahead, n), t).start()

    load(0).wait()

    @pl.loop(0, pieces)
    def _(i):
        here = pl.ds(pl.multiple_of(i // across * piece, piece), piece)
        cols = pl.ds(pl.multiple_of(i % across * width, width), width)
        v = conv_ref[here, cols]
        s = 1.0 / (1.0 + jnp.exp(-v))
        conv_ref[here, cols] = s * (1.0 + v * (1.0 - s))

    for i in range(2, 5):
        load(i).wait()
    for ahead in range(1, n):
        p = lax.rem(t + ahead, n)
        sum_copy(p, p).wait_recv()

    dwx_ref[...] = jnp.zeros_like(dwx_ref)
    dconvw_ref[...] = jnp.zeros_like(dconvw_ref)

    @pl.loop(0, n)
    def _(o):
        @pl.loop(0, across)
        def _(j):
            cols = pl.ds(pl.multiple_of(j * width, width), width)
            here = pl.ds(pl.multiple_of(o * rows, rows), rows)
            mixed = lax.dot_general(done[o], wx_ref[:, cols], tn, preferred_element_type=F32)
            dcv = (e_ref[here, cols] + mixed) * conv_ref[here, cols]
            dcv_ref[pl.ds(pl.multiple_of(o * rows + 8, 8), rows), cols] = dcv
            dwx_ref[:, cols] = dwx_ref[:, cols] + jnp.dot(done[o], low_ref[here, cols], preferred_element_type=F32)

    def shifted(base, size, cols):
        span = dcv_ref[pl.ds(base, size + 8), cols]
        keep = keep_ref[pl.ds(base, size + 8), :]
        total = jnp.zeros((size, span.shape[1]), F32)
        for j in range(taps):
            late = taps - 1 - j
            total = total + taps_ref[j:j + 1, cols] * (span * keep[:, j:j + 1])[late:late + size]
        return total

    if seqs > 1:
        edge_out[...] = shifted(0, 8, slice(None))

        @pl.when(seq > 0)
        def _():
            edge_copy().start()

    @pl.loop(0, pieces)
    def _(i):
        base = pl.multiple_of(i // across * piece, piece)
        cols = pl.ds(pl.multiple_of(i % across * width, width), width)
        dx_ref[pl.ds(base, piece), cols] = shifted(pl.multiple_of(base + 8, 8), piece, cols).astype(BF16)
        here = dcv_ref[pl.ds(pl.multiple_of(base + 8, 8), piece), cols]
        keep = keep_ref[pl.ds(pl.multiple_of(base + 8, 8), piece), :]
        span = x_ref[pl.ds(base, piece + 8), cols]
        for j in range(taps):
            first = 8 - (taps - 1) + j
            tap = jnp.sum(here * keep[:, j:j + 1] * span[first:first + piece], axis=0, keepdims=True)
            dconvw_ref[j:j + 1, cols] = dconvw_ref[j:j + 1, cols] + tap
        dconvw_ref[taps:taps + 1, cols] = dconvw_ref[taps:taps + 1, cols] + jnp.sum(here, axis=0, keepdims=True)

    if seqs > 1:
        @pl.when(seq < seqs - 1)
        def _():
            edge_copy().wait_recv()
            last = shifted(tokens - 16 + 8, 16, slice(None))
            dx_ref[tokens - 16:, :] = (last + jnp.concatenate([jnp.zeros_like(edge_in), edge_in[...]], 0)).astype(BF16)

        @pl.when(seq > 0)
        def _():
            edge_copy().wait_send()

    out = pltpu.make_async_copy(dx_ref, dx_hbm, store)
    out.start()
    for ahead in range(1, n):
        p = lax.rem(t + ahead, n)
        mix_copy(p, t).wait_send()
        sum_copy(p, t).wait_send()
    out.wait()


def mixback(part, e, conv_sum, x_rows, x_low, d_pre_low, step_t, w_x, taps, keeps):
    n, seqs = lax.axis_size("tensor"), lax.axis_size("seq")
    tokens, lanes = x_low.shape
    mixed, rows = part.shape[1:]
    rank = step_t.shape[0]
    vmem, hbm = pl.BlockSpec(memory_space=pltpu.VMEM), pl.BlockSpec(memory_space=pl.ANY)
    dma = pltpu.SemaphoreType.DMA
    peers = dma((n,))
    return pl.pallas_call(
        functools.partial(mixback_kernel, n, seqs),
        out_shape=[
            jax.ShapeDtypeStruct((tokens, lanes), BF16),
            jax.ShapeDtypeStruct((mixed, lanes), F32),
            jax.ShapeDtypeStruct((rank, lanes), F32),
            jax.ShapeDtypeStruct((8, lanes), F32),
        ],
        in_specs=[vmem] + [hbm] * 5 + [vmem] * 4,
        out_specs=[hbm] + [vmem] * 3,
        scratch_shapes=[
            pltpu.VMEM((tokens, lanes), F32),
            pltpu.VMEM((tokens, lanes), F32),
            pltpu.VMEM((tokens + 8, lanes), F32),
            pltpu.VMEM((tokens, lanes), BF16),
            pltpu.VMEM((tokens, lanes), BF16),
            pltpu.VMEM((tokens, lanes), BF16),
            pltpu.VMEM((tokens + 16, lanes), F32),
            pltpu.VMEM((n, mixed, rows), BF16),
            pltpu.VMEM((mixed, rows), F32),
            pltpu.VMEM((n, mixed, rows), BF16),
            pltpu.VMEM((8, lanes), F32),
            pltpu.VMEM((8, lanes), F32),
            dma((5,)), dma, peers, peers, peers, peers, dma, dma,
        ],
        compiler_params=pltpu.CompilerParams(
            collective_id=4, has_side_effects=True, vmem_limit_bytes=60 << 20
        ),
        name="mix_backward",
    )(part, e, conv_sum, x_rows, x_low, d_pre_low, step_t, w_x, taps, keeps)


def on_device(
    hidden_in,
    teacher,
    segment_ids,
    norm_gain,
    input_projection_weight,
    conv_weight,
    conv_bias,
    xproj_weight,
    dtproj_weight,
    dt_bias,
    a_log,
    d_skip,
    output_projection_weight,
):
    tok_rows = segment_ids.shape[0]
    row_share = hidden_in.shape[0]
    model_width = hidden_in.shape[1]
    conv_taps = conv_weight.shape[0]
    chan_lanes = conv_weight.shape[1]
    back_rows = conv_taps - 1
    row_start = lax.axis_index("tensor") * row_share
    valid_mask = (segment_ids != 0).astype(jnp.float32)
    parts = lax.axis_size(("dp", "seq"))
    x_cols, dt_rows = xproj_weight.shape[1], dtproj_weight.shape[0]
    w_small = jnp.concatenate(
        [
            xproj_weight.T,
            jnp.zeros((SMALL_ROWS - x_cols, chan_lanes), BF16),
            dtproj_weight,
            jnp.zeros((-(SMALL_ROWS + dt_rows) % 16, chan_lanes), BF16),
        ],
        0,
    )
    seg_float = segment_ids.astype(F32)
    prev_seg = jnp.where(lax.axis_index("seq") > 0, seg_float[:1], jnp.zeros((back_rows,), F32))
    ext_seg = jnp.concatenate([prev_seg, seg_float], 0)
    tap_keeps = []
    for offset in range(conv_taps):
        tap_keeps.append((ext_seg[offset : offset + tok_rows] == seg_float).astype(F32)[:, None])
    taps = jnp.concatenate(
        [conv_weight.astype(F32), conv_bias.astype(F32)[None], jnp.zeros((7 - conv_taps, chan_lanes), F32)], 0
    )
    x_rows, z_gate, normalized_rows, w_in, conv_sum, x_low, total, gain_rows, w_small, mixed = front(
        hidden_in,
        norm_gain[None],
        segment_ids.reshape(8, -1),
        jnp.swapaxes(input_projection_weight, 0, 1),
        w_small,
        taps,
        jnp.concatenate(tap_keeps, 1),
    )
    w_out_rows, z_gate = lax.optimization_barrier((output_projection_weight.T, z_gate))
    w_out = lax.all_gather(w_out_rows, ("dp", "seq"), axis=0, tiled=True)
    total_count = total[0, 0]
    w_x = w_small[:, :x_cols].reshape(parts * x_cols, chan_lanes)
    w_dt = w_small[:, SMALL_ROWS : SMALL_ROWS + dt_rows].reshape(parts * dt_rows, chan_lanes)
    share_rows = hidden_in.astype(F32)
    full_gain = gain_rows[0]
    inv_share = lax.rsqrt(jnp.mean(share_rows * share_rows, axis=1, keepdims=True) + EPS)
    mixed = mixed.reshape(-1, parts, SMALL_ROWS, row_share)[:, :, :x_cols]
    mixed_rows = mixed.transpose(0, 3, 1, 2).reshape(tok_rows, parts * x_cols).astype(F32)
    rank_width = w_dt.shape[0]
    state_width = (mixed_rows.shape[1] - rank_width) // 2
    step_low = mixed_rows[:, :rank_width].astype(jnp.bfloat16)
    b_in = mixed_rows[:, rank_width : rank_width + state_width]
    c_out = mixed_rows[:, rank_width + state_width :]
    same_doc = (seg_float == ext_seg[back_rows - 1 : back_rows - 1 + tok_rows]).astype(jnp.float32)
    rates = -jnp.exp(a_log) * LOG2E
    block = 128
    col_pair = jnp.concatenate([columns(b_in), columns(c_out)], -1)
    b_diag, c_diag = diagonal(b_in), diagonal(c_out)
    resets = jnp.sum((same_doc == 0).astype(jnp.int32).reshape(-1, block), axis=1)
    alive = (jnp.cumsum(resets) - resets == 0).astype(jnp.int32)
    y_local, marks, state_last, stepd, inject, step_size, step_slope = fwd(
        step_low, w_dt, dt_bias[None], x_low, same_doc[:, None], col_pair, c_diag, rates, tb=block, unroll=8
    )

    def reach():
        return jnp.exp2(rates * jnp.sum(stepd, axis=0)[None])

    state_in = carried(state_last, reach, "seq", 1)
    scan_out, marks, gated_output_rows = correct(
        alive, y_local, stepd, c_diag, rates, marks, state_in, x_low, d_skip[None], z_gate, tb=block
    )
    valid_share = lax.dynamic_slice_in_dim(valid_mask, row_start, row_share, 0)
    total_tokens = float(tok_rows * lax.axis_size(("dp", "seq")))
    scale = (total_tokens / total_count * valid_share)[:, None]
    output, grad_out, d_wout, d_scan, d_z = middle(
        gated_output_rows, w_out, hidden_in, teacher, scale, z_gate, scan_out
    )
    adjoint_first = entry(alive, stepd, d_scan, col_pair, rates, tb=block)
    adjoint_in = carried(adjoint_first, reach, "seq", -1)
    ones = diagonal(jnp.ones((CH, N), F32))
    d_pre_low, d_direct, d_rank_t, d_b_part, d_c_part, a_log_part, dt_bias_part, d_skip_part = bwd(
        stepd, inject, d_scan, col_pair, b_diag, ones, rates, marks, adjoint_in,
        step_size, step_slope, x_low, d_skip[None], w_dt, tb=block, unroll=8
    )
    a_log_part = LN2 * a_log_part
    part = jnp.concatenate(
        [
            jnp.sum(d_rank_t, axis=0),
            jnp.sum(d_b_part, axis=0).reshape(tok_rows, N).T,
            jnp.sum(d_c_part, axis=0).reshape(tok_rows, N).T,
        ],
        0,
    )
    part = part.astype(BF16).reshape(part.shape[0], -1, row_share).transpose(1, 0, 2)
    edge = jnp.zeros((8, conv_taps), F32)
    d_x, d_wx, d_wdt, conv_parts = mixback(
        part, d_direct, conv_sum, x_rows, x_low, d_pre_low, step_low.T, w_x, taps,
        jnp.concatenate([edge] + [jnp.concatenate(tap_keeps, 1)] + [edge], 0),
    )
    d_wx_rank, d_wx_state = d_wx[:rank_width], d_wx[rank_width:]
    conv_weight_part, conv_bias_part = conv_parts[:conv_taps], conv_parts[conv_taps]
    small = jnp.concatenate(
        [
            d_wx_rank.reshape(parts, -1, chan_lanes),
            d_wx_state.reshape(parts, -1, chan_lanes),
            d_wdt.reshape(parts, -1, chan_lanes),
            jnp.zeros((parts, 4, chan_lanes), F32),
        ],
        1,
    )
    whole = jnp.concatenate(
        [a_log_part, conv_weight_part, conv_bias_part[None], dt_bias_part, d_skip_part, d_skip_part], 0
    )
    d_norm_share, g_in, g_small, g_whole = tail(d_x, d_z, w_in, normalized_rows, small, whole)
    g_in = jnp.swapaxes(g_in, 0, 1)
    inner_sum = jnp.sum(d_norm_share * full_gain[None] * share_rows, axis=1, keepdims=True)
    inv_cube = inv_share * inv_share * inv_share
    input_grad = (
        grad_out
        + inv_share * full_gain[None] * d_norm_share
        - share_rows * inv_cube * inner_sum / model_width
    )
    rank_here = rank_width // parts
    state_here = 2 * state_width // parts
    g_x_rank = g_small[:rank_here].T
    g_x_state = g_small[rank_here : rank_here + state_here].T
    g_dt = g_small[rank_here + state_here : rank_here + state_here + rank_here]
    g_out = lax.psum_scatter(d_wout, ("dp", "seq"), scatter_dimension=0, tiled=True).astype(F32).T
    g_gain = jnp.sum(g_whole[N + conv_taps + 4 :, : norm_gain.shape[0]], axis=0) / norm_gain.astype(F32)
    g_alog, g_conv_w = g_whole[:N], g_whole[N : N + conv_taps]
    g_conv_b, g_bias, g_skip = g_whole[N + conv_taps], g_whole[N + conv_taps + 1], g_whole[N + conv_taps + 2]
    return (
        output,
        input_grad,
        g_gain,
        g_in,
        g_conv_w,
        g_conv_b,
        g_x_rank,
        g_x_state,
        g_dt,
        g_bias,
        g_alog,
        g_skip,
        g_out,
    )


def solution(mesh):
    placed = (
        P(("dp", "seq", "tensor"), None),
        P(("dp", "seq", "tensor"), None),
        P(("dp", "seq")),
        P("tensor"),
        P(("dp", "seq"), None, "tensor"),
        P(None, "tensor"),
        P("tensor"),
        P("tensor", ("dp", "seq")),
        P(("dp", "seq"), "tensor"),
        P("tensor"),
        P(None, "tensor"),
        P("tensor"),
        P("tensor", ("dp", "seq")),
    )
    return jax.shard_map(
        on_device,
        mesh=mesh,
        in_specs=placed,
        out_specs=(
            P(("dp", "seq", "tensor"), None),
            P(("dp", "seq", "tensor"), None),
            P("tensor"),
            P(("dp", "seq"), None, "tensor"),
            P(None, "tensor"),
            P("tensor"),
            P("tensor", ("dp", "seq")),
            P("tensor", ("dp", "seq")),
            P(("dp", "seq"), "tensor"),
            P("tensor"),
            P(None, "tensor"),
            P("tensor"),
            P("tensor", ("dp", "seq")),
        ),
        check_vma=False,
    )
```

```python
import functools

import jax
import jax.numpy as jnp
from jax import lax
from jax.experimental import pallas as pl
from jax.experimental.pallas import tpu as pltpu
from jax.sharding import PartitionSpec as P

EPS = 1e-05
LOG2E = 1.4426950408889634
LN2 = 0.6931471805599453
FAR = 1e30
SMALL_ROWS = 24
N = 16
CH = 16
F32, BF16 = jnp.float32, jnp.bfloat16
MESH = pl.DeviceIdType.MESH


def passed_along(x, axis, by):
    size = lax.axis_size(axis)
    pairs = [(i, i + by) for i in range(size) if 0 <= i + by < size]
    return lax.ppermute(x, axis, pairs)


def spread(values_t):
    tokens = values_t.shape[1]
    name = lax.broadcasted_iota(jnp.int32, (N, CH * N), 0)
    lane = lax.broadcasted_iota(jnp.int32, (N, CH * N), 1)
    copies = (name == lane % N).astype(BF16)
    wide = lax.dot_general(values_t.astype(BF16), copies, (((0,), (0,)), ((), ())), preferred_element_type=F32)
    row = lax.broadcasted_iota(jnp.int32, (tokens, CH * N), 0)
    place_of = lax.broadcasted_iota(jnp.int32, (tokens, CH * N), 1)
    return jnp.where(row % CH == place_of // N, wide, 0.0).astype(BF16)


def fwd_kernel(mix_ref, wdt_ref, bias_ref, low_ref, keep_ref, rate_ref,
               y_ref, ckpt_ref, last_ref, stepd_ref, u_ref, step_ref, sig_ref, state_ref, sbf_ref, cdiag_ref):
    @pl.when(pl.program_id(1) == 0)
    def _():
        state_ref[...] = jnp.zeros_like(state_ref)
    ckpt_ref[0] = state_ref[...]
    rank = wdt_ref.shape[0]
    b_t, c_t = mix_ref[rank:rank + N, :], mix_ref[rank + N:rank + 2 * N, :]
    cdiag_ref[...] = spread(c_t)
    tn = (((0,), (0,)), ((), ()))
    pre = lax.dot_general(mix_ref[0:rank, :].astype(BF16), wdt_ref[...], tn, preferred_element_type=F32)
    pre = pre + bias_ref[...]
    small = jnp.exp(-jnp.abs(pre))
    step = jnp.maximum(pre, 0.0) + jnp.log1p(small)
    step_ref[...] = step
    sig_ref[...] = jnp.where(pre >= 0, 1.0, small) / (1.0 + small)
    stepd_ref[...] = jnp.where(keep_ref[...] > 0, step, FAR)
    u_ref[...] = step * low_ref[...].astype(F32)
    rate = rate_ref[...]
    tb = stepd_ref.shape[0]

    s = state_ref[...]
    for base in range(0, tb, CH):
        for k in range(base, base + CH):
            dec = jnp.exp2(rate * stepd_ref[k:k + 1, :])
            s = dec * s + b_t[:, k:k + 1] * u_ref[k:k + 1, :]
            sbf_ref[(k - base) * N:(k - base + 1) * N, :] = s.astype(BF16)
        y_ref[base:base + CH, :] = jnp.dot(cdiag_ref[base:base + CH, :], sbf_ref[...], preferred_element_type=F32)
    state_ref[...] = s
    last_ref[...] = s


def fwd(mix_t, w_dt, bias, low, keep, rate, tb=128, w=512):
    t, c = low.shape
    w = min(w, c)
    grid = (c // w, t // tb)
    mixed, rank = mix_t.shape[0], w_dt.shape[0]
    rows = pl.BlockSpec((tb, w), lambda j, i: (i, j))
    whole = jax.ShapeDtypeStruct((t, c), F32)
    return pl.pallas_call(
        fwd_kernel,
        grid=grid,
        in_specs=[
            pl.BlockSpec((mixed, tb), lambda j, i: (0, i)),
            pl.BlockSpec((rank, w), lambda j, i: (0, j)),
            pl.BlockSpec((1, w), lambda j, i: (0, j)),
            rows,
            pl.BlockSpec((tb, 1), lambda j, i: (i, 0)),
            pl.BlockSpec((N, w), lambda j, i: (0, j)),
        ],
        out_specs=[
            rows,
            pl.BlockSpec((1, N, w), lambda j, i: (i, 0, j)),
            pl.BlockSpec((N, w), lambda j, i: (0, j)),
            rows, rows, rows, rows,
        ],
        out_shape=[
            whole,
            jax.ShapeDtypeStruct((t // tb, N, c), F32),
            jax.ShapeDtypeStruct((N, c), F32),
            whole, whole, whole, whole,
        ],
        scratch_shapes=[pltpu.VMEM((N, w), F32), pltpu.VMEM((CH * N, w), BF16), pltpu.VMEM((tb, CH * N), BF16)],
        compiler_params=pltpu.CompilerParams(vmem_limit_bytes=48 << 20),
        name="scan_forward",
    )(mix_t, w_dt, bias, low, keep, rate)


def bwd_kernel(stepd_ref, u_ref, ds_ref, mix_ref, rate_ref, ckpt_ref, gin_ref,
               step_ref, sig_ref, low_ref, skip_ref, wdt_ref,
               dpl_ref, e_ref, rank_ref, db_ref, dc_ref, acc_ref, bias_ref, dskip_ref,
               g_ref, sbf_ref, abf_ref, rbf_ref, pb_ref, pc_ref, wb_ref, dn_ref, bdiag_ref):
    @pl.when(pl.program_id(1) == 0)
    def _():
        g_ref[...] = gin_ref[...]
        acc_ref[...] = jnp.zeros_like(acc_ref)
        bias_ref[...] = jnp.zeros_like(bias_ref)
        dskip_ref[...] = jnp.zeros_like(dskip_ref)

    rate = rate_ref[...]
    tb = stepd_ref.shape[0]
    nc = tb // CH

    def fold(v):
        p = v[:, 0:128]
        for q in range(1, v.shape[1] // 128):
            p = p + v[:, q * 128:(q + 1) * 128]
        return p

    sbf_ref[0:N, :] = ckpt_ref[0].astype(BF16)
    nt = (((1,), (1,)), ((), ()))
    lanes = jnp.ones((8, 128), BF16)
    rank = wdt_ref.shape[0]
    b_t, c_t = mix_ref[rank:rank + N, :], mix_ref[rank + N:rank + 2 * N, :]
    bdiag_ref[...] = spread(b_t)
    ones = spread(jnp.ones((N, CH), F32))

    s = ckpt_ref[0]
    for c in range(nc):
        base = c * CH
        for k in range(CH):
            at = base + k
            dec = jnp.exp2(rate * stepd_ref[at:at + 1, :])
            s = dec * s + b_t[:, at:at + 1] * u_ref[at:at + 1, :]
            sbf_ref[(at + 1) * N:(at + 2) * N, :] = s.astype(BF16)
            pc_ref[k * N:(k + 1) * N, :] = fold(s * ds_ref[at:at + 1, :])
        dc = lax.dot_general(lanes, pc_ref[...].astype(BF16), nt, preferred_element_type=F32)
        dc_ref[0, c:c + 1, :] = dc[0:1]

    g, acc = g_ref[...], acc_ref[...]
    for c in range(nc - 1, -1, -1):
        base = c * CH
        for k in range(CH - 1, -1, -1):
            at = base + k
            sd = stepd_ref[at:at + 1, :]
            adj = g + c_t[:, at:at + 1] * ds_ref[at:at + 1, :]
            abf_ref[k * N:(k + 1) * N, :] = adj.astype(BF16)
            pb_ref[k * N:(k + 1) * N, :] = fold(adj * u_ref[at:at + 1, :])
            g = jnp.exp2(rate * sd) * adj
            before = sbf_ref[at * N:(at + 1) * N, :].astype(F32)
            r = g * before * rate
            rbf_ref[k * N:(k + 1) * N, :] = r.astype(BF16)
            acc = acc + r * sd
        wb_ref[base:base + CH, :] = jnp.dot(bdiag_ref[base:base + CH, :], abf_ref[...], preferred_element_type=F32)
        dn_ref[base:base + CH, :] = jnp.dot(ones, rbf_ref[...], preferred_element_type=F32)
        db = lax.dot_general(lanes, pb_ref[...].astype(BF16), nt, preferred_element_type=F32)
        db_ref[0, c:c + 1, :] = db[0:1]
    g_ref[...] = g
    acc_ref[...] = acc

    low, ds, weighted = low_ref[...].astype(F32), ds_ref[...], wb_ref[...]
    d_pre = (LN2 * dn_ref[...] + low * weighted) * sig_ref[...]
    d_pre_low = d_pre.astype(BF16)
    dpl_ref[...] = d_pre_low
    e_ref[...] = skip_ref[...] * ds + step_ref[...] * weighted
    bias_ref[...] = bias_ref[...] + jnp.sum(d_pre, axis=0, keepdims=True)
    dskip_ref[...] = dskip_ref[...] + jnp.sum(ds * low, axis=0, keepdims=True)
    rank_ref[0] = lax.dot_general(wdt_ref[...], d_pre_low, nt, preferred_element_type=F32)


def bwd(stepd, u, ds, mix_t, rate, ckpt, gin, step, sig, low, skip, w_dt, tb=128, w=512):
    t, c = stepd.shape
    w = min(w, c)
    nb = t // tb
    grid = (c // w, nb)
    rank = w_dt.shape[0]
    rows = pl.BlockSpec((tb, w), lambda j, i: (nb - 1 - i, j))
    return pl.pallas_call(
        bwd_kernel,
        grid=grid,
        in_specs=[
            rows, rows, rows,
            pl.BlockSpec((mix_t.shape[0], tb), lambda j, i: (0, nb - 1 - i)),
            pl.BlockSpec((N, w), lambda j, i: (0, j)),
            pl.BlockSpec((1, N, w), lambda j, i: (nb - 1 - i, 0, j)),
            pl.BlockSpec((N, w), lambda j, i: (0, j)),
            rows, rows, rows,
            pl.BlockSpec((1, w), lambda j, i: (0, j)),
            pl.BlockSpec((rank, w), lambda j, i: (0, j)),
        ],
        out_specs=[
            rows, rows,
            pl.BlockSpec((1, rank, tb), lambda j, i: (j, 0, nb - 1 - i)),
            pl.BlockSpec((1, tb // CH, CH * N), lambda j, i: (j, nb - 1 - i, 0)),
            pl.BlockSpec((1, tb // CH, CH * N), lambda j, i: (j, nb - 1 - i, 0)),
            pl.BlockSpec((N, w), lambda j, i: (0, j)),
            pl.BlockSpec((1, w), lambda j, i: (0, j)),
            pl.BlockSpec((1, w), lambda j, i: (0, j)),
        ],
        out_shape=[
            jax.ShapeDtypeStruct((t, c), BF16),
            jax.ShapeDtypeStruct((t, c), F32),
            jax.ShapeDtypeStruct((c // w, rank, t), F32),
            jax.ShapeDtypeStruct((c // w, t // CH, CH * N), F32),
            jax.ShapeDtypeStruct((c // w, t // CH, CH * N), F32),
            jax.ShapeDtypeStruct((N, c), F32),
            jax.ShapeDtypeStruct((1, c), F32),
            jax.ShapeDtypeStruct((1, c), F32),
        ],
        scratch_shapes=[pltpu.VMEM((N, w), F32), pltpu.VMEM(((tb + 1) * N, w), BF16),
                        pltpu.VMEM((CH * N, w), BF16), pltpu.VMEM((CH * N, w), BF16), pltpu.VMEM((CH * N, 128), F32), pltpu.VMEM((CH * N, 128), F32),
                        pltpu.VMEM((tb, w), F32), pltpu.VMEM((tb, w), F32), pltpu.VMEM((tb, CH * N), BF16)],
        compiler_params=pltpu.CompilerParams(vmem_limit_bytes=48 << 20),
        name="scan_backward",
    )(stepd, u, ds, mix_t, rate, ckpt, gin, step, sig, low, skip, w_dt)


def correct_kernel(rank, alive_ref, y_ref, stepd_ref, mix_ref, rate_ref, ckpt_ref, sin_ref, low_ref, skip_ref, z_ref,
                   yo_ref, ckpto_ref, gated_ref, state_ref, sbf_ref, cdiag_ref):
    i = pl.program_id(1)

    @pl.when(i == 0)
    def _():
        state_ref[...] = sin_ref[...]

    alive = alive_ref[i] != 0

    @pl.when(alive)
    def _():
        rate = rate_ref[...]
        ckpto_ref[0] = ckpt_ref[0] + state_ref[...]

        cdiag_ref[...] = spread(mix_ref[rank + N:rank + 2 * N, :])
        s = state_ref[...]
        for base in range(0, y_ref.shape[0], CH):
            for k in range(CH):
                s = jnp.exp2(rate * stepd_ref[base + k:base + k + 1, :]) * s
                sbf_ref[k * N:(k + 1) * N, :] = s.astype(BF16)
            yo_ref[base:base + CH, :] = y_ref[base:base + CH, :] + jnp.dot(
                cdiag_ref[base:base + CH, :], sbf_ref[...], preferred_element_type=F32
            )
        state_ref[...] = s

    @pl.when(jnp.logical_not(alive))
    def _():
        yo_ref[...] = y_ref[...]
        ckpto_ref[...] = ckpt_ref[...]

    total = yo_ref[...] + skip_ref[...] * low_ref[...].astype(F32)
    z = z_ref[...]
    yo_ref[...] = total
    gated_ref[...] = (total * (z / (1.0 + jnp.exp(-z)))).astype(BF16)


def correct(rank, alive, y, stepd, mix_t, rate, ckpt, state_in, low, skip, z, tb=128, w=512):
    t, c = stepd.shape
    w = min(w, c)
    rows = pl.BlockSpec((tb, w), lambda j, i, _: (i, j))
    lanes = pl.BlockSpec((N, w), lambda j, i, _: (0, j))
    marks = pl.BlockSpec((1, N, w), lambda j, i, _: (i, 0, j))
    return pl.pallas_call(
        functools.partial(correct_kernel, rank),
        grid_spec=pltpu.PrefetchScalarGridSpec(
            num_scalar_prefetch=1,
            grid=(c // w, t // tb),
            in_specs=[rows, rows, pl.BlockSpec((mix_t.shape[0], tb), lambda j, i, _: (0, i)), lanes, marks, lanes,
                      rows, pl.BlockSpec((1, w), lambda j, i, _: (0, j)), rows],
            out_specs=[rows, marks, rows],
            scratch_shapes=[pltpu.VMEM((N, w), F32), pltpu.VMEM((CH * N, w), BF16), pltpu.VMEM((tb, CH * N), BF16)],
        ),
        out_shape=[jax.ShapeDtypeStruct((t, c), F32), jax.ShapeDtypeStruct(ckpt.shape, F32),
                   jax.ShapeDtypeStruct((t, c), BF16)],
        compiler_params=pltpu.CompilerParams(vmem_limit_bytes=48 << 20),
        name="scan_correct",
    )(alive, y, stepd, mix_t, rate, ckpt, state_in, low, skip, z)


def entry_kernel(rank, alive_ref, stepd_ref, ds_ref, mix_ref, rate_ref, g_ref):
    i = pl.program_id(1)

    @pl.when(i == 0)
    def _():
        g_ref[...] = jnp.zeros_like(g_ref)

    @pl.when(alive_ref[pl.num_programs(1) - 1 - i] != 0)
    def _():
        rate = rate_ref[...]
        c_t = mix_ref[rank + N:rank + 2 * N, :]
        g = g_ref[...]
        for k in range(stepd_ref.shape[0] - 1, -1, -1):
            adj = g + c_t[:, k:k + 1] * ds_ref[k:k + 1, :]
            g = jnp.exp2(rate * stepd_ref[k:k + 1, :]) * adj
        g_ref[...] = g


def entry(rank, alive, stepd, ds, mix_t, rate, tb=128, w=512):
    t, c = stepd.shape
    w = min(w, c)
    nb = t // tb
    rows = pl.BlockSpec((tb, w), lambda j, i, _: (nb - 1 - i, j))
    lanes = pl.BlockSpec((N, w), lambda j, i, _: (0, j))
    return pl.pallas_call(
        functools.partial(entry_kernel, rank),
        grid_spec=pltpu.PrefetchScalarGridSpec(
            num_scalar_prefetch=1,
            grid=(c // w, nb),
            in_specs=[rows, rows, pl.BlockSpec((mix_t.shape[0], tb), lambda j, i, _: (0, nb - 1 - i)), lanes],
            out_specs=lanes,
        ),
        out_shape=jax.ShapeDtypeStruct((N, c), F32),
        compiler_params=pltpu.CompilerParams(vmem_limit_bytes=48 << 20),
        name="scan_entry",
    )(alive, stepd, ds, mix_t, rate)


def carried(local, reach, axis, by):
    found = jnp.zeros_like(local)
    for turn in range(lax.axis_size(axis) - 1):
        found = passed_along(local if turn == 0 else local + reach() * found, axis, by)
    return found


def mesh_copy(src, dst, send, recv, **where):
    return pltpu.make_async_remote_copy(
        src_ref=src, dst_ref=dst, send_sem=send, recv_sem=recv, device_id=where, device_id_type=MESH
    )


def place():
    dp, seq, mine = lax.axis_index("dp"), lax.axis_index("seq"), lax.axis_index("tensor")
    return dp, seq, mine


def tail_kernel(n, dps, seqs, tile, lag, rank, dx_ref, dz_ref, w_hbm, nrm_ref,
                dwx_ref, dwdt_ref, alog_ref, conv_ref, bias_ref, skip_ref,
                dn_ref, gin_ref, gs_ref, ga_ref,
                sm_ref, gacc, gsend, grecv, all_mine,
                zr, zl, w_ref, loads, one_send, one_recv, two_recv, sm_one, sm_two, all_one, all_two,
                r_send, r_recv, l_send, l_recv, w1s, w1r, w2s, w2r, s1s, s1r, s2s, s2r, a1s, a1r, a2s, a2r, gs, gr):
    dp, seq, t = place()
    core, hi = dp % 2, dp // 2
    chips = dps // 2 * seqs
    chip = hi * seqs + seq
    rows = dn_ref.shape[0]
    wide = dn_ref.shape[1]
    wrows = gin_ref.shape[1]
    subs = wide // tile

    def owner(q, c):
        return (q // seqs * 2 + c) * seqs + q % seqs

    def to_chip(q):
        return dict(dp=q // seqs * 2 + core, seq=q % seqs)

    barrier = pltpu.get_barrier_semaphore()
    pl.semaphore_signal(barrier, inc=1, device_id=dict(dp=hi * 2 + 1 - core), device_id_type=MESH)
    for step in range(1, chips):
        q = lax.rem(chip + step, chips)
        pl.semaphore_signal(barrier, inc=1, device_id=to_chip(q), device_id_type=MESH)

    for ahead in range(1, n):
        pl.semaphore_signal(barrier, inc=1, device_id=dict(tensor=lax.rem(t + ahead, n)), device_id_type=MESH)
    pl.semaphore_wait(barrier, chips + n - 1)
    gacc[...] = jnp.zeros_like(gacc)

    partner = dict(dp=hi * 2 + 1 - core)
    right, left = dict(tensor=lax.rem(t + 1, n)), dict(tensor=lax.rem(t + n - 1, n))

    def r_copy(i):
        return mesh_copy(zr.at[i], zr.at[i], r_send.at[i], r_recv.at[i], **right)

    def l_copy(i):
        return mesh_copy(zl.at[i], zl.at[i], l_send.at[i], l_recv.at[i], **left)

    def w1_copy(q):
        return mesh_copy(one_send.at[q], one_recv.at[q], w1s.at[q], w1r.at[q], **partner)

    def w2_copy(q, slot):
        return mesh_copy(one_recv.at[q], two_recv.at[slot], w2s.at[q], w2r.at[slot], **to_chip(q))

    def s1_copy(q):
        return mesh_copy(sm_ref.at[owner(q, 1 - core)], sm_one.at[q], s1s.at[q], s1r.at[q], **partner)

    def s2_copy(q, slot):
        return mesh_copy(sm_one.at[q], sm_two.at[slot], s2s.at[q], s2r.at[slot], **to_chip(q))

    def a1_copy():
        return mesh_copy(all_mine, all_one, a1s, a1r, **partner)

    def a2_copy(q, slot):
        return mesh_copy(all_one, all_two.at[slot], a2s.at[q], a2r.at[slot], **to_chip(q))

    def g_copy(p, slot):
        return mesh_copy(gsend.at[p], grecv.at[slot], gs.at[p], gr.at[slot], tensor=p)

    def cols_of(sub):
        return pl.ds(pl.multiple_of(sub * tile, tile), tile)

    def load(sub):
        ref = w_ref.at[:, cols_of(sub), :]
        return pltpu.make_async_copy(w_hbm.at[:, cols_of(sub), :], ref, loads.at[sub])

    def partial_tile(o, sub):
        here = pl.ds(pl.multiple_of(o * rows, rows), rows)
        cols = cols_of(sub)
        nt = (((1,), (1,)), ((), ()))
        return lax.dot_general(
            dx_ref[here, :], w_ref[0, cols, :], nt, preferred_element_type=F32
        ) + lax.dot_general(dz_ref[here, :], w_ref[1, cols, :], nt, preferred_element_type=F32)

    def weight_rows(p, k):
        cols = pl.ds(pl.multiple_of(p * wrows, wrows), wrows)
        tn = (((0,), (0,)), ((), ()))
        d_ref = dx_ref if k == 0 else dz_ref
        block = lax.dot_general(nrm_ref[:, cols], d_ref[...], tn, preferred_element_type=F32)
        scaled = (block * w_ref[k, cols, :].astype(F32)).astype(BF16)
        lanes = jnp.ones((8, block.shape[1]), BF16)
        nt = (((1,), (1,)), ((), ()))
        gacc[:, cols] = gacc[:, cols] + lax.dot_general(lanes, scaled, nt, preferred_element_type=F32)
        return block

    @pl.loop(0, subs)
    def _(sub):
        load(sub).start()

    parts = sm_ref.shape[0]
    for p in range(parts):
        here, more = rank // parts, (dwx_ref.shape[0] - rank) // parts
        sm_ref[p, 0:here, :] = dwx_ref[p * here:(p + 1) * here, :]
        sm_ref[p, here:2 * here, :] = dwdt_ref[p * here:(p + 1) * here, :]
        sm_ref[p, 2 * here:2 * here + more, :] = dwx_ref[rank + p * more:rank + (p + 1) * more, :]
        sm_ref[p, 2 * here + more:, :] = jnp.zeros((sm_ref.shape[1] - 2 * here - more, sm_ref.shape[2]), F32)
    for q in range(chips):
        s1_copy(q).start()

    def stream(i, limit, start, buf, copy, owner_of):
        @pl.when(jnp.logical_and(i >= 0, i < limit))
        def _():
            block = partial_tile(owner_of(i // subs), i % subs)

            @pl.when(start)
            def _():
                buf[i] = block.astype(BF16)

            @pl.when(jnp.logical_not(start))
            def _():
                copy(i).wait_recv()
                buf[i] = (block + buf[i].astype(F32)).astype(BF16)

            copy(i).start()

    def step(g, _):
        @pl.when(g == 0)
        def _():
            load(0).wait()

        @pl.when(g == 1)
        def _():
            @pl.loop(1, subs)
            def _(sub):
                load(sub).wait()

        stream(g - lag * t, (n - 1 - t) * subs, t == 0, zr, r_copy, lambda k: n - 1 - k)
        stream(g - lag * (n - 1 - t), t * subs, t == n - 1, zl, l_copy, lambda k: k)

        @pl.when(jnp.logical_and(g >= 1, g < chips + 1))
        def _():
            for k in range(2):
                one_send[g - 1, k] = weight_rows(owner(g - 1, 1 - core), k).astype(BF16)
            w1_copy(g - 1).start()

        @pl.when(jnp.logical_and(g >= chips + 1, g < 2 * chips))
        def _():
            q = lax.rem(chip + g - chips, chips)
            w1_copy(q).wait_recv()
            for k in range(2):
                one_recv[q, k] = (weight_rows(owner(q, core), k) + one_recv[q, k].astype(F32)).astype(BF16)
            w2_copy(q, chip).start()

        @pl.when(g == 2 * chips)
        def _():
            for q in range(chips):
                s1_copy(q).wait_recv()
                sm_one[q] = sm_one[q] + sm_ref[owner(q, core)]
            for ahead in range(1, chips):
                q = lax.rem(chip + ahead, chips)
                s2_copy(q, chip).start()
            w1_copy(chip).wait_recv()
            for k in range(2):
                gin_ref[k] = weight_rows(owner(chip, core), k) + one_recv[chip, k].astype(F32)

            share = wide // n
            for p in range(n):
                gsend[p] = gacc[:, p * share:(p + 1) * share]
            for ahead in range(1, n):
                g_copy(lax.rem(t + ahead, n), t).start()

        late = 2 * chips + 1

        @pl.when(jnp.logical_and(g >= late, g < late + subs))
        def _():
            dn_ref[:, cols_of(g - late)] = partial_tile(t, g - late)

        @pl.when(g == late + subs // 2)
        def _():
            share = wide // n
            plain = all_mine.shape[0] - 8
            all_mine[0:N, :] = LN2 * alog_ref[...]
            all_mine[N:N + 8, :] = conv_ref[...]
            all_mine[N + 8:plain, :] = jnp.zeros((plain - N - 8, all_mine.shape[1]), F32)
            all_mine[N + 8:N + 9, :] = bias_ref[...]
            all_mine[N + 9:N + 10, :] = skip_ref[...]
            all_mine[plain:, :] = jnp.zeros((8, all_mine.shape[1]), F32)
            all_mine[plain:, 0:share] = gsend[t]
            for ahead in range(1, n):
                p = lax.rem(t + ahead, n)
                g_copy(p, p).wait_recv()
                all_mine[plain:, 0:share] = all_mine[plain:, 0:share] + grecv[p]
            a1_copy().start()

        @pl.when(g == late + subs)
        def _():
            a1_copy().wait_recv()
            all_one[...] = all_one[...] + all_mine[...]
            for ahead in range(1, chips):
                a2_copy(lax.rem(chip + ahead, chips), chip).start()

        return 0

    steps = max((n - 1) * max(subs, lag), 2 * chips + subs + 2)
    lax.fori_loop(0, steps, step, 0)

    @pl.loop(0, subs)
    def _(s):
        cols = cols_of(s)

        @pl.when(t > 0)
        def _():
            i = (n - 1 - t) * subs + s
            r_copy(i).wait_recv()
            dn_ref[:, cols] = dn_ref[:, cols] + zr[i].astype(F32)

        @pl.when(t < n - 1)
        def _():
            i = t * subs + s
            l_copy(i).wait_recv()
            dn_ref[:, cols] = dn_ref[:, cols] + zl[i].astype(F32)

    gs_ref[...] = sm_one[chip]
    for ahead in range(1, chips):
        q = lax.rem(chip + ahead, chips)
        s2_copy(q, q).wait_recv()
        gs_ref[...] = gs_ref[...] + sm_two[q]
    ga_ref[...] = all_one[...]
    for ahead in range(1, chips):
        q = lax.rem(chip + ahead, chips)
        w2_copy(q, q).wait_recv()
        gin_ref[...] = gin_ref[...] + two_recv[q].astype(F32)
    for ahead in range(1, chips):
        q = lax.rem(chip + ahead, chips)
        a2_copy(q, q).wait_recv()
        ga_ref[...] = ga_ref[...] + all_two[q]

    for q in range(chips):
        s1_copy(q).wait_send()
        w1_copy(q).wait_send()
    a1_copy().wait_send()
    for ahead in range(1, n):
        g_copy(lax.rem(t + ahead, n), t).wait_send()
    for ahead in range(1, chips):
        q = lax.rem(chip + ahead, chips)
        s2_copy(q, chip).wait_send()
        a2_copy(q, chip).wait_send()
        w2_copy(q, chip).wait_send()

    @pl.loop(0, (n - 1) * subs)
    def _(i):
        @pl.when(i < (n - 1 - t) * subs)
        def _():
            r_copy(i).wait_send()

        @pl.when(i < t * subs)
        def _():
            l_copy(i).wait_send()


def tail(dx, dz, w_full, normed, dwx, dwdt, *singles):
    n, dps, seqs = (lax.axis_size(axis) for axis in ("tensor", "dp", "seq"))
    chips = dps // 2 * seqs
    rank = dwdt.shape[0]
    small_rows = -(-(rank + dwx.shape[0]) // (dps * seqs) // 8) * 8
    all_rows = N + 24
    rows = dx.shape[0] // n
    wide, lanes = w_full.shape[1], w_full.shape[2]
    wrows = wide // (dps * seqs)
    tile = 256
    subs = wide // tile
    hops = (n - 1) * subs
    vmem, hbm = pl.BlockSpec(memory_space=pltpu.VMEM), pl.BlockSpec(memory_space=pl.ANY)
    dma = pltpu.SemaphoreType.DMA
    few = dma((chips,))
    return pl.pallas_call(
        functools.partial(tail_kernel, n, dps, seqs, tile, 2, rank),
        out_shape=[
            jax.ShapeDtypeStruct((rows, wide), F32),
            jax.ShapeDtypeStruct((2, wrows, lanes), F32),
            jax.ShapeDtypeStruct((small_rows, lanes), F32),
            jax.ShapeDtypeStruct((all_rows, lanes), F32),
        ],
        in_specs=[vmem] * 2 + [hbm] + [vmem] * 7,
        out_specs=[vmem] * 4,
        scratch_shapes=[
            pltpu.VMEM((dps * seqs, small_rows, lanes), F32),
            pltpu.VMEM((8, wide), F32),
            pltpu.VMEM((n, 8, wide // n), F32),
            pltpu.VMEM((n, 8, wide // n), F32),
            pltpu.VMEM((all_rows, lanes), F32),
            pltpu.VMEM((hops, rows, tile), BF16),
            pltpu.VMEM((hops, rows, tile), BF16),
            pltpu.VMEM((2, wide, lanes), BF16),
            dma((subs,)),
            pltpu.VMEM((chips, 2, wrows, lanes), BF16),
            pltpu.VMEM((chips, 2, wrows, lanes), BF16),
            pltpu.VMEM((chips, 2, wrows, lanes), BF16),
            pltpu.VMEM((chips, small_rows, lanes), F32),
            pltpu.VMEM((chips, small_rows, lanes), F32),
            pltpu.VMEM((all_rows, lanes), F32),
            pltpu.VMEM((chips, all_rows, lanes), F32),
            dma((hops,)), dma((hops,)), dma((hops,)), dma((hops,)),
            few, few, few, few, few, few, few, few, dma, dma, few, few, dma((n,)), dma((n,)),
        ],
        compiler_params=pltpu.CompilerParams(
            collective_id=2, has_side_effects=True, vmem_limit_bytes=60 << 20
        ),
        name="tail_sums",
    )(dx, dz, w_full, normed, dwx, dwdt, *singles)


def mid_kernel(n, tile, lag, gated_ref, w_ref, hid_ref, tea_ref, scale_ref, z_hbm, scan_hbm,
               out_ref, go_ref, dwo_hbm, dscan_hbm, dz_hbm,
               zr, zl, dwo_ref, part_ref, piece_ref, z_ref, scan_ref, acc_ref, dz_ref, loads, stores, wstores,
               r_send, r_recv, l_send, l_recv, ar_send, ar_recv, al_send, al_recv):
    t = lax.axis_index("tensor")
    rows, wide = hid_ref.shape
    tokens, lanes = acc_ref.shape
    waves = wide // tile
    right, left = dict(tensor=lax.rem(t + 1, n)), dict(tensor=lax.rem(t + n - 1, n))

    barrier = pltpu.get_barrier_semaphore()
    for peer in (right, left):
        pl.semaphore_signal(barrier, inc=1, device_id=peer, device_id_type=MESH)
    pl.semaphore_wait(barrier, 2)

    def load(i):
        return pltpu.make_async_copy((z_hbm, scan_hbm)[i], (z_ref, scan_ref)[i], loads.at[i])

    for i in range(2):
        load(i).start()

    def r_copy(i):
        return mesh_copy(zr.at[i], zr.at[i], r_send.at[i], r_recv.at[i], **right)

    def l_copy(i):
        return mesh_copy(zl.at[i], zl.at[i], l_send.at[i], l_recv.at[i], **left)

    def rows_of(o):
        return pl.ds(pl.multiple_of(o * rows, rows), rows)

    def cols_of(w):
        return pl.ds(pl.multiple_of(w * tile, tile), tile)

    def ar_copy(o, w):
        ref = piece_ref.at[rows_of(o), cols_of(w)]
        return mesh_copy(ref, ref, ar_send.at[o * waves + w], ar_recv.at[o * waves + w], **right)

    def al_copy(o, w):
        ref = piece_ref.at[rows_of(o), cols_of(w)]
        return mesh_copy(ref, ref, al_send.at[o * waves + w], al_recv.at[o * waves + w], **left)

    def stream(i, hops, start, buf, copy, owner_of):
        w, k = i // n, i % n

        @pl.when(jnp.logical_and(jnp.logical_and(i >= 0, w < waves), k < hops))
        def _():
            slot = w * (n - 1) + k
            here = part_ref[rows_of(owner_of(k)), cols_of(w)]

            @pl.when(start)
            def _():
                buf[slot] = here.astype(BF16)

            @pl.when(jnp.logical_not(start))
            def _():
                copy(slot).wait_recv()
                buf[slot] = (here + buf[slot].astype(F32)).astype(BF16)

            copy(slot).start()

    def ready(o):
        from_left = jnp.where(o > 0, n - 1 - o + lag * o, 0)
        from_right = jnp.where(o < n - 1, o + lag * (n - 1 - o), 0)
        return jnp.maximum(from_left, from_right)

    def host_ready(o):
        return max((n - 1 - o + lag * o) * (o > 0), (o + lag * (n - 1 - o)) * (o < n - 1))

    def finish(w):
        cols = cols_of(w)
        go_ref[:, cols] = part_ref[rows_of(t), cols]

        @pl.when(t > 0)
        def _():
            slot = w * (n - 1) + n - 1 - t
            r_copy(slot).wait_recv()
            go_ref[:, cols] = go_ref[:, cols] + zr[slot].astype(F32)

        @pl.when(t < n - 1)
        def _():
            slot = w * (n - 1) + t
            l_copy(slot).wait_recv()
            go_ref[:, cols] = go_ref[:, cols] + zl[slot].astype(F32)

        result = hid_ref[:, cols].astype(F32) + go_ref[:, cols]
        out_ref[:, cols] = result.astype(BF16)
        grad = scale_ref[...] * (result - tea_ref[:, cols].astype(F32))
        go_ref[:, cols] = grad
        piece_ref[rows_of(t), cols] = grad.astype(BF16)

        @pl.when(t < n - 1)
        def _():
            ar_copy(t, w).start()

        @pl.when(t > 0)
        def _():
            al_copy(t, w).start()

    def stored(i, o):
        src = (acc_ref, dz_ref)[i].at[rows_of(o), :]
        return pltpu.make_async_copy(src, (dscan_hbm, dz_hbm)[i].at[rows_of(o), :], stores.at[i, o])

    def stored_weight(w):
        here = pl.ds(pl.multiple_of(w * tile, tile), tile)
        return pltpu.make_async_copy(dwo_ref.at[w], dwo_hbm.at[here, :], wstores.at[w])

    def gate(o):
        z = z_ref[rows_of(o), :]
        s = 1.0 / (1.0 + jnp.exp(-z))
        z_ref[rows_of(o), :] = z * s
        scan_ref[rows_of(o), :] = scan_ref[rows_of(o), :] * (s * (1.0 + z * (1.0 - s)))

    def backward(w):
        tn = (((0,), (0,)), ((), ()))
        dwo_ref[w] = lax.dot_general(
            piece_ref[:, cols_of(w)], gated_ref[...], tn, preferred_element_type=F32
        ).astype(BF16)
        stored_weight(w).start()

        @pl.loop(0, n)
        def _(o):
            here = rows_of(o)
            d_gated = jnp.dot(piece_ref[here, cols_of(w)], w_ref[cols_of(w), :], preferred_element_type=F32)

            @pl.when(w == 0)
            def _():
                acc_ref[here, :] = d_gated

            @pl.when(jnp.logical_and(w > 0, w < waves - 1))
            def _():
                acc_ref[here, :] = acc_ref[here, :] + d_gated

            @pl.when(w == waves - 1)
            def _():
                total = acc_ref[here, :] + d_gated
                acc_ref[here, :] = total * z_ref[here, :]
                dz_ref[here, :] = (total * scan_ref[here, :]).astype(BF16)
                stored(0, o).start()
                stored(1, o).start()

    arrived = jnp.int32(0)
    for o in range(n):
        arrived = jnp.maximum(arrived, host_ready(o) + lag * jnp.abs(t - o))

    def step(g, _):
        @pl.when(jnp.logical_and(g % n == 0, g < n * waves))
        def _():
            cols = cols_of(g // n)
            nt = (((1,), (1,)), ((), ()))

            @pl.loop(0, n)
            def _(o):
                part_ref[rows_of(o), cols] = lax.dot_general(
                    gated_ref[rows_of(o), :], w_ref[cols, :], nt, preferred_element_type=F32
                )

        stream(g - lag * t, n - 1 - t, t == 0, zr, r_copy, lambda k: n - 1 - k)
        stream(g - lag * (n - 1 - t), t, t == n - 1, zl, l_copy, lambda k: k)

        own = g - ready(t)

        @pl.when(jnp.logical_and(own >= 0, jnp.logical_and(own % n == 0, own // n < waves)))
        def _():
            finish(own // n)

        @pl.loop(0, n)
        def _(o):
            i = g - ready(o) - lag * jnp.abs(t - o)
            w = i // n

            @pl.when(jnp.logical_and(o != t, jnp.logical_and(i >= 0, jnp.logical_and(i % n == 0, w < waves))))
            def _():
                @pl.when(o < t)
                def _():
                    ar_copy(o, w).wait_recv()

                    @pl.when(t < n - 1)
                    def _():
                        ar_copy(o, w).start()

                @pl.when(o > t)
                def _():
                    al_copy(o, w).wait_recv()

                    @pl.when(t > 0)
                    def _():
                        al_copy(o, w).start()

        @pl.when(g == 1)
        def _():
            for i in range(2):
                load(i).wait()

        @pl.when(jnp.logical_and(g >= 1, g <= n))
        def _():
            gate(g - 1)

        done = g - arrived

        @pl.when(jnp.logical_and(done >= 0, jnp.logical_and(done % n == 0, done // n < waves)))
        def _():
            backward(done // n)

        return 0

    steps = max(host_ready(o) + lag * abs(o - d) for o in range(n) for d in range(n)) + n * (waves - 1) + 1
    lax.fori_loop(0, max(steps, n + 1), step, 0)

    @pl.loop(0, (n - 1) * waves)
    def _(i):
        @pl.when(i % (n - 1) < n - 1 - t)
        def _():
            r_copy(i).wait_send()

        @pl.when(i % (n - 1) < t)
        def _():
            l_copy(i).wait_send()

    @pl.loop(0, n * waves)
    def _(i):
        o, w = i // waves, i % waves

        @pl.when(jnp.logical_and(o <= t, t < n - 1))
        def _():
            ar_copy(o, w).wait_send()

        @pl.when(jnp.logical_and(o >= t, t > 0))
        def _():
            al_copy(o, w).wait_send()

    @pl.loop(0, waves)
    def _(w):
        stored_weight(w).wait()

    @pl.loop(0, n)
    def _(o):
        stored(0, o).wait()
        stored(1, o).wait()


def middle(gated, w_out, hidden, teacher, scale, z_gate, scan_out):
    n = lax.axis_size("tensor")
    rows, wide = hidden.shape
    tokens, lanes = gated.shape
    tile = 256
    waves = wide // tile
    hops = (n - 1) * waves
    vmem, hbm = pl.BlockSpec(memory_space=pltpu.VMEM), pl.BlockSpec(memory_space=pl.ANY)
    dma = pltpu.SemaphoreType.DMA
    return pl.pallas_call(
        functools.partial(mid_kernel, n, tile, 2),
        out_shape=[
            jax.ShapeDtypeStruct((rows, wide), BF16),
            jax.ShapeDtypeStruct((rows, wide), F32),
            jax.ShapeDtypeStruct((wide, lanes), BF16),
            jax.ShapeDtypeStruct((tokens, lanes), F32),
            jax.ShapeDtypeStruct((tokens, lanes), BF16),
        ],
        in_specs=[vmem] * 5 + [hbm] * 2,
        out_specs=[vmem] * 2 + [hbm] * 3,
        scratch_shapes=[
            pltpu.VMEM((hops, rows, tile), BF16),
            pltpu.VMEM((hops, rows, tile), BF16),
            pltpu.VMEM((waves, tile, lanes), BF16),
            pltpu.VMEM((tokens, wide), F32),
            pltpu.VMEM((tokens, wide), BF16),
            pltpu.VMEM((tokens, lanes), F32),
            pltpu.VMEM((tokens, lanes), F32),
            pltpu.VMEM((tokens, lanes), F32),
            pltpu.VMEM((tokens, lanes), BF16),
            dma((2,)), dma((2, n)), dma((waves,)),
            dma((hops,)), dma((hops,)), dma((hops,)), dma((hops,)),
            dma((n * waves,)), dma((n * waves,)), dma((n * waves,)), dma((n * waves,)),
        ],
        compiler_params=pltpu.CompilerParams(
            collective_id=1, has_side_effects=True, vmem_limit_bytes=60 << 20
        ),
        name="middle",
    )(gated, w_out, hidden, teacher, scale, z_gate, scan_out)


def front_kernel(n, dps, seqs, subs, lag, hid_ref, gain_ref, seg_ref, win_ref, wsm_ref, taps_ref, keep_ref,
                 x_out, z_out, nrm_out, w_out, conv_out, low_out, total_ref, gfull, ws_ref, natural_ref,
                 rows_ref, gain_tile, cnt_tile, grecv, cnt_one, cnt_two, x_ref, z_ref, nrm_ref, w_ref, conv_ref, low_ref,
                 mix_send, mix_recv, mix_own, mix_rows_ref, mixed_ref, outs, ms, mr, ns, nr,
                 ar_send, ar_recv, al_send, al_recv, gs, gr, c1s, c1r, c2s, c2r, hs, hr, ls,
                 chip_send, chip_recv, core_send, core_recv):
    dp, seq, t = place()
    core, hi = dp % 2, dp // 2
    chips = dps // 2 * seqs
    chip = hi * seqs + seq
    rows, wide = hid_ref.shape
    part = rows // subs
    share = wide // n
    wrows = win_ref.shape[1]
    tile = 512
    gap = max(subs, lag)
    partner = dict(dp=hi * 2 + 1 - core)
    right, left = dict(tensor=lax.rem(t + 1, n)), dict(tensor=lax.rem(t + n - 1, n))

    def owner(q, c):
        return (q // seqs * 2 + c) * seqs + q % seqs

    def to_chip(q):
        return dict(dp=q // seqs * 2 + core, seq=q % seqs)

    barrier = pltpu.get_barrier_semaphore()
    pl.semaphore_signal(barrier, inc=1, device_id=partner, device_id_type=MESH)
    for ahead in range(1, chips):
        pl.semaphore_signal(barrier, inc=1, device_id=to_chip(lax.rem(chip + ahead, chips)), device_id_type=MESH)
    for ahead in range(1, n):
        pl.semaphore_signal(barrier, inc=1, device_id=dict(tensor=lax.rem(t + ahead, n)), device_id_type=MESH)
    pl.semaphore_wait(barrier, chips + n - 1)

    def at(o, s):
        return pl.ds(pl.multiple_of(o * rows + s * part, part), part)

    def ar_copy(o, s):
        ref = rows_ref.at[at(o, s), :]
        return mesh_copy(ref, ref, ar_send.at[o * subs + s], ar_recv.at[o * subs + s], **right)

    def al_copy(o, s):
        ref = rows_ref.at[at(o, s), :]
        return mesh_copy(ref, ref, al_send.at[o * subs + s], al_recv.at[o * subs + s], **left)

    def g_copy(p, slot):
        return mesh_copy(gain_tile, grecv.at[slot], gs.at[p], gr.at[slot], tensor=p)

    def block(kind, p):
        if kind == 0:
            return w_ref.at[:, pl.ds(pl.multiple_of(p * wrows, wrows), wrows), :]
        return ws_ref.at[p]

    stored = (win_ref, wsm_ref)

    def chip_copy(kind, q, p):
        return mesh_copy(stored[kind], block(kind, p), chip_send.at[kind, q], chip_recv.at[kind, p], **to_chip(q))

    def core_copy(kind, p, own):
        src = stored[kind] if own else block(kind, p)
        return mesh_copy(src, block(kind, p), core_send.at[kind, p], core_recv.at[kind, p], **partner)

    mine = owner(chip, core)

    def count_one():
        return mesh_copy(cnt_tile, cnt_one, c1s, c1r, **partner)

    def count_two(q, slot):
        return mesh_copy(cnt_one, cnt_two.at[slot], c2s.at[q], c2r.at[slot], **to_chip(q))

    def edge_copy():
        last = x_ref.at[pl.ds(x_ref.shape[0] - 8, 8), :]
        return mesh_copy(last, x_ref.at[pl.ds(0, 8), :], hs, hr, seq=lax.rem(seq + 1, seqs))

    def mix_copy(p, slot):
        return mesh_copy(mix_send.at[p], mix_recv.at[slot], ms.at[p], mr.at[slot], tensor=p)

    def sum_copy(p, slot):
        return mesh_copy(mixed_ref.at[slot], mixed_ref.at[slot], ns.at[p], nr.at[slot], tensor=p)

    def written(i):
        src = (w_ref, nrm_ref, z_ref, x_ref, conv_ref, low_ref)[i]
        return pltpu.make_async_copy(src, (w_out, nrm_out, z_out, x_out, conv_out, low_out)[i], outs.at[i])

    def local_copy():
        return pltpu.make_async_copy(wsm_ref, block(1, mine), ls)

    gain_tile[...] = jnp.broadcast_to(gain_ref[...].astype(F32), gain_tile.shape)
    cnt_tile[...] = jnp.full(cnt_tile.shape, jnp.sum((seg_ref[...] != 0).astype(F32)))
    for ahead in range(1, n):
        g_copy(lax.rem(t + ahead, n), t).start()
    count_one().start()
    rows_ref[pl.ds(pl.multiple_of(t * rows, rows), rows), :] = hid_ref[...]

    @pl.loop(0, subs)
    def _(s):
        @pl.when(t < n - 1)
        def _():
            ar_copy(t, s).start()

        @pl.when(t > 0)
        def _():
            al_copy(t, s).start()

    def share_out(kind):
        for ahead in range(1, chips):
            chip_copy(kind, lax.rem(chip + ahead, chips), mine).start()
        core_copy(kind, mine, True).start()

    share_out(1)
    share_out(0)
    local_copy().start()
    w_ref[:, pl.ds(pl.multiple_of(mine * wrows, wrows), wrows), :] = win_ref[...]

    gfull[...] = jnp.zeros_like(gfull)
    for ahead in range(1, n):
        p = lax.rem(t + ahead, n)
        g_copy(p, p).wait_recv()
    grecv[t] = gain_tile[...]
    for p in range(n):
        gfull[:, p * share:(p + 1) * share] = grecv[p]
    count_one().wait_recv()
    count_one().wait_send()
    cnt_one[...] = cnt_one[...] + cnt_tile[...]
    for ahead in range(1, chips):
        count_two(lax.rem(chip + ahead, chips), chip).start()

    def normalize(o):
        @pl.loop(0, subs)
        def _(s):
            here = at(o, s)
            values = rows_ref[here, :].astype(F32)
            inv = lax.rsqrt(jnp.mean(values * values, axis=1, keepdims=True) + EPS)
            nrm_ref[here, :] = (values * inv * gfull[0:1, :]).astype(BF16)

    def project(o):
        here = pl.ds(pl.multiple_of(o * rows, rows), rows)
        for k, dst in enumerate((x_ref, z_ref)):
            lanes = dst.shape[1]
            width = min(tile, lanes)
            there = pl.ds(pl.multiple_of(o * rows + 8 - 8 * k, 8), rows)

            @pl.loop(0, lanes // width)
            def _(j):
                cols = pl.ds(pl.multiple_of(j * width, width), width)
                dst[there, cols] = jnp.dot(nrm_ref[here, :], w_ref[k, :, cols], preferred_element_type=F32)

    lanes = low_ref.shape[1]
    width = min(tile, lanes)
    piece = min(64, rows)
    taps = keep_ref.shape[1]

    def convolve(o):
        @pl.loop(0, rows // piece * (lanes // width))
        def _(i):
            base = o * rows + i // (lanes // width) * piece
            here = pl.ds(pl.multiple_of(base, piece), piece)
            cols = pl.ds(pl.multiple_of(i % (lanes // width) * width, width), width)
            span = x_ref[pl.ds(pl.multiple_of(base, piece), piece + 8), cols]
            keep = keep_ref[here, :]
            total = jnp.broadcast_to(taps_ref[taps:taps + 1, cols], (piece, width))
            for j in range(taps):
                first = 8 - (taps - 1) + j
                total = total + taps_ref[j:j + 1, cols] * span[first:first + piece] * keep[:, j:j + 1]
            conv_ref[here, cols] = total
            low_ref[here, cols] = (total / (1.0 + jnp.exp(-total))).astype(BF16)

    groups, depth = ws_ref.shape[0], ws_ref.shape[1]
    live = natural_ref.shape[0] // groups

    def mix_rows(o):
        convolve(o)
        nt = (((1,), (1,)), ((), ()))
        low = low_ref[pl.ds(pl.multiple_of(o * rows, rows), rows), :]
        weights = ws_ref[...].reshape(groups * depth, lanes)
        mix = lax.dot_general(weights, low, nt, preferred_element_type=F32)
        for p in range(groups):
            mix_rows_ref[p * live:(p + 1) * live, :] = mix[p * depth:p * depth + live]

        @pl.when(o != t)
        def _():
            mix_send[o] = mix_rows_ref[...].astype(BF16)
            mix_copy(o, t).start()

        @pl.when(o == t)
        def _():
            mix_own[...] = mix_rows_ref[...]

    def turn(d, o):
        final = jnp.where(o == 0, (n - 1) * gap + 1, (n - 2 - o) * gap + lag)
        return jnp.where(d == n - 1, final, (d - o) * gap)

    weights_at = (n - 1) * gap

    def step(g, _):
        @pl.when(g == 0)
        def _():
            normalize(t)

        @pl.when(g == weights_at)
        def _():
            for kind in (1, 0):
                for ahead in range(1, chips):
                    q = lax.rem(chip + ahead, chips)
                    chip_copy(kind, q, owner(q, core)).wait_recv()
                    core_copy(kind, owner(q, core), False).start()
            for kind in (1, 0):
                for q in range(chips):
                    core_copy(kind, owner(q, 1 - core), True).wait_recv()
            project(t)

        @pl.loop(0, n)
        def _(o):
            s_right = g - turn(t, o)
            s_left = g - turn(n - 1 - t, n - 1 - o)

            @pl.when(jnp.logical_and(o < t, jnp.logical_and(s_right >= 0, s_right < subs)))
            def _():
                ar_copy(o, s_right).wait_recv()

                @pl.when(t < n - 1)
                def _():
                    ar_copy(o, s_right).start()

            @pl.when(jnp.logical_and(o > t, jnp.logical_and(s_left >= 0, s_left < subs)))
            def _():
                al_copy(o, s_left).wait_recv()

                @pl.when(t > 0)
                def _():
                    al_copy(o, s_left).start()

            landed = jnp.where(o < t, s_right, s_left) - subs + 1

            @pl.when(jnp.logical_and(o != t, landed == 0))
            def _():
                normalize(o)

            ripe = jnp.where(g == weights_at, landed >= 0, jnp.logical_and(g > weights_at, landed == 0))

            @pl.when(jnp.logical_and(o != t, ripe))
            def _():
                project(o)

        return 0

    steps = weights_at + 1 + subs
    lax.fori_loop(0, steps, step, 0)

    @pl.when(seq < seqs - 1)
    def _():
        edge_copy().start()

    @pl.when(seq == 0)
    def _():
        x_ref[0:8, :] = jnp.zeros((8, x_ref.shape[1]), F32)

    for i in range(3):
        written(i).start()

    @pl.when(seq > 0)
    def _():
        edge_copy().wait_recv()

    @pl.when(seq < seqs - 1)
    def _():
        edge_copy().wait_send()

    written(3).start()
    local_copy().wait()
    @pl.loop(0, n)
    def _(i):
        mix_rows(lax.rem(t + 1 + i, n))

    for i in range(4, 6):
        written(i).start()
    for ahead in range(1, n):
        p = lax.rem(t + ahead, n)
        mix_copy(p, p).wait_recv()
        mix_own[...] = mix_own[...] + mix_recv[p].astype(F32)
    mixed_ref[t] = mix_own[...].astype(BF16)
    for ahead in range(1, n):
        sum_copy(lax.rem(t + ahead, n), t).start()
    total_ref[...] = cnt_one[...]
    for ahead in range(1, chips):
        q = lax.rem(chip + ahead, chips)
        count_two(q, q).wait_recv()
        total_ref[...] = total_ref[...] + cnt_two[q]
    for ahead in range(1, n):
        p = lax.rem(t + ahead, n)
        sum_copy(p, p).wait_recv()
    for o in range(n):
        natural_ref[:, o * rows:(o + 1) * rows] = mixed_ref[o].astype(F32)
    for ahead in range(1, n):
        p = lax.rem(t + ahead, n)
        mix_copy(p, t).wait_send()
        sum_copy(p, t).wait_send()
    for i in range(6):
        written(i).wait()
    for kind in range(2):
        for ahead in range(1, chips):
            chip_copy(kind, lax.rem(chip + ahead, chips), mine).wait_send()
        for q in range(chips):
            core_copy(kind, owner(q, core), False).wait_send()
    for ahead in range(1, chips):
        count_two(lax.rem(chip + ahead, chips), chip).wait_send()
    for ahead in range(1, n):
        g_copy(lax.rem(t + ahead, n), t).wait_send()

    @pl.loop(0, n * subs)
    def _(i):
        o, s = i // subs, i % subs

        @pl.when(jnp.logical_and(o <= t, t < n - 1))
        def _():
            ar_copy(o, s).wait_send()

        @pl.when(jnp.logical_and(o >= t, t > 0))
        def _():
            al_copy(o, s).wait_send()


def front(hidden, gain, segments, w_in, w_small, taps, keeps, x_cols):
    n, dps, seqs = (lax.axis_size(axis) for axis in ("tensor", "dp", "seq"))
    parts = dps * seqs
    chips = parts // 2
    rows, wide = hidden.shape
    lanes = w_in.shape[2]
    tokens = rows * n
    mixed = parts * x_cols
    subs = max(1, rows // 32)
    vmem, hbm = pl.BlockSpec(memory_space=pltpu.VMEM), pl.BlockSpec(memory_space=pl.ANY)
    dma = pltpu.SemaphoreType.DMA
    many, few, peers = dma((n * subs,)), dma((chips,)), dma((n,))
    return pl.pallas_call(
        functools.partial(front_kernel, n, dps, seqs, subs, 2),
        out_shape=[
            jax.ShapeDtypeStruct((tokens + 8, lanes), F32),
            jax.ShapeDtypeStruct((tokens, lanes), F32),
            jax.ShapeDtypeStruct((tokens, wide), BF16),
            jax.ShapeDtypeStruct((2, wide, lanes), BF16),
            jax.ShapeDtypeStruct((tokens, lanes), F32),
            jax.ShapeDtypeStruct((tokens, lanes), BF16),
            jax.ShapeDtypeStruct((8, 128), F32),
            jax.ShapeDtypeStruct((8, wide), F32),
            jax.ShapeDtypeStruct((parts,) + w_small.shape, BF16),
            jax.ShapeDtypeStruct((parts * x_cols, tokens), F32),
        ],
        in_specs=[vmem] * 7,
        out_specs=[hbm] * 6 + [vmem] * 4,
        scratch_shapes=[
            pltpu.VMEM((tokens, wide), BF16),
            pltpu.VMEM((8, gain.shape[1]), F32),
            pltpu.VMEM((8, 128), F32),
            pltpu.VMEM((n, 8, gain.shape[1]), F32),
            pltpu.VMEM((8, 128), F32),
            pltpu.VMEM((chips, 8, 128), F32),
            pltpu.VMEM((tokens + 8, lanes), F32),
            pltpu.VMEM((tokens, lanes), F32),
            pltpu.VMEM((tokens, wide), BF16),
            pltpu.VMEM((2, wide, lanes), BF16),
            pltpu.VMEM((tokens, lanes), F32),
            pltpu.VMEM((tokens, lanes), BF16),
            pltpu.VMEM((n, mixed, rows), BF16),
            pltpu.VMEM((n, mixed, rows), BF16),
            pltpu.VMEM((mixed, rows), F32),
            pltpu.VMEM((mixed, rows), F32),
            pltpu.VMEM((n, mixed, rows), BF16),
            dma((6,)), peers, peers, peers, peers,
            many, many, many, many, peers, peers, dma, dma, few, few, dma, dma, dma,
            dma((2, chips)), dma((2, parts)), dma((2, parts)), dma((2, parts)),
        ],
        compiler_params=pltpu.CompilerParams(
            collective_id=3, has_side_effects=True, vmem_limit_bytes=60 << 20
        ),
        name="front",
    )(hidden, gain, segments, w_in, w_small, taps, keeps)


def mixback_kernel(n, seqs, part_ref, e_hbm, conv_hbm, x_hbm, low_hbm, dpl_hbm, step_ref, wx_ref, taps_ref, keep_ref,
                   dx_hbm, dwx_ref, dwdt_ref, dconvw_ref,
                   e_ref, conv_ref, x_ref, low_ref, dpl_ref, dx_ref, dcv_ref, got, own, done, edge_out, edge_in,
                   loads, store, ms, mr, ns, nr, es, er):
    seq, t = lax.axis_index("seq"), lax.axis_index("tensor")
    rows = part_ref.shape[2]
    tokens, lanes = low_ref.shape
    taps = keep_ref.shape[1]
    width = min(512, lanes)
    piece = min(64, rows)
    across = lanes // width
    pieces = tokens // piece * across
    ahead_seq, behind_seq = lax.rem(seq + 1, seqs), lax.rem(seq + seqs - 1, seqs)

    barrier = pltpu.get_barrier_semaphore()
    for ahead in range(1, n):
        pl.semaphore_signal(barrier, inc=1, device_id=dict(tensor=lax.rem(t + ahead, n)), device_id_type=MESH)
    if seqs > 1:
        for peer in (ahead_seq, behind_seq):
            pl.semaphore_signal(barrier, inc=1, device_id=dict(seq=peer), device_id_type=MESH)
    pl.semaphore_wait(barrier, n - 1 + (2 if seqs > 1 else 0))

    def load(i):
        src = (conv_hbm, dpl_hbm, e_hbm, low_hbm, x_hbm)[i]
        return pltpu.make_async_copy(src, (conv_ref, dpl_ref, e_ref, low_ref, x_ref)[i], loads.at[i])

    def mix_copy(p, slot):
        return mesh_copy(part_ref.at[p], got.at[slot], ms.at[p], mr.at[slot], tensor=p)

    def sum_copy(p, slot):
        return mesh_copy(done.at[slot], done.at[slot], ns.at[p], nr.at[slot], tensor=p)

    def edge_copy():
        return mesh_copy(edge_out, edge_in, es, er, seq=behind_seq)

    for ahead in range(1, n):
        mix_copy(lax.rem(t + ahead, n), t).start()
    for i in range(5):
        load(i).start()

    dcv_ref[0:8, :] = jnp.zeros((8, lanes), F32)
    dcv_ref[tokens + 8:, :] = jnp.zeros((8, lanes), F32)
    load(1).wait()
    step = step_ref[0:dwdt_ref.shape[0], :].astype(BF16)
    tn = (((0,), (0,)), ((), ()))

    @pl.loop(0, across)
    def _(j):
        cols = pl.ds(pl.multiple_of(j * width, width), width)
        dwdt_ref[:, cols] = jnp.dot(step, dpl_ref[:, cols], preferred_element_type=F32)

    own[...] = part_ref[t].astype(F32)
    for ahead in range(1, n):
        p = lax.rem(t + ahead, n)
        mix_copy(p, p).wait_recv()
        own[...] = own[...] + got[p].astype(F32)
    done[t] = own[...].astype(BF16)
    for ahead in range(1, n):
        sum_copy(lax.rem(t + ahead, n), t).start()

    load(0).wait()

    @pl.loop(0, pieces)
    def _(i):
        here = pl.ds(pl.multiple_of(i // across * piece, piece), piece)
        cols = pl.ds(pl.multiple_of(i % across * width, width), width)
        v = conv_ref[here, cols]
        s = 1.0 / (1.0 + jnp.exp(-v))
        conv_ref[here, cols] = s * (1.0 + v * (1.0 - s))

    for i in range(2, 5):
        load(i).wait()
    for ahead in range(1, n):
        p = lax.rem(t + ahead, n)
        sum_copy(p, p).wait_recv()

    dwx_ref[...] = jnp.zeros_like(dwx_ref)
    dconvw_ref[...] = jnp.zeros_like(dconvw_ref)

    @pl.loop(0, n)
    def _(o):
        @pl.loop(0, across)
        def _(j):
            cols = pl.ds(pl.multiple_of(j * width, width), width)
            here = pl.ds(pl.multiple_of(o * rows, rows), rows)
            mixed = lax.dot_general(done[o], wx_ref[:, cols], tn, preferred_element_type=F32)
            dcv = (e_ref[here, cols] + mixed) * conv_ref[here, cols]
            dcv_ref[pl.ds(pl.multiple_of(o * rows + 8, 8), rows), cols] = dcv
            dwx_ref[:, cols] = dwx_ref[:, cols] + jnp.dot(done[o], low_ref[here, cols], preferred_element_type=F32)

    def shifted(base, size, cols):
        span = dcv_ref[pl.ds(base, size + 8), cols]
        keep = keep_ref[pl.ds(base, size + 8), :]
        total = jnp.zeros((size, span.shape[1]), F32)
        for j in range(taps):
            late = taps - 1 - j
            total = total + taps_ref[j:j + 1, cols] * (span * keep[:, j:j + 1])[late:late + size]
        return total

    if seqs > 1:
        edge_out[...] = shifted(0, 8, slice(None))

        @pl.when(seq > 0)
        def _():
            edge_copy().start()

    @pl.loop(0, pieces)
    def _(i):
        base = pl.multiple_of(i // across * piece, piece)
        cols = pl.ds(pl.multiple_of(i % across * width, width), width)
        dx_ref[pl.ds(base, piece), cols] = shifted(pl.multiple_of(base + 8, 8), piece, cols).astype(BF16)
        here = dcv_ref[pl.ds(pl.multiple_of(base + 8, 8), piece), cols]
        keep = keep_ref[pl.ds(pl.multiple_of(base + 8, 8), piece), :]
        span = x_ref[pl.ds(base, piece + 8), cols]
        for j in range(taps):
            first = 8 - (taps - 1) + j
            tap = jnp.sum(here * keep[:, j:j + 1] * span[first:first + piece], axis=0, keepdims=True)
            dconvw_ref[j:j + 1, cols] = dconvw_ref[j:j + 1, cols] + tap
        dconvw_ref[taps:taps + 1, cols] = dconvw_ref[taps:taps + 1, cols] + jnp.sum(here, axis=0, keepdims=True)

    if seqs > 1:
        @pl.when(seq < seqs - 1)
        def _():
            edge_copy().wait_recv()
            last = shifted(tokens - 16 + 8, 16, slice(None))
            dx_ref[tokens - 16:, :] = (last + jnp.concatenate([jnp.zeros_like(edge_in), edge_in[...]], 0)).astype(BF16)

        @pl.when(seq > 0)
        def _():
            edge_copy().wait_send()

    out = pltpu.make_async_copy(dx_ref, dx_hbm, store)
    out.start()
    for ahead in range(1, n):
        p = lax.rem(t + ahead, n)
        mix_copy(p, t).wait_send()
        sum_copy(p, t).wait_send()
    out.wait()


def mixback(part, e, conv_sum, x_rows, x_low, d_pre_low, mix_t, w_x, taps, keeps, rank):
    n, seqs = lax.axis_size("tensor"), lax.axis_size("seq")
    tokens, lanes = x_low.shape
    mixed, rows = part.shape[1:]
    vmem, hbm = pl.BlockSpec(memory_space=pltpu.VMEM), pl.BlockSpec(memory_space=pl.ANY)
    dma = pltpu.SemaphoreType.DMA
    peers = dma((n,))
    return pl.pallas_call(
        functools.partial(mixback_kernel, n, seqs),
        out_shape=[
            jax.ShapeDtypeStruct((tokens, lanes), BF16),
            jax.ShapeDtypeStruct((mixed, lanes), F32),
            jax.ShapeDtypeStruct((rank, lanes), F32),
            jax.ShapeDtypeStruct((8, lanes), F32),
        ],
        in_specs=[vmem] + [hbm] * 5 + [vmem] * 4,
        out_specs=[hbm] + [vmem] * 3,
        scratch_shapes=[
            pltpu.VMEM((tokens, lanes), F32),
            pltpu.VMEM((tokens, lanes), F32),
            pltpu.VMEM((tokens + 8, lanes), F32),
            pltpu.VMEM((tokens, lanes), BF16),
            pltpu.VMEM((tokens, lanes), BF16),
            pltpu.VMEM((tokens, lanes), BF16),
            pltpu.VMEM((tokens + 16, lanes), F32),
            pltpu.VMEM((n, mixed, rows), BF16),
            pltpu.VMEM((mixed, rows), F32),
            pltpu.VMEM((n, mixed, rows), BF16),
            pltpu.VMEM((8, lanes), F32),
            pltpu.VMEM((8, lanes), F32),
            dma((5,)), dma, peers, peers, peers, peers, dma, dma,
        ],
        compiler_params=pltpu.CompilerParams(
            collective_id=4, has_side_effects=True, vmem_limit_bytes=60 << 20
        ),
        name="mix_backward",
    )(part, e, conv_sum, x_rows, x_low, d_pre_low, mix_t, w_x, taps, keeps)


def on_device(
    hidden_in,
    teacher,
    segment_ids,
    norm_gain,
    input_projection_weight,
    conv_weight,
    conv_bias,
    xproj_weight,
    dtproj_weight,
    dt_bias,
    a_log,
    d_skip,
    output_projection_weight,
):
    tok_rows = segment_ids.shape[0]
    row_share = hidden_in.shape[0]
    model_width = hidden_in.shape[1]
    conv_taps = conv_weight.shape[0]
    chan_lanes = conv_weight.shape[1]
    back_rows = conv_taps - 1
    row_start = lax.axis_index("tensor") * row_share
    valid_mask = (segment_ids != 0).astype(jnp.float32)
    parts = lax.axis_size(("dp", "seq"))
    x_cols, dt_rows = xproj_weight.shape[1], dtproj_weight.shape[0]
    w_small = jnp.concatenate(
        [
            xproj_weight.T,
            jnp.zeros((SMALL_ROWS - x_cols, chan_lanes), BF16),
            dtproj_weight,
            jnp.zeros((-(SMALL_ROWS + dt_rows) % 16, chan_lanes), BF16),
        ],
        0,
    )
    seg_float = segment_ids.astype(F32)
    prev_seg = jnp.where(lax.axis_index("seq") > 0, seg_float[:1], jnp.zeros((back_rows,), F32))
    ext_seg = jnp.concatenate([prev_seg, seg_float], 0)
    tap_keeps = []
    for offset in range(conv_taps):
        tap_keeps.append((ext_seg[offset : offset + tok_rows] == seg_float).astype(F32)[:, None])
    taps = jnp.concatenate(
        [conv_weight.astype(F32), conv_bias.astype(F32)[None], jnp.zeros((7 - conv_taps, chan_lanes), F32)], 0
    )
    x_rows, z_gate, normalized_rows, w_in, conv_sum, x_low, total, gain_rows, w_small, mix_t = front(
        hidden_in,
        norm_gain[None],
        segment_ids.reshape(8, -1),
        jnp.swapaxes(input_projection_weight, 0, 1),
        w_small,
        taps,
        jnp.concatenate(tap_keeps, 1),
        x_cols,
    )
    w_out_rows, z_gate = lax.optimization_barrier((output_projection_weight.T, z_gate))
    w_out = lax.all_gather(w_out_rows, ("dp", "seq"), axis=0, tiled=True)
    total_count = total[0, 0]
    w_x = w_small[:, :x_cols].reshape(parts * x_cols, chan_lanes)
    w_dt = w_small[:, SMALL_ROWS : SMALL_ROWS + dt_rows].reshape(parts * dt_rows, chan_lanes)
    share_rows = hidden_in.astype(F32)
    full_gain = gain_rows[0]
    inv_share = lax.rsqrt(jnp.mean(share_rows * share_rows, axis=1, keepdims=True) + EPS)
    rank_width = w_dt.shape[0]
    same_doc = (seg_float == ext_seg[back_rows - 1 : back_rows - 1 + tok_rows]).astype(jnp.float32)
    rates = -jnp.exp(a_log) * LOG2E
    block = 128
    first_reset = jnp.min(jnp.where(same_doc == 0, jnp.arange(tok_rows), tok_rows))
    alive = (jnp.arange(0, tok_rows, block) <= first_reset).astype(jnp.int32)
    y_local, marks, state_last, stepd, inject, step_size, step_slope = fwd(
        mix_t, w_dt, dt_bias[None], x_low, same_doc[:, None], rates, tb=block, w=1024
    )

    def reach():
        return jnp.exp2(rates * jnp.sum(stepd, axis=0)[None])

    state_in = carried(state_last, reach, "seq", 1)
    scan_out, marks, gated_output_rows = correct(
        rank_width, alive, y_local, stepd, mix_t, rates, marks, state_in, x_low, d_skip[None], z_gate, tb=block, w=1024
    )
    valid_share = lax.dynamic_slice_in_dim(valid_mask, row_start, row_share, 0)
    total_tokens = float(tok_rows * lax.axis_size(("dp", "seq")))
    scale = (total_tokens / total_count * valid_share)[:, None]
    output, grad_out, d_wout, d_scan, d_z = middle(
        gated_output_rows, w_out, hidden_in, teacher, scale, z_gate, scan_out
    )
    adjoint_first = entry(rank_width, alive, stepd, d_scan, mix_t, rates, tb=block, w=1024)
    adjoint_in = carried(adjoint_first, reach, "seq", -1)
    d_pre_low, d_direct, d_rank_t, d_b_part, d_c_part, a_log_part, dt_bias_part, d_skip_part = bwd(
        stepd, inject, d_scan, mix_t, rates, marks, adjoint_in,
        step_size, step_slope, x_low, d_skip[None], w_dt, tb=block
    )
    part = jnp.concatenate(
        [
            jnp.sum(d_rank_t, axis=0),
            jnp.sum(d_b_part, axis=0).reshape(tok_rows, N).T,
            jnp.sum(d_c_part, axis=0).reshape(tok_rows, N).T,
        ],
        0,
    )
    part = part.astype(BF16).reshape(part.shape[0], -1, row_share).transpose(1, 0, 2)
    edge = jnp.zeros((8, conv_taps), F32)
    d_x, d_wx, d_wdt, conv_parts = mixback(
        part, d_direct, conv_sum, x_rows, x_low, d_pre_low, mix_t, w_x, taps,
        jnp.concatenate([edge] + [jnp.concatenate(tap_keeps, 1)] + [edge], 0),
        rank_width,
    )
    d_norm_share, g_in, g_small, g_whole = tail(
        d_x, d_z, w_in, normalized_rows, d_wx, d_wdt, a_log_part, conv_parts, dt_bias_part, d_skip_part
    )
    g_in = jnp.swapaxes(g_in, 0, 1)
    inner_sum = jnp.sum(d_norm_share * full_gain[None] * share_rows, axis=1, keepdims=True)
    inv_cube = inv_share * inv_share * inv_share
    input_grad = (
        grad_out
        + inv_share * full_gain[None] * d_norm_share
        - share_rows * inv_cube * inner_sum / model_width
    )
    rank_here = rank_width // parts
    state_here = 2 * N // parts
    g_x_rank = g_small[:rank_here].T
    g_dt = g_small[rank_here : 2 * rank_here]
    g_x_state = g_small[2 * rank_here : 2 * rank_here + state_here].T
    g_out = lax.psum_scatter(d_wout, ("dp", "seq"), scatter_dimension=0, tiled=True).astype(F32).T
    g_gain = g_whole[N + 16, : norm_gain.shape[0]] / norm_gain.astype(F32)
    g_alog, g_conv_w, g_conv_b = g_whole[:N], g_whole[N : N + conv_taps], g_whole[N + conv_taps]
    g_bias, g_skip = g_whole[N + 8], g_whole[N + 9]
    return (
        output,
        input_grad,
        g_gain,
        g_in,
        g_conv_w,
        g_conv_b,
        g_x_rank,
        g_x_state,
        g_dt,
        g_bias,
        g_alog,
        g_skip,
        g_out,
    )


def solution(mesh):
    placed = (
        P(("dp", "seq", "tensor"), None),
        P(("dp", "seq", "tensor"), None),
        P(("dp", "seq")),
        P("tensor"),
        P(("dp", "seq"), None, "tensor"),
        P(None, "tensor"),
        P("tensor"),
        P("tensor", ("dp", "seq")),
        P(("dp", "seq"), "tensor"),
        P("tensor"),
        P(None, "tensor"),
        P("tensor"),
        P("tensor", ("dp", "seq")),
    )
    return jax.shard_map(
        on_device,
        mesh=mesh,
        in_specs=placed,
        out_specs=(
            P(("dp", "seq", "tensor"), None),
            P(("dp", "seq", "tensor"), None),
            P("tensor"),
            P(("dp", "seq"), None, "tensor"),
            P(None, "tensor"),
            P("tensor"),
            P("tensor", ("dp", "seq")),
            P("tensor", ("dp", "seq")),
            P(("dp", "seq"), "tensor"),
            P("tensor"),
            P(None, "tensor"),
            P("tensor"),
            P("tensor", ("dp", "seq")),
        ),
        check_vma=False,
    )
```

```python
import functools

import jax
import jax.numpy as jnp
from jax import lax
from jax.experimental import pallas as pl
from jax.experimental.pallas import tpu as pltpu
from jax.sharding import PartitionSpec as P

EPS = 1e-05
LOG2E = 1.4426950408889634
LN2 = 0.6931471805599453
FAR = 1e30
SMALL_ROWS = 24
N = 16
CH = 16
F32, BF16 = jnp.float32, jnp.bfloat16
MESH = pl.DeviceIdType.MESH


def passed_along(x, axis, by):
    size = lax.axis_size(axis)
    pairs = [(i, i + by) for i in range(size) if 0 <= i + by < size]
    return lax.ppermute(x, axis, pairs)


def spread(values_t):
    tokens = values_t.shape[1]
    name = lax.broadcasted_iota(jnp.int32, (N, CH * N), 0)
    lane = lax.broadcasted_iota(jnp.int32, (N, CH * N), 1)
    copies = (name == lane % N).astype(BF16)
    wide = lax.dot_general(values_t.astype(BF16), copies, (((0,), (0,)), ((), ())), preferred_element_type=F32)
    row = lax.broadcasted_iota(jnp.int32, (tokens, CH * N), 0)
    place_of = lax.broadcasted_iota(jnp.int32, (tokens, CH * N), 1)
    return jnp.where(row % CH == place_of // N, wide, 0.0).astype(BF16)


def fwd_kernel(mix_ref, wdt_ref, bias_ref, low_ref, keep_ref, rate_ref,
               y_ref, ckpt_ref, last_ref, stepd_ref, u_ref, step_ref, sig_ref, state_ref, sbf_ref, cdiag_ref):
    @pl.when(pl.program_id(1) == 0)
    def _():
        state_ref[...] = jnp.zeros_like(state_ref)
    ckpt_ref[0] = state_ref[...]
    rank = wdt_ref.shape[0]
    b_t, c_t = mix_ref[rank:rank + N, :], mix_ref[rank + N:rank + 2 * N, :]
    cdiag_ref[...] = spread(c_t)
    tn = (((0,), (0,)), ((), ()))
    pre = lax.dot_general(mix_ref[0:rank, :].astype(BF16), wdt_ref[...], tn, preferred_element_type=F32)
    pre = pre + bias_ref[...]
    small = jnp.exp(-jnp.abs(pre))
    step = jnp.maximum(pre, 0.0) + jnp.log1p(small)
    step_ref[...] = step
    sig_ref[...] = jnp.where(pre >= 0, 1.0, small) / (1.0 + small)
    stepd_ref[...] = jnp.where(keep_ref[...] > 0, step, FAR)
    u_ref[...] = step * low_ref[...].astype(F32)
    rate = rate_ref[...]
    tb = stepd_ref.shape[0]

    s = state_ref[...]
    for base in range(0, tb, CH):
        for k in range(base, base + CH):
            dec = jnp.exp2(rate * stepd_ref[k:k + 1, :])
            s = dec * s + b_t[:, k:k + 1] * u_ref[k:k + 1, :]
            sbf_ref[(k - base) * N:(k - base + 1) * N, :] = s.astype(BF16)
        y_ref[base:base + CH, :] = jnp.dot(cdiag_ref[base:base + CH, :], sbf_ref[...], preferred_element_type=F32)
    state_ref[...] = s
    last_ref[...] = s


def fwd(mix_t, w_dt, bias, low, keep, rate, tb=128, w=512):
    t, c = low.shape
    w = min(w, c)
    grid = (c // w, t // tb)
    mixed, rank = mix_t.shape[0], w_dt.shape[0]
    rows = pl.BlockSpec((tb, w), lambda j, i: (i, j))
    whole = jax.ShapeDtypeStruct((t, c), F32)
    return pl.pallas_call(
        fwd_kernel,
        grid=grid,
        in_specs=[
            pl.BlockSpec((mixed, tb), lambda j, i: (0, i)),
            pl.BlockSpec((rank, w), lambda j, i: (0, j)),
            pl.BlockSpec((1, w), lambda j, i: (0, j)),
            rows,
            pl.BlockSpec((tb, 1), lambda j, i: (i, 0)),
            pl.BlockSpec((N, w), lambda j, i: (0, j)),
        ],
        out_specs=[
            rows,
            pl.BlockSpec((1, N, w), lambda j, i: (i, 0, j)),
            pl.BlockSpec((N, w), lambda j, i: (0, j)),
            rows, rows, rows, rows,
        ],
        out_shape=[
            whole,
            jax.ShapeDtypeStruct((t // tb, N, c), F32),
            jax.ShapeDtypeStruct((N, c), F32),
            whole, whole, whole, whole,
        ],
        scratch_shapes=[pltpu.VMEM((N, w), F32), pltpu.VMEM((CH * N, w), BF16), pltpu.VMEM((tb, CH * N), BF16)],
        compiler_params=pltpu.CompilerParams(vmem_limit_bytes=48 << 20),
        name="scan_forward",
    )(mix_t, w_dt, bias, low, keep, rate)


def bwd_kernel(stepd_ref, u_ref, ds_ref, mix_ref, rate_ref, ckpt_ref, gin_ref,
               step_ref, sig_ref, low_ref, skip_ref, wdt_ref,
               dpl_ref, e_ref, rank_ref, db_ref, dc_ref, acc_ref, bias_ref, dskip_ref,
               g_ref, states_ref, abf_ref, rbf_ref, pb_ref, pc_ref, wb_ref, dn_ref, bdiag_ref, dec_ref):
    @pl.when(pl.program_id(1) == 0)
    def _():
        g_ref[...] = gin_ref[...]
        acc_ref[...] = jnp.zeros_like(acc_ref)
        bias_ref[...] = jnp.zeros_like(bias_ref)
        dskip_ref[...] = jnp.zeros_like(dskip_ref)

    rate = rate_ref[...]
    tb = stepd_ref.shape[0]
    nc = tb // CH

    def fold(v):
        p = v[:, 0:128]
        for q in range(1, v.shape[1] // 128):
            p = p + v[:, q * 128:(q + 1) * 128]
        return p

    states_ref[0:N, :] = ckpt_ref[0]
    nt = (((1,), (1,)), ((), ()))
    lanes = jnp.ones((8, 128), BF16)
    rank = wdt_ref.shape[0]
    b_t, c_t = mix_ref[rank:rank + N, :], mix_ref[rank + N:rank + 2 * N, :]
    bdiag_ref[...] = spread(b_t)
    ones = spread(jnp.ones((N, CH), F32))

    s = ckpt_ref[0]
    for c in range(nc):
        base = c * CH
        for k in range(CH):
            at = base + k
            dec = jnp.exp2(rate * stepd_ref[at:at + 1, :])
            dec_ref[at * N:(at + 1) * N, :] = dec
            s = dec * s + b_t[:, at:at + 1] * u_ref[at:at + 1, :]
            states_ref[(at + 1) * N:(at + 2) * N, :] = s
            pc_ref[k * N:(k + 1) * N, :] = fold(s * ds_ref[at:at + 1, :])
        dc = lax.dot_general(lanes, pc_ref[...].astype(BF16), nt, preferred_element_type=F32)
        dc_ref[0, c:c + 1, :] = dc[0:1]

    g, acc = g_ref[...], acc_ref[...]
    for c in range(nc - 1, -1, -1):
        base = c * CH
        for k in range(CH - 1, -1, -1):
            at = base + k
            sd = stepd_ref[at:at + 1, :]
            adj = g + c_t[:, at:at + 1] * ds_ref[at:at + 1, :]
            abf_ref[k * N:(k + 1) * N, :] = adj.astype(BF16)
            pb_ref[k * N:(k + 1) * N, :] = fold(adj * u_ref[at:at + 1, :])
            g = dec_ref[at * N:(at + 1) * N, :] * adj
            before = states_ref[at * N:(at + 1) * N, :]
            r = g * before * rate
            rbf_ref[k * N:(k + 1) * N, :] = r.astype(BF16)
            acc = acc + r * sd
        wb_ref[base:base + CH, :] = jnp.dot(bdiag_ref[base:base + CH, :], abf_ref[...], preferred_element_type=F32)
        dn_ref[base:base + CH, :] = jnp.dot(ones, rbf_ref[...], preferred_element_type=F32)
        db = lax.dot_general(lanes, pb_ref[...].astype(BF16), nt, preferred_element_type=F32)
        db_ref[0, c:c + 1, :] = db[0:1]
    g_ref[...] = g
    acc_ref[...] = acc

    low, ds, weighted = low_ref[...].astype(F32), ds_ref[...], wb_ref[...]
    d_pre = (LN2 * dn_ref[...] + low * weighted) * sig_ref[...]
    d_pre_low = d_pre.astype(BF16)
    dpl_ref[...] = d_pre_low
    e_ref[...] = skip_ref[...] * ds + step_ref[...] * weighted
    bias_ref[...] = bias_ref[...] + jnp.sum(d_pre, axis=0, keepdims=True)
    dskip_ref[...] = dskip_ref[...] + jnp.sum(ds * low, axis=0, keepdims=True)
    rank_ref[0] = lax.dot_general(wdt_ref[...], d_pre_low, nt, preferred_element_type=F32)


def bwd(stepd, u, ds, mix_t, rate, ckpt, gin, step, sig, low, skip, w_dt, tb=128, w=512):
    t, c = stepd.shape
    w = min(w, c)
    nb = t // tb
    grid = (c // w, nb)
    rank = w_dt.shape[0]
    rows = pl.BlockSpec((tb, w), lambda j, i: (nb - 1 - i, j))
    return pl.pallas_call(
        bwd_kernel,
        grid=grid,
        in_specs=[
            rows, rows, rows,
            pl.BlockSpec((mix_t.shape[0], tb), lambda j, i: (0, nb - 1 - i)),
            pl.BlockSpec((N, w), lambda j, i: (0, j)),
            pl.BlockSpec((1, N, w), lambda j, i: (nb - 1 - i, 0, j)),
            pl.BlockSpec((N, w), lambda j, i: (0, j)),
            rows, rows, rows,
            pl.BlockSpec((1, w), lambda j, i: (0, j)),
            pl.BlockSpec((rank, w), lambda j, i: (0, j)),
        ],
        out_specs=[
            rows, rows,
            pl.BlockSpec((1, rank, tb), lambda j, i: (j, 0, nb - 1 - i)),
            pl.BlockSpec((1, tb // CH, CH * N), lambda j, i: (j, nb - 1 - i, 0)),
            pl.BlockSpec((1, tb // CH, CH * N), lambda j, i: (j, nb - 1 - i, 0)),
            pl.BlockSpec((N, w), lambda j, i: (0, j)),
            pl.BlockSpec((1, w), lambda j, i: (0, j)),
            pl.BlockSpec((1, w), lambda j, i: (0, j)),
        ],
        out_shape=[
            jax.ShapeDtypeStruct((t, c), BF16),
            jax.ShapeDtypeStruct((t, c), F32),
            jax.ShapeDtypeStruct((c // w, rank, t), F32),
            jax.ShapeDtypeStruct((c // w, t // CH, CH * N), F32),
            jax.ShapeDtypeStruct((c // w, t // CH, CH * N), F32),
            jax.ShapeDtypeStruct((N, c), F32),
            jax.ShapeDtypeStruct((1, c), F32),
            jax.ShapeDtypeStruct((1, c), F32),
        ],
        scratch_shapes=[pltpu.VMEM((N, w), F32), pltpu.VMEM(((tb + 1) * N, w), F32),
                        pltpu.VMEM((CH * N, w), BF16), pltpu.VMEM((CH * N, w), BF16), pltpu.VMEM((CH * N, 128), F32), pltpu.VMEM((CH * N, 128), F32),
                        pltpu.VMEM((tb, w), F32), pltpu.VMEM((tb, w), F32), pltpu.VMEM((tb, CH * N), BF16),
                        pltpu.VMEM((tb * N, w), F32)],
        compiler_params=pltpu.CompilerParams(vmem_limit_bytes=48 << 20),
        name="scan_backward",
    )(stepd, u, ds, mix_t, rate, ckpt, gin, step, sig, low, skip, w_dt)


def correct_kernel(rank, alive_ref, y_ref, stepd_ref, mix_ref, rate_ref, ckpt_ref, sin_ref, low_ref, skip_ref, z_ref,
                   yo_ref, ckpto_ref, gated_ref, state_ref, sbf_ref, cdiag_ref):
    i = pl.program_id(1)

    @pl.when(i == 0)
    def _():
        state_ref[...] = sin_ref[...]

    alive = alive_ref[i] != 0

    @pl.when(alive)
    def _():
        rate = rate_ref[...]
        ckpto_ref[0] = ckpt_ref[0] + state_ref[...]

        cdiag_ref[...] = spread(mix_ref[rank + N:rank + 2 * N, :])
        s = state_ref[...]
        for base in range(0, y_ref.shape[0], CH):
            for k in range(CH):
                s = jnp.exp2(rate * stepd_ref[base + k:base + k + 1, :]) * s
                sbf_ref[k * N:(k + 1) * N, :] = s.astype(BF16)
            yo_ref[base:base + CH, :] = y_ref[base:base + CH, :] + jnp.dot(
                cdiag_ref[base:base + CH, :], sbf_ref[...], preferred_element_type=F32
            )
        state_ref[...] = s

    @pl.when(jnp.logical_not(alive))
    def _():
        yo_ref[...] = y_ref[...]
        ckpto_ref[...] = ckpt_ref[...]

    total = yo_ref[...] + skip_ref[...] * low_ref[...].astype(F32)
    z = z_ref[...]
    yo_ref[...] = total
    gated_ref[...] = (total * (z / (1.0 + jnp.exp(-z)))).astype(BF16)


def correct(rank, alive, y, stepd, mix_t, rate, ckpt, state_in, low, skip, z, tb=128, w=512):
    t, c = stepd.shape
    w = min(w, c)
    rows = pl.BlockSpec((tb, w), lambda j, i, _: (i, j))
    lanes = pl.BlockSpec((N, w), lambda j, i, _: (0, j))
    marks = pl.BlockSpec((1, N, w), lambda j, i, _: (i, 0, j))
    return pl.pallas_call(
        functools.partial(correct_kernel, rank),
        grid_spec=pltpu.PrefetchScalarGridSpec(
            num_scalar_prefetch=1,
            grid=(c // w, t // tb),
            in_specs=[rows, rows, pl.BlockSpec((mix_t.shape[0], tb), lambda j, i, _: (0, i)), lanes, marks, lanes,
                      rows, pl.BlockSpec((1, w), lambda j, i, _: (0, j)), rows],
            out_specs=[rows, marks, rows],
            scratch_shapes=[pltpu.VMEM((N, w), F32), pltpu.VMEM((CH * N, w), BF16), pltpu.VMEM((tb, CH * N), BF16)],
        ),
        out_shape=[jax.ShapeDtypeStruct((t, c), F32), jax.ShapeDtypeStruct(ckpt.shape, F32),
                   jax.ShapeDtypeStruct((t, c), BF16)],
        compiler_params=pltpu.CompilerParams(vmem_limit_bytes=48 << 20),
        name="scan_correct",
    )(alive, y, stepd, mix_t, rate, ckpt, state_in, low, skip, z)


def entry_kernel(rank, alive_ref, stepd_ref, ds_ref, mix_ref, rate_ref, g_ref):
    i = pl.program_id(1)

    @pl.when(i == 0)
    def _():
        g_ref[...] = jnp.zeros_like(g_ref)

    @pl.when(alive_ref[pl.num_programs(1) - 1 - i] != 0)
    def _():
        rate = rate_ref[...]
        c_t = mix_ref[rank + N:rank + 2 * N, :]
        g = g_ref[...]
        for k in range(stepd_ref.shape[0] - 1, -1, -1):
            adj = g + c_t[:, k:k + 1] * ds_ref[k:k + 1, :]
            g = jnp.exp2(rate * stepd_ref[k:k + 1, :]) * adj
        g_ref[...] = g


def entry(rank, alive, stepd, ds, mix_t, rate, tb=128, w=512):
    t, c = stepd.shape
    w = min(w, c)
    nb = t // tb
    rows = pl.BlockSpec((tb, w), lambda j, i, _: (nb - 1 - i, j))
    lanes = pl.BlockSpec((N, w), lambda j, i, _: (0, j))
    return pl.pallas_call(
        functools.partial(entry_kernel, rank),
        grid_spec=pltpu.PrefetchScalarGridSpec(
            num_scalar_prefetch=1,
            grid=(c // w, nb),
            in_specs=[rows, rows, pl.BlockSpec((mix_t.shape[0], tb), lambda j, i, _: (0, nb - 1 - i)), lanes],
            out_specs=lanes,
        ),
        out_shape=jax.ShapeDtypeStruct((N, c), F32),
        compiler_params=pltpu.CompilerParams(vmem_limit_bytes=48 << 20),
        name="scan_entry",
    )(alive, stepd, ds, mix_t, rate)


def carried(local, reach, axis, by):
    found = jnp.zeros_like(local)
    for turn in range(lax.axis_size(axis) - 1):
        found = passed_along(local if turn == 0 else local + reach() * found, axis, by)
    return found


def mesh_copy(src, dst, send, recv, **where):
    return pltpu.make_async_remote_copy(
        src_ref=src, dst_ref=dst, send_sem=send, recv_sem=recv, device_id=where, device_id_type=MESH
    )


def place():
    dp, seq, mine = lax.axis_index("dp"), lax.axis_index("seq"), lax.axis_index("tensor")
    return dp, seq, mine


def tail_kernel(n, dps, seqs, tile, lag, rank, dx_ref, dz_ref, w_hbm, nrm_hbm,
                dwx_ref, dwdt_ref, alog_ref, conv_ref, bias_ref, skip_ref,
                dn_ref, gin_ref, gs_ref, ga_ref,
                sm_ref, gacc, gsend, grecv, all_mine,
                zr, zl, w_ref, nrm_ref, loads, nrm_load, one_send, one_recv, two_recv, sm_one, sm_two, all_one, all_two,
                r_send, r_recv, l_send, l_recv, w1s, w1r, w2s, w2r, s1s, s1r, s2s, s2r, a1s, a1r, a2s, a2r, gs, gr):
    dp, seq, t = place()
    core, hi = dp % 2, dp // 2
    chips = dps // 2 * seqs
    chip = hi * seqs + seq
    rows = dn_ref.shape[0]
    wide = dn_ref.shape[1]
    wrows = gin_ref.shape[1]
    subs = wide // tile

    def owner(q, c):
        return (q // seqs * 2 + c) * seqs + q % seqs

    def to_chip(q):
        return dict(dp=q // seqs * 2 + core, seq=q % seqs)

    barrier = pltpu.get_barrier_semaphore()
    pl.semaphore_signal(barrier, inc=1, device_id=dict(dp=hi * 2 + 1 - core), device_id_type=MESH)
    for step in range(1, chips):
        q = lax.rem(chip + step, chips)
        pl.semaphore_signal(barrier, inc=1, device_id=to_chip(q), device_id_type=MESH)

    for ahead in range(1, n):
        pl.semaphore_signal(barrier, inc=1, device_id=dict(tensor=lax.rem(t + ahead, n)), device_id_type=MESH)
    pl.semaphore_wait(barrier, chips + n - 1)
    gacc[...] = jnp.zeros_like(gacc)

    partner = dict(dp=hi * 2 + 1 - core)
    right, left = dict(tensor=lax.rem(t + 1, n)), dict(tensor=lax.rem(t + n - 1, n))

    def r_copy(i):
        return mesh_copy(zr.at[i], zr.at[i], r_send.at[i], r_recv.at[i], **right)

    def l_copy(i):
        return mesh_copy(zl.at[i], zl.at[i], l_send.at[i], l_recv.at[i], **left)

    def w1_copy(q):
        return mesh_copy(one_send.at[q], one_recv.at[q], w1s.at[q], w1r.at[q], **partner)

    def w2_copy(q, slot):
        return mesh_copy(one_recv.at[q], two_recv.at[slot], w2s.at[q], w2r.at[slot], **to_chip(q))

    def s1_copy(q):
        return mesh_copy(sm_ref.at[owner(q, 1 - core)], sm_one.at[q], s1s.at[q], s1r.at[q], **partner)

    def s2_copy(q, slot):
        return mesh_copy(sm_one.at[q], sm_two.at[slot], s2s.at[q], s2r.at[slot], **to_chip(q))

    def a1_copy():
        return mesh_copy(all_mine, all_one, a1s, a1r, **partner)

    def a2_copy(q, slot):
        return mesh_copy(all_one, all_two.at[slot], a2s.at[q], a2r.at[slot], **to_chip(q))

    def g_copy(p, slot):
        return mesh_copy(gsend.at[p], grecv.at[slot], gs.at[p], gr.at[slot], tensor=p)

    def cols_of(sub):
        return pl.ds(pl.multiple_of(sub * tile, tile), tile)

    def load(sub):
        ref = w_ref.at[:, cols_of(sub), :]
        return pltpu.make_async_copy(w_hbm.at[:, cols_of(sub), :], ref, loads.at[sub])

    def partial_tile(o, sub):
        here = pl.ds(pl.multiple_of(o * rows, rows), rows)
        cols = cols_of(sub)
        nt = (((1,), (1,)), ((), ()))
        return lax.dot_general(
            dx_ref[here, :], w_ref[0, cols, :], nt, preferred_element_type=F32
        ) + lax.dot_general(dz_ref[here, :], w_ref[1, cols, :], nt, preferred_element_type=F32)

    def weight_rows(p, k):
        cols = pl.ds(pl.multiple_of(p * wrows, wrows), wrows)
        tn = (((0,), (0,)), ((), ()))
        d_ref = dx_ref if k == 0 else dz_ref
        block = lax.dot_general(nrm_ref[:, cols], d_ref[...], tn, preferred_element_type=F32)
        scaled = (block * w_ref[k, cols, :].astype(F32)).astype(BF16)
        lanes = jnp.ones((8, block.shape[1]), BF16)
        nt = (((1,), (1,)), ((), ()))
        gacc[:, cols] = gacc[:, cols] + lax.dot_general(lanes, scaled, nt, preferred_element_type=F32)
        return block

    def load_rows():
        return pltpu.make_async_copy(nrm_hbm, nrm_ref, nrm_load)

    @pl.loop(0, subs)
    def _(sub):
        load(sub).start()

    load_rows().start()

    parts = sm_ref.shape[0]
    for p in range(parts):
        here, more = rank // parts, (dwx_ref.shape[0] - rank) // parts
        sm_ref[p, 0:here, :] = dwx_ref[p * here:(p + 1) * here, :]
        sm_ref[p, here:2 * here, :] = dwdt_ref[p * here:(p + 1) * here, :]
        sm_ref[p, 2 * here:2 * here + more, :] = dwx_ref[rank + p * more:rank + (p + 1) * more, :]
        sm_ref[p, 2 * here + more:, :] = jnp.zeros((sm_ref.shape[1] - 2 * here - more, sm_ref.shape[2]), F32)
    for q in range(chips):
        s1_copy(q).start()

    def stream(i, limit, start, buf, copy, owner_of):
        @pl.when(jnp.logical_and(i >= 0, i < limit))
        def _():
            block = partial_tile(owner_of(i // subs), i % subs)

            @pl.when(start)
            def _():
                buf[i] = block.astype(BF16)

            @pl.when(jnp.logical_not(start))
            def _():
                copy(i).wait_recv()
                buf[i] = (block + buf[i].astype(F32)).astype(BF16)

            copy(i).start()

    def step(g, _):
        @pl.when(g == 0)
        def _():
            load(0).wait()

        @pl.when(g == 1)
        def _():
            @pl.loop(1, subs)
            def _(sub):
                load(sub).wait()

            load_rows().wait()

        stream(g - lag * t, (n - 1 - t) * subs, t == 0, zr, r_copy, lambda k: n - 1 - k)
        stream(g - lag * (n - 1 - t), t * subs, t == n - 1, zl, l_copy, lambda k: k)

        @pl.when(jnp.logical_and(g >= 1, g < chips + 1))
        def _():
            for k in range(2):
                one_send[g - 1, k] = weight_rows(owner(g - 1, 1 - core), k).astype(BF16)
            w1_copy(g - 1).start()

        @pl.when(jnp.logical_and(g >= chips + 1, g < 2 * chips))
        def _():
            q = lax.rem(chip + g - chips, chips)
            w1_copy(q).wait_recv()
            for k in range(2):
                one_recv[q, k] = (weight_rows(owner(q, core), k) + one_recv[q, k].astype(F32)).astype(BF16)
            w2_copy(q, chip).start()

        @pl.when(g == 2 * chips)
        def _():
            for q in range(chips):
                s1_copy(q).wait_recv()
                sm_one[q] = sm_one[q] + sm_ref[owner(q, core)]
            for ahead in range(1, chips):
                q = lax.rem(chip + ahead, chips)
                s2_copy(q, chip).start()
            w1_copy(chip).wait_recv()
            for k in range(2):
                gin_ref[k] = weight_rows(owner(chip, core), k) + one_recv[chip, k].astype(F32)

            share = wide // n
            for p in range(n):
                gsend[p] = gacc[:, p * share:(p + 1) * share]
            for ahead in range(1, n):
                g_copy(lax.rem(t + ahead, n), t).start()

        late = 2 * chips + 1

        @pl.when(jnp.logical_and(g >= late, g < late + subs))
        def _():
            dn_ref[:, cols_of(g - late)] = partial_tile(t, g - late)

        @pl.when(g == late + subs // 2)
        def _():
            share = wide // n
            plain = all_mine.shape[0] - 8
            all_mine[0:N, :] = LN2 * alog_ref[...]
            all_mine[N:N + 8, :] = conv_ref[...]
            all_mine[N + 8:plain, :] = jnp.zeros((plain - N - 8, all_mine.shape[1]), F32)
            all_mine[N + 8:N + 9, :] = bias_ref[...]
            all_mine[N + 9:N + 10, :] = skip_ref[...]
            all_mine[plain:, :] = jnp.zeros((8, all_mine.shape[1]), F32)
            all_mine[plain:, 0:share] = gsend[t]
            for ahead in range(1, n):
                p = lax.rem(t + ahead, n)
                g_copy(p, p).wait_recv()
                all_mine[plain:, 0:share] = all_mine[plain:, 0:share] + grecv[p]
            a1_copy().start()

        @pl.when(g == late + subs)
        def _():
            a1_copy().wait_recv()
            all_one[...] = all_one[...] + all_mine[...]
            for ahead in range(1, chips):
                a2_copy(lax.rem(chip + ahead, chips), chip).start()

        return 0

    steps = max((n - 1) * max(subs, lag), 2 * chips + subs + 2)
    lax.fori_loop(0, steps, step, 0)

    @pl.loop(0, subs)
    def _(s):
        cols = cols_of(s)

        @pl.when(t > 0)
        def _():
            i = (n - 1 - t) * subs + s
            r_copy(i).wait_recv()
            dn_ref[:, cols] = dn_ref[:, cols] + zr[i].astype(F32)

        @pl.when(t < n - 1)
        def _():
            i = t * subs + s
            l_copy(i).wait_recv()
            dn_ref[:, cols] = dn_ref[:, cols] + zl[i].astype(F32)

    gs_ref[...] = sm_one[chip]
    for ahead in range(1, chips):
        q = lax.rem(chip + ahead, chips)
        s2_copy(q, q).wait_recv()
        gs_ref[...] = gs_ref[...] + sm_two[q]
    ga_ref[...] = all_one[...]
    for ahead in range(1, chips):
        q = lax.rem(chip + ahead, chips)
        w2_copy(q, q).wait_recv()
        gin_ref[...] = gin_ref[...] + two_recv[q].astype(F32)
    for ahead in range(1, chips):
        q = lax.rem(chip + ahead, chips)
        a2_copy(q, q).wait_recv()
        ga_ref[...] = ga_ref[...] + all_two[q]

    for q in range(chips):
        s1_copy(q).wait_send()
        w1_copy(q).wait_send()
    a1_copy().wait_send()
    for ahead in range(1, n):
        g_copy(lax.rem(t + ahead, n), t).wait_send()
    for ahead in range(1, chips):
        q = lax.rem(chip + ahead, chips)
        s2_copy(q, chip).wait_send()
        a2_copy(q, chip).wait_send()
        w2_copy(q, chip).wait_send()

    @pl.loop(0, (n - 1) * subs)
    def _(i):
        @pl.when(i < (n - 1 - t) * subs)
        def _():
            r_copy(i).wait_send()

        @pl.when(i < t * subs)
        def _():
            l_copy(i).wait_send()


def tail(dx, dz, w_full, normed, dwx, dwdt, *singles):
    n, dps, seqs = (lax.axis_size(axis) for axis in ("tensor", "dp", "seq"))
    chips = dps // 2 * seqs
    rank = dwdt.shape[0]
    small_rows = -(-(rank + dwx.shape[0]) // (dps * seqs) // 8) * 8
    all_rows = N + 24
    rows = dx.shape[0] // n
    wide, lanes = w_full.shape[1], w_full.shape[2]
    wrows = wide // (dps * seqs)
    tile = 256
    subs = wide // tile
    hops = (n - 1) * subs
    vmem, hbm = pl.BlockSpec(memory_space=pltpu.VMEM), pl.BlockSpec(memory_space=pl.ANY)
    dma = pltpu.SemaphoreType.DMA
    few = dma((chips,))
    return pl.pallas_call(
        functools.partial(tail_kernel, n, dps, seqs, tile, 2, rank),
        out_shape=[
            jax.ShapeDtypeStruct((rows, wide), F32),
            jax.ShapeDtypeStruct((2, wrows, lanes), F32),
            jax.ShapeDtypeStruct((small_rows, lanes), F32),
            jax.ShapeDtypeStruct((all_rows, lanes), F32),
        ],
        in_specs=[vmem] * 2 + [hbm] * 2 + [vmem] * 6,
        out_specs=[vmem] * 4,
        scratch_shapes=[
            pltpu.VMEM((dps * seqs, small_rows, lanes), F32),
            pltpu.VMEM((8, wide), F32),
            pltpu.VMEM((n, 8, wide // n), F32),
            pltpu.VMEM((n, 8, wide // n), F32),
            pltpu.VMEM((all_rows, lanes), F32),
            pltpu.VMEM((hops, rows, tile), BF16),
            pltpu.VMEM((hops, rows, tile), BF16),
            pltpu.VMEM((2, wide, lanes), BF16),
            pltpu.VMEM(normed.shape, BF16),
            dma((subs,)),
            dma,
            pltpu.VMEM((chips, 2, wrows, lanes), BF16),
            pltpu.VMEM((chips, 2, wrows, lanes), BF16),
            pltpu.VMEM((chips, 2, wrows, lanes), BF16),
            pltpu.VMEM((chips, small_rows, lanes), F32),
            pltpu.VMEM((chips, small_rows, lanes), F32),
            pltpu.VMEM((all_rows, lanes), F32),
            pltpu.VMEM((chips, all_rows, lanes), F32),
            dma((hops,)), dma((hops,)), dma((hops,)), dma((hops,)),
            few, few, few, few, few, few, few, few, dma, dma, few, few, dma((n,)), dma((n,)),
        ],
        compiler_params=pltpu.CompilerParams(
            collective_id=2, has_side_effects=True, vmem_limit_bytes=60 << 20
        ),
        name="tail_sums",
    )(dx, dz, w_full, normed, dwx, dwdt, *singles)


def mid_kernel(n, tile, lag, gated_ref, w_hbm, hid_ref, tea_ref, scale_ref, z_hbm, scan_hbm,
               out_ref, go_ref, dwo_hbm, dscan_hbm, dz_hbm,
               zr, zl, w_ref, wloads, dwo_ref, part_ref, piece_ref, z_ref, scan_ref, acc_ref, dz_ref, loads, stores, wstores,
               r_send, r_recv, l_send, l_recv, ar_send, ar_recv, al_send, al_recv):
    t = lax.axis_index("tensor")
    rows, wide = hid_ref.shape
    tokens, lanes = acc_ref.shape
    waves = wide // tile
    right, left = dict(tensor=lax.rem(t + 1, n)), dict(tensor=lax.rem(t + n - 1, n))

    barrier = pltpu.get_barrier_semaphore()
    for peer in (right, left):
        pl.semaphore_signal(barrier, inc=1, device_id=peer, device_id_type=MESH)
    pl.semaphore_wait(barrier, 2)

    def load(i):
        return pltpu.make_async_copy((z_hbm, scan_hbm)[i], (z_ref, scan_ref)[i], loads.at[i])

    def load_tile(w):
        here = pl.ds(pl.multiple_of(w * tile, tile), tile)
        return pltpu.make_async_copy(w_hbm.at[here, :], w_ref.at[here, :], wloads.at[w])

    @pl.loop(0, waves)
    def _(w):
        load_tile(w).start()

    for i in range(2):
        load(i).start()

    def r_copy(i):
        return mesh_copy(zr.at[i], zr.at[i], r_send.at[i], r_recv.at[i], **right)

    def l_copy(i):
        return mesh_copy(zl.at[i], zl.at[i], l_send.at[i], l_recv.at[i], **left)

    def rows_of(o):
        return pl.ds(pl.multiple_of(o * rows, rows), rows)

    def cols_of(w):
        return pl.ds(pl.multiple_of(w * tile, tile), tile)

    def ar_copy(o, w):
        ref = piece_ref.at[rows_of(o), cols_of(w)]
        return mesh_copy(ref, ref, ar_send.at[o * waves + w], ar_recv.at[o * waves + w], **right)

    def al_copy(o, w):
        ref = piece_ref.at[rows_of(o), cols_of(w)]
        return mesh_copy(ref, ref, al_send.at[o * waves + w], al_recv.at[o * waves + w], **left)

    def stream(i, hops, start, buf, copy, owner_of):
        w, k = i // n, i % n

        @pl.when(jnp.logical_and(jnp.logical_and(i >= 0, w < waves), k < hops))
        def _():
            slot = w * (n - 1) + k
            here = part_ref[rows_of(owner_of(k)), cols_of(w)]

            @pl.when(start)
            def _():
                buf[slot] = here.astype(BF16)

            @pl.when(jnp.logical_not(start))
            def _():
                copy(slot).wait_recv()
                buf[slot] = (here + buf[slot].astype(F32)).astype(BF16)

            copy(slot).start()

    def ready(o):
        from_left = jnp.where(o > 0, n - 1 - o + lag * o, 0)
        from_right = jnp.where(o < n - 1, o + lag * (n - 1 - o), 0)
        return jnp.maximum(from_left, from_right)

    def host_ready(o):
        return max((n - 1 - o + lag * o) * (o > 0), (o + lag * (n - 1 - o)) * (o < n - 1))

    def finish(w):
        cols = cols_of(w)
        go_ref[:, cols] = part_ref[rows_of(t), cols]

        @pl.when(t > 0)
        def _():
            slot = w * (n - 1) + n - 1 - t
            r_copy(slot).wait_recv()
            go_ref[:, cols] = go_ref[:, cols] + zr[slot].astype(F32)

        @pl.when(t < n - 1)
        def _():
            slot = w * (n - 1) + t
            l_copy(slot).wait_recv()
            go_ref[:, cols] = go_ref[:, cols] + zl[slot].astype(F32)

        result = hid_ref[:, cols].astype(F32) + go_ref[:, cols]
        out_ref[:, cols] = result.astype(BF16)
        grad = scale_ref[...] * (result - tea_ref[:, cols].astype(F32))
        go_ref[:, cols] = grad
        piece_ref[rows_of(t), cols] = grad.astype(BF16)

        @pl.when(t < n - 1)
        def _():
            ar_copy(t, w).start()

        @pl.when(t > 0)
        def _():
            al_copy(t, w).start()

    def stored(i, o):
        src = (acc_ref, dz_ref)[i].at[rows_of(o), :]
        return pltpu.make_async_copy(src, (dscan_hbm, dz_hbm)[i].at[rows_of(o), :], stores.at[i, o])

    def stored_weight(w):
        here = pl.ds(pl.multiple_of(w * tile, tile), tile)
        return pltpu.make_async_copy(dwo_ref.at[w], dwo_hbm.at[here, :], wstores.at[w])

    def gate(o):
        z = z_ref[rows_of(o), :]
        s = 1.0 / (1.0 + jnp.exp(-z))
        z_ref[rows_of(o), :] = z * s
        scan_ref[rows_of(o), :] = scan_ref[rows_of(o), :] * (s * (1.0 + z * (1.0 - s)))

    def backward(w):
        tn = (((0,), (0,)), ((), ()))
        dwo_ref[w] = lax.dot_general(
            piece_ref[:, cols_of(w)], gated_ref[...], tn, preferred_element_type=F32
        ).astype(BF16)
        stored_weight(w).start()

        @pl.loop(0, n)
        def _(o):
            here = rows_of(o)
            d_gated = jnp.dot(piece_ref[here, cols_of(w)], w_ref[cols_of(w), :], preferred_element_type=F32)

            @pl.when(w == 0)
            def _():
                acc_ref[here, :] = d_gated

            @pl.when(jnp.logical_and(w > 0, w < waves - 1))
            def _():
                acc_ref[here, :] = acc_ref[here, :] + d_gated

            @pl.when(w == waves - 1)
            def _():
                total = acc_ref[here, :] + d_gated
                acc_ref[here, :] = total * z_ref[here, :]
                dz_ref[here, :] = (total * scan_ref[here, :]).astype(BF16)
                stored(0, o).start()
                stored(1, o).start()

    arrived = jnp.int32(0)
    for o in range(n):
        arrived = jnp.maximum(arrived, host_ready(o) + lag * jnp.abs(t - o))

    def step(g, _):
        @pl.when(jnp.logical_and(g % n == 0, g < n * waves))
        def _():
            cols = cols_of(g // n)
            nt = (((1,), (1,)), ((), ()))
            load_tile(g // n).wait()

            @pl.loop(0, n)
            def _(o):
                part_ref[rows_of(o), cols] = lax.dot_general(
                    gated_ref[rows_of(o), :], w_ref[cols, :], nt, preferred_element_type=F32
                )

        stream(g - lag * t, n - 1 - t, t == 0, zr, r_copy, lambda k: n - 1 - k)
        stream(g - lag * (n - 1 - t), t, t == n - 1, zl, l_copy, lambda k: k)

        own = g - ready(t)

        @pl.when(jnp.logical_and(own >= 0, jnp.logical_and(own % n == 0, own // n < waves)))
        def _():
            finish(own // n)

        @pl.loop(0, n)
        def _(o):
            i = g - ready(o) - lag * jnp.abs(t - o)
            w = i // n

            @pl.when(jnp.logical_and(o != t, jnp.logical_and(i >= 0, jnp.logical_and(i % n == 0, w < waves))))
            def _():
                @pl.when(o < t)
                def _():
                    ar_copy(o, w).wait_recv()

                    @pl.when(t < n - 1)
                    def _():
                        ar_copy(o, w).start()

                @pl.when(o > t)
                def _():
                    al_copy(o, w).wait_recv()

                    @pl.when(t > 0)
                    def _():
                        al_copy(o, w).start()

        @pl.when(g == 1)
        def _():
            for i in range(2):
                load(i).wait()

        @pl.when(jnp.logical_and(g >= 1, g <= n))
        def _():
            gate(g - 1)

        done = g - arrived

        @pl.when(jnp.logical_and(done >= 0, jnp.logical_and(done % n == 0, done // n < waves)))
        def _():
            backward(done // n)

        return 0

    steps = max(host_ready(o) + lag * abs(o - d) for o in range(n) for d in range(n)) + n * (waves - 1) + 1
    lax.fori_loop(0, max(steps, n + 1), step, 0)

    @pl.loop(0, (n - 1) * waves)
    def _(i):
        @pl.when(i % (n - 1) < n - 1 - t)
        def _():
            r_copy(i).wait_send()

        @pl.when(i % (n - 1) < t)
        def _():
            l_copy(i).wait_send()

    @pl.loop(0, n * waves)
    def _(i):
        o, w = i // waves, i % waves

        @pl.when(jnp.logical_and(o <= t, t < n - 1))
        def _():
            ar_copy(o, w).wait_send()

        @pl.when(jnp.logical_and(o >= t, t > 0))
        def _():
            al_copy(o, w).wait_send()

    @pl.loop(0, waves)
    def _(w):
        stored_weight(w).wait()

    @pl.loop(0, n)
    def _(o):
        stored(0, o).wait()
        stored(1, o).wait()


def middle(gated, w_out, hidden, teacher, scale, z_gate, scan_out):
    n = lax.axis_size("tensor")
    rows, wide = hidden.shape
    tokens, lanes = gated.shape
    tile = 256
    waves = wide // tile
    hops = (n - 1) * waves
    vmem, hbm = pl.BlockSpec(memory_space=pltpu.VMEM), pl.BlockSpec(memory_space=pl.ANY)
    dma = pltpu.SemaphoreType.DMA
    return pl.pallas_call(
        functools.partial(mid_kernel, n, tile, 2),
        out_shape=[
            jax.ShapeDtypeStruct((rows, wide), BF16),
            jax.ShapeDtypeStruct((rows, wide), F32),
            jax.ShapeDtypeStruct((wide, lanes), BF16),
            jax.ShapeDtypeStruct((tokens, lanes), F32),
            jax.ShapeDtypeStruct((tokens, lanes), BF16),
        ],
        in_specs=[vmem, hbm] + [vmem] * 3 + [hbm] * 2,
        out_specs=[vmem] * 2 + [hbm] * 3,
        scratch_shapes=[
            pltpu.VMEM((hops, rows, tile), BF16),
            pltpu.VMEM((hops, rows, tile), BF16),
            pltpu.VMEM((wide, lanes), BF16),
            dma((waves,)),
            pltpu.VMEM((waves, tile, lanes), BF16),
            pltpu.VMEM((tokens, wide), F32),
            pltpu.VMEM((tokens, wide), BF16),
            pltpu.VMEM((tokens, lanes), F32),
            pltpu.VMEM((tokens, lanes), F32),
            pltpu.VMEM((tokens, lanes), F32),
            pltpu.VMEM((tokens, lanes), BF16),
            dma((2,)), dma((2, n)), dma((waves,)),
            dma((hops,)), dma((hops,)), dma((hops,)), dma((hops,)),
            dma((n * waves,)), dma((n * waves,)), dma((n * waves,)), dma((n * waves,)),
        ],
        compiler_params=pltpu.CompilerParams(
            collective_id=1, has_side_effects=True, vmem_limit_bytes=60 << 20
        ),
        name="middle",
    )(gated, w_out, hidden, teacher, scale, z_gate, scan_out)


def front_kernel(n, dps, seqs, subs, lag, hid_ref, gain_ref, seg_ref, win_ref, wsm_ref, taps_ref, keep_ref,
                 x_out, z_out, nrm_out, w_out, conv_out, low_out, total_ref, gfull, ws_ref, natural_ref,
                 rows_ref, gain_tile, cnt_tile, grecv, cnt_one, cnt_two, x_ref, z_ref, nrm_ref, w_ref, conv_ref, low_ref,
                 mix_send, mix_recv, mix_own, mix_rows_ref, mixed_ref, outs, ms, mr, ns, nr,
                 ar_send, ar_recv, al_send, al_recv, gs, gr, c1s, c1r, c2s, c2r, hs, hr, ls,
                 chip_send, chip_recv, core_send, core_recv):
    dp, seq, t = place()
    core, hi = dp % 2, dp // 2
    chips = dps // 2 * seqs
    chip = hi * seqs + seq
    rows, wide = hid_ref.shape
    part = rows // subs
    share = wide // n
    wrows = win_ref.shape[1]
    tile = 512
    gap = max(subs, lag)
    partner = dict(dp=hi * 2 + 1 - core)
    right, left = dict(tensor=lax.rem(t + 1, n)), dict(tensor=lax.rem(t + n - 1, n))

    def owner(q, c):
        return (q // seqs * 2 + c) * seqs + q % seqs

    def to_chip(q):
        return dict(dp=q // seqs * 2 + core, seq=q % seqs)

    barrier = pltpu.get_barrier_semaphore()
    pl.semaphore_signal(barrier, inc=1, device_id=partner, device_id_type=MESH)
    for ahead in range(1, chips):
        pl.semaphore_signal(barrier, inc=1, device_id=to_chip(lax.rem(chip + ahead, chips)), device_id_type=MESH)
    for ahead in range(1, n):
        pl.semaphore_signal(barrier, inc=1, device_id=dict(tensor=lax.rem(t + ahead, n)), device_id_type=MESH)
    pl.semaphore_wait(barrier, chips + n - 1)

    def at(o, s):
        return pl.ds(pl.multiple_of(o * rows + s * part, part), part)

    def ar_copy(o, s):
        ref = rows_ref.at[at(o, s), :]
        return mesh_copy(ref, ref, ar_send.at[o * subs + s], ar_recv.at[o * subs + s], **right)

    def al_copy(o, s):
        ref = rows_ref.at[at(o, s), :]
        return mesh_copy(ref, ref, al_send.at[o * subs + s], al_recv.at[o * subs + s], **left)

    def g_copy(p, slot):
        return mesh_copy(gain_tile, grecv.at[slot], gs.at[p], gr.at[slot], tensor=p)

    def block(kind, p):
        if kind == 0:
            return w_ref.at[:, pl.ds(pl.multiple_of(p * wrows, wrows), wrows), :]
        return ws_ref.at[p]

    stored = (win_ref, wsm_ref)

    def chip_copy(kind, q, p):
        return mesh_copy(stored[kind], block(kind, p), chip_send.at[kind, q], chip_recv.at[kind, p], **to_chip(q))

    def core_copy(kind, p, own):
        src = stored[kind] if own else block(kind, p)
        return mesh_copy(src, block(kind, p), core_send.at[kind, p], core_recv.at[kind, p], **partner)

    mine = owner(chip, core)

    def count_one():
        return mesh_copy(cnt_tile, cnt_one, c1s, c1r, **partner)

    def count_two(q, slot):
        return mesh_copy(cnt_one, cnt_two.at[slot], c2s.at[q], c2r.at[slot], **to_chip(q))

    def edge_copy():
        last = x_ref.at[pl.ds(x_ref.shape[0] - 8, 8), :]
        return mesh_copy(last, x_ref.at[pl.ds(0, 8), :], hs, hr, seq=lax.rem(seq + 1, seqs))

    def mix_copy(p, slot):
        return mesh_copy(mix_send.at[p], mix_recv.at[slot], ms.at[p], mr.at[slot], tensor=p)

    def sum_copy(p, slot):
        return mesh_copy(mixed_ref.at[slot], mixed_ref.at[slot], ns.at[p], nr.at[slot], tensor=p)

    def written(i):
        src = (w_ref, nrm_ref, z_ref, x_ref, conv_ref, low_ref)[i]
        return pltpu.make_async_copy(src, (w_out, nrm_out, z_out, x_out, conv_out, low_out)[i], outs.at[i])

    def local_copy():
        return pltpu.make_async_copy(wsm_ref, block(1, mine), ls)

    gain_tile[...] = jnp.broadcast_to(gain_ref[...].astype(F32), gain_tile.shape)
    cnt_tile[...] = jnp.full(cnt_tile.shape, jnp.sum((seg_ref[...] != 0).astype(F32)))
    for ahead in range(1, n):
        g_copy(lax.rem(t + ahead, n), t).start()
    count_one().start()
    rows_ref[pl.ds(pl.multiple_of(t * rows, rows), rows), :] = hid_ref[...]

    @pl.loop(0, subs)
    def _(s):
        @pl.when(t < n - 1)
        def _():
            ar_copy(t, s).start()

        @pl.when(t > 0)
        def _():
            al_copy(t, s).start()

    def share_out(kind):
        for ahead in range(1, chips):
            chip_copy(kind, lax.rem(chip + ahead, chips), mine).start()
        core_copy(kind, mine, True).start()

    share_out(1)
    share_out(0)
    local_copy().start()
    w_ref[:, pl.ds(pl.multiple_of(mine * wrows, wrows), wrows), :] = win_ref[...]

    gfull[...] = jnp.zeros_like(gfull)
    for ahead in range(1, n):
        p = lax.rem(t + ahead, n)
        g_copy(p, p).wait_recv()
    grecv[t] = gain_tile[...]
    for p in range(n):
        gfull[:, p * share:(p + 1) * share] = grecv[p]
    count_one().wait_recv()
    count_one().wait_send()
    cnt_one[...] = cnt_one[...] + cnt_tile[...]
    for ahead in range(1, chips):
        count_two(lax.rem(chip + ahead, chips), chip).start()

    def normalize(o):
        @pl.loop(0, subs)
        def _(s):
            here = at(o, s)
            values = rows_ref[here, :].astype(F32)
            inv = lax.rsqrt(jnp.mean(values * values, axis=1, keepdims=True) + EPS)
            nrm_ref[here, :] = (values * inv * gfull[0:1, :]).astype(BF16)

    def project(o):
        here = pl.ds(pl.multiple_of(o * rows, rows), rows)
        for k, dst in enumerate((x_ref, z_ref)):
            lanes = dst.shape[1]
            width = min(tile, lanes)
            there = pl.ds(pl.multiple_of(o * rows + 8 - 8 * k, 8), rows)

            @pl.loop(0, lanes // width)
            def _(j):
                cols = pl.ds(pl.multiple_of(j * width, width), width)
                dst[there, cols] = jnp.dot(nrm_ref[here, :], w_ref[k, :, cols], preferred_element_type=F32)

    lanes = low_ref.shape[1]
    width = min(tile, lanes)
    piece = min(64, rows)
    taps = keep_ref.shape[1]

    def convolve(o):
        @pl.loop(0, rows // piece * (lanes // width))
        def _(i):
            base = o * rows + i // (lanes // width) * piece
            here = pl.ds(pl.multiple_of(base, piece), piece)
            cols = pl.ds(pl.multiple_of(i % (lanes // width) * width, width), width)
            span = x_ref[pl.ds(pl.multiple_of(base, piece), piece + 8), cols]
            keep = keep_ref[here, :]
            total = jnp.broadcast_to(taps_ref[taps:taps + 1, cols], (piece, width))
            for j in range(taps):
                first = 8 - (taps - 1) + j
                total = total + taps_ref[j:j + 1, cols] * span[first:first + piece] * keep[:, j:j + 1]
            conv_ref[here, cols] = total
            low_ref[here, cols] = (total / (1.0 + jnp.exp(-total))).astype(BF16)

    groups, depth = ws_ref.shape[0], ws_ref.shape[1]
    live = natural_ref.shape[0] // groups

    def mix_rows(o):
        convolve(o)
        nt = (((1,), (1,)), ((), ()))
        low = low_ref[pl.ds(pl.multiple_of(o * rows, rows), rows), :]
        weights = ws_ref[...].reshape(groups * depth, lanes)
        mix = lax.dot_general(weights, low, nt, preferred_element_type=F32)
        for p in range(groups):
            mix_rows_ref[p * live:(p + 1) * live, :] = mix[p * depth:p * depth + live]

        @pl.when(o != t)
        def _():
            mix_send[o] = mix_rows_ref[...].astype(BF16)
            mix_copy(o, t).start()

        @pl.when(o == t)
        def _():
            mix_own[...] = mix_rows_ref[...]

    def turn(d, o):
        final = jnp.where(o == 0, (n - 1) * gap + 1, (n - 2 - o) * gap + lag)
        return jnp.where(d == n - 1, final, (d - o) * gap)

    weights_at = (n - 1) * gap

    def step(g, _):
        @pl.when(g == 0)
        def _():
            normalize(t)

        @pl.when(g == weights_at)
        def _():
            for kind in (1, 0):
                for ahead in range(1, chips):
                    q = lax.rem(chip + ahead, chips)
                    chip_copy(kind, q, owner(q, core)).wait_recv()
                    core_copy(kind, owner(q, core), False).start()
            for kind in (1, 0):
                for q in range(chips):
                    core_copy(kind, owner(q, 1 - core), True).wait_recv()
            project(t)

        @pl.loop(0, n)
        def _(o):
            s_right = g - turn(t, o)
            s_left = g - turn(n - 1 - t, n - 1 - o)

            @pl.when(jnp.logical_and(o < t, jnp.logical_and(s_right >= 0, s_right < subs)))
            def _():
                ar_copy(o, s_right).wait_recv()

                @pl.when(t < n - 1)
                def _():
                    ar_copy(o, s_right).start()

            @pl.when(jnp.logical_and(o > t, jnp.logical_and(s_left >= 0, s_left < subs)))
            def _():
                al_copy(o, s_left).wait_recv()

                @pl.when(t > 0)
                def _():
                    al_copy(o, s_left).start()

            landed = jnp.where(o < t, s_right, s_left) - subs + 1

            @pl.when(jnp.logical_and(o != t, landed == 0))
            def _():
                normalize(o)

            ripe = jnp.where(g == weights_at, landed >= 0, jnp.logical_and(g > weights_at, landed == 0))

            @pl.when(jnp.logical_and(o != t, ripe))
            def _():
                project(o)

        return 0

    steps = weights_at + 1 + subs
    lax.fori_loop(0, steps, step, 0)

    @pl.when(seq < seqs - 1)
    def _():
        edge_copy().start()

    @pl.when(seq == 0)
    def _():
        x_ref[0:8, :] = jnp.zeros((8, x_ref.shape[1]), F32)

    for i in range(3):
        written(i).start()

    @pl.when(seq > 0)
    def _():
        edge_copy().wait_recv()

    @pl.when(seq < seqs - 1)
    def _():
        edge_copy().wait_send()

    written(3).start()
    local_copy().wait()
    @pl.loop(0, n)
    def _(i):
        mix_rows(lax.rem(t + 1 + i, n))

    for i in range(4, 6):
        written(i).start()
    for ahead in range(1, n):
        p = lax.rem(t + ahead, n)
        mix_copy(p, p).wait_recv()
        mix_own[...] = mix_own[...] + mix_recv[p].astype(F32)
    mixed_ref[t] = mix_own[...].astype(BF16)
    for ahead in range(1, n):
        sum_copy(lax.rem(t + ahead, n), t).start()
    total_ref[...] = cnt_one[...]
    for ahead in range(1, chips):
        q = lax.rem(chip + ahead, chips)
        count_two(q, q).wait_recv()
        total_ref[...] = total_ref[...] + cnt_two[q]
    for ahead in range(1, n):
        p = lax.rem(t + ahead, n)
        sum_copy(p, p).wait_recv()
    for o in range(n):
        natural_ref[:, o * rows:(o + 1) * rows] = mixed_ref[o].astype(F32)
    for ahead in range(1, n):
        p = lax.rem(t + ahead, n)
        mix_copy(p, t).wait_send()
        sum_copy(p, t).wait_send()
    for i in range(6):
        written(i).wait()
    for kind in range(2):
        for ahead in range(1, chips):
            chip_copy(kind, lax.rem(chip + ahead, chips), mine).wait_send()
        for q in range(chips):
            core_copy(kind, owner(q, core), False).wait_send()
    for ahead in range(1, chips):
        count_two(lax.rem(chip + ahead, chips), chip).wait_send()
    for ahead in range(1, n):
        g_copy(lax.rem(t + ahead, n), t).wait_send()

    @pl.loop(0, n * subs)
    def _(i):
        o, s = i // subs, i % subs

        @pl.when(jnp.logical_and(o <= t, t < n - 1))
        def _():
            ar_copy(o, s).wait_send()

        @pl.when(jnp.logical_and(o >= t, t > 0))
        def _():
            al_copy(o, s).wait_send()


def front(hidden, gain, segments, w_in, w_small, taps, keeps, x_cols):
    n, dps, seqs = (lax.axis_size(axis) for axis in ("tensor", "dp", "seq"))
    parts = dps * seqs
    chips = parts // 2
    rows, wide = hidden.shape
    lanes = w_in.shape[2]
    tokens = rows * n
    mixed = parts * x_cols
    subs = max(1, rows // 32)
    vmem, hbm = pl.BlockSpec(memory_space=pltpu.VMEM), pl.BlockSpec(memory_space=pl.ANY)
    dma = pltpu.SemaphoreType.DMA
    many, few, peers = dma((n * subs,)), dma((chips,)), dma((n,))
    return pl.pallas_call(
        functools.partial(front_kernel, n, dps, seqs, subs, 2),
        out_shape=[
            jax.ShapeDtypeStruct((tokens + 8, lanes), F32),
            jax.ShapeDtypeStruct((tokens, lanes), F32),
            jax.ShapeDtypeStruct((tokens, wide), BF16),
            jax.ShapeDtypeStruct((2, wide, lanes), BF16),
            jax.ShapeDtypeStruct((tokens, lanes), F32),
            jax.ShapeDtypeStruct((tokens, lanes), BF16),
            jax.ShapeDtypeStruct((8, 128), F32),
            jax.ShapeDtypeStruct((8, wide), F32),
            jax.ShapeDtypeStruct((parts,) + w_small.shape, BF16),
            jax.ShapeDtypeStruct((parts * x_cols, tokens), F32),
        ],
        in_specs=[vmem] * 7,
        out_specs=[hbm] * 6 + [vmem] * 4,
        scratch_shapes=[
            pltpu.VMEM((tokens, wide), BF16),
            pltpu.VMEM((8, gain.shape[1]), F32),
            pltpu.VMEM((8, 128), F32),
            pltpu.VMEM((n, 8, gain.shape[1]), F32),
            pltpu.VMEM((8, 128), F32),
            pltpu.VMEM((chips, 8, 128), F32),
            pltpu.VMEM((tokens + 8, lanes), F32),
            pltpu.VMEM((tokens, lanes), F32),
            pltpu.VMEM((tokens, wide), BF16),
            pltpu.VMEM((2, wide, lanes), BF16),
            pltpu.VMEM((tokens, lanes), F32),
            pltpu.VMEM((tokens, lanes), BF16),
            pltpu.VMEM((n, mixed, rows), BF16),
            pltpu.VMEM((n, mixed, rows), BF16),
            pltpu.VMEM((mixed, rows), F32),
            pltpu.VMEM((mixed, rows), F32),
            pltpu.VMEM((n, mixed, rows), BF16),
            dma((6,)), peers, peers, peers, peers,
            many, many, many, many, peers, peers, dma, dma, few, few, dma, dma, dma,
            dma((2, chips)), dma((2, parts)), dma((2, parts)), dma((2, parts)),
        ],
        compiler_params=pltpu.CompilerParams(
            collective_id=3, has_side_effects=True, vmem_limit_bytes=60 << 20
        ),
        name="front",
    )(hidden, gain, segments, w_in, w_small, taps, keeps)


def mixback_kernel(n, seqs, part_ref, e_hbm, conv_hbm, x_hbm, low_hbm, dpl_hbm, step_ref, wx_ref, taps_ref, keep_ref,
                   dx_hbm, dwx_ref, dwdt_ref, dconvw_ref,
                   e_ref, conv_ref, x_ref, low_ref, dpl_ref, dx_ref, dcv_ref, got, own, done, edge_out, edge_in,
                   loads, store, ms, mr, ns, nr, es, er):
    seq, t = lax.axis_index("seq"), lax.axis_index("tensor")
    rows = part_ref.shape[2]
    tokens, lanes = low_ref.shape
    taps = keep_ref.shape[1]
    width = min(512, lanes)
    piece = min(64, rows)
    across = lanes // width
    pieces = tokens // piece * across
    ahead_seq, behind_seq = lax.rem(seq + 1, seqs), lax.rem(seq + seqs - 1, seqs)

    barrier = pltpu.get_barrier_semaphore()
    for ahead in range(1, n):
        pl.semaphore_signal(barrier, inc=1, device_id=dict(tensor=lax.rem(t + ahead, n)), device_id_type=MESH)
    if seqs > 1:
        for peer in (ahead_seq, behind_seq):
            pl.semaphore_signal(barrier, inc=1, device_id=dict(seq=peer), device_id_type=MESH)
    pl.semaphore_wait(barrier, n - 1 + (2 if seqs > 1 else 0))

    def load(i):
        src = (conv_hbm, dpl_hbm, e_hbm, low_hbm, x_hbm)[i]
        return pltpu.make_async_copy(src, (conv_ref, dpl_ref, e_ref, low_ref, x_ref)[i], loads.at[i])

    def mix_copy(p, slot):
        return mesh_copy(part_ref.at[p], got.at[slot], ms.at[p], mr.at[slot], tensor=p)

    def sum_copy(p, slot):
        return mesh_copy(done.at[slot], done.at[slot], ns.at[p], nr.at[slot], tensor=p)

    def edge_copy():
        return mesh_copy(edge_out, edge_in, es, er, seq=behind_seq)

    for ahead in range(1, n):
        mix_copy(lax.rem(t + ahead, n), t).start()
    for i in range(5):
        load(i).start()

    dcv_ref[0:8, :] = jnp.zeros((8, lanes), F32)
    dcv_ref[tokens + 8:, :] = jnp.zeros((8, lanes), F32)
    load(1).wait()
    step = step_ref[0:dwdt_ref.shape[0], :].astype(BF16)
    tn = (((0,), (0,)), ((), ()))

    @pl.loop(0, across)
    def _(j):
        cols = pl.ds(pl.multiple_of(j * width, width), width)
        dwdt_ref[:, cols] = jnp.dot(step, dpl_ref[:, cols], preferred_element_type=F32)

    own[...] = part_ref[t].astype(F32)
    for ahead in range(1, n):
        p = lax.rem(t + ahead, n)
        mix_copy(p, p).wait_recv()
        own[...] = own[...] + got[p].astype(F32)
    done[t] = own[...].astype(BF16)
    for ahead in range(1, n):
        sum_copy(lax.rem(t + ahead, n), t).start()

    load(0).wait()

    @pl.loop(0, pieces)
    def _(i):
        here = pl.ds(pl.multiple_of(i // across * piece, piece), piece)
        cols = pl.ds(pl.multiple_of(i % across * width, width), width)
        v = conv_ref[here, cols]
        s = 1.0 / (1.0 + jnp.exp(-v))
        conv_ref[here, cols] = s * (1.0 + v * (1.0 - s))

    for i in range(2, 5):
        load(i).wait()
    for ahead in range(1, n):
        p = lax.rem(t + ahead, n)
        sum_copy(p, p).wait_recv()

    dwx_ref[...] = jnp.zeros_like(dwx_ref)
    dconvw_ref[...] = jnp.zeros_like(dconvw_ref)

    @pl.loop(0, n)
    def _(o):
        @pl.loop(0, across)
        def _(j):
            cols = pl.ds(pl.multiple_of(j * width, width), width)
            here = pl.ds(pl.multiple_of(o * rows, rows), rows)
            mixed = lax.dot_general(done[o], wx_ref[:, cols], tn, preferred_element_type=F32)
            dcv = (e_ref[here, cols] + mixed) * conv_ref[here, cols]
            dcv_ref[pl.ds(pl.multiple_of(o * rows + 8, 8), rows), cols] = dcv
            dwx_ref[:, cols] = dwx_ref[:, cols] + jnp.dot(done[o], low_ref[here, cols], preferred_element_type=F32)

    def shifted(base, size, cols):
        span = dcv_ref[pl.ds(base, size + 8), cols]
        keep = keep_ref[pl.ds(base, size + 8), :]
        total = jnp.zeros((size, span.shape[1]), F32)
        for j in range(taps):
            late = taps - 1 - j
            total = total + taps_ref[j:j + 1, cols] * (span * keep[:, j:j + 1])[late:late + size]
        return total

    if seqs > 1:
        edge_out[...] = shifted(0, 8, slice(None))

        @pl.when(seq > 0)
        def _():
            edge_copy().start()

    @pl.loop(0, pieces)
    def _(i):
        base = pl.multiple_of(i // across * piece, piece)
        cols = pl.ds(pl.multiple_of(i % across * width, width), width)
        dx_ref[pl.ds(base, piece), cols] = shifted(pl.multiple_of(base + 8, 8), piece, cols).astype(BF16)
        here = dcv_ref[pl.ds(pl.multiple_of(base + 8, 8), piece), cols]
        keep = keep_ref[pl.ds(pl.multiple_of(base + 8, 8), piece), :]
        span = x_ref[pl.ds(base, piece + 8), cols]
        for j in range(taps):
            first = 8 - (taps - 1) + j
            tap = jnp.sum(here * keep[:, j:j + 1] * span[first:first + piece], axis=0, keepdims=True)
            dconvw_ref[j:j + 1, cols] = dconvw_ref[j:j + 1, cols] + tap
        dconvw_ref[taps:taps + 1, cols] = dconvw_ref[taps:taps + 1, cols] + jnp.sum(here, axis=0, keepdims=True)

    if seqs > 1:
        @pl.when(seq < seqs - 1)
        def _():
            edge_copy().wait_recv()
            last = shifted(tokens - 16 + 8, 16, slice(None))
            dx_ref[tokens - 16:, :] = (last + jnp.concatenate([jnp.zeros_like(edge_in), edge_in[...]], 0)).astype(BF16)

        @pl.when(seq > 0)
        def _():
            edge_copy().wait_send()

    out = pltpu.make_async_copy(dx_ref, dx_hbm, store)
    out.start()
    for ahead in range(1, n):
        p = lax.rem(t + ahead, n)
        mix_copy(p, t).wait_send()
        sum_copy(p, t).wait_send()
    out.wait()


def mixback(part, e, conv_sum, x_rows, x_low, d_pre_low, mix_t, w_x, taps, keeps, rank):
    n, seqs = lax.axis_size("tensor"), lax.axis_size("seq")
    tokens, lanes = x_low.shape
    mixed, rows = part.shape[1:]
    vmem, hbm = pl.BlockSpec(memory_space=pltpu.VMEM), pl.BlockSpec(memory_space=pl.ANY)
    dma = pltpu.SemaphoreType.DMA
    peers = dma((n,))
    return pl.pallas_call(
        functools.partial(mixback_kernel, n, seqs),
        out_shape=[
            jax.ShapeDtypeStruct((tokens, lanes), BF16),
            jax.ShapeDtypeStruct((mixed, lanes), F32),
            jax.ShapeDtypeStruct((rank, lanes), F32),
            jax.ShapeDtypeStruct((8, lanes), F32),
        ],
        in_specs=[vmem] + [hbm] * 5 + [vmem] * 4,
        out_specs=[hbm] + [vmem] * 3,
        scratch_shapes=[
            pltpu.VMEM((tokens, lanes), F32),
            pltpu.VMEM((tokens, lanes), F32),
            pltpu.VMEM((tokens + 8, lanes), F32),
            pltpu.VMEM((tokens, lanes), BF16),
            pltpu.VMEM((tokens, lanes), BF16),
            pltpu.VMEM((tokens, lanes), BF16),
            pltpu.VMEM((tokens + 16, lanes), F32),
            pltpu.VMEM((n, mixed, rows), BF16),
            pltpu.VMEM((mixed, rows), F32),
            pltpu.VMEM((n, mixed, rows), BF16),
            pltpu.VMEM((8, lanes), F32),
            pltpu.VMEM((8, lanes), F32),
            dma((5,)), dma, peers, peers, peers, peers, dma, dma,
        ],
        compiler_params=pltpu.CompilerParams(
            collective_id=4, has_side_effects=True, vmem_limit_bytes=60 << 20
        ),
        name="mix_backward",
    )(part, e, conv_sum, x_rows, x_low, d_pre_low, mix_t, w_x, taps, keeps)


def on_device(
    hidden_in,
    teacher,
    segment_ids,
    norm_gain,
    input_projection_weight,
    conv_weight,
    conv_bias,
    xproj_weight,
    dtproj_weight,
    dt_bias,
    a_log,
    d_skip,
    output_projection_weight,
):
    tok_rows = segment_ids.shape[0]
    row_share = hidden_in.shape[0]
    model_width = hidden_in.shape[1]
    conv_taps = conv_weight.shape[0]
    chan_lanes = conv_weight.shape[1]
    back_rows = conv_taps - 1
    row_start = lax.axis_index("tensor") * row_share
    valid_mask = (segment_ids != 0).astype(jnp.float32)
    parts = lax.axis_size(("dp", "seq"))
    x_cols, dt_rows = xproj_weight.shape[1], dtproj_weight.shape[0]
    w_small = jnp.concatenate(
        [
            xproj_weight.T,
            jnp.zeros((SMALL_ROWS - x_cols, chan_lanes), BF16),
            dtproj_weight,
            jnp.zeros((-(SMALL_ROWS + dt_rows) % 16, chan_lanes), BF16),
        ],
        0,
    )
    seg_float = segment_ids.astype(F32)
    prev_seg = jnp.where(lax.axis_index("seq") > 0, seg_float[:1], jnp.zeros((back_rows,), F32))
    ext_seg = jnp.concatenate([prev_seg, seg_float], 0)
    tap_keeps = []
    for offset in range(conv_taps):
        tap_keeps.append((ext_seg[offset : offset + tok_rows] == seg_float).astype(F32)[:, None])
    taps = jnp.concatenate(
        [conv_weight.astype(F32), conv_bias.astype(F32)[None], jnp.zeros((7 - conv_taps, chan_lanes), F32)], 0
    )
    x_rows, z_gate, normalized_rows, w_in, conv_sum, x_low, total, gain_rows, w_small, mix_t = front(
        hidden_in,
        norm_gain[None],
        segment_ids.reshape(8, -1),
        jnp.swapaxes(input_projection_weight, 0, 1),
        w_small,
        taps,
        jnp.concatenate(tap_keeps, 1),
        x_cols,
    )
    w_out_rows, z_gate = lax.optimization_barrier((output_projection_weight.T, z_gate))
    w_out = lax.all_gather(w_out_rows, ("dp", "seq"), axis=0, tiled=True)
    total_count = total[0, 0]
    w_x = w_small[:, :x_cols].reshape(parts * x_cols, chan_lanes)
    w_dt = w_small[:, SMALL_ROWS : SMALL_ROWS + dt_rows].reshape(parts * dt_rows, chan_lanes)
    share_rows = hidden_in.astype(F32)
    full_gain = gain_rows[0]
    inv_share = lax.rsqrt(jnp.mean(share_rows * share_rows, axis=1, keepdims=True) + EPS)
    rank_width = w_dt.shape[0]
    same_doc = (seg_float == ext_seg[back_rows - 1 : back_rows - 1 + tok_rows]).astype(jnp.float32)
    rates = -jnp.exp(a_log) * LOG2E
    block = 128
    first_reset = jnp.min(jnp.where(same_doc == 0, jnp.arange(tok_rows), tok_rows))
    alive = (jnp.arange(0, tok_rows, block) <= first_reset).astype(jnp.int32)
    y_local, marks, state_last, stepd, inject, step_size, step_slope = fwd(
        mix_t, w_dt, dt_bias[None], x_low, same_doc[:, None], rates, tb=block, w=1024
    )

    def reach():
        return jnp.exp2(rates * jnp.sum(stepd, axis=0)[None])

    state_in = carried(state_last, reach, "seq", 1)
    scan_out, marks, gated_output_rows = correct(
        rank_width, alive, y_local, stepd, mix_t, rates, marks, state_in, x_low, d_skip[None], z_gate, tb=block, w=1024
    )
    valid_share = lax.dynamic_slice_in_dim(valid_mask, row_start, row_share, 0)
    total_tokens = float(tok_rows * lax.axis_size(("dp", "seq")))
    scale = (total_tokens / total_count * valid_share)[:, None]
    output, grad_out, d_wout, d_scan, d_z = middle(
        gated_output_rows, w_out, hidden_in, teacher, scale, z_gate, scan_out
    )
    adjoint_first = entry(rank_width, alive, stepd, d_scan, mix_t, rates, tb=block, w=1024)
    adjoint_in = carried(adjoint_first, reach, "seq", -1)
    d_pre_low, d_direct, d_rank_t, d_b_part, d_c_part, a_log_part, dt_bias_part, d_skip_part = bwd(
        stepd, inject, d_scan, mix_t, rates, marks, adjoint_in,
        step_size, step_slope, x_low, d_skip[None], w_dt, tb=block
    )
    part = jnp.concatenate(
        [
            jnp.sum(d_rank_t, axis=0),
            jnp.sum(d_b_part, axis=0).reshape(tok_rows, N).T,
            jnp.sum(d_c_part, axis=0).reshape(tok_rows, N).T,
        ],
        0,
    )
    part = part.astype(BF16).reshape(part.shape[0], -1, row_share).transpose(1, 0, 2)
    edge = jnp.zeros((8, conv_taps), F32)
    d_x, d_wx, d_wdt, conv_parts = mixback(
        part, d_direct, conv_sum, x_rows, x_low, d_pre_low, mix_t, w_x, taps,
        jnp.concatenate([edge] + [jnp.concatenate(tap_keeps, 1)] + [edge], 0),
        rank_width,
    )
    d_norm_share, g_in, g_small, g_whole = tail(
        d_x, d_z, w_in, normalized_rows, d_wx, d_wdt, a_log_part, conv_parts, dt_bias_part, d_skip_part
    )
    g_in = jnp.swapaxes(g_in, 0, 1)
    inner_sum = jnp.sum(d_norm_share * full_gain[None] * share_rows, axis=1, keepdims=True)
    inv_cube = inv_share * inv_share * inv_share
    input_grad = (
        grad_out
        + inv_share * full_gain[None] * d_norm_share
        - share_rows * inv_cube * inner_sum / model_width
    )
    rank_here = rank_width // parts
    state_here = 2 * N // parts
    g_x_rank = g_small[:rank_here].T
    g_dt = g_small[rank_here : 2 * rank_here]
    g_x_state = g_small[2 * rank_here : 2 * rank_here + state_here].T
    g_out = lax.psum_scatter(d_wout, ("dp", "seq"), scatter_dimension=0, tiled=True).astype(F32).T
    g_gain = g_whole[N + 16, : norm_gain.shape[0]] / norm_gain.astype(F32)
    g_alog, g_conv_w, g_conv_b = g_whole[:N], g_whole[N : N + conv_taps], g_whole[N + conv_taps]
    g_bias, g_skip = g_whole[N + 8], g_whole[N + 9]
    return (
        output,
        input_grad,
        g_gain,
        g_in,
        g_conv_w,
        g_conv_b,
        g_x_rank,
        g_x_state,
        g_dt,
        g_bias,
        g_alog,
        g_skip,
        g_out,
    )


def solution(mesh):
    placed = (
        P(("dp", "seq", "tensor"), None),
        P(("dp", "seq", "tensor"), None),
        P(("dp", "seq")),
        P("tensor"),
        P(("dp", "seq"), None, "tensor"),
        P(None, "tensor"),
        P("tensor"),
        P("tensor", ("dp", "seq")),
        P(("dp", "seq"), "tensor"),
        P("tensor"),
        P(None, "tensor"),
        P("tensor"),
        P("tensor", ("dp", "seq")),
    )
    return jax.shard_map(
        on_device,
        mesh=mesh,
        in_specs=placed,
        out_specs=(
            P(("dp", "seq", "tensor"), None),
            P(("dp", "seq", "tensor"), None),
            P("tensor"),
            P(("dp", "seq"), None, "tensor"),
            P(None, "tensor"),
            P("tensor"),
            P("tensor", ("dp", "seq")),
            P("tensor", ("dp", "seq")),
            P(("dp", "seq"), "tensor"),
            P("tensor"),
            P(None, "tensor"),
            P("tensor"),
            P("tensor", ("dp", "seq")),
        ),
        check_vma=False,
    )
```

```python
import functools

import jax
import jax.numpy as jnp
from jax import lax
from jax.experimental import pallas as pl
from jax.experimental.pallas import tpu as pltpu
from jax.sharding import PartitionSpec as P

EPS = 1e-05
LOG2E = 1.4426950408889634
LN2 = 0.6931471805599453
FAR = 1e30
SMALL_ROWS = 24
N = 16
CH = 16
F32, BF16 = jnp.float32, jnp.bfloat16
MESH = pl.DeviceIdType.MESH


def passed_along(x, axis, by):
    size = lax.axis_size(axis)
    pairs = [(i, i + by) for i in range(size) if 0 <= i + by < size]
    return lax.ppermute(x, axis, pairs)


def spread(values_t):
    tokens = values_t.shape[1]
    name = lax.broadcasted_iota(jnp.int32, (N, CH * N), 0)
    lane = lax.broadcasted_iota(jnp.int32, (N, CH * N), 1)
    copies = (name == lane % N).astype(BF16)
    wide = lax.dot_general(values_t.astype(BF16), copies, (((0,), (0,)), ((), ())), preferred_element_type=F32)
    row = lax.broadcasted_iota(jnp.int32, (tokens, CH * N), 0)
    place_of = lax.broadcasted_iota(jnp.int32, (tokens, CH * N), 1)
    return jnp.where(row % CH == place_of // N, wide, 0.0).astype(BF16)


def fwd_kernel(mix_ref, wdt_ref, bias_ref, low_ref, keep_ref, rate_ref,
               y_ref, ckpt_ref, last_ref, stepd_ref, u_ref, step_ref, sig_ref, state_ref, sbf_ref, cdiag_ref):
    @pl.when(pl.program_id(1) == 0)
    def _():
        state_ref[...] = jnp.zeros_like(state_ref)
    ckpt_ref[0] = state_ref[...]
    rank = wdt_ref.shape[0]
    b_t, c_t = mix_ref[rank:rank + N, :], mix_ref[rank + N:rank + 2 * N, :]
    cdiag_ref[...] = spread(c_t)
    tn = (((0,), (0,)), ((), ()))
    pre = lax.dot_general(mix_ref[0:rank, :].astype(BF16), wdt_ref[...], tn, preferred_element_type=F32)
    pre = pre + bias_ref[...]
    small = jnp.exp(-jnp.abs(pre))
    step = jnp.maximum(pre, 0.0) + jnp.log1p(small)
    step_ref[...] = step
    sig_ref[...] = jnp.where(pre >= 0, 1.0, small) / (1.0 + small)
    stepd_ref[...] = jnp.where(keep_ref[...] > 0, step, FAR)
    u_ref[...] = step * low_ref[...].astype(F32)
    rate = rate_ref[...]
    tb = stepd_ref.shape[0]

    s = state_ref[...]
    for base in range(0, tb, CH):
        for k in range(base, base + CH):
            dec = jnp.exp2(rate * stepd_ref[k:k + 1, :])
            s = dec * s + b_t[:, k:k + 1] * u_ref[k:k + 1, :]
            sbf_ref[(k - base) * N:(k - base + 1) * N, :] = s.astype(BF16)
        y_ref[base:base + CH, :] = jnp.dot(cdiag_ref[base:base + CH, :], sbf_ref[...], preferred_element_type=F32)
    state_ref[...] = s
    last_ref[...] = s


def fwd(mix_t, w_dt, bias, low, keep, rate, tb=128, w=512):
    t, c = low.shape
    w = min(w, c)
    grid = (c // w, t // tb)
    mixed, rank = mix_t.shape[0], w_dt.shape[0]
    rows = pl.BlockSpec((tb, w), lambda j, i: (i, j))
    whole = jax.ShapeDtypeStruct((t, c), F32)
    return pl.pallas_call(
        fwd_kernel,
        grid=grid,
        in_specs=[
            pl.BlockSpec((mixed, tb), lambda j, i: (0, i)),
            pl.BlockSpec((rank, w), lambda j, i: (0, j)),
            pl.BlockSpec((1, w), lambda j, i: (0, j)),
            rows,
            pl.BlockSpec((tb, 1), lambda j, i: (i, 0)),
            pl.BlockSpec((N, w), lambda j, i: (0, j)),
        ],
        out_specs=[
            rows,
            pl.BlockSpec((1, N, w), lambda j, i: (i, 0, j)),
            pl.BlockSpec((N, w), lambda j, i: (0, j)),
            rows, rows, rows, rows,
        ],
        out_shape=[
            whole,
            jax.ShapeDtypeStruct((t // tb, N, c), F32),
            jax.ShapeDtypeStruct((N, c), F32),
            whole, whole, whole, whole,
        ],
        scratch_shapes=[pltpu.VMEM((N, w), F32), pltpu.VMEM((CH * N, w), BF16), pltpu.VMEM((tb, CH * N), BF16)],
        compiler_params=pltpu.CompilerParams(vmem_limit_bytes=48 << 20),
        name="scan_forward",
    )(mix_t, w_dt, bias, low, keep, rate)


def bwd_kernel(stepd_ref, u_ref, ds_ref, mix_ref, rate_ref, ckpt_ref, gin_ref,
               step_ref, sig_ref, low_ref, skip_ref, wdt_ref,
               dpl_ref, e_ref, rank_ref, db_ref, dc_ref, acc_ref, bias_ref, dskip_ref,
               g_ref, states_ref, abf_ref, rbf_ref, pb_ref, pc_ref, wb_ref, dn_ref, bdiag_ref, dec_ref):
    @pl.when(pl.program_id(1) == 0)
    def _():
        g_ref[...] = gin_ref[...]
        acc_ref[...] = jnp.zeros_like(acc_ref)
        bias_ref[...] = jnp.zeros_like(bias_ref)
        dskip_ref[...] = jnp.zeros_like(dskip_ref)

    rate = rate_ref[...]
    tb = stepd_ref.shape[0]
    nc = tb // CH

    def fold(v):
        p = v[:, 0:128]
        for q in range(1, v.shape[1] // 128):
            p = p + v[:, q * 128:(q + 1) * 128]
        return p

    states_ref[0:N, :] = ckpt_ref[0]
    nt = (((1,), (1,)), ((), ()))
    lanes = jnp.ones((8, 128), BF16)
    rank = wdt_ref.shape[0]
    b_t, c_t = mix_ref[rank:rank + N, :], mix_ref[rank + N:rank + 2 * N, :]
    bdiag_ref[...] = spread(b_t)
    ones = spread(jnp.ones((N, CH), F32))

    s = ckpt_ref[0]
    for c in range(nc):
        base = c * CH
        for k in range(CH):
            at = base + k
            dec = jnp.exp2(rate * stepd_ref[at:at + 1, :])
            dec_ref[at * N:(at + 1) * N, :] = dec
            s = dec * s + b_t[:, at:at + 1] * u_ref[at:at + 1, :]
            states_ref[(at + 1) * N:(at + 2) * N, :] = s
            pc_ref[k * N:(k + 1) * N, :] = fold(s * ds_ref[at:at + 1, :])
        dc = lax.dot_general(lanes, pc_ref[...].astype(BF16), nt, preferred_element_type=F32)
        dc_ref[0, c:c + 1, :] = dc[0:1]

    g, acc = g_ref[...], acc_ref[...]
    for c in range(nc - 1, -1, -1):
        base = c * CH
        for k in range(CH - 1, -1, -1):
            at = base + k
            sd = stepd_ref[at:at + 1, :]
            adj = g + c_t[:, at:at + 1] * ds_ref[at:at + 1, :]
            abf_ref[k * N:(k + 1) * N, :] = adj.astype(BF16)
            pb_ref[k * N:(k + 1) * N, :] = fold(adj * u_ref[at:at + 1, :])
            g = dec_ref[at * N:(at + 1) * N, :] * adj
            before = states_ref[at * N:(at + 1) * N, :]
            r = g * before * rate
            rbf_ref[k * N:(k + 1) * N, :] = r.astype(BF16)
            acc = acc + r * sd
        wb_ref[base:base + CH, :] = jnp.dot(bdiag_ref[base:base + CH, :], abf_ref[...], preferred_element_type=F32)
        dn_ref[base:base + CH, :] = jnp.dot(ones, rbf_ref[...], preferred_element_type=F32)
        db = lax.dot_general(lanes, pb_ref[...].astype(BF16), nt, preferred_element_type=F32)
        db_ref[0, c:c + 1, :] = db[0:1]
    g_ref[...] = g
    acc_ref[...] = acc

    low, ds, weighted = low_ref[...].astype(F32), ds_ref[...], wb_ref[...]
    d_pre = (LN2 * dn_ref[...] + low * weighted) * sig_ref[...]
    d_pre_low = d_pre.astype(BF16)
    dpl_ref[...] = d_pre_low
    e_ref[...] = skip_ref[...] * ds + step_ref[...] * weighted
    bias_ref[...] = bias_ref[...] + jnp.sum(d_pre, axis=0, keepdims=True)
    dskip_ref[...] = dskip_ref[...] + jnp.sum(ds * low, axis=0, keepdims=True)
    rank_ref[0] = lax.dot_general(wdt_ref[...], d_pre_low, nt, preferred_element_type=F32)


def bwd(stepd, u, ds, mix_t, rate, ckpt, gin, step, sig, low, skip, w_dt, tb=128, w=512):
    t, c = stepd.shape
    w = min(w, c)
    nb = t // tb
    grid = (c // w, nb)
    rank = w_dt.shape[0]
    rows = pl.BlockSpec((tb, w), lambda j, i: (nb - 1 - i, j))
    return pl.pallas_call(
        bwd_kernel,
        grid=grid,
        in_specs=[
            rows, rows, rows,
            pl.BlockSpec((mix_t.shape[0], tb), lambda j, i: (0, nb - 1 - i)),
            pl.BlockSpec((N, w), lambda j, i: (0, j)),
            pl.BlockSpec((1, N, w), lambda j, i: (nb - 1 - i, 0, j)),
            pl.BlockSpec((N, w), lambda j, i: (0, j)),
            rows, rows, rows,
            pl.BlockSpec((1, w), lambda j, i: (0, j)),
            pl.BlockSpec((rank, w), lambda j, i: (0, j)),
        ],
        out_specs=[
            rows, rows,
            pl.BlockSpec((1, rank, tb), lambda j, i: (j, 0, nb - 1 - i)),
            pl.BlockSpec((1, tb // CH, CH * N), lambda j, i: (j, nb - 1 - i, 0)),
            pl.BlockSpec((1, tb // CH, CH * N), lambda j, i: (j, nb - 1 - i, 0)),
            pl.BlockSpec((N, w), lambda j, i: (0, j)),
            pl.BlockSpec((1, w), lambda j, i: (0, j)),
            pl.BlockSpec((1, w), lambda j, i: (0, j)),
        ],
        out_shape=[
            jax.ShapeDtypeStruct((t, c), BF16),
            jax.ShapeDtypeStruct((t, c), F32),
            jax.ShapeDtypeStruct((c // w, rank, t), F32),
            jax.ShapeDtypeStruct((c // w, t // CH, CH * N), F32),
            jax.ShapeDtypeStruct((c // w, t // CH, CH * N), F32),
            jax.ShapeDtypeStruct((N, c), F32),
            jax.ShapeDtypeStruct((1, c), F32),
            jax.ShapeDtypeStruct((1, c), F32),
        ],
        scratch_shapes=[pltpu.VMEM((N, w), F32), pltpu.VMEM(((tb + 1) * N, w), F32),
                        pltpu.VMEM((CH * N, w), BF16), pltpu.VMEM((CH * N, w), BF16), pltpu.VMEM((CH * N, 128), F32), pltpu.VMEM((CH * N, 128), F32),
                        pltpu.VMEM((tb, w), F32), pltpu.VMEM((tb, w), F32), pltpu.VMEM((tb, CH * N), BF16),
                        pltpu.VMEM((tb * N, w), F32)],
        compiler_params=pltpu.CompilerParams(vmem_limit_bytes=48 << 20),
        name="scan_backward",
    )(stepd, u, ds, mix_t, rate, ckpt, gin, step, sig, low, skip, w_dt)


def correct_kernel(rank, alive_ref, y_ref, stepd_ref, mix_ref, rate_ref, ckpt_ref, sin_ref, low_ref, skip_ref, z_ref,
                   yo_ref, ckpto_ref, gated_ref, state_ref, sbf_ref, cdiag_ref):
    i = pl.program_id(1)

    @pl.when(i == 0)
    def _():
        state_ref[...] = sin_ref[...]

    alive = alive_ref[i] != 0

    @pl.when(alive)
    def _():
        rate = rate_ref[...]
        ckpto_ref[0] = ckpt_ref[0] + state_ref[...]

        cdiag_ref[...] = spread(mix_ref[rank + N:rank + 2 * N, :])
        s = state_ref[...]
        for base in range(0, y_ref.shape[0], CH):
            for k in range(CH):
                s = jnp.exp2(rate * stepd_ref[base + k:base + k + 1, :]) * s
                sbf_ref[k * N:(k + 1) * N, :] = s.astype(BF16)
            yo_ref[base:base + CH, :] = y_ref[base:base + CH, :] + jnp.dot(
                cdiag_ref[base:base + CH, :], sbf_ref[...], preferred_element_type=F32
            )
        state_ref[...] = s

    @pl.when(jnp.logical_not(alive))
    def _():
        yo_ref[...] = y_ref[...]
        ckpto_ref[...] = ckpt_ref[...]

    total = yo_ref[...] + skip_ref[...] * low_ref[...].astype(F32)
    z = z_ref[...]
    yo_ref[...] = total
    gated_ref[...] = (total * (z / (1.0 + jnp.exp(-z)))).astype(BF16)


def correct(rank, alive, y, stepd, mix_t, rate, ckpt, state_in, low, skip, z, tb=128, w=512):
    t, c = stepd.shape
    w = min(w, c)
    rows = pl.BlockSpec((tb, w), lambda j, i, _: (i, j))
    lanes = pl.BlockSpec((N, w), lambda j, i, _: (0, j))
    marks = pl.BlockSpec((1, N, w), lambda j, i, _: (i, 0, j))
    return pl.pallas_call(
        functools.partial(correct_kernel, rank),
        grid_spec=pltpu.PrefetchScalarGridSpec(
            num_scalar_prefetch=1,
            grid=(c // w, t // tb),
            in_specs=[rows, rows, pl.BlockSpec((mix_t.shape[0], tb), lambda j, i, _: (0, i)), lanes, marks, lanes,
                      rows, pl.BlockSpec((1, w), lambda j, i, _: (0, j)), rows],
            out_specs=[rows, marks, rows],
            scratch_shapes=[pltpu.VMEM((N, w), F32), pltpu.VMEM((CH * N, w), BF16), pltpu.VMEM((tb, CH * N), BF16)],
        ),
        out_shape=[jax.ShapeDtypeStruct((t, c), F32), jax.ShapeDtypeStruct(ckpt.shape, F32),
                   jax.ShapeDtypeStruct((t, c), BF16)],
        compiler_params=pltpu.CompilerParams(vmem_limit_bytes=48 << 20),
        name="scan_correct",
    )(alive, y, stepd, mix_t, rate, ckpt, state_in, low, skip, z)


def entry_kernel(rank, alive_ref, stepd_ref, ds_ref, mix_ref, rate_ref, g_ref):
    i = pl.program_id(1)

    @pl.when(i == 0)
    def _():
        g_ref[...] = jnp.zeros_like(g_ref)

    @pl.when(alive_ref[pl.num_programs(1) - 1 - i] != 0)
    def _():
        rate = rate_ref[...]
        c_t = mix_ref[rank + N:rank + 2 * N, :]
        g = g_ref[...]
        for k in range(stepd_ref.shape[0] - 1, -1, -1):
            adj = g + c_t[:, k:k + 1] * ds_ref[k:k + 1, :]
            g = jnp.exp2(rate * stepd_ref[k:k + 1, :]) * adj
        g_ref[...] = g


def entry(rank, alive, stepd, ds, mix_t, rate, tb=128, w=512):
    t, c = stepd.shape
    w = min(w, c)
    nb = t // tb
    rows = pl.BlockSpec((tb, w), lambda j, i, _: (nb - 1 - i, j))
    lanes = pl.BlockSpec((N, w), lambda j, i, _: (0, j))
    return pl.pallas_call(
        functools.partial(entry_kernel, rank),
        grid_spec=pltpu.PrefetchScalarGridSpec(
            num_scalar_prefetch=1,
            grid=(c // w, nb),
            in_specs=[rows, rows, pl.BlockSpec((mix_t.shape[0], tb), lambda j, i, _: (0, nb - 1 - i)), lanes],
            out_specs=lanes,
        ),
        out_shape=jax.ShapeDtypeStruct((N, c), F32),
        compiler_params=pltpu.CompilerParams(vmem_limit_bytes=48 << 20),
        name="scan_entry",
    )(alive, stepd, ds, mix_t, rate)


def carried(local, reach, axis, by):
    found = jnp.zeros_like(local)
    for turn in range(lax.axis_size(axis) - 1):
        found = passed_along(local if turn == 0 else local + reach() * found, axis, by)
    return found


def mesh_copy(src, dst, send, recv, **where):
    return pltpu.make_async_remote_copy(
        src_ref=src, dst_ref=dst, send_sem=send, recv_sem=recv, device_id=where, device_id_type=MESH
    )


def place():
    dp, seq, mine = lax.axis_index("dp"), lax.axis_index("seq"), lax.axis_index("tensor")
    return dp, seq, mine


def tail_kernel(n, dps, seqs, tile, lag, rank, dx_ref, dz_ref, w_hbm, nrm_hbm,
                dwx_ref, dwdt_ref, alog_ref, conv_ref, bias_ref, skip_ref,
                dn_ref, gin_ref, gs_ref, ga_ref,
                sm_ref, gacc, gsend, grecv, all_mine,
                zr, zl, w_ref, nrm_ref, loads, nrm_load, one_send, one_recv, two_recv, sm_one, sm_two, all_one, all_two,
                r_send, r_recv, l_send, l_recv, w1s, w1r, w2s, w2r, s1s, s1r, s2s, s2r, a1s, a1r, a2s, a2r, gs, gr):
    dp, seq, t = place()
    core, hi = dp % 2, dp // 2
    chips = dps // 2 * seqs
    chip = hi * seqs + seq
    rows = dn_ref.shape[0]
    wide = dn_ref.shape[1]
    wrows = gin_ref.shape[1]
    subs = wide // tile

    def owner(q, c):
        return (q // seqs * 2 + c) * seqs + q % seqs

    def to_chip(q):
        return dict(dp=q // seqs * 2 + core, seq=q % seqs)

    barrier = pltpu.get_barrier_semaphore()
    pl.semaphore_signal(barrier, inc=1, device_id=dict(dp=hi * 2 + 1 - core), device_id_type=MESH)
    for step in range(1, chips):
        q = lax.rem(chip + step, chips)
        pl.semaphore_signal(barrier, inc=1, device_id=to_chip(q), device_id_type=MESH)

    for ahead in range(1, n):
        pl.semaphore_signal(barrier, inc=1, device_id=dict(tensor=lax.rem(t + ahead, n)), device_id_type=MESH)
    pl.semaphore_wait(barrier, chips + n - 1)
    gacc[...] = jnp.zeros_like(gacc)

    partner = dict(dp=hi * 2 + 1 - core)
    right, left = dict(tensor=lax.rem(t + 1, n)), dict(tensor=lax.rem(t + n - 1, n))

    def r_copy(i):
        return mesh_copy(zr.at[i], zr.at[i], r_send.at[i], r_recv.at[i], **right)

    def l_copy(i):
        return mesh_copy(zl.at[i], zl.at[i], l_send.at[i], l_recv.at[i], **left)

    def w1_copy(q):
        return mesh_copy(one_send.at[q], one_recv.at[q], w1s.at[q], w1r.at[q], **partner)

    def w2_copy(q, slot):
        return mesh_copy(one_recv.at[q], two_recv.at[slot], w2s.at[q], w2r.at[slot], **to_chip(q))

    def s1_copy(q):
        return mesh_copy(sm_ref.at[owner(q, 1 - core)], sm_one.at[q], s1s.at[q], s1r.at[q], **partner)

    def s2_copy(q, slot):
        return mesh_copy(sm_one.at[q], sm_two.at[slot], s2s.at[q], s2r.at[slot], **to_chip(q))

    def a1_copy():
        return mesh_copy(all_mine, all_one, a1s, a1r, **partner)

    def a2_copy(q, slot):
        return mesh_copy(all_one, all_two.at[slot], a2s.at[q], a2r.at[slot], **to_chip(q))

    def g_copy(p, slot):
        return mesh_copy(gsend.at[p], grecv.at[slot], gs.at[p], gr.at[slot], tensor=p)

    def cols_of(sub):
        return pl.ds(pl.multiple_of(sub * tile, tile), tile)

    def load(sub):
        ref = w_ref.at[:, cols_of(sub), :]
        return pltpu.make_async_copy(w_hbm.at[:, cols_of(sub), :], ref, loads.at[sub])

    def partial_tile(o, sub):
        here = pl.ds(pl.multiple_of(o * rows, rows), rows)
        cols = cols_of(sub)
        nt = (((1,), (1,)), ((), ()))
        return lax.dot_general(
            dx_ref[here, :], w_ref[0, cols, :], nt, preferred_element_type=F32
        ) + lax.dot_general(dz_ref[here, :], w_ref[1, cols, :], nt, preferred_element_type=F32)

    def weight_rows(p, k):
        cols = pl.ds(pl.multiple_of(p * wrows, wrows), wrows)
        tn = (((0,), (0,)), ((), ()))
        d_ref = dx_ref if k == 0 else dz_ref
        block = lax.dot_general(nrm_ref[:, cols], d_ref[...], tn, preferred_element_type=F32)
        scaled = (block * w_ref[k, cols, :].astype(F32)).astype(BF16)
        lanes = jnp.ones((8, block.shape[1]), BF16)
        nt = (((1,), (1,)), ((), ()))
        gacc[:, cols] = gacc[:, cols] + lax.dot_general(lanes, scaled, nt, preferred_element_type=F32)
        return block

    def load_rows():
        return pltpu.make_async_copy(nrm_hbm, nrm_ref, nrm_load)

    @pl.loop(0, subs)
    def _(sub):
        load(sub).start()

    load_rows().start()

    parts = sm_ref.shape[0]
    for p in range(parts):
        here, more = rank // parts, (dwx_ref.shape[0] - rank) // parts
        sm_ref[p, 0:here, :] = dwx_ref[p * here:(p + 1) * here, :]
        sm_ref[p, here:2 * here, :] = dwdt_ref[p * here:(p + 1) * here, :]
        sm_ref[p, 2 * here:2 * here + more, :] = dwx_ref[rank + p * more:rank + (p + 1) * more, :]
        sm_ref[p, 2 * here + more:, :] = jnp.zeros((sm_ref.shape[1] - 2 * here - more, sm_ref.shape[2]), F32)
    for q in range(chips):
        s1_copy(q).start()

    def stream(i, limit, start, buf, copy, owner_of):
        @pl.when(jnp.logical_and(i >= 0, i < limit))
        def _():
            block = partial_tile(owner_of(i // subs), i % subs)

            @pl.when(start)
            def _():
                buf[i] = block.astype(BF16)

            @pl.when(jnp.logical_not(start))
            def _():
                copy(i).wait_recv()
                buf[i] = (block + buf[i].astype(F32)).astype(BF16)

            copy(i).start()

    def step(g, _):
        @pl.when(g == 0)
        def _():
            load(0).wait()

        @pl.when(g == 1)
        def _():
            @pl.loop(1, subs)
            def _(sub):
                load(sub).wait()

            load_rows().wait()

        stream(g - lag * t, (n - 1 - t) * subs, t == 0, zr, r_copy, lambda k: n - 1 - k)
        stream(g - lag * (n - 1 - t), t * subs, t == n - 1, zl, l_copy, lambda k: k)

        @pl.when(jnp.logical_and(g >= 1, g < chips + 1))
        def _():
            for k in range(2):
                one_send[g - 1, k] = weight_rows(owner(g - 1, 1 - core), k).astype(BF16)
            w1_copy(g - 1).start()

        @pl.when(jnp.logical_and(g >= chips + 1, g < 2 * chips))
        def _():
            q = lax.rem(chip + g - chips, chips)
            w1_copy(q).wait_recv()
            for k in range(2):
                one_recv[q, k] = (weight_rows(owner(q, core), k) + one_recv[q, k].astype(F32)).astype(BF16)
            w2_copy(q, chip).start()

        @pl.when(g == 2 * chips)
        def _():
            for q in range(chips):
                s1_copy(q).wait_recv()
                sm_one[q] = sm_one[q] + sm_ref[owner(q, core)]
            for ahead in range(1, chips):
                q = lax.rem(chip + ahead, chips)
                s2_copy(q, chip).start()
            w1_copy(chip).wait_recv()
            for k in range(2):
                gin_ref[k] = weight_rows(owner(chip, core), k) + one_recv[chip, k].astype(F32)

            share = wide // n
            for p in range(n):
                gsend[p] = gacc[:, p * share:(p + 1) * share]
            for ahead in range(1, n):
                g_copy(lax.rem(t + ahead, n), t).start()

        late = 2 * chips + 1

        @pl.when(jnp.logical_and(g >= late, g < late + subs))
        def _():
            dn_ref[:, cols_of(g - late)] = partial_tile(t, g - late)

        @pl.when(g == late + subs // 2)
        def _():
            share = wide // n
            plain = all_mine.shape[0] - 8
            all_mine[0:N, :] = LN2 * alog_ref[...]
            all_mine[N:N + 8, :] = conv_ref[...]
            all_mine[N + 8:plain, :] = jnp.zeros((plain - N - 8, all_mine.shape[1]), F32)
            all_mine[N + 8:N + 9, :] = bias_ref[...]
            all_mine[N + 9:N + 10, :] = skip_ref[...]
            all_mine[plain:, :] = jnp.zeros((8, all_mine.shape[1]), F32)
            all_mine[plain:, 0:share] = gsend[t]
            for ahead in range(1, n):
                p = lax.rem(t + ahead, n)
                g_copy(p, p).wait_recv()
                all_mine[plain:, 0:share] = all_mine[plain:, 0:share] + grecv[p]
            a1_copy().start()

        @pl.when(g == late + subs)
        def _():
            a1_copy().wait_recv()
            all_one[...] = all_one[...] + all_mine[...]
            for ahead in range(1, chips):
                a2_copy(lax.rem(chip + ahead, chips), chip).start()

        return 0

    steps = max((n - 1) * max(subs, lag), 2 * chips + subs + 2)
    lax.fori_loop(0, steps, step, 0)

    @pl.loop(0, subs)
    def _(s):
        cols = cols_of(s)

        @pl.when(t > 0)
        def _():
            i = (n - 1 - t) * subs + s
            r_copy(i).wait_recv()
            dn_ref[:, cols] = dn_ref[:, cols] + zr[i].astype(F32)

        @pl.when(t < n - 1)
        def _():
            i = t * subs + s
            l_copy(i).wait_recv()
            dn_ref[:, cols] = dn_ref[:, cols] + zl[i].astype(F32)

    gs_ref[...] = sm_one[chip]
    for ahead in range(1, chips):
        q = lax.rem(chip + ahead, chips)
        s2_copy(q, q).wait_recv()
        gs_ref[...] = gs_ref[...] + sm_two[q]
    ga_ref[...] = all_one[...]
    for ahead in range(1, chips):
        q = lax.rem(chip + ahead, chips)
        w2_copy(q, q).wait_recv()
        gin_ref[...] = gin_ref[...] + two_recv[q].astype(F32)
    for ahead in range(1, chips):
        q = lax.rem(chip + ahead, chips)
        a2_copy(q, q).wait_recv()
        ga_ref[...] = ga_ref[...] + all_two[q]

    for q in range(chips):
        s1_copy(q).wait_send()
        w1_copy(q).wait_send()
    a1_copy().wait_send()
    for ahead in range(1, n):
        g_copy(lax.rem(t + ahead, n), t).wait_send()
    for ahead in range(1, chips):
        q = lax.rem(chip + ahead, chips)
        s2_copy(q, chip).wait_send()
        a2_copy(q, chip).wait_send()
        w2_copy(q, chip).wait_send()

    @pl.loop(0, (n - 1) * subs)
    def _(i):
        @pl.when(i < (n - 1 - t) * subs)
        def _():
            r_copy(i).wait_send()

        @pl.when(i < t * subs)
        def _():
            l_copy(i).wait_send()


def tail(dx, dz, w_full, normed, dwx, dwdt, *singles):
    n, dps, seqs = (lax.axis_size(axis) for axis in ("tensor", "dp", "seq"))
    chips = dps // 2 * seqs
    rank = dwdt.shape[0]
    small_rows = -(-(rank + dwx.shape[0]) // (dps * seqs) // 8) * 8
    all_rows = N + 24
    rows = dx.shape[0] // n
    wide, lanes = w_full.shape[1], w_full.shape[2]
    wrows = wide // (dps * seqs)
    tile = 256
    subs = wide // tile
    hops = (n - 1) * subs
    vmem, hbm = pl.BlockSpec(memory_space=pltpu.VMEM), pl.BlockSpec(memory_space=pl.ANY)
    dma = pltpu.SemaphoreType.DMA
    few = dma((chips,))
    return pl.pallas_call(
        functools.partial(tail_kernel, n, dps, seqs, tile, 3, rank),
        out_shape=[
            jax.ShapeDtypeStruct((rows, wide), F32),
            jax.ShapeDtypeStruct((2, wrows, lanes), F32),
            jax.ShapeDtypeStruct((small_rows, lanes), F32),
            jax.ShapeDtypeStruct((all_rows, lanes), F32),
        ],
        in_specs=[vmem] * 2 + [hbm] * 2 + [vmem] * 6,
        out_specs=[vmem] * 4,
        scratch_shapes=[
            pltpu.VMEM((dps * seqs, small_rows, lanes), F32),
            pltpu.VMEM((8, wide), F32),
            pltpu.VMEM((n, 8, wide // n), F32),
            pltpu.VMEM((n, 8, wide // n), F32),
            pltpu.VMEM((all_rows, lanes), F32),
            pltpu.VMEM((hops, rows, tile), BF16),
            pltpu.VMEM((hops, rows, tile), BF16),
            pltpu.VMEM((2, wide, lanes), BF16),
            pltpu.VMEM(normed.shape, BF16),
            dma((subs,)),
            dma,
            pltpu.VMEM((chips, 2, wrows, lanes), BF16),
            pltpu.VMEM((chips, 2, wrows, lanes), BF16),
            pltpu.VMEM((chips, 2, wrows, lanes), BF16),
            pltpu.VMEM((chips, small_rows, lanes), F32),
            pltpu.VMEM((chips, small_rows, lanes), F32),
            pltpu.VMEM((all_rows, lanes), F32),
            pltpu.VMEM((chips, all_rows, lanes), F32),
            dma((hops,)), dma((hops,)), dma((hops,)), dma((hops,)),
            few, few, few, few, few, few, few, few, dma, dma, few, few, dma((n,)), dma((n,)),
        ],
        compiler_params=pltpu.CompilerParams(
            collective_id=2, has_side_effects=True, vmem_limit_bytes=60 << 20
        ),
        name="tail_sums",
    )(dx, dz, w_full, normed, dwx, dwdt, *singles)


def mid_kernel(n, tile, lag, gated_ref, w_hbm, hid_ref, tea_ref, scale_ref, z_hbm, scan_hbm,
               out_ref, go_ref, dwo_hbm, dscan_hbm, dz_hbm,
               zr, zl, w_ref, wloads, dwo_ref, part_ref, piece_ref, z_ref, scan_ref, acc_ref, dz_ref, loads, stores, wstores,
               r_send, r_recv, l_send, l_recv, ar_send, ar_recv, al_send, al_recv):
    t = lax.axis_index("tensor")
    rows, wide = hid_ref.shape
    tokens, lanes = acc_ref.shape
    waves = wide // tile
    right, left = dict(tensor=lax.rem(t + 1, n)), dict(tensor=lax.rem(t + n - 1, n))

    barrier = pltpu.get_barrier_semaphore()
    for peer in (right, left):
        pl.semaphore_signal(barrier, inc=1, device_id=peer, device_id_type=MESH)
    pl.semaphore_wait(barrier, 2)

    def load(i):
        return pltpu.make_async_copy((z_hbm, scan_hbm)[i], (z_ref, scan_ref)[i], loads.at[i])

    def load_tile(w):
        here = pl.ds(pl.multiple_of(w * tile, tile), tile)
        return pltpu.make_async_copy(w_hbm.at[here, :], w_ref.at[here, :], wloads.at[w])

    @pl.loop(0, waves)
    def _(w):
        load_tile(w).start()

    for i in range(2):
        load(i).start()

    def r_copy(i):
        return mesh_copy(zr.at[i], zr.at[i], r_send.at[i], r_recv.at[i], **right)

    def l_copy(i):
        return mesh_copy(zl.at[i], zl.at[i], l_send.at[i], l_recv.at[i], **left)

    def rows_of(o):
        return pl.ds(pl.multiple_of(o * rows, rows), rows)

    def cols_of(w):
        return pl.ds(pl.multiple_of(w * tile, tile), tile)

    def ar_copy(o, w):
        ref = piece_ref.at[rows_of(o), cols_of(w)]
        return mesh_copy(ref, ref, ar_send.at[o * waves + w], ar_recv.at[o * waves + w], **right)

    def al_copy(o, w):
        ref = piece_ref.at[rows_of(o), cols_of(w)]
        return mesh_copy(ref, ref, al_send.at[o * waves + w], al_recv.at[o * waves + w], **left)

    def stream(i, hops, start, buf, copy, owner_of):
        w, k = i // n, i % n

        @pl.when(jnp.logical_and(jnp.logical_and(i >= 0, w < waves), k < hops))
        def _():
            slot = w * (n - 1) + k
            here = part_ref[rows_of(owner_of(k)), cols_of(w)]

            @pl.when(start)
            def _():
                buf[slot] = here.astype(BF16)

            @pl.when(jnp.logical_not(start))
            def _():
                copy(slot).wait_recv()
                buf[slot] = (here + buf[slot].astype(F32)).astype(BF16)

            copy(slot).start()

    def ready(o):
        from_left = jnp.where(o > 0, n - 1 - o + lag * o, 0)
        from_right = jnp.where(o < n - 1, o + lag * (n - 1 - o), 0)
        return jnp.maximum(from_left, from_right)

    def host_ready(o):
        return max((n - 1 - o + lag * o) * (o > 0), (o + lag * (n - 1 - o)) * (o < n - 1))

    def finish(w):
        cols = cols_of(w)
        go_ref[:, cols] = part_ref[rows_of(t), cols]

        @pl.when(t > 0)
        def _():
            slot = w * (n - 1) + n - 1 - t
            r_copy(slot).wait_recv()
            go_ref[:, cols] = go_ref[:, cols] + zr[slot].astype(F32)

        @pl.when(t < n - 1)
        def _():
            slot = w * (n - 1) + t
            l_copy(slot).wait_recv()
            go_ref[:, cols] = go_ref[:, cols] + zl[slot].astype(F32)

        result = hid_ref[:, cols].astype(F32) + go_ref[:, cols]
        out_ref[:, cols] = result.astype(BF16)
        grad = scale_ref[...] * (result - tea_ref[:, cols].astype(F32))
        go_ref[:, cols] = grad
        piece_ref[rows_of(t), cols] = grad.astype(BF16)

        @pl.when(t < n - 1)
        def _():
            ar_copy(t, w).start()

        @pl.when(t > 0)
        def _():
            al_copy(t, w).start()

    def stored(i, o):
        src = (acc_ref, dz_ref)[i].at[rows_of(o), :]
        return pltpu.make_async_copy(src, (dscan_hbm, dz_hbm)[i].at[rows_of(o), :], stores.at[i, o])

    def stored_weight(w):
        here = pl.ds(pl.multiple_of(w * tile, tile), tile)
        return pltpu.make_async_copy(dwo_ref.at[w], dwo_hbm.at[here, :], wstores.at[w])

    def gate(o):
        z = z_ref[rows_of(o), :]
        s = 1.0 / (1.0 + jnp.exp(-z))
        z_ref[rows_of(o), :] = z * s
        scan_ref[rows_of(o), :] = scan_ref[rows_of(o), :] * (s * (1.0 + z * (1.0 - s)))

    def backward(w):
        tn = (((0,), (0,)), ((), ()))
        dwo_ref[w] = lax.dot_general(
            piece_ref[:, cols_of(w)], gated_ref[...], tn, preferred_element_type=F32
        ).astype(BF16)
        stored_weight(w).start()

        @pl.loop(0, n)
        def _(o):
            here = rows_of(o)
            d_gated = jnp.dot(piece_ref[here, cols_of(w)], w_ref[cols_of(w), :], preferred_element_type=F32)

            @pl.when(w == 0)
            def _():
                acc_ref[here, :] = d_gated

            @pl.when(jnp.logical_and(w > 0, w < waves - 1))
            def _():
                acc_ref[here, :] = acc_ref[here, :] + d_gated

            @pl.when(w == waves - 1)
            def _():
                total = acc_ref[here, :] + d_gated
                acc_ref[here, :] = total * z_ref[here, :]
                dz_ref[here, :] = (total * scan_ref[here, :]).astype(BF16)
                stored(0, o).start()
                stored(1, o).start()

    arrived = jnp.int32(0)
    for o in range(n):
        arrived = jnp.maximum(arrived, host_ready(o) + lag * jnp.abs(t - o))

    def step(g, _):
        @pl.when(jnp.logical_and(g % n == 0, g < n * waves))
        def _():
            cols = cols_of(g // n)
            nt = (((1,), (1,)), ((), ()))
            load_tile(g // n).wait()

            @pl.loop(0, n)
            def _(o):
                part_ref[rows_of(o), cols] = lax.dot_general(
                    gated_ref[rows_of(o), :], w_ref[cols, :], nt, preferred_element_type=F32
                )

        stream(g - lag * t, n - 1 - t, t == 0, zr, r_copy, lambda k: n - 1 - k)
        stream(g - lag * (n - 1 - t), t, t == n - 1, zl, l_copy, lambda k: k)

        own = g - ready(t)

        @pl.when(jnp.logical_and(own >= 0, jnp.logical_and(own % n == 0, own // n < waves)))
        def _():
            finish(own // n)

        @pl.loop(0, n)
        def _(o):
            i = g - ready(o) - lag * jnp.abs(t - o)
            w = i // n

            @pl.when(jnp.logical_and(o != t, jnp.logical_and(i >= 0, jnp.logical_and(i % n == 0, w < waves))))
            def _():
                @pl.when(o < t)
                def _():
                    ar_copy(o, w).wait_recv()

                    @pl.when(t < n - 1)
                    def _():
                        ar_copy(o, w).start()

                @pl.when(o > t)
                def _():
                    al_copy(o, w).wait_recv()

                    @pl.when(t > 0)
                    def _():
                        al_copy(o, w).start()

        @pl.when(g == 1)
        def _():
            for i in range(2):
                load(i).wait()

        @pl.when(jnp.logical_and(g >= 1, g <= n))
        def _():
            gate(g - 1)

        done = g - arrived

        @pl.when(jnp.logical_and(done >= 0, jnp.logical_and(done % n == 0, done // n < waves)))
        def _():
            backward(done // n)

        return 0

    steps = max(host_ready(o) + lag * abs(o - d) for o in range(n) for d in range(n)) + n * (waves - 1) + 1
    lax.fori_loop(0, max(steps, n + 1), step, 0)

    @pl.loop(0, (n - 1) * waves)
    def _(i):
        @pl.when(i % (n - 1) < n - 1 - t)
        def _():
            r_copy(i).wait_send()

        @pl.when(i % (n - 1) < t)
        def _():
            l_copy(i).wait_send()

    @pl.loop(0, n * waves)
    def _(i):
        o, w = i // waves, i % waves

        @pl.when(jnp.logical_and(o <= t, t < n - 1))
        def _():
            ar_copy(o, w).wait_send()

        @pl.when(jnp.logical_and(o >= t, t > 0))
        def _():
            al_copy(o, w).wait_send()

    @pl.loop(0, waves)
    def _(w):
        stored_weight(w).wait()

    @pl.loop(0, n)
    def _(o):
        stored(0, o).wait()
        stored(1, o).wait()


def middle(gated, w_out, hidden, teacher, scale, z_gate, scan_out):
    n = lax.axis_size("tensor")
    rows, wide = hidden.shape
    tokens, lanes = gated.shape
    tile = 256
    waves = wide // tile
    hops = (n - 1) * waves
    vmem, hbm = pl.BlockSpec(memory_space=pltpu.VMEM), pl.BlockSpec(memory_space=pl.ANY)
    dma = pltpu.SemaphoreType.DMA
    return pl.pallas_call(
        functools.partial(mid_kernel, n, tile, 2),
        out_shape=[
            jax.ShapeDtypeStruct((rows, wide), BF16),
            jax.ShapeDtypeStruct((rows, wide), F32),
            jax.ShapeDtypeStruct((wide, lanes), BF16),
            jax.ShapeDtypeStruct((tokens, lanes), F32),
            jax.ShapeDtypeStruct((tokens, lanes), BF16),
        ],
        in_specs=[vmem, hbm] + [vmem] * 3 + [hbm] * 2,
        out_specs=[vmem] * 2 + [hbm] * 3,
        scratch_shapes=[
            pltpu.VMEM((hops, rows, tile), BF16),
            pltpu.VMEM((hops, rows, tile), BF16),
            pltpu.VMEM((wide, lanes), BF16),
            dma((waves,)),
            pltpu.VMEM((waves, tile, lanes), BF16),
            pltpu.VMEM((tokens, wide), F32),
            pltpu.VMEM((tokens, wide), BF16),
            pltpu.VMEM((tokens, lanes), F32),
            pltpu.VMEM((tokens, lanes), F32),
            pltpu.VMEM((tokens, lanes), F32),
            pltpu.VMEM((tokens, lanes), BF16),
            dma((2,)), dma((2, n)), dma((waves,)),
            dma((hops,)), dma((hops,)), dma((hops,)), dma((hops,)),
            dma((n * waves,)), dma((n * waves,)), dma((n * waves,)), dma((n * waves,)),
        ],
        compiler_params=pltpu.CompilerParams(
            collective_id=1, has_side_effects=True, vmem_limit_bytes=60 << 20
        ),
        name="middle",
    )(gated, w_out, hidden, teacher, scale, z_gate, scan_out)


def front_kernel(n, dps, seqs, subs, lag, hid_ref, gain_ref, seg_ref, win_ref, wsm_ref, taps_ref, keep_ref,
                 x_out, z_out, nrm_out, w_out, conv_out, low_out, total_ref, gfull, ws_ref, natural_ref,
                 rows_ref, gain_tile, cnt_tile, grecv, cnt_one, cnt_two, x_ref, z_ref, nrm_ref, w_ref, conv_ref, low_ref,
                 mix_send, mix_recv, mix_own, mix_rows_ref, mixed_ref, outs, ms, mr, ns, nr,
                 ar_send, ar_recv, al_send, al_recv, gs, gr, c1s, c1r, c2s, c2r, hs, hr, ls,
                 chip_send, chip_recv, core_send, core_recv):
    dp, seq, t = place()
    core, hi = dp % 2, dp // 2
    chips = dps // 2 * seqs
    chip = hi * seqs + seq
    rows, wide = hid_ref.shape
    part = rows // subs
    share = wide // n
    wrows = win_ref.shape[1]
    tile = 512
    gap = max(subs, lag)
    partner = dict(dp=hi * 2 + 1 - core)
    right, left = dict(tensor=lax.rem(t + 1, n)), dict(tensor=lax.rem(t + n - 1, n))

    def owner(q, c):
        return (q // seqs * 2 + c) * seqs + q % seqs

    def to_chip(q):
        return dict(dp=q // seqs * 2 + core, seq=q % seqs)

    barrier = pltpu.get_barrier_semaphore()
    pl.semaphore_signal(barrier, inc=1, device_id=partner, device_id_type=MESH)
    for ahead in range(1, chips):
        pl.semaphore_signal(barrier, inc=1, device_id=to_chip(lax.rem(chip + ahead, chips)), device_id_type=MESH)
    for ahead in range(1, n):
        pl.semaphore_signal(barrier, inc=1, device_id=dict(tensor=lax.rem(t + ahead, n)), device_id_type=MESH)
    pl.semaphore_wait(barrier, chips + n - 1)

    def at(o, s):
        return pl.ds(pl.multiple_of(o * rows + s * part, part), part)

    def ar_copy(o, s):
        ref = rows_ref.at[at(o, s), :]
        return mesh_copy(ref, ref, ar_send.at[o * subs + s], ar_recv.at[o * subs + s], **right)

    def al_copy(o, s):
        ref = rows_ref.at[at(o, s), :]
        return mesh_copy(ref, ref, al_send.at[o * subs + s], al_recv.at[o * subs + s], **left)

    def g_copy(p, slot):
        return mesh_copy(gain_tile, grecv.at[slot], gs.at[p], gr.at[slot], tensor=p)

    def block(kind, p):
        if kind == 0:
            return w_ref.at[:, pl.ds(pl.multiple_of(p * wrows, wrows), wrows), :]
        return ws_ref.at[p]

    stored = (win_ref, wsm_ref)

    def chip_copy(kind, q, p):
        return mesh_copy(stored[kind], block(kind, p), chip_send.at[kind, q], chip_recv.at[kind, p], **to_chip(q))

    def core_copy(kind, p, own):
        src = stored[kind] if own else block(kind, p)
        return mesh_copy(src, block(kind, p), core_send.at[kind, p], core_recv.at[kind, p], **partner)

    mine = owner(chip, core)

    def count_one():
        return mesh_copy(cnt_tile, cnt_one, c1s, c1r, **partner)

    def count_two(q, slot):
        return mesh_copy(cnt_one, cnt_two.at[slot], c2s.at[q], c2r.at[slot], **to_chip(q))

    def edge_copy():
        last = x_ref.at[pl.ds(x_ref.shape[0] - 8, 8), :]
        return mesh_copy(last, x_ref.at[pl.ds(0, 8), :], hs, hr, seq=lax.rem(seq + 1, seqs))

    def mix_copy(p, slot):
        return mesh_copy(mix_send.at[p], mix_recv.at[slot], ms.at[p], mr.at[slot], tensor=p)

    def sum_copy(p, slot):
        return mesh_copy(mixed_ref.at[slot], mixed_ref.at[slot], ns.at[p], nr.at[slot], tensor=p)

    def written(i):
        src = (w_ref, nrm_ref, z_ref, x_ref, conv_ref, low_ref)[i]
        return pltpu.make_async_copy(src, (w_out, nrm_out, z_out, x_out, conv_out, low_out)[i], outs.at[i])

    def local_copy():
        return pltpu.make_async_copy(wsm_ref, block(1, mine), ls)

    gain_tile[...] = jnp.broadcast_to(gain_ref[...].astype(F32), gain_tile.shape)
    cnt_tile[...] = jnp.full(cnt_tile.shape, jnp.sum((seg_ref[...] != 0).astype(F32)))
    for ahead in range(1, n):
        g_copy(lax.rem(t + ahead, n), t).start()
    count_one().start()
    rows_ref[pl.ds(pl.multiple_of(t * rows, rows), rows), :] = hid_ref[...]

    @pl.loop(0, subs)
    def _(s):
        @pl.when(t < n - 1)
        def _():
            ar_copy(t, s).start()

        @pl.when(t > 0)
        def _():
            al_copy(t, s).start()

    def share_out(kind):
        for ahead in range(1, chips):
            chip_copy(kind, lax.rem(chip + ahead, chips), mine).start()
        core_copy(kind, mine, True).start()

    share_out(1)
    share_out(0)
    local_copy().start()
    w_ref[:, pl.ds(pl.multiple_of(mine * wrows, wrows), wrows), :] = win_ref[...]

    gfull[...] = jnp.zeros_like(gfull)
    for ahead in range(1, n):
        p = lax.rem(t + ahead, n)
        g_copy(p, p).wait_recv()
    grecv[t] = gain_tile[...]
    for p in range(n):
        gfull[:, p * share:(p + 1) * share] = grecv[p]
    count_one().wait_recv()
    count_one().wait_send()
    cnt_one[...] = cnt_one[...] + cnt_tile[...]
    for ahead in range(1, chips):
        count_two(lax.rem(chip + ahead, chips), chip).start()

    def normalize(o):
        @pl.loop(0, subs)
        def _(s):
            here = at(o, s)
            values = rows_ref[here, :].astype(F32)
            inv = lax.rsqrt(jnp.mean(values * values, axis=1, keepdims=True) + EPS)
            nrm_ref[here, :] = (values * inv * gfull[0:1, :]).astype(BF16)

    def project(o):
        here = pl.ds(pl.multiple_of(o * rows, rows), rows)
        for k, dst in enumerate((x_ref, z_ref)):
            lanes = dst.shape[1]
            width = min(tile, lanes)
            there = pl.ds(pl.multiple_of(o * rows + 8 - 8 * k, 8), rows)

            @pl.loop(0, lanes // width)
            def _(j):
                cols = pl.ds(pl.multiple_of(j * width, width), width)
                dst[there, cols] = jnp.dot(nrm_ref[here, :], w_ref[k, :, cols], preferred_element_type=F32)

    lanes = low_ref.shape[1]
    width = min(tile, lanes)
    piece = min(64, rows)
    taps = keep_ref.shape[1]

    def convolve(o):
        @pl.loop(0, rows // piece * (lanes // width))
        def _(i):
            base = o * rows + i // (lanes // width) * piece
            here = pl.ds(pl.multiple_of(base, piece), piece)
            cols = pl.ds(pl.multiple_of(i % (lanes // width) * width, width), width)
            span = x_ref[pl.ds(pl.multiple_of(base, piece), piece + 8), cols]
            keep = keep_ref[here, :]
            total = jnp.broadcast_to(taps_ref[taps:taps + 1, cols], (piece, width))
            for j in range(taps):
                first = 8 - (taps - 1) + j
                total = total + taps_ref[j:j + 1, cols] * span[first:first + piece] * keep[:, j:j + 1]
            conv_ref[here, cols] = total
            low_ref[here, cols] = (total / (1.0 + jnp.exp(-total))).astype(BF16)

    groups, depth = ws_ref.shape[0], ws_ref.shape[1]
    live = natural_ref.shape[0] // groups

    def mix_rows(o):
        convolve(o)
        nt = (((1,), (1,)), ((), ()))
        low = low_ref[pl.ds(pl.multiple_of(o * rows, rows), rows), :]
        weights = ws_ref[...].reshape(groups * depth, lanes)
        mix = lax.dot_general(weights, low, nt, preferred_element_type=F32)
        for p in range(groups):
            mix_rows_ref[p * live:(p + 1) * live, :] = mix[p * depth:p * depth + live]

        @pl.when(o != t)
        def _():
            mix_send[o] = mix_rows_ref[...].astype(BF16)
            mix_copy(o, t).start()

        @pl.when(o == t)
        def _():
            mix_own[...] = mix_rows_ref[...]

    def turn(d, o):
        final = jnp.where(o == 0, (n - 1) * gap + 1, (n - 2 - o) * gap + lag)
        return jnp.where(d == n - 1, final, (d - o) * gap)

    weights_at = (n - 1) * gap

    def step(g, _):
        @pl.when(g == 0)
        def _():
            normalize(t)

        @pl.when(g == weights_at)
        def _():
            for kind in (1, 0):
                for ahead in range(1, chips):
                    q = lax.rem(chip + ahead, chips)
                    chip_copy(kind, q, owner(q, core)).wait_recv()
                    core_copy(kind, owner(q, core), False).start()
            for kind in (1, 0):
                for q in range(chips):
                    core_copy(kind, owner(q, 1 - core), True).wait_recv()
            project(t)

        @pl.loop(0, n)
        def _(o):
            s_right = g - turn(t, o)
            s_left = g - turn(n - 1 - t, n - 1 - o)

            @pl.when(jnp.logical_and(o < t, jnp.logical_and(s_right >= 0, s_right < subs)))
            def _():
                ar_copy(o, s_right).wait_recv()

                @pl.when(t < n - 1)
                def _():
                    ar_copy(o, s_right).start()

            @pl.when(jnp.logical_and(o > t, jnp.logical_and(s_left >= 0, s_left < subs)))
            def _():
                al_copy(o, s_left).wait_recv()

                @pl.when(t > 0)
                def _():
                    al_copy(o, s_left).start()

            landed = jnp.where(o < t, s_right, s_left) - subs + 1

            @pl.when(jnp.logical_and(o != t, landed == 0))
            def _():
                normalize(o)

            ripe = jnp.where(g == weights_at, landed >= 0, jnp.logical_and(g > weights_at, landed == 0))

            @pl.when(jnp.logical_and(o != t, ripe))
            def _():
                project(o)

        return 0

    steps = weights_at + 1 + subs
    lax.fori_loop(0, steps, step, 0)

    @pl.when(seq < seqs - 1)
    def _():
        edge_copy().start()

    @pl.when(seq == 0)
    def _():
        x_ref[0:8, :] = jnp.zeros((8, x_ref.shape[1]), F32)

    for i in range(3):
        written(i).start()

    @pl.when(seq > 0)
    def _():
        edge_copy().wait_recv()

    @pl.when(seq < seqs - 1)
    def _():
        edge_copy().wait_send()

    written(3).start()
    local_copy().wait()
    @pl.loop(0, n)
    def _(i):
        mix_rows(lax.rem(t + 1 + i, n))

    for i in range(4, 6):
        written(i).start()
    for ahead in range(1, n):
        p = lax.rem(t + ahead, n)
        mix_copy(p, p).wait_recv()
        mix_own[...] = mix_own[...] + mix_recv[p].astype(F32)
    mixed_ref[t] = mix_own[...].astype(BF16)
    for ahead in range(1, n):
        sum_copy(lax.rem(t + ahead, n), t).start()
    total_ref[...] = cnt_one[...]
    for ahead in range(1, chips):
        q = lax.rem(chip + ahead, chips)
        count_two(q, q).wait_recv()
        total_ref[...] = total_ref[...] + cnt_two[q]
    for ahead in range(1, n):
        p = lax.rem(t + ahead, n)
        sum_copy(p, p).wait_recv()
    for o in range(n):
        natural_ref[:, o * rows:(o + 1) * rows] = mixed_ref[o].astype(F32)
    for ahead in range(1, n):
        p = lax.rem(t + ahead, n)
        mix_copy(p, t).wait_send()
        sum_copy(p, t).wait_send()
    for i in range(6):
        written(i).wait()
    for kind in range(2):
        for ahead in range(1, chips):
            chip_copy(kind, lax.rem(chip + ahead, chips), mine).wait_send()
        for q in range(chips):
            core_copy(kind, owner(q, core), False).wait_send()
    for ahead in range(1, chips):
        count_two(lax.rem(chip + ahead, chips), chip).wait_send()
    for ahead in range(1, n):
        g_copy(lax.rem(t + ahead, n), t).wait_send()

    @pl.loop(0, n * subs)
    def _(i):
        o, s = i // subs, i % subs

        @pl.when(jnp.logical_and(o <= t, t < n - 1))
        def _():
            ar_copy(o, s).wait_send()

        @pl.when(jnp.logical_and(o >= t, t > 0))
        def _():
            al_copy(o, s).wait_send()


def front(hidden, gain, segments, w_in, w_small, taps, keeps, x_cols):
    n, dps, seqs = (lax.axis_size(axis) for axis in ("tensor", "dp", "seq"))
    parts = dps * seqs
    chips = parts // 2
    rows, wide = hidden.shape
    lanes = w_in.shape[2]
    tokens = rows * n
    mixed = parts * x_cols
    subs = max(1, rows // 64)
    vmem, hbm = pl.BlockSpec(memory_space=pltpu.VMEM), pl.BlockSpec(memory_space=pl.ANY)
    dma = pltpu.SemaphoreType.DMA
    many, few, peers = dma((n * subs,)), dma((chips,)), dma((n,))
    return pl.pallas_call(
        functools.partial(front_kernel, n, dps, seqs, subs, 2),
        out_shape=[
            jax.ShapeDtypeStruct((tokens + 8, lanes), F32),
            jax.ShapeDtypeStruct((tokens, lanes), F32),
            jax.ShapeDtypeStruct((tokens, wide), BF16),
            jax.ShapeDtypeStruct((2, wide, lanes), BF16),
            jax.ShapeDtypeStruct((tokens, lanes), F32),
            jax.ShapeDtypeStruct((tokens, lanes), BF16),
            jax.ShapeDtypeStruct((8, 128), F32),
            jax.ShapeDtypeStruct((8, wide), F32),
            jax.ShapeDtypeStruct((parts,) + w_small.shape, BF16),
            jax.ShapeDtypeStruct((parts * x_cols, tokens), F32),
        ],
        in_specs=[vmem] * 7,
        out_specs=[hbm] * 6 + [vmem] * 4,
        scratch_shapes=[
            pltpu.VMEM((tokens, wide), BF16),
            pltpu.VMEM((8, gain.shape[1]), F32),
            pltpu.VMEM((8, 128), F32),
            pltpu.VMEM((n, 8, gain.shape[1]), F32),
            pltpu.VMEM((8, 128), F32),
            pltpu.VMEM((chips, 8, 128), F32),
            pltpu.VMEM((tokens + 8, lanes), F32),
            pltpu.VMEM((tokens, lanes), F32),
            pltpu.VMEM((tokens, wide), BF16),
            pltpu.VMEM((2, wide, lanes), BF16),
            pltpu.VMEM((tokens, lanes), F32),
            pltpu.VMEM((tokens, lanes), BF16),
            pltpu.VMEM((n, mixed, rows), BF16),
            pltpu.VMEM((n, mixed, rows), BF16),
            pltpu.VMEM((mixed, rows), F32),
            pltpu.VMEM((mixed, rows), F32),
            pltpu.VMEM((n, mixed, rows), BF16),
            dma((6,)), peers, peers, peers, peers,
            many, many, many, many, peers, peers, dma, dma, few, few, dma, dma, dma,
            dma((2, chips)), dma((2, parts)), dma((2, parts)), dma((2, parts)),
        ],
        compiler_params=pltpu.CompilerParams(
            collective_id=3, has_side_effects=True, vmem_limit_bytes=60 << 20
        ),
        name="front",
    )(hidden, gain, segments, w_in, w_small, taps, keeps)


def mixback_kernel(n, seqs, part_ref, e_hbm, conv_hbm, x_hbm, low_hbm, dpl_hbm, step_ref, wx_ref, taps_ref, keep_ref,
                   dx_hbm, dwx_ref, dwdt_ref, dconvw_ref,
                   e_ref, conv_ref, x_ref, low_ref, dpl_ref, dx_ref, dcv_ref, got, own, done, edge_out, edge_in,
                   loads, store, ms, mr, ns, nr, es, er):
    seq, t = lax.axis_index("seq"), lax.axis_index("tensor")
    rows = part_ref.shape[2]
    tokens, lanes = low_ref.shape
    taps = keep_ref.shape[1]
    width = min(512, lanes)
    piece = min(64, rows)
    across = lanes // width
    pieces = tokens // piece * across
    ahead_seq, behind_seq = lax.rem(seq + 1, seqs), lax.rem(seq + seqs - 1, seqs)

    barrier = pltpu.get_barrier_semaphore()
    for ahead in range(1, n):
        pl.semaphore_signal(barrier, inc=1, device_id=dict(tensor=lax.rem(t + ahead, n)), device_id_type=MESH)
    if seqs > 1:
        for peer in (ahead_seq, behind_seq):
            pl.semaphore_signal(barrier, inc=1, device_id=dict(seq=peer), device_id_type=MESH)
    pl.semaphore_wait(barrier, n - 1 + (2 if seqs > 1 else 0))

    def load(i):
        src = (conv_hbm, dpl_hbm, e_hbm, low_hbm, x_hbm)[i]
        return pltpu.make_async_copy(src, (conv_ref, dpl_ref, e_ref, low_ref, x_ref)[i], loads.at[i])

    def mix_copy(p, slot):
        return mesh_copy(part_ref.at[p], got.at[slot], ms.at[p], mr.at[slot], tensor=p)

    def sum_copy(p, slot):
        return mesh_copy(done.at[slot], done.at[slot], ns.at[p], nr.at[slot], tensor=p)

    def edge_copy():
        return mesh_copy(edge_out, edge_in, es, er, seq=behind_seq)

    for ahead in range(1, n):
        mix_copy(lax.rem(t + ahead, n), t).start()
    for i in range(5):
        load(i).start()

    dcv_ref[0:8, :] = jnp.zeros((8, lanes), F32)
    dcv_ref[tokens + 8:, :] = jnp.zeros((8, lanes), F32)
    load(1).wait()
    step = step_ref[0:dwdt_ref.shape[0], :].astype(BF16)
    tn = (((0,), (0,)), ((), ()))

    @pl.loop(0, across)
    def _(j):
        cols = pl.ds(pl.multiple_of(j * width, width), width)
        dwdt_ref[:, cols] = jnp.dot(step, dpl_ref[:, cols], preferred_element_type=F32)

    own[...] = part_ref[t].astype(F32)
    for ahead in range(1, n):
        p = lax.rem(t + ahead, n)
        mix_copy(p, p).wait_recv()
        own[...] = own[...] + got[p].astype(F32)
    done[t] = own[...].astype(BF16)
    for ahead in range(1, n):
        sum_copy(lax.rem(t + ahead, n), t).start()

    load(0).wait()

    @pl.loop(0, pieces)
    def _(i):
        here = pl.ds(pl.multiple_of(i // across * piece, piece), piece)
        cols = pl.ds(pl.multiple_of(i % across * width, width), width)
        v = conv_ref[here, cols]
        s = 1.0 / (1.0 + jnp.exp(-v))
        conv_ref[here, cols] = s * (1.0 + v * (1.0 - s))

    for i in range(2, 5):
        load(i).wait()
    for ahead in range(1, n):
        p = lax.rem(t + ahead, n)
        sum_copy(p, p).wait_recv()

    dwx_ref[...] = jnp.zeros_like(dwx_ref)
    dconvw_ref[...] = jnp.zeros_like(dconvw_ref)

    @pl.loop(0, n)
    def _(o):
        @pl.loop(0, across)
        def _(j):
            cols = pl.ds(pl.multiple_of(j * width, width), width)
            here = pl.ds(pl.multiple_of(o * rows, rows), rows)
            mixed = lax.dot_general(done[o], wx_ref[:, cols], tn, preferred_element_type=F32)
            dcv = (e_ref[here, cols] + mixed) * conv_ref[here, cols]
            dcv_ref[pl.ds(pl.multiple_of(o * rows + 8, 8), rows), cols] = dcv
            dwx_ref[:, cols] = dwx_ref[:, cols] + jnp.dot(done[o], low_ref[here, cols], preferred_element_type=F32)

    def shifted(base, size, cols):
        span = dcv_ref[pl.ds(base, size + 8), cols]
        keep = keep_ref[pl.ds(base, size + 8), :]
        total = jnp.zeros((size, span.shape[1]), F32)
        for j in range(taps):
            late = taps - 1 - j
            total = total + taps_ref[j:j + 1, cols] * (span * keep[:, j:j + 1])[late:late + size]
        return total

    if seqs > 1:
        edge_out[...] = shifted(0, 8, slice(None))

        @pl.when(seq > 0)
        def _():
            edge_copy().start()

    @pl.loop(0, pieces)
    def _(i):
        base = pl.multiple_of(i // across * piece, piece)
        cols = pl.ds(pl.multiple_of(i % across * width, width), width)
        dx_ref[pl.ds(base, piece), cols] = shifted(pl.multiple_of(base + 8, 8), piece, cols).astype(BF16)
        here = dcv_ref[pl.ds(pl.multiple_of(base + 8, 8), piece), cols]
        keep = keep_ref[pl.ds(pl.multiple_of(base + 8, 8), piece), :]
        span = x_ref[pl.ds(base, piece + 8), cols]
        for j in range(taps):
            first = 8 - (taps - 1) + j
            tap = jnp.sum(here * keep[:, j:j + 1] * span[first:first + piece], axis=0, keepdims=True)
            dconvw_ref[j:j + 1, cols] = dconvw_ref[j:j + 1, cols] + tap
        dconvw_ref[taps:taps + 1, cols] = dconvw_ref[taps:taps + 1, cols] + jnp.sum(here, axis=0, keepdims=True)

    if seqs > 1:
        @pl.when(seq < seqs - 1)
        def _():
            edge_copy().wait_recv()
            last = shifted(tokens - 16 + 8, 16, slice(None))
            dx_ref[tokens - 16:, :] = (last + jnp.concatenate([jnp.zeros_like(edge_in), edge_in[...]], 0)).astype(BF16)

        @pl.when(seq > 0)
        def _():
            edge_copy().wait_send()

    out = pltpu.make_async_copy(dx_ref, dx_hbm, store)
    out.start()
    for ahead in range(1, n):
        p = lax.rem(t + ahead, n)
        mix_copy(p, t).wait_send()
        sum_copy(p, t).wait_send()
    out.wait()


def mixback(part, e, conv_sum, x_rows, x_low, d_pre_low, mix_t, w_x, taps, keeps, rank):
    n, seqs = lax.axis_size("tensor"), lax.axis_size("seq")
    tokens, lanes = x_low.shape
    mixed, rows = part.shape[1:]
    vmem, hbm = pl.BlockSpec(memory_space=pltpu.VMEM), pl.BlockSpec(memory_space=pl.ANY)
    dma = pltpu.SemaphoreType.DMA
    peers = dma((n,))
    return pl.pallas_call(
        functools.partial(mixback_kernel, n, seqs),
        out_shape=[
            jax.ShapeDtypeStruct((tokens, lanes), BF16),
            jax.ShapeDtypeStruct((mixed, lanes), F32),
            jax.ShapeDtypeStruct((rank, lanes), F32),
            jax.ShapeDtypeStruct((8, lanes), F32),
        ],
        in_specs=[vmem] + [hbm] * 5 + [vmem] * 4,
        out_specs=[hbm] + [vmem] * 3,
        scratch_shapes=[
            pltpu.VMEM((tokens, lanes), F32),
            pltpu.VMEM((tokens, lanes), F32),
            pltpu.VMEM((tokens + 8, lanes), F32),
            pltpu.VMEM((tokens, lanes), BF16),
            pltpu.VMEM((tokens, lanes), BF16),
            pltpu.VMEM((tokens, lanes), BF16),
            pltpu.VMEM((tokens + 16, lanes), F32),
            pltpu.VMEM((n, mixed, rows), BF16),
            pltpu.VMEM((mixed, rows), F32),
            pltpu.VMEM((n, mixed, rows), BF16),
            pltpu.VMEM((8, lanes), F32),
            pltpu.VMEM((8, lanes), F32),
            dma((5,)), dma, peers, peers, peers, peers, dma, dma,
        ],
        compiler_params=pltpu.CompilerParams(
            collective_id=4, has_side_effects=True, vmem_limit_bytes=60 << 20
        ),
        name="mix_backward",
    )(part, e, conv_sum, x_rows, x_low, d_pre_low, mix_t, w_x, taps, keeps)


def on_device(
    hidden_in,
    teacher,
    segment_ids,
    norm_gain,
    input_projection_weight,
    conv_weight,
    conv_bias,
    xproj_weight,
    dtproj_weight,
    dt_bias,
    a_log,
    d_skip,
    output_projection_weight,
):
    tok_rows = segment_ids.shape[0]
    row_share = hidden_in.shape[0]
    model_width = hidden_in.shape[1]
    conv_taps = conv_weight.shape[0]
    chan_lanes = conv_weight.shape[1]
    back_rows = conv_taps - 1
    row_start = lax.axis_index("tensor") * row_share
    valid_mask = (segment_ids != 0).astype(jnp.float32)
    parts = lax.axis_size(("dp", "seq"))
    x_cols, dt_rows = xproj_weight.shape[1], dtproj_weight.shape[0]
    w_small = jnp.concatenate(
        [
            xproj_weight.T,
            jnp.zeros((SMALL_ROWS - x_cols, chan_lanes), BF16),
            dtproj_weight,
            jnp.zeros((-(SMALL_ROWS + dt_rows) % 16, chan_lanes), BF16),
        ],
        0,
    )
    seg_float = segment_ids.astype(F32)
    prev_seg = jnp.where(lax.axis_index("seq") > 0, seg_float[:1], jnp.zeros((back_rows,), F32))
    ext_seg = jnp.concatenate([prev_seg, seg_float], 0)
    tap_keeps = []
    for offset in range(conv_taps):
        tap_keeps.append((ext_seg[offset : offset + tok_rows] == seg_float).astype(F32)[:, None])
    taps = jnp.concatenate(
        [conv_weight.astype(F32), conv_bias.astype(F32)[None], jnp.zeros((7 - conv_taps, chan_lanes), F32)], 0
    )
    x_rows, z_gate, normalized_rows, w_in, conv_sum, x_low, total, gain_rows, w_small, mix_t = front(
        hidden_in,
        norm_gain[None],
        segment_ids.reshape(8, -1),
        jnp.swapaxes(input_projection_weight, 0, 1),
        w_small,
        taps,
        jnp.concatenate(tap_keeps, 1),
        x_cols,
    )
    w_out_rows, z_gate = lax.optimization_barrier((output_projection_weight.T, z_gate))
    w_out = lax.all_gather(w_out_rows, ("dp", "seq"), axis=0, tiled=True)
    total_count = total[0, 0]
    w_x = w_small[:, :x_cols].reshape(parts * x_cols, chan_lanes)
    w_dt = w_small[:, SMALL_ROWS : SMALL_ROWS + dt_rows].reshape(parts * dt_rows, chan_lanes)
    share_rows = hidden_in.astype(F32)
    full_gain = gain_rows[0]
    inv_share = lax.rsqrt(jnp.mean(share_rows * share_rows, axis=1, keepdims=True) + EPS)
    rank_width = w_dt.shape[0]
    same_doc = (seg_float == ext_seg[back_rows - 1 : back_rows - 1 + tok_rows]).astype(jnp.float32)
    rates = -jnp.exp(a_log) * LOG2E
    block = 128
    first_reset = jnp.min(jnp.where(same_doc == 0, jnp.arange(tok_rows), tok_rows))
    alive = (jnp.arange(0, tok_rows, block) <= first_reset).astype(jnp.int32)
    y_local, marks, state_last, stepd, inject, step_size, step_slope = fwd(
        mix_t, w_dt, dt_bias[None], x_low, same_doc[:, None], rates, tb=block, w=1024
    )

    def reach():
        return jnp.exp2(rates * jnp.sum(stepd, axis=0)[None])

    state_in = carried(state_last, reach, "seq", 1)
    scan_out, marks, gated_output_rows = correct(
        rank_width, alive, y_local, stepd, mix_t, rates, marks, state_in, x_low, d_skip[None], z_gate, tb=block, w=1024
    )
    valid_share = lax.dynamic_slice_in_dim(valid_mask, row_start, row_share, 0)
    total_tokens = float(tok_rows * lax.axis_size(("dp", "seq")))
    scale = (total_tokens / total_count * valid_share)[:, None]
    output, grad_out, d_wout, d_scan, d_z = middle(
        gated_output_rows, w_out, hidden_in, teacher, scale, z_gate, scan_out
    )
    adjoint_first = entry(rank_width, alive, stepd, d_scan, mix_t, rates, tb=block, w=1024)
    adjoint_in = carried(adjoint_first, reach, "seq", -1)
    d_pre_low, d_direct, d_rank_t, d_b_part, d_c_part, a_log_part, dt_bias_part, d_skip_part = bwd(
        stepd, inject, d_scan, mix_t, rates, marks, adjoint_in,
        step_size, step_slope, x_low, d_skip[None], w_dt, tb=block
    )
    part = jnp.concatenate(
        [
            jnp.sum(d_rank_t, axis=0),
            jnp.sum(d_b_part, axis=0).reshape(tok_rows, N).T,
            jnp.sum(d_c_part, axis=0).reshape(tok_rows, N).T,
        ],
        0,
    )
    part = part.astype(BF16).reshape(part.shape[0], -1, row_share).transpose(1, 0, 2)
    edge = jnp.zeros((8, conv_taps), F32)
    d_x, d_wx, d_wdt, conv_parts = mixback(
        part, d_direct, conv_sum, x_rows, x_low, d_pre_low, mix_t, w_x, taps,
        jnp.concatenate([edge] + [jnp.concatenate(tap_keeps, 1)] + [edge], 0),
        rank_width,
    )
    d_norm_share, g_in, g_small, g_whole = tail(
        d_x, d_z, w_in, normalized_rows, d_wx, d_wdt, a_log_part, conv_parts, dt_bias_part, d_skip_part
    )
    g_in = jnp.swapaxes(g_in, 0, 1)
    inner_sum = jnp.sum(d_norm_share * full_gain[None] * share_rows, axis=1, keepdims=True)
    inv_cube = inv_share * inv_share * inv_share
    input_grad = (
        grad_out
        + inv_share * full_gain[None] * d_norm_share
        - share_rows * inv_cube * inner_sum / model_width
    )
    rank_here = rank_width // parts
    state_here = 2 * N // parts
    g_x_rank = g_small[:rank_here].T
    g_dt = g_small[rank_here : 2 * rank_here]
    g_x_state = g_small[2 * rank_here : 2 * rank_here + state_here].T
    g_out = lax.psum_scatter(d_wout, ("dp", "seq"), scatter_dimension=0, tiled=True).astype(F32).T
    g_gain = g_whole[N + 16, : norm_gain.shape[0]] / norm_gain.astype(F32)
    g_alog, g_conv_w, g_conv_b = g_whole[:N], g_whole[N : N + conv_taps], g_whole[N + conv_taps]
    g_bias, g_skip = g_whole[N + 8], g_whole[N + 9]
    return (
        output,
        input_grad,
        g_gain,
        g_in,
        g_conv_w,
        g_conv_b,
        g_x_rank,
        g_x_state,
        g_dt,
        g_bias,
        g_alog,
        g_skip,
        g_out,
    )


def solution(mesh):
    placed = (
        P(("dp", "seq", "tensor"), None),
        P(("dp", "seq", "tensor"), None),
        P(("dp", "seq")),
        P("tensor"),
        P(("dp", "seq"), None, "tensor"),
        P(None, "tensor"),
        P("tensor"),
        P("tensor", ("dp", "seq")),
        P(("dp", "seq"), "tensor"),
        P("tensor"),
        P(None, "tensor"),
        P("tensor"),
        P("tensor", ("dp", "seq")),
    )
    return jax.shard_map(
        on_device,
        mesh=mesh,
        in_specs=placed,
        out_specs=(
            P(("dp", "seq", "tensor"), None),
            P(("dp", "seq", "tensor"), None),
            P("tensor"),
            P(("dp", "seq"), None, "tensor"),
            P(None, "tensor"),
            P("tensor"),
            P("tensor", ("dp", "seq")),
            P("tensor", ("dp", "seq")),
            P(("dp", "seq"), "tensor"),
            P("tensor"),
            P(None, "tensor"),
            P("tensor"),
            P("tensor", ("dp", "seq")),
        ),
        check_vma=False,
    )
```
